128 devices in a mesh: gx: 8 (over y, core), gy: 8 (over z, x_hi), gz: 2 (over x_lo).
Axes of the slice: x: 4 (x_hi: 2, x_lo: 2; x = x_hi * 2 + x_lo), y: 4, z: 4, core: 2. Of those that a mesh axis runs over, the one named last changes fastest.
Arguments:
- mode_fields: float32 [2, 3, 64, 256, 512], P(None, None, 'gx', 'gy', 'gz'), may hold values from -6 to 6
- design: float32 [64, 256, 512], P('gx', 'gy', 'gz'), may hold values from 0.05 to 1
- solid_mask: int32 [64, 256, 512], P('gx', 'gy', 'gz'), may hold values 0 or 1
- eigenvalues: float32 [6], replicated, may hold values from 0.5 to 5
- mode_order: int32 [6], replicated, may hold values from 0 to 5, each once
Outputs:
- sensitivity: float32 [2, 64, 256, 512], P(None, 'gx', 'gy', 'gz')
The draws below stay inside these ranges and needn't reach their ends.
Inputs may be any that keep to these rules, and one draw needn't show every extreme that they name: `mode_order`: each of 0 to 5 appears once.
All inputs are finite; a program needn't handle non-finite values. No bound on the sum of `solid_mask` on one device may be relied on, other than what follows from the above.
Results may differ from the reference program's by a relative error of at most 0.0003.
Values sent between devices are 32-bit elements; how exact they have to be, the bound alone decides.
No kernel may reach another device: no remote copies, remote signals or barrier semaphores. Data moves between devices by JAX's collectives and lax.ppermute only.
A program may use at most 128 MiB of HBM per device.

```python
import math
import jax
import jax.numpy as jnp
import numpy as np
from jax import lax

CX = 8
MODES = 2
SAVED = 6
ITERS = 4
NX = 64
NY = 256
NZ = 512


def set_ends(drawn, rng, least, top_value):
    longest = drawn.shape.index(max(drawn.shape))
    spots = []
    for shift in (0, 1):
        where = [jax.random.randint(jax.random.fold_in(rng, axis), (), 0, length) for axis, length in enumerate(drawn.shape)]
        where[longest] = (where[longest] + shift) % drawn.shape[longest]
        spots.append(tuple(where))
    return drawn.at[spots[0]].set(least).at[spots[1]].set(top_value)


def block_levels(rng, shape, shards, least, largest):
    factor_of = 1.0
    for axis_at, shards_of in shards:
        steps = jax.random.uniform(jax.random.fold_in(jax.random.fold_in(rng, 6), axis_at), (shards_of,), jnp.float32, least / len(shards), largest / len(shards))
        factor_of = factor_of * jnp.repeat(jnp.exp(steps), shape[axis_at] // shards_of).reshape((-1,) + (1,) * (len(shape) - 1 - axis_at))
    return factor_of


def centred(key, extent, scale, reach, pieces=(), kind=jnp.bfloat16):
    entries = scale * jax.random.normal(key, extent, jnp.float32)
    if pieces:
        entries = entries * block_levels(key, extent, pieces, -0.22, 0.18)
    return jnp.clip(entries, -reach, reach).astype(kind)


def setup_inputs(seed: int = 0) -> dict:
    streams_of = jax.random.split(jax.random.key(seed), 6)
    mode_fields = centred(streams_of[0], (MODES, 3, NX, NY, NZ), 1.0, 6.0, ((2, 8), (3, 8), (4, 2)), jnp.float32)
    design = jnp.clip(0.05 + 0.95 * jax.random.uniform(streams_of[1], (NX, NY, NZ), jnp.float32) ** block_levels(streams_of[1], (NX, NY, NZ), ((0, 8), (1, 8), (2, 2)), -0.2, 0.2), 0.05, 1.0)
    solid_mask = set_ends((jax.random.randint(streams_of[2], (NX, NY, NZ), 0, 4) < 3).astype(jnp.int32), jax.random.fold_in(streams_of[2], 1), 0, 1)
    eigenvalues = jnp.clip(jnp.exp(jax.random.uniform(streams_of[3], (SAVED,), jnp.float32, math.log(0.5), math.log(5.0))), 0.5, 5.0)
    mode_order = jax.random.permutation(streams_of[4], SAVED).astype(jnp.int32)
    return dict(mode_fields=mode_fields, design=design, solid_mask=solid_mask, eigenvalues=eigenvalues, mode_order=mode_order)


poisson = 0.3
radius_sq = 3.0
stiff_floor = 0.001

def hex_stiffness():
    lame_first = poisson / ((1.0 + poisson) * (1.0 - 2.0 * poisson))
    shear = 0.5 / (1.0 + poisson)
    elastic = np.zeros((6, 6))
    elastic[:3, :3] = lame_first
    for row in range(3):
        elastic[row, row] = lame_first + 2.0 * shear
        elastic[row + 3, row + 3] = shear
    points = [0.5 - 0.5 / np.sqrt(3.0), 0.5 + 0.5 / np.sqrt(3.0)]
    stiffness = np.zeros((24, 24))
    for point_x in points:
        for point_y in points:
            for point_z in points:
                coords = (point_x, point_y, point_z)
                grads = np.zeros((3, 8))
                for corner in range(8):
                    bits = (corner >> 2 & 1, corner >> 1 & 1, corner & 1)
                    for direction in range(3):
                        value = 1.0
                        for other in range(3):
                            if other == direction:
                                value *= 1.0 if bits[other] else -1.0
                            else:
                                value *= coords[other] if bits[other] else 1.0 - coords[other]
                        grads[direction, corner] = value
                strain = np.zeros((6, 24))
                strain[0, 0:8] = grads[0]
                strain[1, 8:16] = grads[1]
                strain[2, 16:24] = grads[2]
                strain[3, 0:8] = grads[1]
                strain[3, 8:16] = grads[0]
                strain[4, 8:16] = grads[2]
                strain[4, 16:24] = grads[1]
                strain[5, 0:8] = grads[2]
                strain[5, 16:24] = grads[0]
                stiffness += 0.125 * strain.T @ elastic @ strain
    return stiffness.astype(np.float32)

def neighbour_total(padded):
    total = padded[2:, 1:-1, 1:-1] + padded[:-2, 1:-1, 1:-1]
    total = total + padded[1:-1, 2:, 1:-1] + padded[1:-1, :-2, 1:-1]
    return total + padded[1:-1, 1:-1, 2:] + padded[1:-1, 1:-1, :-2]

def filter_scale():
    shape = (NX, NY, NZ)
    counts = jnp.full(shape, 6.0, jnp.float32)
    for axis_pos, length in enumerate(shape):
        place = lax.broadcasted_iota(jnp.int32, shape, axis_pos)
        counts = counts - (place == 0).astype(jnp.float32) - (place == length - 1).astype(jnp.float32)
    return 1.0 / (1.0 + radius_sq * counts)

def sweeps(source, scale):
    state = source * scale
    for step in range(ITERS):
        state = (source + radius_sq * neighbour_total(jnp.pad(state, 1))) * scale
    return state

def reference(mode_fields, design, solid_mask, eigenvalues, mode_order):
    mask = solid_mask.astype(jnp.float32)
    scale = filter_scale()
    physical = sweeps(mask * design, scale)
    stiffness = jnp.asarray(hex_stiffness(), dtype=jnp.float32)
    padded = jnp.pad(mode_fields, ((0, 0), (0, 0), (0, 1), (0, 1), (0, 1)))
    results = []
    for mode in range(MODES):

        def slab_energy(slab):
            start = (slab * CX).astype(jnp.int32)
            zero = jnp.zeros((), jnp.int32)
            block = lax.dynamic_slice(padded, (jnp.int32(mode), zero, start, zero, zero), (1, 3, CX + 1, NY + 1, NZ + 1))[0]
            corners = []
            for corner in range(8):
                off_x, off_y, off_z = (corner >> 2 & 1, corner >> 1 & 1, corner & 1)
                corners.append(block[:, off_x:off_x + CX, off_y:off_y + NY, off_z:off_z + NZ])
            element = jnp.stack(corners, axis=1).reshape(24, CX * NY * NZ)
            kinetic = jnp.dot(stiffness, element, precision=lax.Precision.HIGHEST, preferred_element_type=jnp.float32)
            energy_k = lax.optimization_barrier(jnp.sum(element * kinetic, axis=0)).reshape(CX, NY, NZ)
            energy_m = (0.125 * lax.optimization_barrier(jnp.sum(element * element, axis=0))).reshape(CX, NY, NZ)
            return (energy_k, energy_m)
        energy_k, energy_m = lax.map(slab_energy, jnp.arange(NX // CX, dtype=jnp.int32))
        energy_k = energy_k.reshape(NX, NY, NZ)
        energy_m = energy_m.reshape(NX, NY, NZ)
        eigen_value = eigenvalues[mode_order[mode]]
        raw = 3.0 * (1.0 - stiff_floor) * physical * physical * energy_k - eigen_value * energy_m
        results.append(mask * sweeps(raw, scale))
    return jnp.stack(results, axis=0)
```

```python
import jax
import jax.numpy as jnp
from jax import lax
from jax.experimental import pallas as pl
from jax.experimental.pallas import tpu as pltpu
from jax.sharding import PartitionSpec as P

ITERS = 4
MODES = 2
CX, CY, CZ = 8, 32, 256
W = ITERS
PX = CX + 2 * W
PY = CY + 8
PZ = CZ + 128
LANES = 128

poisson = 0.3
radius_sq = 3.0
stiff_floor = 0.001
LAME = poisson / ((1.0 + poisson) * (1.0 - 2.0 * poisson))
SHEAR = 0.5 / (1.0 + poisson)

F32 = jnp.float32


def iota(shape, dim):
    return lax.broadcasted_iota(jnp.int32, shape, dim)


def pos(ref):
    return ref[0], ref[1], ref[2]


def fill_table(table, where):
    gx, gy, gz = where
    shape = (PY, PZ)
    y, z = iota(shape, 0), iota(shape, 1)
    y = jnp.where(y < CY + W, y, y - PY) + gy * CY
    z = jnp.where(z < CZ + LANES // 2, z, z - PZ)
    near = (z >= -W) & (z < CZ + W)
    z = z + gz * CZ
    inside = near & (y >= 0) & (y < 8 * CY) & (z >= 0) & (z < 2 * CZ)
    count = 4.0
    for place, last in ((y, 8 * CY - 1), (z, 2 * CZ - 1)):
        count = count - (place == 0).astype(F32) - (place == last).astype(F32)
    table[0] = jnp.zeros(shape, F32)
    table[1] = jnp.where(inside, 1.0 / (1.0 + radius_sq * (count + 1.0)), 0.0)
    table[2] = jnp.where(inside, 1.0 / (1.0 + radius_sq * (count + 2.0)), 0.0)


def row_of(gx, plane):
    x = gx * CX + plane - W
    out = (x < 0) | (x > 8 * CX - 1)
    end = (x == 0) | (x == 8 * CX - 1)
    return jnp.where(out, 0, jnp.where(end, 1, 2))


def sweep_plane(table, gx, p, sb, old):
    mid = old[p]
    total = old[p - 1] + old[p + 1]
    total = total + pltpu.roll(mid, 1, 0) + pltpu.roll(mid, PY - 1, 0)
    total = total + pltpu.roll(mid, 1, 1) + pltpu.roll(mid, PZ - 1, 1)
    return sb[p] + (radius_sq * table[row_of(gx, p)]) * total


def pack_x1(design, mask, modes, src, down, up):
    for x in range(CX):
        plane = design[x] * mask[x].astype(F32)
        src[x] = plane
        if x < W:
            down[x] = plane
        if x >= CX - W:
            up[x - (CX - W)] = plane
    for m in range(MODES):
        for c in range(3):
            down[W + 3 * m + c] = modes[m, c, 0]


def pick_plane(own, above, below, p):
    if p < W:
        return below, p
    if p < W + CX:
        return own, p - W
    return above, p - W - CX


def pack_y1(where, src, modes, above, below, down, up):
    gx, gy, gz = pos(where)
    low = iota((8, CZ), 0) < 4
    for q in range(8):
        a, i = pick_plane(src, above, below, q)
        b, j = pick_plane(src, above, below, q + 8)
        down[q] = jnp.where(low, a[i, 0:8, :], pltpu.roll(b[j, 0:8, :], 4, 0))
        up[q] = jnp.where(low, pltpu.roll(b[j, 24:32, :], 4, 0), a[i, 24:32, :])
    keep = jnp.where(gx < 7, 1.0, 0.0)
    for m in range(MODES):
        for c in range(3):
            for x in range(CX + 1):
                n = c * (CX + 1) + x
                if x < CX:
                    row = modes[m, c, x, 0:1, :]
                else:
                    row = above[W + 3 * m + c, 0:1, :] * keep
                down[8 + 4 * m + n // 8, n % 8 : n % 8 + 1, :] = row
        down[8 + 4 * m + 3, 3:8, :] = jnp.zeros((5, CZ), F32)


def halo_tile(y_above, y_below, p, lanes=slice(None)):
    a, b = y_above[p % 8, :, lanes], y_below[p % 8, :, lanes]
    if p >= 8:
        a, b = pltpu.roll(a, 4, 0), pltpu.roll(b, 4, 0)
    return jnp.where(iota(a.shape, 0) < 4, a, b)


def pack_z1(where, src, modes, above, below, y_above, y_below, out):
    gx, gy, gz = pos(where)
    start = pl.multiple_of((1 - gz) * LANES, LANES)
    edge = pl.ds(start, LANES)
    lane = iota((PY, LANES), 1)
    sub = iota((8, LANES), 0)
    acc = jnp.zeros((PY, LANES), F32)
    for p in range(PX):
        a, i = pick_plane(src, above, below, p)
        tile = jnp.concatenate([a[i, :, edge], halo_tile(y_above, y_below, p, edge)], axis=0)
        tile = pltpu.roll(tile, (4 * p + 4 * (1 - gz)) % LANES, 1)
        acc = jnp.where((lane >= 4 * p) & (lane < 4 * p + 4), tile, acc)
    keep_x = jnp.where(gx < 7, 1.0, 0.0)
    keep_y = jnp.where(gy < 7, 1.0, 0.0)
    for m in range(MODES):
        for c in range(3):
            for x in range(CX + 1):
                n = c * (CX + 1) + x
                t = 8 + 4 * m + n // 8
                rim = y_above[t, n % 8 : n % 8 + 1, 0:LANES] * keep_y
                rim = jnp.where(sub == 0, rim, 0.0)
                body = modes[m, c, x] if x < CX else above[W + 3 * m + c, :, 0:LANES] * keep_x
                tile = jnp.concatenate([body, rim], axis=0)
                to = 64 + 32 * m + n
                acc = jnp.where(lane == to, pltpu.roll(tile, to, 1), acc)
    out[...] = acc


def energy_terms(prev, cur):
    (paa, pad, pda, pdd), (caa, cad, cda, cdd) = prev, cur
    u, v, w = 0, 1, 2
    aad = [cad[i] + pad[i] for i in range(3)]
    ada = [cda[i] + pda[i] for i in range(3)]
    add = [cdd[i] + pdd[i] for i in range(3)]
    daa = [caa[i] - paa[i] for i in range(3)]
    dad = [cad[i] - pad[i] for i in range(3)]
    dda = [cda[i] - pda[i] for i in range(3)]
    ddd = [cdd[i] - pdd[i] for i in range(3)]

    def sq(x):
        return x * x

    trace = sq(daa[u] + ada[v] + aad[w])
    lines = sq(dda[v] + dad[w]) + sq(dda[u] + add[w]) + sq(dad[u] + add[v])
    diag = sq(daa[u]) + sq(ada[v]) + sq(aad[w])
    shear = sq(ada[u] + daa[v]) + sq(aad[u] + daa[w]) + sq(aad[v] + ada[w])
    mixed = sq(dda[u]) + sq(dda[v]) + sq(dad[u]) + sq(dad[w]) + sq(add[v]) + sq(add[w])
    cross = sq(add[u] + dad[v]) + sq(add[u] + dda[w]) + sq(dad[v] + dda[w])
    cubic = sq(ddd[u]) + sq(ddd[v]) + sq(ddd[w])
    return (
        LAME * (trace + lines * (1.0 / 3.0))
        + SHEAR * (2.0 * diag + shear + mixed + cross * (1.0 / 3.0))
        + ((LAME + 4.0 * SHEAR) / 9.0) * cubic
    )


def main_kernel(
    eigenvalues, order, where, src, modes, above, below, y_above, y_below, z_in,
    low, high, table, sb, one, two,
):
    gx, gy, gz = pos(where)
    fill_table(table, (gx, gy, gz))
    back = (LANES - 4) * gz
    for p in range(PX):
        a, i = pick_plane(src, above, below, p)
        scale = table.at[row_of(gx, p)]
        sb[p, 0:CY, 0:CZ] = a[i] * scale[0:CY, 0:CZ]
        sb[p, CY:PY, 0:CZ] = halo_tile(y_above, y_below, p) * scale[CY:PY, 0:CZ]
        sb[p, :, CZ:PZ] = pltpu.roll(z_in[...], (back + LANES - 4 * p) % LANES, 1) * scale[:, CZ:PZ]
    old = sb
    for k in range(1, ITERS + 1):
        new = one if k % 2 else two

        def body(p, carry, old=old, new=new):
            new[p] = sweep_plane(table, gx, p, sb, old)
            return carry

        lax.fori_loop(k, PX - k, body, 0)
        old = new
    physical = old

    keep_x = jnp.where(gx < 7, 1.0, 0.0)
    keep_y = jnp.where(gy < 7, 1.0, 0.0)
    keep_z = jnp.where(gz < 1, 1.0, 0.0)
    last_lane = iota((8, CZ), 1) == CZ - 1
    last_sub = iota((8, CZ), 0) == 7
    stiff = 3.0 * (1.0 - stiff_floor) / 16.0

    def mode_step(m, carry):
        lam = eigenvalues[order[m]] * (0.125 * 0.25)

        def along_z(x, c, chunk):
            n = c * (CX + 1) + x
            t, s = n // 8, n % 8
            if chunk == CY // 8:
                here = jnp.broadcast_to(y_above[8 + 4 * m + t, s : s + 1, :] * keep_y, (8, CZ))
            elif x < CX:
                here = modes[m, c, x, 8 * chunk : 8 * chunk + 8, :]
            else:
                here = above[W + 3 * m + c, 8 * chunk : 8 * chunk + 8, :] * keep_x
            col = pltpu.roll(
                z_in[8 * chunk : 8 * chunk + 8, :], LANES - 1 - (64 + 32 * m + n), 1
            ) * keep_z
            if chunk == CY // 8:
                col = jnp.broadcast_to(col[0:1], (8, LANES))
            col = jnp.concatenate([col, col], axis=1)
            after = jnp.where(last_lane, col, pltpu.roll(here, CZ - 1, 1))
            return here + after, after - here

        for chunk in range(CY // 8):
            prev = None
            prev_mass = None
            for x in range(CX + 1):
                aa, ad, da, dd = [], [], [], []
                mass = None
                for c in range(3):
                    a0, d0 = along_z(x, c, chunk)
                    a1, d1 = along_z(x, c, chunk + 1)

                    def next_row(t, n):
                        return jnp.where(last_sub, pltpu.roll(n, 7, 0), pltpu.roll(t, 7, 0))

                    a1, d1 = next_row(a0, a1), next_row(d0, d1)
                    aa.append(a0 + a1)
                    da.append(a1 - a0)
                    ad.append(d0 + d1)
                    dd.append(d1 - d0)
                    for part in (aa[-1], da[-1], ad[-1], dd[-1]):
                        mass = part * part if mass is None else mass + part * part
                cur = (aa, ad, da, dd)
                if x:
                    rows = slice(8 * chunk, 8 * chunk + 8)
                    phys = physical[W + x - 1, rows, 0:CZ]
                    energy = energy_terms(prev, cur)
                    raw = stiff * phys * phys * energy - lam * (mass + prev_mass)
                    if x - 1 < W:
                        low[x - 1, m, rows, :] = raw
                    else:
                        high[x - 1 - W, m, rows, :] = raw
                prev, prev_mass = cur, mass
        return carry

    lax.fori_loop(0, MODES, mode_step, 0)


def raw_plane(low, high, above, below, p):
    if p < W:
        return below, p
    if p < 2 * W:
        return low, p - W
    if p < 3 * W:
        return high, p - 2 * W
    return above, p - 3 * W


def pack_y2(low, high, above, below, down, up):
    first = iota((8, CZ), 0) < 4
    for p in range(PX):
        a, i = raw_plane(low, high, above, below, p)
        down[p] = jnp.where(first, a[i, 0, 0:8, :], pltpu.roll(a[i, 1, 0:8, :], 4, 0))
        up[p] = jnp.where(first, pltpu.roll(a[i, 0, 24:32, :], 4, 0), a[i, 1, 24:32, :])


def raw_halo(y_above, y_below, p, m, lanes=slice(None)):
    a, b = y_above[p, :, lanes], y_below[p, :, lanes]
    if m == 0:
        b = pltpu.roll(b, 4, 0)
    else:
        a = pltpu.roll(a, 4, 0)
    return jnp.where(iota(a.shape, 0) < 4, a, b)


def pack_z2(where, low, high, above, below, y_above, y_below, out):
    gx, gy, gz = pos(where)
    edge = pl.ds(pl.multiple_of((1 - gz) * LANES, LANES), LANES)
    lane = iota((PY, LANES), 1)
    acc = jnp.zeros((PY, LANES), F32)
    for p in range(PX):
        a, i = raw_plane(low, high, above, below, p)
        for m in range(MODES):
            tile = jnp.concatenate([a[i, m, :, edge], raw_halo(y_above, y_below, p, m, edge)], axis=0)
            to = 64 * m + 4 * p
            tile = pltpu.roll(tile, (to + 4 * (1 - gz)) % LANES, 1)
            acc = jnp.where((lane >= to) & (lane < to + 4), tile, acc)
    out[...] = acc


def final_kernel(
    where, mask, low, high, above, below, y_above, y_below, z_in,
    out, table, sb0, sb1, one0, one1, two0, two1,
):
    gx, gy, gz = pos(where)
    fill_table(table, (gx, gy, gz))
    back = (LANES - 4) * gz
    sbs, ones, twos = (sb0, sb1), (one0, one1), (two0, two1)
    for p in range(PX):
        a, i = raw_plane(low, high, above, below, p)
        scale = table.at[row_of(gx, p)]
        for m in range(MODES):
            sb = sbs[m]
            sb[p, 0:CY, 0:CZ] = a[i, m] * scale[0:CY, 0:CZ]
            sb[p, CY:PY, 0:CZ] = raw_halo(y_above, y_below, p, m) * scale[CY:PY, 0:CZ]
            turn = (back + 2 * LANES - 64 * m - 4 * p) % LANES
            sb[p, :, CZ:PZ] = pltpu.roll(z_in[...], turn, 1) * scale[:, CZ:PZ]
    old = sbs
    for k in range(1, ITERS + 1):
        new = ones if k % 2 else twos

        def body(p, carry, old=old, new=new, k=k):
            for m in range(MODES):
                plane = sweep_plane(table, gx, p, sbs[m], old[m])
                if k < ITERS:
                    new[m][p] = plane
                else:
                    out[m, p - W] = plane[0:CY, 0:CZ] * mask[p - W].astype(F32)
            return carry

        lax.fori_loop(k, PX - k, body, 0)
        old = new


def call(kernel, outs, specs, args, scratch=(), name=None):
    shapes = tuple(jax.ShapeDtypeStruct(s, F32) for s in outs)
    return pl.pallas_call(
        kernel,
        grid=(1,),
        out_shape=shapes if len(shapes) > 1 else shapes[0],
        in_specs=specs,
        scratch_shapes=scratch,
        compiler_params=pltpu.CompilerParams(vmem_limit_bytes=24 * 1024 * 1024),
        name=name,
    )(*args)


SMEM = pl.BlockSpec(memory_space=pltpu.SMEM)


def whole(x):
    return pl.BlockSpec(x.shape, lambda i: (0,) * x.ndim)


def ring(axis, step):
    size = lax.axis_size(axis)
    return [(i, (i + step) % size) for i in range(size)]


def shift(x, axis, step):
    return lax.ppermute(x, axis, ring(axis, step))


def local(mode_fields, design, solid_mask, eigenvalues, mode_order):
    where = jnp.stack([lax.axis_index(a) for a in ("gx", "gy", "gz")]).astype(jnp.int32)
    big = pltpu.VMEM((PX, PY, PZ), F32)
    table = pltpu.VMEM((3, PY, PZ), F32)

    first_x = pl.BlockSpec((MODES, 3, 1, CY, CZ), lambda i: (0, 0, 0, 0, 0))
    src, down, up = call(
        pack_x1, [(CX, CY, CZ), (W + 6, CY, CZ), (W, CY, CZ)],
        [whole(design), whole(solid_mask), first_x], (design, solid_mask, mode_fields), name="pack_x1",
    )
    above, below = shift(down, "gx", -1), shift(up, "gx", 1)

    first_y = pl.BlockSpec((MODES, 3, CX, 8, CZ), lambda i: (0, 0, 0, 0, 0))
    down, up = call(
        pack_y1, [(16, 8, CZ), (8, 8, CZ)],
        [SMEM, whole(src), first_y, whole(above), whole(below)],
        (where, src, mode_fields, above, below), name="pack_y1",
    )
    y_above, y_below = shift(down, "gy", -1), shift(up, "gy", 1)

    first_z = pl.BlockSpec((MODES, 3, CX, CY, LANES), lambda i: (0, 0, 0, 0, 0))
    halos = (above, below, y_above, y_below)
    edge = call(
        pack_z1, [(PY, LANES)],
        [SMEM, whole(src), first_z, *map(whole, halos)],
        (where, src, mode_fields, *halos), name="pack_z1",
    )
    z_in = shift(edge, "gz", 1)

    low, high = call(
        main_kernel, [(W, MODES, CY, CZ)] * 2,
        [SMEM, SMEM, SMEM, *map(whole, (src, mode_fields, *halos, z_in))],
        (eigenvalues, mode_order, where, src, mode_fields, *halos, z_in),
        [table, big, big, big], name="raw",
    )

    above, below = shift(low, "gx", -1), shift(high, "gx", 1)
    planes = (low, high, above, below)
    down, up = call(pack_y2, [(PX, 8, CZ)] * 2, list(map(whole, planes)), planes, name="pack_y2")
    y_above, y_below = shift(down, "gy", -1), shift(up, "gy", 1)
    args = (*planes, y_above, y_below)
    edge = call(pack_z2, [(PY, LANES)], [SMEM, *map(whole, args)], (where, *args), name="pack_z2")
    z_in = shift(edge, "gz", 1)
    return call(
        final_kernel, [(MODES, CX, CY, CZ)],
        [SMEM, *map(whole, (solid_mask, *args, z_in))],
        (where, solid_mask, *args, z_in),
        [table] + [big] * 6, name="filter",
    )


def solution(mesh):
    return jax.shard_map(
        local,
        mesh=mesh,
        in_specs=(
            P(None, None, "gx", "gy", "gz"),
            P("gx", "gy", "gz"),
            P("gx", "gy", "gz"),
            P(),
            P(),
        ),
        out_specs=P(None, "gx", "gy", "gz"),
        check_vma=False,
    )
```

```python
import jax
import jax.numpy as jnp
from jax import lax
from jax.experimental import pallas as pl
from jax.experimental.pallas import tpu as pltpu
from jax.sharding import PartitionSpec as P

ITERS = 4
MODES = 2
CX, CY, CZ = 8, 32, 256
W = ITERS
PX = CX + 2 * W
PY = CY + 8
NODES = CX + 1
LANES = 128

poisson = 0.3
radius_sq = 3.0
stiff_floor = 0.001
LAME = poisson / ((1.0 + poisson) * (1.0 - 2.0 * poisson))
SHEAR = 0.5 / (1.0 + poisson)

F32 = jnp.float32


def iota(shape, dim):
    return lax.broadcasted_iota(jnp.int32, shape, dim)


def pos(ref):
    return ref[0], ref[1], ref[2]


def sub_lane():
    return iota((8, LANES), 0), iota((8, LANES), 1)


def total_of(terms):
    terms = [t for t in terms if t is not None]
    while len(terms) > 1:
        pairs = [terms[i] + terms[i + 1] for i in range(0, len(terms) - 1, 2)]
        terms = pairs + ([terms[-1]] if len(terms) % 2 else [])
    return terms[0]


def scales(count, inside):
    outside = jnp.zeros(count.shape, F32)
    end = jnp.where(inside, radius_sq / (1.0 + radius_sq * (count + 1.0)), 0.0)
    mid = jnp.where(inside, radius_sq / (1.0 + radius_sq * (count + 2.0)), 0.0)
    return outside, end, mid


def yz_scales(y, z, gy, gz):
    y, z = y + gy * CY, z + gz * CZ
    inside = (y >= 0) & (y < 8 * CY)
    count = 4.0
    for place, last in ((y, 8 * CY - 1), (z, 2 * CZ - 1)):
        count = count - (place == 0).astype(F32) - (place == last).astype(F32)
    return scales(count, inside)


def kind_of(gx, plane):
    x = gx * CX + plane - W
    out = (x < 0) | (x > 8 * CX - 1)
    end = (x == 0) | (x == 8 * CX - 1)
    return jnp.where(out, 0, jnp.where(end, 1, 2))


def fill_bulk(table, gy, gz):
    shape = (CY, CZ)
    for i, part in enumerate(yz_scales(iota(shape, 0), iota(shape, 1), gy, gz)):
        table[i] = part


def fill_strips(table, gy, gz):
    shape = (16, CZ)
    row = iota(shape, 0)
    top = jnp.where(row < 4, row + CY, row + CY - 8)
    bottom = jnp.where(row < 12, row - 8, row - 16)
    for i, part in enumerate(yz_scales(jnp.where(row < 8, top, bottom), iota(shape, 1), gy, gz)):
        table[i] = part


def strip_scale(gx, gy):
    shape = (PY, LANES)
    row = iota(shape, 0)
    y = jnp.where(row < CY + W, row, row - PY) + gy * CY
    x = gx * CX - W + lax.div(iota(shape, 1), 8)
    inside = (y >= 0) & (y < 8 * CY) & (x >= 0) & (x < 8 * CX)
    count = 6.0
    for place, last in ((y, 8 * CY - 1), (x, 8 * CX - 1)):
        count = count - (place == 0).astype(F32) - (place == last).astype(F32)
    return jnp.where(inside, radius_sq / (1.0 + radius_sq * count), 0.0)


def tiles_of(ref, index, rows, cols):
    return [
        [ref[index + (slice(8 * i, 8 * i + 8), slice(LANES * j, LANES * j + LANES))] for j in range(cols)]
        for i in range(rows)
    ]


def along_lanes(row, lane):
    right = [pltpu.roll(t, 1, 1) for t in row]
    left = [pltpu.roll(t, LANES - 1, 1) for t in row]
    out = []
    for j in range(len(row)):
        before = right[j - 1] if j else 0.0
        after = left[j + 1] if j + 1 < len(row) else 0.0
        out.append(
            jnp.where(lane == 0, before, right[j]) + jnp.where(lane == LANES - 1, after, left[j])
        )
    return out


def along_rows(tiles, sub):
    rows, cols = len(tiles), len(tiles[0])
    down = [[pltpu.roll(t, 1, 0) for t in row] for row in tiles]
    up = [[pltpu.roll(t, 7, 0) for t in row] for row in tiles]
    out = []
    for i in range(rows):
        line = []
        for j in range(cols):
            before = down[i - 1][j] if i else 0.0
            after = up[i + 1][j] if i + 1 < rows else 0.0
            line.append(jnp.where(sub == 0, before, down[i][j]) + jnp.where(sub == 7, after, up[i][j]))
        out.append(line)
    return out


def send_edge(edges, index, tile, p, gz, lane):
    turned = pltpu.roll(tile, lax.rem(8 * p + 5 - 2 * gz, LANES), 1)
    edges[index] = jnp.where(lane == 8 * p + 4 - gz, turned, edges[index])


def bulk_sweeps(fields, where, table, source, states, ends, edges, out):
    gx, gy, gz = where
    sub, lane = sub_lane()
    sb = states[0]
    edges[...] = jnp.zeros(edges.shape, F32)
    ends[...] = jnp.zeros(ends.shape, F32)
    for p in range(PX):
        kind = kind_of(gx, p)
        for m in range(fields):
            for i in range(CY // 8):
                rows = slice(8 * i, 8 * i + 8)
                sb[m, p, rows, :] = source(m, p, i) * (table[kind, rows, :] * (1.0 / radius_sq))
    for k in range(ITERS):
        old = states[0] if k == 0 else states[1 + (k - 1) % 2]
        new = states[1 + k % 2]

        def body(p, carry, old=old, new=new, k=k):
            scale = tiles_of(table, (kind_of(gx, p),), CY // 8, 2)
            for m in range(fields):
                mid = tiles_of(old, (m, p), CY // 8, 2)
                low = tiles_of(old, (m, p - 1), CY // 8, 2)
                high = tiles_of(old, (m, p + 1), CY // 8, 2)
                base = tiles_of(sb, (m, p), CY // 8, 2)
                yy = along_rows(mid, sub)
                for i in range(CY // 8):
                    zz = along_lanes(mid[i], lane)
                    rows = slice(8 * i, 8 * i + 8)
                    for j in range(2):
                        total = (low[i][j] + high[i][j]) + (yy[i][j] + zz[j])
                        value = base[i][j] + scale[i][j] * total
                        cols = slice(LANES * j, LANES * j + LANES)
                        if k + 1 < ITERS:
                            new[m, p, rows, cols] = value
                        else:
                            out[m, p - W, rows, cols] = value
                    edge = jnp.where(gz == 0, mid[i][1], mid[i][0])
                    send_edge(edges, (m, k, rows), edge, p, gz, lane)
                for j in range(2):
                    cols = slice(LANES * j, LANES * j + LANES)
                    ends[m, k, p, 0, 0:1, cols] = mid[CY // 8 - 1][j][7:8]
                    ends[m, k, p, 1, 0:1, cols] = mid[0][j][0:1]
            return carry

        lax.fori_loop(k + 1, PX - 1 - k, body, 0)


def strip_sweeps(fields, where, table, source, ends, states, edges, out):
    gx, gy, gz = where
    sub, lane = sub_lane()
    sb = states[0]
    edges[...] = jnp.zeros(edges.shape, F32)
    wide = iota((8, CZ), 0)
    for p in range(PX):
        kind = kind_of(gx, p)
        for m in range(fields):
            halo = source(m, p) * (1.0 / radius_sq)
            sb[m, p, 0:8, :] = jnp.where(wide < 4, halo * table[kind, 0:8, :], 0.0)
            sb[m, p, 8:16, :] = jnp.where(wide < 4, 0.0, halo * table[kind, 8:16, :])
    for k in range(ITERS):
        old = states[0] if k == 0 else states[1 + (k - 1) % 2]
        new = states[1 + k % 2]

        def body(p, carry, old=old, new=new, k=k):
            scale = tiles_of(table, (kind_of(gx, p),), 2, 2)
            for m in range(fields):
                mid = tiles_of(old, (m, p), 2, 2)
                low = tiles_of(old, (m, p - 1), 2, 2)
                high = tiles_of(old, (m, p + 1), 2, 2)
                base = tiles_of(sb, (m, p), 2, 2)
                for i in range(2):
                    rows = slice(8 * i, 8 * i + 8)
                    zz = along_lanes(mid[i], lane)
                    for j in range(2):
                        cols = slice(LANES * j, LANES * j + LANES)
                        end = jnp.broadcast_to(ends[m, k, p, i, 0:1, cols], (8, LANES))
                        down = pltpu.roll(mid[i][j], 1, 0)
                        up = pltpu.roll(mid[i][j], 7, 0)
                        if i == 0:
                            down = jnp.where(sub == 4, 0.0, down) + jnp.where(sub == 0, end, 0.0)
                        else:
                            up = jnp.where(sub == 3, 0.0, up) + jnp.where(sub == 7, end, 0.0)
                        total = (low[i][j] + high[i][j]) + (down + up) + zz[j]
                        value = base[i][j] + scale[i][j] * total
                        if k + 1 < ITERS:
                            new[m, p, rows, cols] = value
                        else:
                            out[m, p - W, rows, cols] = value
                    edge = jnp.where(gz == 0, mid[i][1], mid[i][0])
                    send_edge(edges, (m, k, rows), edge, p, gz, lane)
            return carry

        lax.fori_loop(k + 1, PX - 1 - k, body, 0)


def z_sweeps(m, scale, halo, bulk_edges, strip_edges):
    sub = iota((8, LANES), 0)
    column = lax.rem(iota((PY, LANES), 1), 8)
    base = halo * (scale * (1.0 / radius_sq))
    state = base
    for k in range(ITERS):
        top, bottom = strip_edges[m, k, 0:8, :], strip_edges[m, k, 8:16, :]
        own = bulk_edges[m, k]
        fed = jnp.concatenate(
            [
                own[0:8] + jnp.where(sub < 4, bottom, 0.0),
                own[8 : CY - 8],
                own[CY - 8 : CY] + jnp.where(sub < 4, 0.0, top),
                jnp.where(sub < 4, top, bottom),
            ],
            axis=0,
        )
        total = pltpu.roll(state, 8, 1) + pltpu.roll(state, LANES - 8, 1)
        total = total + pltpu.roll(state, 1, 0) + pltpu.roll(state, PY - 1, 0)
        total = total + jnp.where(column == 0, 0.0, pltpu.roll(state, 1, 1))
        total = total + jnp.where(column == 7, 0.0, pltpu.roll(state, LANES - 1, 1))
        state = base + scale * (total + fed)
    return state


def result_tile(m, x, i, j, bulk, strips, z_state, beside, sub):
    rows, cols = slice(8 * i, 8 * i + 8), slice(LANES * j, LANES * j + LANES)
    value = bulk[m, x, rows, cols]
    if i == 0:
        value = value + jnp.where(sub < 4, strips[m, x, 8:16, cols], 0.0)
    if i == CY // 8 - 1:
        value = value + jnp.where(sub < 4, 0.0, strips[m, x, 0:8, cols])
    turned = pltpu.roll(z_state[rows], (LANES - 4 - 8 * (x + W)) % LANES, 1)
    return value + jnp.where(beside[j], turned, 0.0)


def beside_halo(gz, lane):
    return (lane < 4 * gz), (lane >= LANES - 4 * (1 - gz))


def pack_strip(gz, tile, p, acc, lane):
    first = 8 * p + 4 * gz
    turned = pltpu.roll(tile, (8 * p + 4) % LANES, 1)
    return jnp.where((lane >= first) & (lane < first + 4), turned, acc)


def edge_tiles(gz):
    return pl.ds(pl.multiple_of((1 - gz) * LANES, LANES), LANES)


def energy_terms(prev, cur):
    (paa, pad, pda, pdd), (caa, cad, cda, cdd) = prev, cur
    u, v, w = 0, 1, 2
    aad = [cad[i] + pad[i] for i in range(3)]
    ada = [cda[i] + pda[i] for i in range(3)]
    add = [cdd[i] + pdd[i] for i in range(3)]
    daa = [caa[i] - paa[i] for i in range(3)]
    dad = [cad[i] - pad[i] for i in range(3)]
    dda = [cda[i] - pda[i] for i in range(3)]
    ddd = [cdd[i] - pdd[i] for i in range(3)]

    def sq(x):
        return x * x

    trace = sq(daa[u] + ada[v] + aad[w])
    lines = sq(dda[v] + dad[w]) + sq(dda[u] + add[w]) + sq(dad[u] + add[v])
    diag = sq(daa[u]) + sq(ada[v]) + sq(aad[w])
    shear = sq(ada[u] + daa[v]) + sq(aad[u] + daa[w]) + sq(aad[v] + ada[w])
    mixed = sq(dda[u]) + sq(dda[v]) + sq(dad[u]) + sq(dad[w]) + sq(add[v]) + sq(add[w])
    cross = sq(add[u] + dad[v]) + sq(add[u] + dda[w]) + sq(dad[v] + dda[w])
    cubic = sq(ddd[u]) + sq(ddd[v]) + sq(ddd[w])
    return (
        LAME * (trace + lines * (1.0 / 3.0))
        + SHEAR * (2.0 * diag + shear + mixed + cross * (1.0 / 3.0))
        + ((LAME + 4.0 * SHEAR) / 9.0) * cubic
    )


def y_parts(pairs):
    aa = [a0 + a1 for a0, d0, a1, d1 in pairs]
    ad = [d0 + d1 for a0, d0, a1, d1 in pairs]
    da = [a1 - a0 for a0, d0, a1, d1 in pairs]
    dd = [d1 - d0 for a0, d0, a1, d1 in pairs]
    return aa, ad, da, dd


def mass_of(parts):
    return total_of([x * x for part in parts for x in part])


def z_pair(here):
    after = pltpu.roll(here, CZ - 1, 1)
    return here + after, after - here


def own_parts(load, chunk):
    sub = iota((8, CZ), 0)
    pairs = []
    for c in range(3):
        a0, d0 = z_pair(load(c, 8 * chunk))
        following = min(chunk + 1, CY // 8 - 1)
        a1, d1 = z_pair(load(c, 8 * following))

        def next_row(t, n):
            return jnp.where(sub == 7, pltpu.roll(n, 7, 0), pltpu.roll(t, 7, 0))

        pairs.append((a0, d0, next_row(a0, a1), next_row(d0, d1)))
    return y_parts(pairs)


def pack_columns(load, lane):
    first = jnp.zeros((CY, LANES), F32)
    last = first
    for m in range(MODES):
        for c in range(3):
            for x in range(CX):
                to = 32 * m + NODES * c + x
                here = lane == to
                first = jnp.where(here, pltpu.roll(load(m, c, x, 0), to, 1), first)
                last = jnp.where(here, pltpu.roll(load(m, c, x, 1), to + 1, 1), last)
    return first, last


def with_rims(packed, above, y_above, keep_x, keep_y, last):
    cols = slice(CZ - LANES, CZ) if last else slice(0, LANES)
    lane = iota((CY, LANES), 1)
    sub, short = sub_lane()
    rim = jnp.zeros((8, LANES), F32)
    for m in range(MODES):
        for c in range(3):
            to = 32 * m + NODES * c + CX
            turned = pltpu.roll(above[W + 3 * m + c, :, cols], to + last, 1)
            packed = jnp.where(lane == to, turned * keep_x, packed)
            for x in range(NODES):
                n = NODES * c + x
                to = 32 * m + n
                row = y_above[8 + 4 * m + n // 8, n % 8 : n % 8 + 1, cols]
                turned = pltpu.roll(jnp.broadcast_to(row, (8, LANES)), to + last, 1)
                rim = jnp.where((short == to) & (sub == 0), turned, rim)
    return jnp.concatenate([packed, rim * keep_y], axis=0)


def pack_x1(design, mask, modes, src, down, up):
    for x in range(CX):
        plane = design[x] * mask[x].astype(F32)
        src[x] = plane
        if x < W:
            down[x] = plane
        if x >= CX - W:
            up[x - (CX - W)] = plane
    for m in range(MODES):
        for c in range(3):
            down[W + 3 * m + c] = modes[m, c, 0]


def energy_kernel(modes, stiff, mass, columns):
    lane = iota((CY, LANES), 1)
    columns[0], columns[1] = pack_columns(
        lambda m, c, x, j: modes[m, c, x, :, LANES * j : LANES * j + LANES], lane
    )

    def mode_step(m, carry):
        for chunk in range(CY // 8):
            rows = slice(8 * chunk, 8 * chunk + 8)
            prev = prev_mass = None
            for x in range(CX):
                cur = own_parts(lambda c, r: modes[m, c, x, r : r + 8, :], chunk)
                cur_mass = mass_of(cur)
                if x:
                    stiff[m, x - 1, rows, :] = energy_terms(prev, cur)
                    mass[m, x - 1, rows, :] = cur_mass + prev_mass
                prev, prev_mass = cur, cur_mass
        return carry

    lax.fori_loop(0, MODES, mode_step, 0)


def pick_plane(own, above, below, p):
    if p < W:
        return below, p
    if p < W + CX:
        return own, p - W
    return above, p - W - CX


def pack_y1(where, src, modes, above, below, down, up):
    gx, gy, gz = pos(where)
    low = iota((8, CZ), 0) < 4
    for q in range(8):
        a, i = pick_plane(src, above, below, q)
        b, j = pick_plane(src, above, below, q + 8)
        down[q] = jnp.where(low, a[i, 0:8, :], pltpu.roll(b[j, 0:8, :], 4, 0))
        up[q] = jnp.where(low, pltpu.roll(b[j, 24:32, :], 4, 0), a[i, 24:32, :])
    keep = jnp.where(gx < 7, 1.0, 0.0)
    for m in range(MODES):
        for c in range(3):
            for x in range(NODES):
                n = c * NODES + x
                if x < CX:
                    row = modes[m, c, x, 0:1, :]
                else:
                    row = above[W + 3 * m + c, 0:1, :] * keep
                down[8 + 4 * m + n // 8, n % 8 : n % 8 + 1, :] = row
        down[8 + 4 * m + 3, 3:8, :] = jnp.zeros((5, CZ), F32)


def bulk_kernel1(
    where, src, modes, above, below, bulk, ends, edges, stiff, mass, table, sb, one, two
):
    at = pos(where)
    gx, gy, gz = at
    fill_bulk(table, gy, gz)

    def source(m, p, i):
        a, at_plane = pick_plane(src, above, below, p)
        return a[at_plane, 8 * i : 8 * i + 8, :]

    bulk_sweeps(1, at, table, source, (sb, one, two), ends, edges, bulk)
    keep = jnp.where(gx < 7, 1.0, 0.0)
    for m in range(MODES):
        for chunk in range(CY // 8):
            rows = slice(8 * chunk, 8 * chunk + 8)
            prev = own_parts(lambda c, r: modes[m, c, CX - 1, r : r + 8, :], chunk)
            cur = own_parts(lambda c, r: above[W + 3 * m + c, r : r + 8, :] * keep, chunk)
            stiff[m, rows, :] = energy_terms(prev, cur)
            mass[m, rows, :] = mass_of(cur) + mass_of(prev)


def halo_tile(y_above, y_below, p, lanes=slice(None)):
    a, b = y_above[p % 8, :, lanes], y_below[p % 8, :, lanes]
    if p >= 8:
        a, b = pltpu.roll(a, 4, 0), pltpu.roll(b, 4, 0)
    return jnp.where(iota(a.shape, 0) < 4, a, b)


def pack_z1(where, src, columns, above, below, y_above, y_below, out):
    gx, gy, gz = pos(where)
    edge = edge_tiles(gz)
    lane = iota((PY, LANES), 1)
    acc = jnp.zeros((PY, LANES), F32)
    for p in range(PX):
        a, i = pick_plane(src, above, below, p)
        tile = jnp.concatenate([a[i, :, edge], halo_tile(y_above, y_below, p, edge)], axis=0)
        acc = pack_strip(gz, tile, p, acc, lane)
    out[0] = acc
    keep_x = jnp.where(gx < 7, 1.0, 0.0)
    keep_y = jnp.where(gy < 7, 1.0, 0.0)
    out[1] = with_rims(columns[0], above, y_above, keep_x, keep_y, 0)


def strip_kernel1(
    where, modes, columns, above, y_above, y_below, ends,
    strips, edges, rim, packed, table, sb, one, two, near, far,
):
    at = pos(where)
    gx, gy, gz = at
    fill_strips(table, gy, gz)
    strip_sweeps(
        1, at, table, lambda m, p: halo_tile(y_above, y_below, p), ends, (sb, one, two), edges, strips
    )
    keep_x = jnp.where(gx < 7, 1.0, 0.0)
    keep_y = jnp.where(gy < 7, 1.0, 0.0)
    packed[...] = with_rims(columns[1], above, y_above, keep_x, keep_y, 1)
    for m in range(MODES):
        for c in range(3):
            for x in range(NODES):
                n = c * NODES + x
                row = above[W + 3 * m + c, CY - 1 : CY, :] * keep_x
                if x < CX:
                    row = modes[m, c, x, CY - 1 : CY, :]
                near[c, x : x + 1, :] = row
                far[c, x : x + 1, :] = (
                    y_above[8 + 4 * m + n // 8, n % 8 : n % 8 + 1, :] * keep_y
                )

        def parts(first):
            pairs = []
            for c in range(3):
                a0, d0 = z_pair(near[c, first : first + 8, :])
                a1, d1 = z_pair(far[c, first : first + 8, :])
                pairs.append((a0, d0, a1, d1))
            return y_parts(pairs)

        prev, cur = parts(0), parts(1)
        rim[m, 0] = energy_terms(prev, cur)
        rim[m, 1] = mass_of(cur) + mass_of(prev)


def raw_kernel(
    eigenvalues, order, where, z_in, packed, bulk, bulk_edges, strips, strip_edges,
    stiff, mass, stiff7, mass7, rim, low, high,
):
    gx, gy, gz = pos(where)
    sub, lane = sub_lane()
    z_state = z_sweeps(0, strip_scale(gx, gy), z_in[0], bulk_edges, strip_edges)
    beside = beside_halo(gz, lane)

    near, far = packed[...], z_in[1] * jnp.where(gz < 1, 1.0, 0.0)
    a0, d0 = near + far, far - near
    a1, d1 = pltpu.roll(a0, PY - 1, 0), pltpu.roll(d0, PY - 1, 0)
    parts = [(x[0][0:CY]) for x in y_parts([(a0, d0, a1, d1)])]

    def turned(t, by):
        return pltpu.roll(t, (LANES - by) % LANES, 1) if by else t

    prev = [[turned(t, NODES * c) for c in range(3)] for t in parts]
    cur = [[turned(t, NODES * c + 1) for c in range(3)] for t in parts]
    column_stiff = energy_terms(prev, cur)
    column_mass = mass_of(cur) + mass_of(prev)

    factor = 3.0 * (1.0 - stiff_floor) / 16.0
    lams = [eigenvalues[order[m]] * (0.125 * 0.25) for m in range(MODES)]
    for x in range(CX):
        for i in range(CY // 8):
            rows = slice(8 * i, 8 * i + 8)
            for j in range(2):
                cols = slice(LANES * j, LANES * j + LANES)
                phys = result_tile(0, x, i, j, bulk, strips, z_state, beside, sub)
                phys = (factor * phys) * phys
                for m in range(MODES):
                    if x < CX - 1:
                        k, e = stiff[m, x, rows, cols], mass[m, x, rows, cols]
                    else:
                        k, e = stiff7[m, rows, cols], mass7[m, rows, cols]
                    if i == CY // 8 - 1:
                        k = jnp.where(sub == 7, jnp.broadcast_to(rim[m, 0, x : x + 1, cols], (8, LANES)), k)
                        e = jnp.where(sub == 7, jnp.broadcast_to(rim[m, 1, x : x + 1, cols], (8, LANES)), e)
                    if j == 1:
                        by = LANES - 1 - (32 * m + x)
                        k = jnp.where(lane == LANES - 1, pltpu.roll(column_stiff[rows], by, 1), k)
                        e = jnp.where(lane == LANES - 1, pltpu.roll(column_mass[rows], by, 1), e)
                    raw = phys * k - lams[m] * e
                    if x < W:
                        low[x, m, rows, cols] = raw
                    else:
                        high[x - W, m, rows, cols] = raw


def raw_plane(low, high, above, below, p):
    if p < W:
        return below, p
    if p < 2 * W:
        return low, p - W
    if p < 3 * W:
        return high, p - 2 * W
    return above, p - 3 * W


def pack_y2(low, high, above, below, down, up):
    first = iota((8, CZ), 0) < 4
    for p in range(PX):
        a, i = raw_plane(low, high, above, below, p)
        down[p] = jnp.where(first, a[i, 0, 0:8, :], pltpu.roll(a[i, 1, 0:8, :], 4, 0))
        up[p] = jnp.where(first, pltpu.roll(a[i, 0, 24:32, :], 4, 0), a[i, 1, 24:32, :])


def raw_halo(y_above, y_below, m, p, lanes=slice(None)):
    a, b = y_above[p, :, lanes], y_below[p, :, lanes]
    if m == 0:
        b = pltpu.roll(b, 4, 0)
    else:
        a = pltpu.roll(a, 4, 0)
    return jnp.where(iota(a.shape, 0) < 4, a, b)


def bulk_kernel2(where, low, high, above, below, bulk, ends, edges, table, sb, one, two):
    at = pos(where)
    fill_bulk(table, at[1], at[2])

    def source(m, p, i):
        a, at_plane = raw_plane(low, high, above, below, p)
        return a[at_plane, m, 8 * i : 8 * i + 8, :]

    bulk_sweeps(MODES, at, table, source, (sb, one, two), ends, edges, bulk)


def pack_z2(where, low, high, above, below, y_above, y_below, out):
    gx, gy, gz = pos(where)
    edge = edge_tiles(gz)
    lane = iota((PY, LANES), 1)
    for m in range(MODES):
        acc = jnp.zeros((PY, LANES), F32)
        for p in range(PX):
            a, i = raw_plane(low, high, above, below, p)
            halo = raw_halo(y_above, y_below, m, p, edge)
            acc = pack_strip(gz, jnp.concatenate([a[i, m, :, edge], halo], axis=0), p, acc, lane)
        out[m] = acc


def strip_kernel2(where, y_above, y_below, ends, strips, edges, table, sb, one, two):
    at = pos(where)
    fill_strips(table, at[1], at[2])

    def source(m, p):
        return raw_halo(y_above, y_below, m, p)

    strip_sweeps(MODES, at, table, source, ends, (sb, one, two), edges, strips)


def final_kernel(where, mask, z_in, bulk, bulk_edges, strips, strip_edges, out):
    gx, gy, gz = pos(where)
    sub, lane = sub_lane()
    beside = beside_halo(gz, lane)
    scale = strip_scale(gx, gy)
    for m in range(MODES):
        z_state = z_sweeps(m, scale, z_in[m], bulk_edges, strip_edges)
        for x in range(CX):
            for i in range(CY // 8):
                rows = slice(8 * i, 8 * i + 8)
                for j in range(2):
                    cols = slice(LANES * j, LANES * j + LANES)
                    value = result_tile(m, x, i, j, bulk, strips, z_state, beside, sub)
                    out[m, x, rows, cols] = value * mask[x, rows, cols].astype(F32)


SMEM = pl.BlockSpec(memory_space=pltpu.SMEM)


def whole(x):
    return pl.BlockSpec(x.shape, lambda i: (0,) * x.ndim)


def call(kernel, name, outs, args, specs=None, scratch=(), flops=0):
    specs = specs or {}
    shapes = tuple(jax.ShapeDtypeStruct(s, F32) for s in outs)
    return pl.pallas_call(
        kernel,
        grid=(1,),
        out_shape=shapes if len(shapes) > 1 else shapes[0],
        in_specs=[specs.get(i, SMEM if a.ndim == 1 else whole(a)) for i, a in enumerate(args)],
        scratch_shapes=[pltpu.VMEM(s, F32) for s in scratch],
        compiler_params=pltpu.CompilerParams(vmem_limit_bytes=24 * 1024 * 1024),
        cost_estimate=pl.CostEstimate(flops=flops, bytes_accessed=2_000_000, transcendentals=0),
        name=name,
    )(*args)


def ring(axis, step):
    size = lax.axis_size(axis)
    return [(i, (i + step) % size) for i in range(size)]


def shift(x, axis, step):
    return lax.ppermute(x, axis, ring(axis, step))


def sweep_outs(fields):
    return (
        [(fields, CX, CY, CZ), (fields, ITERS, PX, 2, 1, CZ), (fields, ITERS, CY, LANES)],
        [(3, CY, CZ)] + [(fields, PX, CY, CZ)] * 3,
        [(fields, CX, 16, CZ), (fields, ITERS, 16, LANES)],
        [(3, 16, CZ)] + [(fields, PX, 16, CZ)] * 3,
    )


def local(mode_fields, design, solid_mask, eigenvalues, mode_order):
    where = jnp.stack([lax.axis_index(a) for a in ("gx", "gy", "gz")]).astype(jnp.int32)
    bulk_outs, bulk_scratch, strip_outs, strip_scratch = sweep_outs(1)

    block = pl.BlockSpec((MODES, 3, 1, CY, CZ), lambda i: (0, 0, 0, 0, 0))
    src, down, up = call(
        pack_x1, "pack_x1", [(CX, CY, CZ), (W + 6, CY, CZ), (W, CY, CZ)],
        (design, solid_mask, mode_fields), {2: block},
    )
    above, below = shift(down, "gx", -1), shift(up, "gx", 1)
    field = (MODES, CX - 1, CY, CZ)
    stiff, mass, columns = call(
        energy_kernel, "energy", [field, field, (2, CY, LANES)], (mode_fields,), flops=40_000_000
    )

    block = pl.BlockSpec((MODES, 3, CX, 8, CZ), lambda i: (0, 0, 0, 0, 0))
    down, up = call(
        pack_y1, "pack_y1", [(16, 8, CZ), (8, 8, CZ)],
        (where, src, mode_fields, above, below), {2: block},
    )
    y_above, y_below = shift(down, "gy", -1), shift(up, "gy", 1)
    plane = (MODES, CY, CZ)
    bulk, ends, bulk_edges, stiff7, mass7 = call(
        bulk_kernel1, "bulk1", bulk_outs + [plane, plane],
        (where, src, mode_fields, above, below), scratch=bulk_scratch, flops=30_000_000,
    )

    edge = call(
        pack_z1, "pack_z1", [(2, PY, LANES)], (where, src, columns, above, below, y_above, y_below)
    )
    z_in = shift(edge, "gz", 1)
    strips, strip_edges, rim, packed = call(
        strip_kernel1, "strips1", strip_outs + [(MODES, 2, 8, CZ), (PY, LANES)],
        (where, mode_fields, columns, above, y_above, y_below, ends),
        scratch=strip_scratch + [(3, 16, CZ)] * 2, flops=20_000_000,
    )
    low, high = call(
        raw_kernel, "raw", [(W, MODES, CY, CZ)] * 2,
        (eigenvalues, mode_order, where, z_in, packed, bulk, bulk_edges, strips, strip_edges,
         stiff, mass, stiff7, mass7, rim),
    )

    bulk_outs, bulk_scratch, strip_outs, strip_scratch = sweep_outs(MODES)
    above, below = shift(low, "gx", -1), shift(high, "gx", 1)
    planes = (low, high, above, below)
    down, up = call(pack_y2, "pack_y2", [(PX, 8, CZ)] * 2, planes)
    y_above, y_below = shift(down, "gy", -1), shift(up, "gy", 1)
    bulk, ends, bulk_edges = call(
        bulk_kernel2, "bulk2", bulk_outs, (where, *planes), scratch=bulk_scratch, flops=40_000_000
    )
    edge = call(pack_z2, "pack_z2", [(MODES, PY, LANES)], (where, *planes, y_above, y_below))
    z_in = shift(edge, "gz", 1)
    strips, strip_edges = call(
        strip_kernel2, "strips2", strip_outs, (where, y_above, y_below, ends),
        scratch=strip_scratch, flops=20_000_000,
    )
    return call(
        final_kernel, "final", [(MODES, CX, CY, CZ)],
        (where, solid_mask, z_in, bulk, bulk_edges, strips, strip_edges),
    )


def solution(mesh):
    return jax.shard_map(
        local,
        mesh=mesh,
        in_specs=(
            P(None, None, "gx", "gy", "gz"),
            P("gx", "gy", "gz"),
            P("gx", "gy", "gz"),
            P(),
            P(),
        ),
        out_specs=P(None, "gx", "gy", "gz"),
        check_vma=False,
    )
```

```python
import jax
import jax.numpy as jnp
from jax import lax
from jax.experimental import pallas as pl
from jax.experimental.pallas import tpu as pltpu
from jax.sharding import PartitionSpec as P

ITERS = 4
MODES = 2
CX, CY, CZ = 8, 32, 256
W = ITERS
PX = CX + 2 * W
PY = CY + 8
NODES = CX + 1
LANES = 128

poisson = 0.3
radius_sq = 3.0
stiff_floor = 0.001
LAME = poisson / ((1.0 + poisson) * (1.0 - 2.0 * poisson))
SHEAR = 0.5 / (1.0 + poisson)

F32 = jnp.float32


def iota(shape, dim):
    return lax.broadcasted_iota(jnp.int32, shape, dim)


def pos(ref):
    return ref[0], ref[1], ref[2]


def sub_lane():
    return iota((8, LANES), 0), iota((8, LANES), 1)


def total_of(terms):
    terms = [t for t in terms if t is not None]
    while len(terms) > 1:
        pairs = [terms[i] + terms[i + 1] for i in range(0, len(terms) - 1, 2)]
        terms = pairs + ([terms[-1]] if len(terms) % 2 else [])
    return terms[0]


def scales(count, inside):
    outside = jnp.zeros(count.shape, F32)
    end = jnp.where(inside, radius_sq / (1.0 + radius_sq * (count + 1.0)), 0.0)
    mid = jnp.where(inside, radius_sq / (1.0 + radius_sq * (count + 2.0)), 0.0)
    return outside, end, mid


def yz_scales(y, z, gy, gz):
    y, z = y + gy * CY, z + gz * CZ
    inside = (y >= 0) & (y < 8 * CY)
    count = 4.0
    for place, last in ((y, 8 * CY - 1), (z, 2 * CZ - 1)):
        count = count - (place == 0).astype(F32) - (place == last).astype(F32)
    return scales(count, inside)


def kind_of(gx, plane):
    x = gx * CX + plane - W
    out = (x < 0) | (x > 8 * CX - 1)
    end = (x == 0) | (x == 8 * CX - 1)
    return jnp.where(out, 0, jnp.where(end, 1, 2))


def fill_bulk(table, gy, gz):
    shape = (CY, CZ)
    for i, part in enumerate(yz_scales(iota(shape, 0), iota(shape, 1), gy, gz)):
        table[i] = part


def fill_strips(table, gy, gz):
    shape = (16, CZ)
    row = iota(shape, 0)
    top = jnp.where(row < 4, row + CY, row + CY - 8)
    bottom = jnp.where(row < 12, row - 8, row - 16)
    for i, part in enumerate(yz_scales(jnp.where(row < 8, top, bottom), iota(shape, 1), gy, gz)):
        table[i] = part


def strip_scale(gx, gy):
    shape = (PY, LANES)
    row = iota(shape, 0)
    y = jnp.where(row < CY + W, row, row - PY) + gy * CY
    x = gx * CX - W + lax.div(iota(shape, 1), 8)
    inside = (y >= 0) & (y < 8 * CY) & (x >= 0) & (x < 8 * CX)
    count = 6.0
    for place, last in ((y, 8 * CY - 1), (x, 8 * CX - 1)):
        count = count - (place == 0).astype(F32) - (place == last).astype(F32)
    return jnp.where(inside, radius_sq / (1.0 + radius_sq * count), 0.0)


def tiles_of(ref, index, rows, cols):
    return [
        [ref[index + (slice(8 * i, 8 * i + 8), slice(LANES * j, LANES * j + LANES))] for j in range(cols)]
        for i in range(rows)
    ]


def along_lanes(row, lane):
    right = [pltpu.roll(t, 1, 1) for t in row]
    left = [pltpu.roll(t, LANES - 1, 1) for t in row]
    out = []
    for j in range(len(row)):
        before = right[j - 1] if j else 0.0
        after = left[j + 1] if j + 1 < len(row) else 0.0
        out.append(
            jnp.where(lane == 0, before, right[j]) + jnp.where(lane == LANES - 1, after, left[j])
        )
    return out


def along_rows(tiles, sub):
    rows, cols = len(tiles), len(tiles[0])
    down = [[pltpu.roll(t, 1, 0) for t in row] for row in tiles]
    up = [[pltpu.roll(t, 7, 0) for t in row] for row in tiles]
    out = []
    for i in range(rows):
        line = []
        for j in range(cols):
            before = down[i - 1][j] if i else 0.0
            after = up[i + 1][j] if i + 1 < rows else 0.0
            line.append(jnp.where(sub == 0, before, down[i][j]) + jnp.where(sub == 7, after, up[i][j]))
        out.append(line)
    return out


def turn_edge(tile, p, gz):
    return pltpu.roll(tile, lax.rem(8 * p + 5 - 2 * gz, LANES), 1)


def kind_at(gx, p):
    return 2 if W < p < PX - W - 1 else kind_of(gx, p)


def bulk_sweeps(fields, where, table, source, states, ends, edges, out):
    gx, gy, gz = where
    sub, lane = sub_lane()
    sb = states[0]
    for p in range(PX):
        kind = kind_at(gx, p)
        for m in range(fields):
            for i in range(CY // 8):
                rows = slice(8 * i, 8 * i + 8)
                sb[m, p, rows, :] = source(m, p, i) * (table[kind, rows, :] * (1.0 / radius_sq))
    for k in range(ITERS):
        old = states[0] if k == 0 else states[1 + (k - 1) % 2]
        new = states[1 + k % 2]
        for m in range(fields):
            edge = [jnp.zeros((8, LANES), F32)] * (CY // 8)
            for p in range(k + 1, PX - 1 - k):
                kind = kind_at(gx, p)
                mid = tiles_of(old, (m, p), CY // 8, 2)
                yy = along_rows(mid, sub)
                for i in range(CY // 8):
                    zz = along_lanes(mid[i], lane)
                    rows = slice(8 * i, 8 * i + 8)
                    for j in range(2):
                        cols = slice(LANES * j, LANES * j + LANES)
                        total = old[m, p - 1, rows, cols] + old[m, p + 1, rows, cols]
                        total = total + (yy[i][j] + zz[j])
                        value = sb[m, p, rows, cols] + table[kind, rows, cols] * total
                        if k + 1 < ITERS:
                            new[m, p, rows, cols] = value
                        else:
                            out[m, p - W, rows, cols] = value
                    side = jnp.where(gz == 0, mid[i][1], mid[i][0])
                    edge[i] = jnp.where(lane == 8 * p + 4 - gz, turn_edge(side, p, gz), edge[i])
                for j in range(2):
                    cols = slice(LANES * j, LANES * j + LANES)
                    ends[m, k, p, 0, 0:1, cols] = mid[CY // 8 - 1][j][7:8]
                    ends[m, k, p, 1, 0:1, cols] = mid[0][j][0:1]
            for i in range(CY // 8):
                edges[m, k, 8 * i : 8 * i + 8, :] = edge[i]


def strip_sweeps(fields, where, table, source, ends, states, edges, out):
    gx, gy, gz = where
    sub, lane = sub_lane()
    sb = states[0]
    wide = iota((8, CZ), 0)
    for p in range(PX):
        kind = kind_at(gx, p)
        for m in range(fields):
            halo = source(m, p) * (1.0 / radius_sq)
            sb[m, p, 0:8, :] = jnp.where(wide < 4, halo * table[kind, 0:8, :], 0.0)
            sb[m, p, 8:16, :] = jnp.where(wide < 4, 0.0, halo * table[kind, 8:16, :])
    for k in range(ITERS):
        old = states[0] if k == 0 else states[1 + (k - 1) % 2]
        new = states[1 + k % 2]
        for m in range(fields):
            edge = [jnp.zeros((8, LANES), F32)] * 2
            for p in range(k + 1, PX - 1 - k):
                kind = kind_at(gx, p)
                mid = tiles_of(old, (m, p), 2, 2)
                for i in range(2):
                    rows = slice(8 * i, 8 * i + 8)
                    zz = along_lanes(mid[i], lane)
                    for j in range(2):
                        cols = slice(LANES * j, LANES * j + LANES)
                        end = jnp.broadcast_to(ends[m, k, p, i, 0:1, cols], (8, LANES))
                        down = pltpu.roll(mid[i][j], 1, 0)
                        up = pltpu.roll(mid[i][j], 7, 0)
                        if i == 0:
                            down = jnp.where(sub == 4, 0.0, down) + jnp.where(sub == 0, end, 0.0)
                        else:
                            up = jnp.where(sub == 3, 0.0, up) + jnp.where(sub == 7, end, 0.0)
                        total = old[m, p - 1, rows, cols] + old[m, p + 1, rows, cols]
                        total = total + (down + up) + zz[j]
                        value = sb[m, p, rows, cols] + table[kind, rows, cols] * total
                        if k + 1 < ITERS:
                            new[m, p, rows, cols] = value
                        else:
                            out[m, p - W, rows, cols] = value
                    side = jnp.where(gz == 0, mid[i][1], mid[i][0])
                    edge[i] = jnp.where(lane == 8 * p + 4 - gz, turn_edge(side, p, gz), edge[i])
            for i in range(2):
                edges[m, k, 8 * i : 8 * i + 8, :] = edge[i]


def z_sweeps(m, scale, halo, bulk_edges, strip_edges):
    sub = iota((8, LANES), 0)
    column = lax.rem(iota((PY, LANES), 1), 8)
    base = halo * (scale * (1.0 / radius_sq))
    state = base
    for k in range(ITERS):
        top, bottom = strip_edges[m, k, 0:8, :], strip_edges[m, k, 8:16, :]
        own = bulk_edges[m, k]
        fed = jnp.concatenate(
            [
                own[0:8] + jnp.where(sub < 4, bottom, 0.0),
                own[8 : CY - 8],
                own[CY - 8 : CY] + jnp.where(sub < 4, 0.0, top),
                jnp.where(sub < 4, top, bottom),
            ],
            axis=0,
        )
        total = pltpu.roll(state, 8, 1) + pltpu.roll(state, LANES - 8, 1)
        total = total + pltpu.roll(state, 1, 0) + pltpu.roll(state, PY - 1, 0)
        total = total + jnp.where(column == 0, 0.0, pltpu.roll(state, 1, 1))
        total = total + jnp.where(column == 7, 0.0, pltpu.roll(state, LANES - 1, 1))
        state = base + scale * (total + fed)
    return state


def result_tile(m, x, i, j, bulk, strips, z_state, beside, sub):
    rows, cols = slice(8 * i, 8 * i + 8), slice(LANES * j, LANES * j + LANES)
    value = bulk[m, x, rows, cols]
    if i == 0:
        value = value + jnp.where(sub < 4, strips[m, x, 8:16, cols], 0.0)
    if i == CY // 8 - 1:
        value = value + jnp.where(sub < 4, 0.0, strips[m, x, 0:8, cols])
    turned = pltpu.roll(z_state[rows], (LANES - 4 - 8 * (x + W)) % LANES, 1)
    return value + jnp.where(beside[j], turned, 0.0)


def beside_halo(gz, lane):
    return (lane < 4 * gz), (lane >= LANES - 4 * (1 - gz))


def pack_strip(gz, tile, p, acc, lane):
    first = 8 * p + 4 * gz
    turned = pltpu.roll(tile, (8 * p + 4) % LANES, 1)
    return jnp.where((lane >= first) & (lane < first + 4), turned, acc)


def edge_tiles(gz):
    return pl.ds(pl.multiple_of((1 - gz) * LANES, LANES), LANES)


def energy_terms(prev, cur):
    (paa, pad, pda, pdd), (caa, cad, cda, cdd) = prev, cur
    u, v, w = 0, 1, 2
    aad = [cad[i] + pad[i] for i in range(3)]
    ada = [cda[i] + pda[i] for i in range(3)]
    add = [cdd[i] + pdd[i] for i in range(3)]
    daa = [caa[i] - paa[i] for i in range(3)]
    dad = [cad[i] - pad[i] for i in range(3)]
    dda = [cda[i] - pda[i] for i in range(3)]
    ddd = [cdd[i] - pdd[i] for i in range(3)]

    def sq(x):
        return x * x

    trace = sq(daa[u] + ada[v] + aad[w])
    lines = sq(dda[v] + dad[w]) + sq(dda[u] + add[w]) + sq(dad[u] + add[v])
    diag = sq(daa[u]) + sq(ada[v]) + sq(aad[w])
    shear = sq(ada[u] + daa[v]) + sq(aad[u] + daa[w]) + sq(aad[v] + ada[w])
    mixed = sq(dda[u]) + sq(dda[v]) + sq(dad[u]) + sq(dad[w]) + sq(add[v]) + sq(add[w])
    cross = sq(add[u] + dad[v]) + sq(add[u] + dda[w]) + sq(dad[v] + dda[w])
    cubic = sq(ddd[u]) + sq(ddd[v]) + sq(ddd[w])
    return (
        LAME * (trace + lines * (1.0 / 3.0))
        + SHEAR * (2.0 * diag + shear + mixed + cross * (1.0 / 3.0))
        + ((LAME + 4.0 * SHEAR) / 9.0) * cubic
    )


def y_parts(pairs):
    aa = [a0 + a1 for a0, d0, a1, d1 in pairs]
    ad = [d0 + d1 for a0, d0, a1, d1 in pairs]
    da = [a1 - a0 for a0, d0, a1, d1 in pairs]
    dd = [d1 - d0 for a0, d0, a1, d1 in pairs]
    return aa, ad, da, dd


def mass_of(parts):
    return total_of([x * x for part in parts for x in part])


def z_pair(here):
    after = pltpu.roll(here, CZ - 1, 1)
    return here + after, after - here


def own_parts(load, chunk):
    sub = iota((8, CZ), 0)
    pairs = []
    for c in range(3):
        a0, d0 = z_pair(load(c, 8 * chunk))
        following = min(chunk + 1, CY // 8 - 1)
        a1, d1 = z_pair(load(c, 8 * following))

        def next_row(t, n):
            return jnp.where(sub == 7, pltpu.roll(n, 7, 0), pltpu.roll(t, 7, 0))

        pairs.append((a0, d0, next_row(a0, a1), next_row(d0, d1)))
    return y_parts(pairs)


def pack_columns(load, lane):
    first = jnp.zeros((CY, LANES), F32)
    last = first
    for m in range(MODES):
        for c in range(3):
            for x in range(CX):
                to = 32 * m + NODES * c + x
                here = lane == to
                first = jnp.where(here, pltpu.roll(load(m, c, x, 0), to, 1), first)
                last = jnp.where(here, pltpu.roll(load(m, c, x, 1), to + 1, 1), last)
    return first, last


def with_rims(packed, above, y_above, keep_x, keep_y, last):
    cols = slice(CZ - LANES, CZ) if last else slice(0, LANES)
    lane = iota((CY, LANES), 1)
    sub, short = sub_lane()
    rim = jnp.zeros((8, LANES), F32)
    for m in range(MODES):
        for c in range(3):
            to = 32 * m + NODES * c + CX
            turned = pltpu.roll(above[W + 3 * m + c, :, cols], to + last, 1)
            packed = jnp.where(lane == to, turned * keep_x, packed)
            for x in range(NODES):
                n = NODES * c + x
                to = 32 * m + n
                row = y_above[8 + 4 * m + n // 8, n % 8 : n % 8 + 1, cols]
                turned = pltpu.roll(jnp.broadcast_to(row, (8, LANES)), to + last, 1)
                rim = jnp.where((short == to) & (sub == 0), turned, rim)
    return jnp.concatenate([packed, rim * keep_y], axis=0)


def pack_x1(design, mask, modes, src, down, up, field, solid, arrived):
    copies = []
    for x in range(CX):
        copies.append(pltpu.make_async_copy(design.at[x], field.at[x], arrived.at[2 * x]))
        copies.append(pltpu.make_async_copy(mask.at[x], solid.at[x], arrived.at[2 * x + 1]))
    for n in range(3 * MODES):
        to = down.at[W + n]
        copies.append(pltpu.make_async_copy(modes.at[n // 3, n % 3, 0], to, arrived.at[2 * CX + n]))
    for copy in copies:
        copy.start()
    for x in range(CX):
        copies[2 * x].wait()
        copies[2 * x + 1].wait()
        plane = field[x] * solid[x].astype(F32)
        src[x] = plane
        if x < W:
            down[x] = plane
        if x >= CX - W:
            up[x - (CX - W)] = plane
    for copy in copies[2 * CX :]:
        copy.wait()


def energy_kernel(modes, stiff, mass, columns):
    lane = iota((CY, LANES), 1)
    columns[0], columns[1] = pack_columns(
        lambda m, c, x, j: modes[m, c, x, :, LANES * j : LANES * j + LANES], lane
    )

    def mode_step(m, carry):
        for chunk in range(CY // 8):
            rows = slice(8 * chunk, 8 * chunk + 8)
            prev = prev_mass = None
            for x in range(CX):
                cur = own_parts(lambda c, r: modes[m, c, x, r : r + 8, :], chunk)
                cur_mass = mass_of(cur)
                if x:
                    stiff[m, x - 1, rows, :] = energy_terms(prev, cur)
                    mass[m, x - 1, rows, :] = cur_mass + prev_mass
                prev, prev_mass = cur, cur_mass
        return carry

    lax.fori_loop(0, MODES, mode_step, 0)


def pick_plane(own, above, below, p):
    if p < W:
        return below, p
    if p < W + CX:
        return own, p - W
    return above, p - W - CX


def pack_y1(where, src, modes, above, below, ahead, down, up):
    gx, gy, gz = pos(where)
    low = iota((8, CZ), 0) < 4
    for q in range(8):
        a, i = pick_plane(src, above, below, q)
        b, j = pick_plane(src, above, below, q + 8)
        down[q] = jnp.where(low, a[i, 0:8, :], pltpu.roll(b[j, 0:8, :], 4, 0))
        up[q] = jnp.where(low, pltpu.roll(b[j, 24:32, :], 4, 0), a[i, 24:32, :])
    keep = jnp.where(gx < 7, 1.0, 0.0)
    for m in range(MODES):
        for c in range(3):
            for x in range(NODES):
                n = c * NODES + x
                if x < CX:
                    row = modes[m, c, x, 0:1, :]
                else:
                    row = above[W + 3 * m + c, 0:1, :] * keep
                down[8 + 4 * m + n // 8, n % 8 : n % 8 + 1, :] = row
        down[8 + 4 * m + 3, 3:8, :] = jnp.zeros((5, CZ), F32)


def bulk_kernel1(
    where, src, modes, above, below, bulk, ends, edges, stiff, mass, table, sb, one, two
):
    at = pos(where)
    gx, gy, gz = at
    fill_bulk(table, gy, gz)

    def source(m, p, i):
        a, at_plane = pick_plane(src, above, below, p)
        return a[at_plane, 8 * i : 8 * i + 8, :]

    bulk_sweeps(1, at, table, source, (sb, one, two), ends, edges, bulk)
    keep = jnp.where(gx < 7, 1.0, 0.0)
    for m in range(MODES):
        for chunk in range(CY // 8):
            rows = slice(8 * chunk, 8 * chunk + 8)
            prev = own_parts(lambda c, r: modes[m, c, CX - 1, r : r + 8, :], chunk)
            cur = own_parts(lambda c, r: above[W + 3 * m + c, r : r + 8, :] * keep, chunk)
            stiff[m, rows, :] = energy_terms(prev, cur)
            mass[m, rows, :] = mass_of(cur) + mass_of(prev)


def halo_tile(y_above, y_below, p, lanes=slice(None)):
    a, b = y_above[p % 8, :, lanes], y_below[p % 8, :, lanes]
    if p >= 8:
        a, b = pltpu.roll(a, 4, 0), pltpu.roll(b, 4, 0)
    return jnp.where(iota(a.shape, 0) < 4, a, b)


def pack_z1(where, src, columns, above, below, y_above, y_below, ahead, out):
    gx, gy, gz = pos(where)
    edge = edge_tiles(gz)
    lane = iota((PY, LANES), 1)
    acc = jnp.zeros((PY, LANES), F32)
    for p in range(PX):
        a, i = pick_plane(src, above, below, p)
        tile = jnp.concatenate([a[i, :, edge], halo_tile(y_above, y_below, p, edge)], axis=0)
        acc = pack_strip(gz, tile, p, acc, lane)
    out[0] = acc
    keep_x = jnp.where(gx < 7, 1.0, 0.0)
    keep_y = jnp.where(gy < 7, 1.0, 0.0)
    out[1] = with_rims(columns[0], above, y_above, keep_x, keep_y, 0)


def strip_kernel1(
    where, modes, columns, above, y_above, y_below, ends,
    strips, edges, rim, packed, table, sb, one, two, near, far,
):
    at = pos(where)
    gx, gy, gz = at
    fill_strips(table, gy, gz)
    strip_sweeps(
        1, at, table, lambda m, p: halo_tile(y_above, y_below, p), ends, (sb, one, two), edges, strips
    )
    keep_x = jnp.where(gx < 7, 1.0, 0.0)
    keep_y = jnp.where(gy < 7, 1.0, 0.0)
    packed[...] = with_rims(columns[1], above, y_above, keep_x, keep_y, 1)
    for m in range(MODES):
        for c in range(3):
            for x in range(NODES):
                n = c * NODES + x
                row = above[W + 3 * m + c, CY - 1 : CY, :] * keep_x
                if x < CX:
                    row = modes[m, c, x, CY - 1 : CY, :]
                near[c, x : x + 1, :] = row
                far[c, x : x + 1, :] = (
                    y_above[8 + 4 * m + n // 8, n % 8 : n % 8 + 1, :] * keep_y
                )

        def parts(first):
            pairs = []
            for c in range(3):
                a0, d0 = z_pair(near[c, first : first + 8, :])
                a1, d1 = z_pair(far[c, first : first + 8, :])
                pairs.append((a0, d0, a1, d1))
            return y_parts(pairs)

        prev, cur = parts(0), parts(1)
        rim[m, 0] = energy_terms(prev, cur)
        rim[m, 1] = mass_of(cur) + mass_of(prev)


def raw_kernel(
    eigenvalues, order, where, z_in, packed, bulk, bulk_edges, strips, strip_edges,
    stiff, mass, stiff7, mass7, rim, low, high,
):
    gx, gy, gz = pos(where)
    sub, lane = sub_lane()
    z_state = z_sweeps(0, strip_scale(gx, gy), z_in[0], bulk_edges, strip_edges)
    beside = beside_halo(gz, lane)

    near, far = packed[...], z_in[1] * jnp.where(gz < 1, 1.0, 0.0)
    a0, d0 = near + far, far - near
    a1, d1 = pltpu.roll(a0, PY - 1, 0), pltpu.roll(d0, PY - 1, 0)
    parts = [(x[0][0:CY]) for x in y_parts([(a0, d0, a1, d1)])]

    def turned(t, by):
        return pltpu.roll(t, (LANES - by) % LANES, 1) if by else t

    prev = [[turned(t, NODES * c) for c in range(3)] for t in parts]
    cur = [[turned(t, NODES * c + 1) for c in range(3)] for t in parts]
    column_stiff = energy_terms(prev, cur)
    column_mass = mass_of(cur) + mass_of(prev)

    factor = 3.0 * (1.0 - stiff_floor) / 16.0
    lams = [eigenvalues[order[m]] * (0.125 * 0.25) for m in range(MODES)]
    for x in range(CX):
        for i in range(CY // 8):
            rows = slice(8 * i, 8 * i + 8)
            for j in range(2):
                cols = slice(LANES * j, LANES * j + LANES)
                phys = result_tile(0, x, i, j, bulk, strips, z_state, beside, sub)
                phys = (factor * phys) * phys
                for m in range(MODES):
                    if x < CX - 1:
                        k, e = stiff[m, x, rows, cols], mass[m, x, rows, cols]
                    else:
                        k, e = stiff7[m, rows, cols], mass7[m, rows, cols]
                    if i == CY // 8 - 1:
                        k = jnp.where(sub == 7, jnp.broadcast_to(rim[m, 0, x : x + 1, cols], (8, LANES)), k)
                        e = jnp.where(sub == 7, jnp.broadcast_to(rim[m, 1, x : x + 1, cols], (8, LANES)), e)
                    if j == 1:
                        by = LANES - 1 - (32 * m + x)
                        k = jnp.where(lane == LANES - 1, pltpu.roll(column_stiff[rows], by, 1), k)
                        e = jnp.where(lane == LANES - 1, pltpu.roll(column_mass[rows], by, 1), e)
                    raw = phys * k - lams[m] * e
                    if x < W:
                        low[x, m, rows, cols] = raw
                    else:
                        high[x - W, m, rows, cols] = raw


def raw_plane(low, high, above, below, p):
    if p < W:
        return below, p
    if p < 2 * W:
        return low, p - W
    if p < 3 * W:
        return high, p - 2 * W
    return above, p - 3 * W


SHARED = ((PX - W, PX - W + 2, 3), (W - 1, W - 3, 3), (PX - W + 1, W - 2, 2))


def rolled(tile, by):
    return pltpu.roll(tile, by % 8, 0) if by % 8 else tile


def pack_y2(low, high, above, below, down, up):
    sub = iota((8, CZ), 0)

    def rows(p, m, start):
        a, i = raw_plane(low, high, above, below, p)
        return a[i, m, start : start + 8, :]

    def both(tiles, first):
        return jnp.where(sub < 4, rolled(tiles[0], -first), rolled(tiles[1], 4 - first))

    for p in range(W, W + CX):
        down[p - W] = both([rows(p, m, 0) for m in range(MODES)], 0)
        up[p - W] = both([rows(p, m, 24) for m in range(MODES)], 4)
    for n, (p, q, count) in enumerate(SHARED):
        down[CX + n] = both(
            [jnp.where(sub < count, rows(p, m, 0), rolled(rows(q, m, 0), count)) for m in range(MODES)], 0
        )
        up[CX + n] = both(
            [jnp.where(sub >= 8 - count, rows(p, m, 24), rolled(rows(q, m, 24), -count)) for m in range(MODES)], 4
        )


def raw_halo(y_above, y_below, m, p, lanes=slice(None)):
    if W <= p < W + CX:
        n, skip = p - W, 0
    else:
        found = [(CX + n, 0 if p == s[0] else s[2]) for n, s in enumerate(SHARED) if p in s[:2]]
        if not found:
            return jnp.zeros(y_above[0, :, lanes].shape, F32)
        n, skip = found[0]
    a = rolled(y_above[n, :, lanes], 4 * m - skip)
    b = rolled(y_below[n, :, lanes], 4 * (1 - m) + skip)
    return jnp.where(iota(a.shape, 0) < 4, a, b)


def bulk_kernel2(where, low, high, above, below, bulk, ends, edges, table, sb, one, two):
    at = pos(where)
    fill_bulk(table, at[1], at[2])

    def source(m, p, i):
        a, at_plane = raw_plane(low, high, above, below, p)
        return a[at_plane, m, 8 * i : 8 * i + 8, :]

    bulk_sweeps(MODES, at, table, source, (sb, one, two), ends, edges, bulk)


def pack_z2(where, low, high, above, below, y_above, y_below, ahead, out):
    gx, gy, gz = pos(where)
    edge = edge_tiles(gz)
    lane = iota((PY, LANES), 1)
    for m in range(MODES):
        acc = jnp.zeros((PY, LANES), F32)
        for p in range(PX):
            a, i = raw_plane(low, high, above, below, p)
            halo = raw_halo(y_above, y_below, m, p, edge)
            acc = pack_strip(gz, jnp.concatenate([a[i, m, :, edge], halo], axis=0), p, acc, lane)
        out[m] = acc


def strip_kernel2(where, y_above, y_below, ends, strips, edges, table, sb, one, two):
    at = pos(where)
    fill_strips(table, at[1], at[2])

    def source(m, p):
        return raw_halo(y_above, y_below, m, p)

    strip_sweeps(MODES, at, table, source, ends, (sb, one, two), edges, strips)


def final_kernel(where, mask, z_in, bulk, bulk_edges, strips, strip_edges, out, held, left):
    gx, gy, gz = pos(where)
    sub, lane = sub_lane()
    beside = beside_halo(gz, lane)
    scale = strip_scale(gx, gy)
    states = [z_sweeps(m, scale, z_in[m], bulk_edges, strip_edges) for m in range(MODES)]
    copies = []
    for m in range(MODES):
        for x in range(CX):
            for i in range(CY // 8):
                rows = slice(8 * i, 8 * i + 8)
                for j in range(2):
                    cols = slice(LANES * j, LANES * j + LANES)
                    value = result_tile(m, x, i, j, bulk, strips, states[m], beside, sub)
                    held[m, x, rows, cols] = value * mask[x, rows, cols].astype(F32)
            if x % 2:
                part = (m, slice(x - 1, x + 1))
                copy = pltpu.make_async_copy(held.at[part], out.at[part], left.at[len(copies)])
                copy.start()
                copies.append(copy)
    for copy in copies:
        copy.wait()


SMEM = pl.BlockSpec(memory_space=pltpu.SMEM)


def whole(x):
    return pl.BlockSpec(x.shape, lambda i: (0,) * x.ndim)


def call(kernel, name, outs, args, specs=None, out_spec=None, scratch=(), flops=0):
    specs = specs or {}
    shapes = tuple(jax.ShapeDtypeStruct(s, F32) for s in outs)
    more = {} if out_spec is None else {"out_specs": out_spec}
    return pl.pallas_call(
        kernel,
        grid=(1,),
        out_shape=shapes if len(shapes) > 1 else shapes[0],
        in_specs=[specs.get(i, SMEM if a.ndim == 1 else whole(a)) for i, a in enumerate(args)],
        scratch_shapes=[pltpu.VMEM(s, F32) if isinstance(s, tuple) else s for s in scratch],
        compiler_params=pltpu.CompilerParams(vmem_limit_bytes=24 * 1024 * 1024),
        cost_estimate=pl.CostEstimate(flops=flops, bytes_accessed=2_000_000, transcendentals=0),
        name=name,
        **more,
    )(*args)


HBM = pl.BlockSpec(memory_space=pltpu.HBM)
ANY = pl.BlockSpec(memory_space=pl.ANY)


def ring(axis, step):
    size = lax.axis_size(axis)
    return [(i, (i + step) % size) for i in range(size)]


def shift(x, axis, step):
    return lax.ppermute(x, axis, ring(axis, step))


def sweep_outs(fields):
    return (
        [(fields, CX, CY, CZ), (fields, ITERS, PX, 2, 1, CZ), (fields, ITERS, CY, LANES)],
        [(3, CY, CZ)] + [(fields, PX, CY, CZ)] * 3,
        [(fields, CX, 16, CZ), (fields, ITERS, 16, LANES)],
        [(3, 16, CZ)] + [(fields, PX, 16, CZ)] * 3,
    )


def local(mode_fields, design, solid_mask, eigenvalues, mode_order):
    where = jnp.stack([lax.axis_index(a) for a in ("gx", "gy", "gz")]).astype(jnp.int32)
    bulk_outs, bulk_scratch, strip_outs, strip_scratch = sweep_outs(1)

    src, down, up = call(
        pack_x1, "pack_x1", [(CX, CY, CZ), (W + 6, CY, CZ), (W, CY, CZ)],
        tuple(pltpu.with_memory_space_constraint(x, pltpu.HBM) for x in (design, solid_mask, mode_fields)),
        {0: HBM, 1: HBM, 2: HBM},
        scratch=[(CX, CY, CZ), pltpu.VMEM((CX, CY, CZ), jnp.int32), pltpu.SemaphoreType.DMA((2 * CX + 6,))],
    )
    above, below = shift(down, "gx", -1), shift(up, "gx", 1)
    field = (MODES, CX - 1, CY, CZ)
    stiff, mass, columns = call(
        energy_kernel, "energy", [field, field, (2, CY, LANES)], (mode_fields,), flops=40_000_000
    )

    block = pl.BlockSpec((MODES, 3, CX, 8, CZ), lambda i: (0, 0, 0, 0, 0))
    down, up = call(
        pack_y1, "pack_y1", [(16, 8, CZ), (8, 8, CZ)],
        (where, src, mode_fields, above, below, columns), {2: block, 5: ANY},
    )
    y_above, y_below = shift(down, "gy", -1), shift(up, "gy", 1)
    plane = (MODES, CY, CZ)
    bulk, ends, bulk_edges, stiff7, mass7 = call(
        bulk_kernel1, "bulk1", bulk_outs + [plane, plane],
        (where, src, mode_fields, above, below), scratch=bulk_scratch, flops=30_000_000,
    )

    edge = call(
        pack_z1, "pack_z1", [(2, PY, LANES)],
        (where, src, columns, above, below, y_above, y_below, bulk_edges), {7: ANY},
    )
    z_in = shift(edge, "gz", 1)
    strips, strip_edges, rim, packed = call(
        strip_kernel1, "strips1", strip_outs + [(MODES, 2, 8, CZ), (PY, LANES)],
        (where, mode_fields, columns, above, y_above, y_below, ends),
        scratch=strip_scratch + [(3, 16, CZ)] * 2, flops=20_000_000,
    )
    low, high = call(
        raw_kernel, "raw", [(W, MODES, CY, CZ)] * 2,
        (eigenvalues, mode_order, where, z_in, packed, bulk, bulk_edges, strips, strip_edges,
         stiff, mass, stiff7, mass7, rim),
    )

    bulk_outs, bulk_scratch, strip_outs, strip_scratch = sweep_outs(MODES)
    above, below = shift(low, "gx", -1), shift(high, "gx", 1)
    planes = (low, high, above, below)
    down, up = call(pack_y2, "pack_y2", [(CX + 3, 8, CZ)] * 2, planes)
    y_above, y_below = shift(down, "gy", -1), shift(up, "gy", 1)
    bulk, ends, bulk_edges = call(
        bulk_kernel2, "bulk2", bulk_outs, (where, *planes), scratch=bulk_scratch, flops=40_000_000
    )
    edge = call(
        pack_z2, "pack_z2", [(MODES, PY, LANES)],
        (where, *planes, y_above, y_below, bulk_edges), {7: ANY},
    )
    z_in = shift(edge, "gz", 1)
    strips, strip_edges = call(
        strip_kernel2, "strips2", strip_outs, (where, y_above, y_below, ends),
        scratch=strip_scratch, flops=20_000_000,
    )
    return call(
        final_kernel, "final", [(MODES, CX, CY, CZ)],
        (where, solid_mask, z_in, bulk, bulk_edges, strips, strip_edges), out_spec=HBM,
        scratch=[(MODES, CX, CY, CZ), pltpu.SemaphoreType.DMA((MODES * CX // 2,))],
    )


def solution(mesh):
    return jax.shard_map(
        local,
        mesh=mesh,
        in_specs=(
            P(None, None, "gx", "gy", "gz"),
            P("gx", "gy", "gz"),
            P("gx", "gy", "gz"),
            P(),
            P(),
        ),
        out_specs=P(None, "gx", "gy", "gz"),
        check_vma=False,
    )
```

```python
import jax
import jax.numpy as jnp
from jax import lax
from jax.experimental import pallas as pl
from jax.experimental.pallas import tpu as pltpu
from jax.sharding import PartitionSpec as P

ITERS = 4
MODES = 2
CX, CY, CZ = 8, 32, 256
W = ITERS
PX = CX + 2 * W
PY = CY + 8
NODES = CX + 1
LANES = 128

poisson = 0.3
radius_sq = 3.0
stiff_floor = 0.001
LAME = poisson / ((1.0 + poisson) * (1.0 - 2.0 * poisson))
SHEAR = 0.5 / (1.0 + poisson)

F32 = jnp.float32


def iota(shape, dim):
    return lax.broadcasted_iota(jnp.int32, shape, dim)


def pos(ref):
    return ref[0], ref[1], ref[2]


def sub_lane():
    return iota((8, LANES), 0), iota((8, LANES), 1)


def total_of(terms):
    terms = [t for t in terms if t is not None]
    while len(terms) > 1:
        pairs = [terms[i] + terms[i + 1] for i in range(0, len(terms) - 1, 2)]
        terms = pairs + ([terms[-1]] if len(terms) % 2 else [])
    return terms[0]


def scales(count, inside):
    outside = jnp.zeros(count.shape, F32)
    end = jnp.where(inside, radius_sq / (1.0 + radius_sq * (count + 1.0)), 0.0)
    mid = jnp.where(inside, radius_sq / (1.0 + radius_sq * (count + 2.0)), 0.0)
    return outside, end, mid


def yz_scales(y, z, gy, gz):
    y, z = y + gy * CY, z + gz * CZ
    inside = (y >= 0) & (y < 8 * CY)
    count = 4.0
    for place, last in ((y, 8 * CY - 1), (z, 2 * CZ - 1)):
        count = count - (place == 0).astype(F32) - (place == last).astype(F32)
    return scales(count, inside)


def kind_of(gx, plane):
    x = gx * CX + plane - W
    out = (x < 0) | (x > 8 * CX - 1)
    end = (x == 0) | (x == 8 * CX - 1)
    return jnp.where(out, 0, jnp.where(end, 1, 2))


def fill_bulk(table, gy, gz):
    shape = (CY, CZ)
    for i, part in enumerate(yz_scales(iota(shape, 0), iota(shape, 1), gy, gz)):
        table[i] = part


def fill_strips(table, gy, gz):
    shape = (16, CZ)
    row = iota(shape, 0)
    top = jnp.where(row < 4, row + CY, row + CY - 8)
    bottom = jnp.where(row < 12, row - 8, row - 16)
    for i, part in enumerate(yz_scales(jnp.where(row < 8, top, bottom), iota(shape, 1), gy, gz)):
        table[i] = part


def strip_scale(gx, gy):
    shape = (PY, LANES)
    row = iota(shape, 0)
    y = jnp.where(row < CY + W, row, row - PY) + gy * CY
    x = gx * CX - W + lax.div(iota(shape, 1), 8)
    inside = (y >= 0) & (y < 8 * CY) & (x >= 0) & (x < 8 * CX)
    count = 6.0
    for place, last in ((y, 8 * CY - 1), (x, 8 * CX - 1)):
        count = count - (place == 0).astype(F32) - (place == last).astype(F32)
    return jnp.where(inside, radius_sq / (1.0 + radius_sq * count), 0.0)


def tiles_of(ref, index, rows, cols):
    return [
        [ref[index + (slice(8 * i, 8 * i + 8), slice(LANES * j, LANES * j + LANES))] for j in range(cols)]
        for i in range(rows)
    ]


def along_lanes(row, lane):
    right = [pltpu.roll(t, 1, 1) for t in row]
    left = [pltpu.roll(t, LANES - 1, 1) for t in row]
    out = []
    for j in range(len(row)):
        before = right[j - 1] if j else 0.0
        after = left[j + 1] if j + 1 < len(row) else 0.0
        out.append(
            jnp.where(lane == 0, before, right[j]) + jnp.where(lane == LANES - 1, after, left[j])
        )
    return out


def along_rows(tiles, sub):
    rows, cols = len(tiles), len(tiles[0])
    down = [[pltpu.roll(t, 1, 0) for t in row] for row in tiles]
    up = [[pltpu.roll(t, 7, 0) for t in row] for row in tiles]
    out = []
    for i in range(rows):
        line = []
        for j in range(cols):
            before = down[i - 1][j] if i else 0.0
            after = up[i + 1][j] if i + 1 < rows else 0.0
            line.append(jnp.where(sub == 0, before, down[i][j]) + jnp.where(sub == 7, after, up[i][j]))
        out.append(line)
    return out


def turn_edge(tile, p, gz):
    return pltpu.roll(tile, lax.rem(8 * p + 5 - 2 * gz, LANES), 1)


def kind_at(gx, p):
    return 2 if W < p < PX - W - 1 else kind_of(gx, p)


def bulk_sweeps(fields, where, table, source, states, ends, edges, out):
    gx, gy, gz = where
    sub, lane = sub_lane()
    sb = states[0]
    for p in range(PX):
        kind = kind_at(gx, p)
        for m in range(fields):
            for i in range(CY // 8):
                rows = slice(8 * i, 8 * i + 8)
                sb[m, p, rows, :] = source(m, p, i) * (table[kind, rows, :] * (1.0 / radius_sq))
    for k in range(ITERS):
        old = states[0] if k == 0 else states[1 + (k - 1) % 2]
        new = states[1 + k % 2]
        for m in range(fields):
            edge = [jnp.zeros((8, LANES), F32)] * (CY // 8)
            for p in range(k + 1, PX - 1 - k):
                kind = kind_at(gx, p)
                mid = tiles_of(old, (m, p), CY // 8, 2)
                yy = along_rows(mid, sub)
                for i in range(CY // 8):
                    zz = along_lanes(mid[i], lane)
                    rows = slice(8 * i, 8 * i + 8)
                    for j in range(2):
                        cols = slice(LANES * j, LANES * j + LANES)
                        total = old[m, p - 1, rows, cols] + old[m, p + 1, rows, cols]
                        total = total + (yy[i][j] + zz[j])
                        value = sb[m, p, rows, cols] + table[kind, rows, cols] * total
                        if k + 1 < ITERS:
                            new[m, p, rows, cols] = value
                        else:
                            out[m, p - W, rows, cols] = value
                    side = jnp.where(gz == 0, mid[i][1], mid[i][0])
                    edge[i] = jnp.where(lane == 8 * p + 4 - gz, turn_edge(side, p, gz), edge[i])
                for j in range(2):
                    cols = slice(LANES * j, LANES * j + LANES)
                    ends[m, k, p, 0, 0:1, cols] = mid[CY // 8 - 1][j][7:8]
                    ends[m, k, p, 1, 0:1, cols] = mid[0][j][0:1]
            for i in range(CY // 8):
                edges[m, k, 8 * i : 8 * i + 8, :] = edge[i]


def strip_sweeps(fields, where, table, source, ends, states, edges, out):
    gx, gy, gz = where
    sub, lane = sub_lane()
    sb = states[0]
    wide = iota((8, CZ), 0)
    for p in range(PX):
        kind = kind_at(gx, p)
        for m in range(fields):
            halo = source(m, p) * (1.0 / radius_sq)
            sb[m, p, 0:8, :] = jnp.where(wide < 4, halo * table[kind, 0:8, :], 0.0)
            sb[m, p, 8:16, :] = jnp.where(wide < 4, 0.0, halo * table[kind, 8:16, :])
    for k in range(ITERS):
        old = states[0] if k == 0 else states[1 + (k - 1) % 2]
        new = states[1 + k % 2]
        for m in range(fields):
            edge = [jnp.zeros((8, LANES), F32)] * 2
            for p in range(k + 1, PX - 1 - k):
                kind = kind_at(gx, p)
                mid = tiles_of(old, (m, p), 2, 2)
                for i in range(2):
                    rows = slice(8 * i, 8 * i + 8)
                    zz = along_lanes(mid[i], lane)
                    for j in range(2):
                        cols = slice(LANES * j, LANES * j + LANES)
                        end = jnp.broadcast_to(ends[m, k, p, i, 0:1, cols], (8, LANES))
                        down = pltpu.roll(mid[i][j], 1, 0)
                        up = pltpu.roll(mid[i][j], 7, 0)
                        if i == 0:
                            down = jnp.where(sub == 4, 0.0, down) + jnp.where(sub == 0, end, 0.0)
                        else:
                            up = jnp.where(sub == 3, 0.0, up) + jnp.where(sub == 7, end, 0.0)
                        total = old[m, p - 1, rows, cols] + old[m, p + 1, rows, cols]
                        total = total + (down + up) + zz[j]
                        value = sb[m, p, rows, cols] + table[kind, rows, cols] * total
                        if k + 1 < ITERS:
                            new[m, p, rows, cols] = value
                        else:
                            out[m, p - W, rows, cols] = value
                    side = jnp.where(gz == 0, mid[i][1], mid[i][0])
                    edge[i] = jnp.where(lane == 8 * p + 4 - gz, turn_edge(side, p, gz), edge[i])
            for i in range(2):
                edges[m, k, 8 * i : 8 * i + 8, :] = edge[i]


def z_sweeps(m, scale, halo, bulk_edges, strip_edges):
    sub = iota((8, LANES), 0)
    column = lax.rem(iota((PY, LANES), 1), 8)
    base = halo * (scale * (1.0 / radius_sq))
    state = base
    for k in range(ITERS):
        top, bottom = strip_edges[m, k, 0:8, :], strip_edges[m, k, 8:16, :]
        own = bulk_edges[m, k]
        fed = jnp.concatenate(
            [
                own[0:8] + jnp.where(sub < 4, bottom, 0.0),
                own[8 : CY - 8],
                own[CY - 8 : CY] + jnp.where(sub < 4, 0.0, top),
                jnp.where(sub < 4, top, bottom),
            ],
            axis=0,
        )
        total = pltpu.roll(state, 8, 1) + pltpu.roll(state, LANES - 8, 1)
        total = total + pltpu.roll(state, 1, 0) + pltpu.roll(state, PY - 1, 0)
        total = total + jnp.where(column == 0, 0.0, pltpu.roll(state, 1, 1))
        total = total + jnp.where(column == 7, 0.0, pltpu.roll(state, LANES - 1, 1))
        state = base + scale * (total + fed)
    return state


def pair_tile(m, x, i, j, bulk, strips, sub):
    rows, cols = slice(8 * i, 8 * i + 8), slice(LANES * j, LANES * j + LANES)
    value = bulk[m, x, rows, cols]
    if i == 0:
        value = value + jnp.where(sub < 4, strips[m, x, 8:16, cols], 0.0)
    if i == CY // 8 - 1:
        value = value + jnp.where(sub < 4, 0.0, strips[m, x, 0:8, cols])
    return value


def z_tile(z_state, x, i):
    return pltpu.roll(z_state[8 * i : 8 * i + 8], (LANES - 4 - 8 * (x + W)) % LANES, 1)


def beside_halo(gz, lane):
    return (lane < 4 * gz), (lane >= LANES - 4 * (1 - gz))


def pack_strip(gz, tile, p, acc, lane):
    first = 8 * p + 4 * gz
    turned = pltpu.roll(tile, (8 * p + 4) % LANES, 1)
    return jnp.where((lane >= first) & (lane < first + 4), turned, acc)


def own_strip(gz, load, rows=CY):
    lane = iota((rows, LANES), 1)
    acc = jnp.zeros((rows, LANES), F32)
    for p in range(PX):
        acc = pack_strip(gz, load(p), p, acc, lane)
    return acc


def edge_tiles(gz):
    return pl.ds(pl.multiple_of((1 - gz) * LANES, LANES), LANES)


def energy_terms(prev, cur):
    (paa, pad, pda, pdd), (caa, cad, cda, cdd) = prev, cur
    u, v, w = 0, 1, 2
    aad = [cad[i] + pad[i] for i in range(3)]
    ada = [cda[i] + pda[i] for i in range(3)]
    add = [cdd[i] + pdd[i] for i in range(3)]
    daa = [caa[i] - paa[i] for i in range(3)]
    dad = [cad[i] - pad[i] for i in range(3)]
    dda = [cda[i] - pda[i] for i in range(3)]
    ddd = [cdd[i] - pdd[i] for i in range(3)]

    def sq(x):
        return x * x

    trace = sq(daa[u] + ada[v] + aad[w])
    lines = sq(dda[v] + dad[w]) + sq(dda[u] + add[w]) + sq(dad[u] + add[v])
    diag = sq(daa[u]) + sq(ada[v]) + sq(aad[w])
    shear = sq(ada[u] + daa[v]) + sq(aad[u] + daa[w]) + sq(aad[v] + ada[w])
    mixed = sq(dda[u]) + sq(dda[v]) + sq(dad[u]) + sq(dad[w]) + sq(add[v]) + sq(add[w])
    cross = sq(add[u] + dad[v]) + sq(add[u] + dda[w]) + sq(dad[v] + dda[w])
    cubic = sq(ddd[u]) + sq(ddd[v]) + sq(ddd[w])
    return (
        LAME * (trace + lines * (1.0 / 3.0))
        + SHEAR * (2.0 * diag + shear + mixed + cross * (1.0 / 3.0))
        + ((LAME + 4.0 * SHEAR) / 9.0) * cubic
    )


def y_parts(pairs):
    aa = [a0 + a1 for a0, d0, a1, d1 in pairs]
    ad = [d0 + d1 for a0, d0, a1, d1 in pairs]
    da = [a1 - a0 for a0, d0, a1, d1 in pairs]
    dd = [d1 - d0 for a0, d0, a1, d1 in pairs]
    return aa, ad, da, dd


def mass_of(parts):
    return total_of([x * x for part in parts for x in part])


def z_pair(here):
    after = pltpu.roll(here, CZ - 1, 1)
    return here + after, after - here


def own_parts(load, chunk):
    sub = iota((8, CZ), 0)
    pairs = []
    for c in range(3):
        a0, d0 = z_pair(load(c, 8 * chunk))
        following = min(chunk + 1, CY // 8 - 1)
        a1, d1 = z_pair(load(c, 8 * following))

        def next_row(t, n):
            return jnp.where(sub == 7, pltpu.roll(n, 7, 0), pltpu.roll(t, 7, 0))

        pairs.append((a0, d0, next_row(a0, a1), next_row(d0, d1)))
    return y_parts(pairs)


def pack_columns(load, lane):
    first = jnp.zeros((CY, LANES), F32)
    last = first
    for m in range(MODES):
        for c in range(3):
            for x in range(CX):
                to = 32 * m + NODES * c + x
                here = lane == to
                first = jnp.where(here, pltpu.roll(load(m, c, x, 0), to, 1), first)
                last = jnp.where(here, pltpu.roll(load(m, c, x, 1), to + 1, 1), last)
    return first, last


def with_plane8(packed, above, keep_x, last):
    cols = slice(CZ - LANES, CZ) if last else slice(0, LANES)
    rows = packed.shape[0]
    lane = iota(packed.shape, 1)
    for m in range(MODES):
        for c in range(3):
            to = 32 * m + NODES * c + CX
            turned = pltpu.roll(above[W + 3 * m + c, 0:rows, cols], to + last, 1)
            packed = jnp.where(lane == to, turned * keep_x, packed)
    return packed


def with_row32(packed, y_above, keep_y, last):
    sub, lane = sub_lane()
    row = y_above[11, 3:4, LANES * last : LANES * last + LANES] * keep_y
    return jnp.concatenate([packed, jnp.where(sub == 0, jnp.broadcast_to(row, (8, LANES)), 0.0)], axis=0)


def pack_x1(design, mask, modes, src, down, up, field, solid, arrived):
    copies = []
    for x in range(CX):
        copies.append(pltpu.make_async_copy(design.at[x], field.at[x], arrived.at[2 * x]))
        copies.append(pltpu.make_async_copy(mask.at[x], solid.at[x], arrived.at[2 * x + 1]))
    for n in range(3 * MODES):
        to = down.at[W + n]
        copies.append(pltpu.make_async_copy(modes.at[n // 3, n % 3, 0], to, arrived.at[2 * CX + n]))
    for copy in copies:
        copy.start()
    for x in range(CX):
        copies[2 * x].wait()
        copies[2 * x + 1].wait()
        plane = field[x] * solid[x].astype(F32)
        src[x] = plane
        if x < W:
            down[x] = plane
        if x >= CX - W:
            up[x - (CX - W)] = plane
    for copy in copies[2 * CX :]:
        copy.wait()


def energy_kernel(modes, stiff, mass, columns, first_rows):
    lane = iota((CY, LANES), 1)
    columns[0], columns[1] = pack_columns(
        lambda m, c, x, j: modes[m, c, x, :, LANES * j : LANES * j + LANES], lane
    )

    for m in range(MODES):
        first_rows[4 * m + 3] = jnp.zeros((8, CZ), F32)
        for c in range(3):
            for x in range(CX):
                n = NODES * c + x
                first_rows[4 * m + n // 8, n % 8 : n % 8 + 1, :] = modes[m, c, x, 0:1, :]

    def mode_step(m, carry):
        for chunk in range(CY // 8):
            rows = slice(8 * chunk, 8 * chunk + 8)
            prev = prev_mass = None
            for x in range(CX):
                cur = own_parts(lambda c, r: modes[m, c, x, r : r + 8, :], chunk)
                cur_mass = mass_of(cur)
                if x:
                    stiff[m, x - 1, rows, :] = energy_terms(prev, cur)
                    mass[m, x - 1, rows, :] = cur_mass + prev_mass
                prev, prev_mass = cur, cur_mass
        return carry

    lax.fori_loop(0, MODES, mode_step, 0)


def pick_plane(own, above, below, p):
    if p < W:
        return below, p
    if p < W + CX:
        return own, p - W
    return above, p - W - CX


def pack_y1(where, src, first_rows, columns, above, below, down, up):
    gx, gy, gz = pos(where)
    low = iota((8, CZ), 0) < 4
    for q in range(8):
        a, i = pick_plane(src, above, below, q)
        b, j = pick_plane(src, above, below, q + 8)
        down[q] = jnp.where(low, a[i, 0:8, :], pltpu.roll(b[j, 0:8, :], 4, 0))
        up[q] = jnp.where(low, pltpu.roll(b[j, 24:32, :], 4, 0), a[i, 24:32, :])
    keep = jnp.where(gx < 7, 1.0, 0.0)
    down[8:16] = first_rows[...]
    for m in range(MODES):
        for c in range(3):
            n = NODES * c + CX
            down[8 + 4 * m + n // 8, n % 8 : n % 8 + 1, :] = above[W + 3 * m + c, 0:1, :] * keep
    for last in range(2):
        row = with_plane8(columns[last, 0:8, :], above, keep, last)
        down[11, 3:4, LANES * last : LANES * last + LANES] = row[0:1]


def bulk_kernel1(
    where, src, modes, columns, above, below,
    bulk, ends, edges, stiff, mass, own, rims, table, sb, one, two,
):
    at = pos(where)
    gx, gy, gz = at
    fill_bulk(table, gy, gz)

    def source(m, p, i):
        a, at_plane = pick_plane(src, above, below, p)
        return a[at_plane, 8 * i : 8 * i + 8, :]

    bulk_sweeps(1, at, table, source, (sb, one, two), ends, edges, bulk)
    edge = edge_tiles(gz)
    own[0] = own_strip(gz, lambda p: plane_edge(src, above, below, p, edge))
    keep = jnp.where(gx < 7, 1.0, 0.0)
    for last in range(2):
        rims[last] = with_plane8(columns[last], above, keep, last)
    for m in range(MODES):
        for chunk in range(CY // 8):
            rows = slice(8 * chunk, 8 * chunk + 8)
            prev = own_parts(lambda c, r: modes[m, c, CX - 1, r : r + 8, :], chunk)
            cur = own_parts(lambda c, r: above[W + 3 * m + c, r : r + 8, :] * keep, chunk)
            stiff[m, rows, :] = energy_terms(prev, cur)
            mass[m, rows, :] = mass_of(cur) + mass_of(prev)


def halo_tile(y_above, y_below, p, lanes=slice(None)):
    a, b = y_above[p % 8, :, lanes], y_below[p % 8, :, lanes]
    if p >= 8:
        a, b = pltpu.roll(a, 4, 0), pltpu.roll(b, 4, 0)
    return jnp.where(iota(a.shape, 0) < 4, a, b)


def plane_edge(own, above, below, p, edge):
    a, i = pick_plane(own, above, below, p)
    return a[i, :, edge]


def pack_z1(where, own, rims, y_above, y_below, out):
    gx, gy, gz = pos(where)
    edge = edge_tiles(gz)
    out[0, 0:CY, :] = own[0]
    out[0, CY:PY, :] = own_strip(gz, lambda p: halo_tile(y_above, y_below, p, edge), 8)
    out[1] = with_row32(rims[0], y_above, jnp.where(gy < 7, 1.0, 0.0), 0)


def strip_kernel1(
    where, modes, rims, above, y_above, y_below, ends,
    strips, edges, rim, packed, table, sb, one, two, near, far,
):
    at = pos(where)
    gx, gy, gz = at
    fill_strips(table, gy, gz)
    strip_sweeps(
        1, at, table, lambda m, p: halo_tile(y_above, y_below, p), ends, (sb, one, two), edges, strips
    )
    keep_x = jnp.where(gx < 7, 1.0, 0.0)
    keep_y = jnp.where(gy < 7, 1.0, 0.0)
    packed[...] = with_row32(rims[1], y_above, keep_y, 1)
    for m in range(MODES):
        for c in range(3):
            for x in range(NODES):
                n = c * NODES + x
                row = above[W + 3 * m + c, CY - 1 : CY, :] * keep_x
                if x < CX:
                    row = modes[m, c, x, CY - 1 : CY, :]
                near[c, x : x + 1, :] = row
                far[c, x : x + 1, :] = (
                    y_above[8 + 4 * m + n // 8, n % 8 : n % 8 + 1, :] * keep_y
                )

        def parts(first):
            pairs = []
            for c in range(3):
                a0, d0 = z_pair(near[c, first : first + 8, :])
                a1, d1 = z_pair(far[c, first : first + 8, :])
                pairs.append((a0, d0, a1, d1))
            return y_parts(pairs)

        prev, cur = parts(0), parts(1)
        rim[m, 0] = energy_terms(prev, cur)
        rim[m, 1] = mass_of(cur) + mass_of(prev)


def raw_planes(
    planes, eigenvalues, order, gz, z_state, column_stiff, column_mass, bulk, strips,
    stiff, mass, stiff7, mass7, rim, out,
):
    sub, lane = sub_lane()
    beside = beside_halo(gz, lane)
    factor = 3.0 * (1.0 - stiff_floor) / 16.0
    lams = [eigenvalues[order[m]] * (0.125 * 0.25) for m in range(MODES)]
    for x in planes:
        for i in range(CY // 8):
            rows = slice(8 * i, 8 * i + 8)
            correction = z_tile(z_state, x, i)
            for j in range(2):
                cols = slice(LANES * j, LANES * j + LANES)
                phys = pair_tile(0, x, i, j, bulk, strips, sub) + jnp.where(beside[j], correction, 0.0)
                phys = (factor * phys) * phys
                for m in range(MODES):
                    if x < CX - 1:
                        k, e = stiff[m, x, rows, cols], mass[m, x, rows, cols]
                    else:
                        k, e = stiff7[m, rows, cols], mass7[m, rows, cols]
                    if i == CY // 8 - 1:
                        k = jnp.where(sub == 7, jnp.broadcast_to(rim[m, 0, x : x + 1, cols], (8, LANES)), k)
                        e = jnp.where(sub == 7, jnp.broadcast_to(rim[m, 1, x : x + 1, cols], (8, LANES)), e)
                    if j == 1:
                        by = LANES - 1 - (32 * m + x)
                        k = jnp.where(lane == LANES - 1, pltpu.roll(column_stiff[rows, :], by, 1), k)
                        e = jnp.where(lane == LANES - 1, pltpu.roll(column_mass[rows, :], by, 1), e)
                    out[x % W, m, rows, cols] = phys * k - lams[m] * e


def raw_kernel1(
    eigenvalues, order, where, z_in, packed, bulk, bulk_edges, strips, strip_edges,
    stiff, mass, stiff7, mass7, rim, low, z_parts,
):
    gx, gy, gz = pos(where)
    z_state = z_sweeps(0, strip_scale(gx, gy), z_in[0], bulk_edges, strip_edges)

    near, far = packed[...], z_in[1] * jnp.where(gz < 1, 1.0, 0.0)
    a0, d0 = near + far, far - near
    a1, d1 = pltpu.roll(a0, PY - 1, 0), pltpu.roll(d0, PY - 1, 0)
    parts = [(x[0][0:CY]) for x in y_parts([(a0, d0, a1, d1)])]

    def turned(t, by):
        return pltpu.roll(t, (LANES - by) % LANES, 1) if by else t

    prev = [[turned(t, NODES * c) for c in range(3)] for t in parts]
    cur = [[turned(t, NODES * c + 1) for c in range(3)] for t in parts]
    column_stiff = energy_terms(prev, cur)
    column_mass = mass_of(cur) + mass_of(prev)
    z_parts[0], z_parts[1], z_parts[2] = z_state[0:CY], column_stiff, column_mass
    raw_planes(
        range(W), eigenvalues, order, gz, z_state, column_stiff, column_mass, bulk, strips,
        stiff, mass, stiff7, mass7, rim, low,
    )


def raw_kernel2(
    eigenvalues, order, where, z_parts, bulk, strips, stiff, mass, stiff7, mass7, rim, high
):
    gx, gy, gz = pos(where)
    raw_planes(
        range(W, CX), eigenvalues, order, gz, z_parts[0], z_parts.at[1], z_parts.at[2], bulk, strips,
        stiff, mass, stiff7, mass7, rim, high,
    )


def raw_plane(low, high, above, below, p):
    if p < W:
        return below, p
    if p < 2 * W:
        return low, p - W
    if p < 3 * W:
        return high, p - 2 * W
    return above, p - 3 * W


SHARED = ((PX - W, PX - W + 2, 3), (W - 1, W - 3, 3), (PX - W + 1, W - 2, 2))


def rolled(tile, by):
    return pltpu.roll(tile, by % 8, 0) if by % 8 else tile


def pack_y2(low, high, above, below, down, up):
    sub = iota((8, CZ), 0)

    def rows(p, m, start):
        a, i = raw_plane(low, high, above, below, p)
        return a[i, m, start : start + 8, :]

    def both(tiles, first):
        return jnp.where(sub < 4, rolled(tiles[0], -first), rolled(tiles[1], 4 - first))

    for p in range(W, W + CX):
        down[p - W] = both([rows(p, m, 0) for m in range(MODES)], 0)
        up[p - W] = both([rows(p, m, 24) for m in range(MODES)], 4)
    for n, (p, q, count) in enumerate(SHARED):
        down[CX + n] = both(
            [jnp.where(sub < count, rows(p, m, 0), rolled(rows(q, m, 0), count)) for m in range(MODES)], 0
        )
        up[CX + n] = both(
            [jnp.where(sub >= 8 - count, rows(p, m, 24), rolled(rows(q, m, 24), -count)) for m in range(MODES)], 4
        )


def raw_halo(y_above, y_below, m, p, lanes=slice(None)):
    if W <= p < W + CX:
        n, skip = p - W, 0
    else:
        found = [(CX + n, 0 if p == s[0] else s[2]) for n, s in enumerate(SHARED) if p in s[:2]]
        if not found:
            return jnp.zeros(y_above[0, :, lanes].shape, F32)
        n, skip = found[0]
    a = rolled(y_above[n, :, lanes], 4 * m - skip)
    b = rolled(y_below[n, :, lanes], 4 * (1 - m) + skip)
    return jnp.where(iota(a.shape, 0) < 4, a, b)


def bulk_kernel2(where, low, high, above, below, bulk, ends, edges, own, table, sb, one, two):
    at = pos(where)
    fill_bulk(table, at[1], at[2])

    def source(m, p, i):
        a, at_plane = raw_plane(low, high, above, below, p)
        return a[at_plane, m, 8 * i : 8 * i + 8, :]

    bulk_sweeps(MODES, at, table, source, (sb, one, two), ends, edges, bulk)
    edge = edge_tiles(at[2])
    for m in range(MODES):

        def load(p, m=m):
            a, i = raw_plane(low, high, above, below, p)
            return a[i, m, :, edge]

        own[m] = own_strip(at[2], load)


def pack_z2(where, own, y_above, y_below, out):
    gx, gy, gz = pos(where)
    edge = edge_tiles(gz)
    for m in range(MODES):
        out[m, 0:CY, :] = own[m]
        out[m, CY:PY, :] = own_strip(gz, lambda p, m=m: raw_halo(y_above, y_below, m, p, edge), 8)


def strip_kernel2(
    where, mask, y_above, y_below, ends, bulk, out, side, edges, strips, table, sb, one, two, held, left
):
    gx, gy, gz = at = pos(where)
    sub, lane = sub_lane()
    fill_strips(table, gy, gz)

    def source(m, p):
        return raw_halo(y_above, y_below, m, p)

    strip_sweeps(MODES, at, table, source, ends, (sb, one, two), edges, strips)
    copies = []
    for m in range(MODES):
        for x in range(CX):
            for i in range(CY // 8):
                rows = slice(8 * i, 8 * i + 8)
                pair = []
                for j in range(2):
                    cols = slice(LANES * j, LANES * j + LANES)
                    value = pair_tile(m, x, i, j, bulk, strips, sub)
                    held[m, x, rows, cols] = value * mask[x, rows, cols].astype(F32)
                    pair.append(value)
                side[m, x, rows, :] = jnp.where(gz == 0, pair[1], pair[0])
            if x % 4 == 3:
                part = (m, slice(x - 3, x + 1))
                copy = pltpu.make_async_copy(held.at[part], out.at[part], left.at[len(copies)])
                copy.start()
                copies.append(copy)
    for copy in copies:
        copy.wait()


def final_kernel(where, mask, z_in, bulk_edges, strip_edges, side, given, out, held, left):
    gx, gy, gz = pos(where)
    sub, lane = sub_lane()
    at_end = beside_halo(gz, lane)
    beside = at_end[0] | at_end[1]
    edge = edge_tiles(gz)
    scale = strip_scale(gx, gy)
    copies = []
    for m in range(MODES):
        z_state = z_sweeps(m, scale, z_in[m], bulk_edges, strip_edges)
        for x in range(CX):
            for i in range(CY // 8):
                rows = slice(8 * i, 8 * i + 8)
                value = side[m, x, rows, :] + jnp.where(beside, z_tile(z_state, x, i), 0.0)
                held[m, x, rows, :] = value * mask[x, rows, edge].astype(F32)
            if x % 4 == 3:
                planes = slice(x - 3, x + 1)
                copy = pltpu.make_async_copy(
                    held.at[m, planes], out.at[m, planes, :, edge], left.at[len(copies)]
                )
                copy.start()
                copies.append(copy)
    for copy in copies:
        copy.wait()


SMEM = pl.BlockSpec(memory_space=pltpu.SMEM)


def whole(x):
    return pl.BlockSpec(x.shape, lambda i: (0,) * x.ndim)


def call(kernel, name, outs, args, specs=None, out_specs=None, scratch=(), flops=0, aliases=None):
    specs = specs or {}
    shapes = tuple(jax.ShapeDtypeStruct(s, F32) for s in outs)
    out_specs = out_specs or {}
    out_specs = tuple(out_specs.get(i, whole(s)) for i, s in enumerate(shapes))
    return pl.pallas_call(
        kernel,
        grid=(1,),
        out_shape=shapes if len(shapes) > 1 else shapes[0],
        in_specs=[specs.get(i, SMEM if a.ndim == 1 else whole(a)) for i, a in enumerate(args)],
        scratch_shapes=[pltpu.VMEM(s, F32) if isinstance(s, tuple) else s for s in scratch],
        compiler_params=pltpu.CompilerParams(vmem_limit_bytes=24 * 1024 * 1024),
        cost_estimate=pl.CostEstimate(flops=flops, bytes_accessed=2_000_000, transcendentals=0),
        name=name,
        out_specs=out_specs if len(shapes) > 1 else out_specs[0],
        input_output_aliases=aliases or {},
    )(*args)


HBM = pl.BlockSpec(memory_space=pltpu.HBM)


def ring(axis, step):
    size = lax.axis_size(axis)
    return [(i, (i + step) % size) for i in range(size)]


def shift(x, axis, step):
    return lax.ppermute(x, axis, ring(axis, step))


def sweep_outs(fields):
    return (
        [(fields, CX, CY, CZ), (fields, ITERS, PX, 2, 1, CZ), (fields, ITERS, CY, LANES)],
        [(3, CY, CZ)] + [(fields, PX, CY, CZ)] * 3,
        [(fields, CX, 16, CZ), (fields, ITERS, 16, LANES)],
        [(3, 16, CZ)] + [(fields, PX, 16, CZ)] * 3,
    )


def local(mode_fields, design, solid_mask, eigenvalues, mode_order):
    where = jnp.stack([lax.axis_index(a) for a in ("gx", "gy", "gz")]).astype(jnp.int32)
    bulk_outs, bulk_scratch, strip_outs, strip_scratch = sweep_outs(1)

    src, down, up = call(
        pack_x1, "pack_x1", [(CX, CY, CZ), (W + 6, CY, CZ), (W, CY, CZ)],
        tuple(pltpu.with_memory_space_constraint(x, pltpu.HBM) for x in (design, solid_mask, mode_fields)),
        {0: HBM, 1: HBM, 2: HBM},
        scratch=[(CX, CY, CZ), pltpu.VMEM((CX, CY, CZ), jnp.int32), pltpu.SemaphoreType.DMA((2 * CX + 6,))],
    )
    above, below = shift(down, "gx", -1), shift(up, "gx", 1)
    field = (MODES, CX - 1, CY, CZ)
    stiff, mass, columns, first_rows = call(
        energy_kernel, "energy", [field, field, (2, CY, LANES), (8, 8, CZ)], (mode_fields,), flops=40_000_000
    )

    down, up = call(
        pack_y1, "pack_y1", [(16, 8, CZ), (8, 8, CZ)], (where, src, first_rows, columns, above, below)
    )
    y_above, y_below = shift(down, "gy", -1), shift(up, "gy", 1)
    plane = (MODES, CY, CZ)
    bulk, ends, bulk_edges, stiff7, mass7, own, rims = call(
        bulk_kernel1, "bulk1", bulk_outs + [plane, plane, (1, CY, LANES), (2, CY, LANES)],
        (where, src, mode_fields, columns, above, below), scratch=bulk_scratch, flops=30_000_000,
    )

    z_in = shift(call(pack_z1, "pack_z1", [(2, PY, LANES)], (where, own, rims, y_above, y_below)), "gz", 1)
    strips, strip_edges, rim, packed = call(
        strip_kernel1, "strips1", strip_outs + [(MODES, 2, 8, CZ), (PY, LANES)],
        (where, mode_fields, rims, above, y_above, y_below, ends),
        scratch=strip_scratch + [(3, 16, CZ)] * 2, flops=20_000_000,
    )
    half = (W, MODES, CY, CZ)
    scalars = (eigenvalues, mode_order, where)
    energies = (stiff, mass, stiff7, mass7, rim)
    low, z_parts = call(
        raw_kernel1, "raw1", [half, (3, CY, LANES)],
        (*scalars, z_in, packed, bulk, bulk_edges, strips, strip_edges, *energies),
    )
    above = shift(low, "gx", -1)
    high = call(raw_kernel2, "raw2", [half], (*scalars, z_parts, bulk, strips, *energies), flops=60_000_000)
    below = shift(high, "gx", 1)

    bulk_outs, bulk_scratch, strip_outs, strip_scratch = sweep_outs(MODES)
    planes = (low, high, above, below)
    down, up = call(pack_y2, "pack_y2", [(CX + 3, 8, CZ)] * 2, planes)
    y_above, y_below = shift(down, "gy", -1), shift(up, "gy", 1)
    bulk, ends, bulk_edges, own = call(
        bulk_kernel2, "bulk2", bulk_outs + [(MODES, CY, LANES)], (where, *planes),
        scratch=bulk_scratch, flops=40_000_000,
    )
    z_in = shift(call(pack_z2, "pack_z2", [(MODES, PY, LANES)], (where, own, y_above, y_below)), "gz", 1)
    result = (MODES, CX, CY, CZ)
    out, side, strip_edges = call(
        strip_kernel2, "strips2", [result, (MODES, CX, CY, LANES), strip_outs[1]],
        (where, solid_mask, y_above, y_below, ends, bulk), out_specs={0: HBM},
        scratch=[strip_outs[0]] + strip_scratch + [result, pltpu.SemaphoreType.DMA((4,))],
        flops=20_000_000,
    )
    return call(
        final_kernel, "final", [result],
        (where, solid_mask, z_in, bulk_edges, strip_edges, side, out), {6: HBM}, {0: HBM},
        scratch=[(MODES, CX, CY, LANES), pltpu.SemaphoreType.DMA((4,))], aliases={6: 0},
    )


def solution(mesh):
    return jax.shard_map(
        local,
        mesh=mesh,
        in_specs=(
            P(None, None, "gx", "gy", "gz"),
            P("gx", "gy", "gz"),
            P("gx", "gy", "gz"),
            P(),
            P(),
        ),
        out_specs=P(None, "gx", "gy", "gz"),
        check_vma=False,
    )
```

```python
import jax
import jax.numpy as jnp
from jax import lax
from jax.experimental import pallas as pl
from jax.experimental.pallas import tpu as pltpu
from jax.sharding import PartitionSpec as P

ITERS = 4
MODES = 2
CX, CY, CZ = 8, 32, 256
W = ITERS
PX = CX + 2 * W
PY = CY + 8
NODES = CX + 1
LANES = 128

poisson = 0.3
radius_sq = 3.0
stiff_floor = 0.001
LAME = poisson / ((1.0 + poisson) * (1.0 - 2.0 * poisson))
SHEAR = 0.5 / (1.0 + poisson)

F32 = jnp.float32


def iota(shape, dim):
    return lax.broadcasted_iota(jnp.int32, shape, dim)


def pos():
    return tuple(lax.axis_index(a) for a in ("gx", "gy", "gz"))


def sub_lane():
    return iota((8, LANES), 0), iota((8, LANES), 1)


def total_of(terms):
    terms = [t for t in terms if t is not None]
    while len(terms) > 1:
        pairs = [terms[i] + terms[i + 1] for i in range(0, len(terms) - 1, 2)]
        terms = pairs + ([terms[-1]] if len(terms) % 2 else [])
    return terms[0]


def scales(count, inside):
    outside = jnp.zeros(count.shape, F32)
    end = jnp.where(inside, radius_sq / (1.0 + radius_sq * (count + 1.0)), 0.0)
    mid = jnp.where(inside, radius_sq / (1.0 + radius_sq * (count + 2.0)), 0.0)
    return outside, end, mid


def yz_scales(y, z, gy, gz):
    y, z = y + gy * CY, z + gz * CZ
    inside = (y >= 0) & (y < 8 * CY)
    count = 4.0
    for place, last in ((y, 8 * CY - 1), (z, 2 * CZ - 1)):
        count = count - (place == 0).astype(F32) - (place == last).astype(F32)
    return scales(count, inside)


def kind_of(gx, plane):
    x = gx * CX + plane - W
    out = (x < 0) | (x > 8 * CX - 1)
    end = (x == 0) | (x == 8 * CX - 1)
    return jnp.where(out, 0, jnp.where(end, 1, 2))


def fill_bulk(table, gy, gz):
    shape = (CY, CZ)
    for i, part in enumerate(yz_scales(iota(shape, 0), iota(shape, 1), gy, gz)):
        table[i] = part


def fill_strips(table, gy, gz):
    shape = (16, CZ)
    row = iota(shape, 0)
    top = jnp.where(row < 4, row + CY, row + CY - 8)
    bottom = jnp.where(row < 12, row - 8, row - 16)
    for i, part in enumerate(yz_scales(jnp.where(row < 8, top, bottom), iota(shape, 1), gy, gz)):
        table[i] = part


def strip_scale(gx, gy):
    shape = (PY, LANES)
    row = iota(shape, 0)
    y = jnp.where(row < CY + W, row, row - PY) + gy * CY
    x = gx * CX - W + lax.div(iota(shape, 1), 8)
    inside = (y >= 0) & (y < 8 * CY) & (x >= 0) & (x < 8 * CX)
    count = 6.0
    for place, last in ((y, 8 * CY - 1), (x, 8 * CX - 1)):
        count = count - (place == 0).astype(F32) - (place == last).astype(F32)
    return jnp.where(inside, radius_sq / (1.0 + radius_sq * count), 0.0)


def tiles_of(ref, index, rows, cols):
    return [
        [ref[index + (slice(8 * i, 8 * i + 8), slice(LANES * j, LANES * j + LANES))] for j in range(cols)]
        for i in range(rows)
    ]


def along_lanes(row, lane):
    right = [pltpu.roll(t, 1, 1) for t in row]
    left = [pltpu.roll(t, LANES - 1, 1) for t in row]
    out = []
    for j in range(len(row)):
        before = right[j - 1] if j else 0.0
        after = left[j + 1] if j + 1 < len(row) else 0.0
        out.append(
            jnp.where(lane == 0, before, right[j]) + jnp.where(lane == LANES - 1, after, left[j])
        )
    return out


def along_rows(tiles, sub):
    rows, cols = len(tiles), len(tiles[0])
    down = [[pltpu.roll(t, 1, 0) for t in row] for row in tiles]
    up = [[pltpu.roll(t, 7, 0) for t in row] for row in tiles]
    out = []
    for i in range(rows):
        line = []
        for j in range(cols):
            before = down[i - 1][j] if i else 0.0
            after = up[i + 1][j] if i + 1 < rows else 0.0
            line.append(jnp.where(sub == 0, before, down[i][j]) + jnp.where(sub == 7, after, up[i][j]))
        out.append(line)
    return out


def turn_edge(tile, p, gz):
    return pltpu.roll(tile, lax.rem(8 * p + 5 - 2 * gz, LANES), 1)


def kind_at(gx, p):
    return 2 if W < p < PX - W - 1 else kind_of(gx, p)


def bulk_sweeps(fields, where, table, source, states, ends, edges, out):
    gx, gy, gz = where
    sub, lane = sub_lane()
    sb = states[0]
    for p in range(PX):
        kind = kind_at(gx, p)
        for m in range(fields):
            for i in range(CY // 8):
                rows = slice(8 * i, 8 * i + 8)
                sb[m, p, rows, :] = source(m, p, i) * (table[kind, rows, :] * (1.0 / radius_sq))
    for k in range(ITERS):
        old = states[0] if k == 0 else states[1 + (k - 1) % 2]
        new = states[1 + k % 2]
        for m in range(fields):
            edge = [jnp.zeros((8, LANES), F32)] * (CY // 8)
            for p in range(k + 1, PX - 1 - k):
                kind = kind_at(gx, p)
                mid = tiles_of(old, (m, p), CY // 8, 2)
                yy = along_rows(mid, sub)
                for i in range(CY // 8):
                    zz = along_lanes(mid[i], lane)
                    rows = slice(8 * i, 8 * i + 8)
                    for j in range(2):
                        cols = slice(LANES * j, LANES * j + LANES)
                        total = old[m, p - 1, rows, cols] + old[m, p + 1, rows, cols]
                        total = total + (yy[i][j] + zz[j])
                        value = sb[m, p, rows, cols] + table[kind, rows, cols] * total
                        if k + 1 < ITERS:
                            new[m, p, rows, cols] = value
                        else:
                            out[m, p - W, rows, cols] = value
                    side = jnp.where(gz == 0, mid[i][1], mid[i][0])
                    edge[i] = jnp.where(lane == 8 * p + 4 - gz, turn_edge(side, p, gz), edge[i])
                for j in range(2):
                    cols = slice(LANES * j, LANES * j + LANES)
                    ends[m, k, p, 0, 0:1, cols] = mid[CY // 8 - 1][j][7:8]
                    ends[m, k, p, 1, 0:1, cols] = mid[0][j][0:1]
            for i in range(CY // 8):
                edges[m, k, 8 * i : 8 * i + 8, :] = edge[i]


def strip_sweeps(fields, where, table, source, ends, states, edges, out):
    gx, gy, gz = where
    sub, lane = sub_lane()
    sb = states[0]
    wide = iota((8, CZ), 0)
    for p in range(PX):
        kind = kind_at(gx, p)
        for m in range(fields):
            halo = source(m, p) * (1.0 / radius_sq)
            sb[m, p, 0:8, :] = jnp.where(wide < 4, halo * table[kind, 0:8, :], 0.0)
            sb[m, p, 8:16, :] = jnp.where(wide < 4, 0.0, halo * table[kind, 8:16, :])
    for k in range(ITERS):
        old = states[0] if k == 0 else states[1 + (k - 1) % 2]
        new = states[1 + k % 2]
        for m in range(fields):
            edge = [jnp.zeros((8, LANES), F32)] * 2
            for p in range(k + 1, PX - 1 - k):
                kind = kind_at(gx, p)
                mid = tiles_of(old, (m, p), 2, 2)
                for i in range(2):
                    rows = slice(8 * i, 8 * i + 8)
                    zz = along_lanes(mid[i], lane)
                    for j in range(2):
                        cols = slice(LANES * j, LANES * j + LANES)
                        end = jnp.broadcast_to(ends[m, k, p, i, 0:1, cols], (8, LANES))
                        down = pltpu.roll(mid[i][j], 1, 0)
                        up = pltpu.roll(mid[i][j], 7, 0)
                        if i == 0:
                            down = jnp.where(sub == 4, 0.0, down) + jnp.where(sub == 0, end, 0.0)
                        else:
                            up = jnp.where(sub == 3, 0.0, up) + jnp.where(sub == 7, end, 0.0)
                        total = old[m, p - 1, rows, cols] + old[m, p + 1, rows, cols]
                        total = total + (down + up) + zz[j]
                        value = sb[m, p, rows, cols] + table[kind, rows, cols] * total
                        if k + 1 < ITERS:
                            new[m, p, rows, cols] = value
                        else:
                            out[m, p - W, rows, cols] = value
                    side = jnp.where(gz == 0, mid[i][1], mid[i][0])
                    edge[i] = jnp.where(lane == 8 * p + 4 - gz, turn_edge(side, p, gz), edge[i])
            for i in range(2):
                edges[m, k, 8 * i : 8 * i + 8, :] = edge[i]


def z_sweeps(m, scale, halo, bulk_edges, strip_edges):
    sub = iota((8, LANES), 0)
    column = lax.rem(iota((PY, LANES), 1), 8)
    base = halo * (scale * (1.0 / radius_sq))
    state = base
    for k in range(ITERS):
        top, bottom = strip_edges[m, k, 0:8, :], strip_edges[m, k, 8:16, :]
        own = bulk_edges[m, k]
        fed = jnp.concatenate(
            [
                own[0:8] + jnp.where(sub < 4, bottom, 0.0),
                own[8 : CY - 8],
                own[CY - 8 : CY] + jnp.where(sub < 4, 0.0, top),
                jnp.where(sub < 4, top, bottom),
            ],
            axis=0,
        )
        total = pltpu.roll(state, 8, 1) + pltpu.roll(state, LANES - 8, 1)
        total = total + pltpu.roll(state, 1, 0) + pltpu.roll(state, PY - 1, 0)
        total = total + jnp.where(column == 0, 0.0, pltpu.roll(state, 1, 1))
        total = total + jnp.where(column == 7, 0.0, pltpu.roll(state, LANES - 1, 1))
        state = base + scale * (total + fed)
    return state


def pair_tile(m, x, i, j, bulk, strips, sub):
    rows, cols = slice(8 * i, 8 * i + 8), slice(LANES * j, LANES * j + LANES)
    value = bulk[m, x, rows, cols]
    if i == 0:
        value = value + jnp.where(sub < 4, strips[m, x, 8:16, cols], 0.0)
    if i == CY // 8 - 1:
        value = value + jnp.where(sub < 4, 0.0, strips[m, x, 0:8, cols])
    return value


def z_tile(z_state, x, i):
    return pltpu.roll(z_state[8 * i : 8 * i + 8], (LANES - 4 - 8 * (x + W)) % LANES, 1)


def beside_halo(gz, lane):
    return (lane < 4 * gz), (lane >= LANES - 4 * (1 - gz))


def pack_strip(gz, tile, p, acc, lane):
    first = 8 * p + 4 * gz
    turned = pltpu.roll(tile, (8 * p + 4) % LANES, 1)
    return jnp.where((lane >= first) & (lane < first + 4), turned, acc)


def own_strip(gz, load, rows=CY):
    lane = iota((rows, LANES), 1)
    acc = jnp.zeros((rows, LANES), F32)
    for p in range(PX):
        acc = pack_strip(gz, load(p), p, acc, lane)
    return acc


def edge_tiles(gz):
    return pl.ds(pl.multiple_of((1 - gz) * LANES, LANES), LANES)


def energy_terms(prev, cur):
    (paa, pad, pda, pdd), (caa, cad, cda, cdd) = prev, cur
    u, v, w = 0, 1, 2
    aad = [cad[i] + pad[i] for i in range(3)]
    ada = [cda[i] + pda[i] for i in range(3)]
    add = [cdd[i] + pdd[i] for i in range(3)]
    daa = [caa[i] - paa[i] for i in range(3)]
    dad = [cad[i] - pad[i] for i in range(3)]
    dda = [cda[i] - pda[i] for i in range(3)]
    ddd = [cdd[i] - pdd[i] for i in range(3)]

    def sq(x):
        return x * x

    trace = sq(daa[u] + ada[v] + aad[w])
    lines = sq(dda[v] + dad[w]) + sq(dda[u] + add[w]) + sq(dad[u] + add[v])
    diag = sq(daa[u]) + sq(ada[v]) + sq(aad[w])
    shear = sq(ada[u] + daa[v]) + sq(aad[u] + daa[w]) + sq(aad[v] + ada[w])
    mixed = sq(dda[u]) + sq(dda[v]) + sq(dad[u]) + sq(dad[w]) + sq(add[v]) + sq(add[w])
    cross = sq(add[u] + dad[v]) + sq(add[u] + dda[w]) + sq(dad[v] + dda[w])
    cubic = sq(ddd[u]) + sq(ddd[v]) + sq(ddd[w])
    return (
        LAME * (trace + lines * (1.0 / 3.0))
        + SHEAR * (2.0 * diag + shear + mixed + cross * (1.0 / 3.0))
        + ((LAME + 4.0 * SHEAR) / 9.0) * cubic
    )


def y_parts(pairs):
    aa = [a0 + a1 for a0, d0, a1, d1 in pairs]
    ad = [d0 + d1 for a0, d0, a1, d1 in pairs]
    da = [a1 - a0 for a0, d0, a1, d1 in pairs]
    dd = [d1 - d0 for a0, d0, a1, d1 in pairs]
    return aa, ad, da, dd


def mass_of(parts):
    return total_of([x * x for part in parts for x in part])


def z_pair(here):
    after = pltpu.roll(here, CZ - 1, 1)
    return here + after, after - here


def own_parts(load, chunk):
    sub = iota((8, CZ), 0)
    pairs = []
    for c in range(3):
        a0, d0 = z_pair(load(c, 8 * chunk))
        following = min(chunk + 1, CY // 8 - 1)
        a1, d1 = z_pair(load(c, 8 * following))

        def next_row(t, n):
            return jnp.where(sub == 7, pltpu.roll(n, 7, 0), pltpu.roll(t, 7, 0))

        pairs.append((a0, d0, next_row(a0, a1), next_row(d0, d1)))
    return y_parts(pairs)


def pack_columns(load, lane):
    first = jnp.zeros((CY, LANES), F32)
    last = first
    for m in range(MODES):
        for c in range(3):
            for x in range(CX):
                to = 32 * m + NODES * c + x
                here = lane == to
                first = jnp.where(here, pltpu.roll(load(m, c, x, 0), to, 1), first)
                last = jnp.where(here, pltpu.roll(load(m, c, x, 1), to + 1, 1), last)
    return first, last


def with_plane8(packed, above, keep_x, last):
    cols = slice(CZ - LANES, CZ) if last else slice(0, LANES)
    rows = packed.shape[0]
    lane = iota(packed.shape, 1)
    for m in range(MODES):
        for c in range(3):
            to = 32 * m + NODES * c + CX
            turned = pltpu.roll(above[W + 3 * m + c, 0:rows, cols], to + last, 1)
            packed = jnp.where(lane == to, turned * keep_x, packed)
    return packed


def with_row32(packed, y_above, keep_y, last):
    sub, lane = sub_lane()
    row = y_above[11, 3:4, LANES * last : LANES * last + LANES] * keep_y
    return jnp.concatenate([packed, jnp.where(sub == 0, jnp.broadcast_to(row, (8, LANES)), 0.0)], axis=0)


def pack_x1(design, mask, modes, src, down, up, field, solid, arrived):
    copies = []
    for x in range(CX):
        copies.append(pltpu.make_async_copy(design.at[x], field.at[x], arrived.at[2 * x]))
        copies.append(pltpu.make_async_copy(mask.at[x], solid.at[x], arrived.at[2 * x + 1]))
    for n in range(3 * MODES):
        to = down.at[W + n]
        copies.append(pltpu.make_async_copy(modes.at[n // 3, n % 3, 0], to, arrived.at[2 * CX + n]))
    for copy in copies:
        copy.start()
    for x in range(CX):
        copies[2 * x].wait()
        copies[2 * x + 1].wait()
        plane = field[x] * solid[x].astype(F32)
        src[x] = plane
        if x < W:
            down[x] = plane
        if x >= CX - W:
            up[x - (CX - W)] = plane
    for copy in copies[2 * CX :]:
        copy.wait()


def energy_kernel(modes, stiff, mass, columns, first_rows):
    lane = iota((CY, LANES), 1)
    columns[0], columns[1] = pack_columns(
        lambda m, c, x, j: modes[m, c, x, :, LANES * j : LANES * j + LANES], lane
    )

    for m in range(MODES):
        first_rows[4 * m + 3] = jnp.zeros((8, CZ), F32)
        for c in range(3):
            for x in range(CX):
                n = NODES * c + x
                first_rows[4 * m + n // 8, n % 8 : n % 8 + 1, :] = modes[m, c, x, 0:1, :]

    def mode_step(m, carry):
        for chunk in range(CY // 8):
            rows = slice(8 * chunk, 8 * chunk + 8)
            prev = prev_mass = None
            for x in range(CX):
                cur = own_parts(lambda c, r: modes[m, c, x, r : r + 8, :], chunk)
                cur_mass = mass_of(cur)
                if x:
                    stiff[m, x - 1, rows, :] = energy_terms(prev, cur)
                    mass[m, x - 1, rows, :] = cur_mass + prev_mass
                prev, prev_mass = cur, cur_mass
        return carry

    lax.fori_loop(0, MODES, mode_step, 0)


def pick_plane(own, above, below, p):
    if p < W:
        return below, p
    if p < W + CX:
        return own, p - W
    return above, p - W - CX


def pack_y1(src, first_rows, columns, above, below, down, up):
    gx, gy, gz = pos()
    low = iota((8, CZ), 0) < 4
    for q in range(8):
        a, i = pick_plane(src, above, below, q)
        b, j = pick_plane(src, above, below, q + 8)
        down[q] = jnp.where(low, a[i, 0:8, :], pltpu.roll(b[j, 0:8, :], 4, 0))
        up[q] = jnp.where(low, pltpu.roll(b[j, 24:32, :], 4, 0), a[i, 24:32, :])
    keep = jnp.where(gx < 7, 1.0, 0.0)
    down[8:16] = first_rows[...]
    for m in range(MODES):
        for c in range(3):
            n = NODES * c + CX
            down[8 + 4 * m + n // 8, n % 8 : n % 8 + 1, :] = above[W + 3 * m + c, 0:1, :] * keep
    for last in range(2):
        row = with_plane8(columns[last, 0:8, :], above, keep, last)
        down[11, 3:4, LANES * last : LANES * last + LANES] = row[0:1]


def bulk_kernel1(
    src, modes, columns, above, below,
    bulk, ends, edges, stiff, mass, own, rims, table, sb, one, two,
):
    at = pos()
    gx, gy, gz = at
    fill_bulk(table, gy, gz)

    def source(m, p, i):
        a, at_plane = pick_plane(src, above, below, p)
        return a[at_plane, 8 * i : 8 * i + 8, :]

    bulk_sweeps(1, at, table, source, (sb, one, two), ends, edges, bulk)
    edge = edge_tiles(gz)
    own[0] = own_strip(gz, lambda p: plane_edge(src, above, below, p, edge))
    keep = jnp.where(gx < 7, 1.0, 0.0)
    for last in range(2):
        rims[last] = with_plane8(columns[last], above, keep, last)
    for m in range(MODES):
        for chunk in range(CY // 8):
            rows = slice(8 * chunk, 8 * chunk + 8)
            prev = own_parts(lambda c, r: modes[m, c, CX - 1, r : r + 8, :], chunk)
            cur = own_parts(lambda c, r: above[W + 3 * m + c, r : r + 8, :] * keep, chunk)
            stiff[m, rows, :] = energy_terms(prev, cur)
            mass[m, rows, :] = mass_of(cur) + mass_of(prev)


def halo_tile(y_above, y_below, p, lanes=slice(None)):
    a, b = y_above[p % 8, :, lanes], y_below[p % 8, :, lanes]
    if p >= 8:
        a, b = pltpu.roll(a, 4, 0), pltpu.roll(b, 4, 0)
    return jnp.where(iota(a.shape, 0) < 4, a, b)


def plane_edge(own, above, below, p, edge):
    a, i = pick_plane(own, above, below, p)
    return a[i, :, edge]


def pack_z1(own, rims, y_above, y_below, out):
    gx, gy, gz = pos()
    edge = edge_tiles(gz)
    out[0, 0:CY, :] = own[0]
    out[0, CY:PY, :] = own_strip(gz, lambda p: halo_tile(y_above, y_below, p, edge), 8)
    out[1] = with_row32(rims[0], y_above, jnp.where(gy < 7, 1.0, 0.0), 0)


def strip_kernel1(
    modes, rims, above, y_above, y_below, ends,
    strips, edges, rim, packed, table, sb, one, two, near, far,
):
    at = pos()
    gx, gy, gz = at
    fill_strips(table, gy, gz)
    strip_sweeps(
        1, at, table, lambda m, p: halo_tile(y_above, y_below, p), ends, (sb, one, two), edges, strips
    )
    keep_x = jnp.where(gx < 7, 1.0, 0.0)
    keep_y = jnp.where(gy < 7, 1.0, 0.0)
    packed[...] = with_row32(rims[1], y_above, keep_y, 1)
    for m in range(MODES):
        for c in range(3):
            for x in range(NODES):
                n = c * NODES + x
                row = above[W + 3 * m + c, CY - 1 : CY, :] * keep_x
                if x < CX:
                    row = modes[m, c, x, CY - 1 : CY, :]
                near[c, x : x + 1, :] = row
                far[c, x : x + 1, :] = (
                    y_above[8 + 4 * m + n // 8, n % 8 : n % 8 + 1, :] * keep_y
                )

        def parts(first):
            pairs = []
            for c in range(3):
                a0, d0 = z_pair(near[c, first : first + 8, :])
                a1, d1 = z_pair(far[c, first : first + 8, :])
                pairs.append((a0, d0, a1, d1))
            return y_parts(pairs)

        prev, cur = parts(0), parts(1)
        rim[m, 0] = energy_terms(prev, cur)
        rim[m, 1] = mass_of(cur) + mass_of(prev)


def raw_planes(
    planes, lams, gz, z_state, column_stiff, column_mass, bulk, strips,
    stiff, mass, stiff7, mass7, rim, out,
):
    sub, lane = sub_lane()
    beside = beside_halo(gz, lane)
    factor = 3.0 * (1.0 - stiff_floor) / 16.0
    for x in planes:
        for i in range(CY // 8):
            rows = slice(8 * i, 8 * i + 8)
            correction = z_tile(z_state, x, i)
            for j in range(2):
                cols = slice(LANES * j, LANES * j + LANES)
                phys = pair_tile(0, x, i, j, bulk, strips, sub) + jnp.where(beside[j], correction, 0.0)
                phys = (factor * phys) * phys
                for m in range(MODES):
                    if x < CX - 1:
                        k, e = stiff[m, x, rows, cols], mass[m, x, rows, cols]
                    else:
                        k, e = stiff7[m, rows, cols], mass7[m, rows, cols]
                    if i == CY // 8 - 1:
                        k = jnp.where(sub == 7, jnp.broadcast_to(rim[m, 0, x : x + 1, cols], (8, LANES)), k)
                        e = jnp.where(sub == 7, jnp.broadcast_to(rim[m, 1, x : x + 1, cols], (8, LANES)), e)
                    if j == 1:
                        by = LANES - 1 - (32 * m + x)
                        k = jnp.where(lane == LANES - 1, pltpu.roll(column_stiff[rows, :], by, 1), k)
                        e = jnp.where(lane == LANES - 1, pltpu.roll(column_mass[rows, :], by, 1), e)
                    out[x % W, m, rows, cols] = phys * k - lams[m] * e


def raw_kernel1(
    lams, z_in, packed, bulk, bulk_edges, strips, strip_edges,
    stiff, mass, stiff7, mass7, rim, low, z_parts,
):
    gx, gy, gz = pos()
    z_state = z_sweeps(0, strip_scale(gx, gy), z_in[0], bulk_edges, strip_edges)

    near, far = packed[...], z_in[1] * jnp.where(gz < 1, 1.0, 0.0)
    a0, d0 = near + far, far - near
    a1, d1 = pltpu.roll(a0, PY - 1, 0), pltpu.roll(d0, PY - 1, 0)
    parts = [(x[0][0:CY]) for x in y_parts([(a0, d0, a1, d1)])]

    def turned(t, by):
        return pltpu.roll(t, (LANES - by) % LANES, 1) if by else t

    prev = [[turned(t, NODES * c) for c in range(3)] for t in parts]
    cur = [[turned(t, NODES * c + 1) for c in range(3)] for t in parts]
    column_stiff = energy_terms(prev, cur)
    column_mass = mass_of(cur) + mass_of(prev)
    z_parts[0], z_parts[1], z_parts[2] = z_state[0:CY], column_stiff, column_mass
    raw_planes(
        range(W), lams, gz, z_state, column_stiff, column_mass, bulk, strips,
        stiff, mass, stiff7, mass7, rim, low,
    )


def raw_kernel2(
    lams, z_parts, bulk, strips, stiff, mass, stiff7, mass7, rim, high
):
    gx, gy, gz = pos()
    raw_planes(
        range(W, CX), lams, gz, z_parts[0], z_parts.at[1], z_parts.at[2], bulk, strips,
        stiff, mass, stiff7, mass7, rim, high,
    )


def raw_plane(low, high, above, below, p):
    if p < W:
        return below, p
    if p < 2 * W:
        return low, p - W
    if p < 3 * W:
        return high, p - 2 * W
    return above, p - 3 * W


SHARED = ((PX - W, PX - W + 2, 3), (W - 1, W - 3, 3), (PX - W + 1, W - 2, 2))


def rolled(tile, by):
    return pltpu.roll(tile, by % 8, 0) if by % 8 else tile


def pack_y2(low, high, above, below, down, up):
    sub = iota((8, CZ), 0)

    def rows(p, m, start):
        a, i = raw_plane(low, high, above, below, p)
        return a[i, m, start : start + 8, :]

    def both(tiles, first):
        return jnp.where(sub < 4, rolled(tiles[0], -first), rolled(tiles[1], 4 - first))

    for p in range(W, W + CX):
        down[p - W] = both([rows(p, m, 0) for m in range(MODES)], 0)
        up[p - W] = both([rows(p, m, 24) for m in range(MODES)], 4)
    for n, (p, q, count) in enumerate(SHARED):
        down[CX + n] = both(
            [jnp.where(sub < count, rows(p, m, 0), rolled(rows(q, m, 0), count)) for m in range(MODES)], 0
        )
        up[CX + n] = both(
            [jnp.where(sub >= 8 - count, rows(p, m, 24), rolled(rows(q, m, 24), -count)) for m in range(MODES)], 4
        )


def raw_halo(y_above, y_below, m, p, lanes=slice(None)):
    if W <= p < W + CX:
        n, skip = p - W, 0
    else:
        found = [(CX + n, 0 if p == s[0] else s[2]) for n, s in enumerate(SHARED) if p in s[:2]]
        if not found:
            return jnp.zeros(y_above[0, :, lanes].shape, F32)
        n, skip = found[0]
    a = rolled(y_above[n, :, lanes], 4 * m - skip)
    b = rolled(y_below[n, :, lanes], 4 * (1 - m) + skip)
    return jnp.where(iota(a.shape, 0) < 4, a, b)


def bulk_kernel2(low, high, above, below, bulk, ends, edges, own, table, sb, one, two):
    at = pos()
    fill_bulk(table, at[1], at[2])

    def source(m, p, i):
        a, at_plane = raw_plane(low, high, above, below, p)
        return a[at_plane, m, 8 * i : 8 * i + 8, :]

    bulk_sweeps(MODES, at, table, source, (sb, one, two), ends, edges, bulk)
    edge = edge_tiles(at[2])
    for m in range(MODES):

        def load(p, m=m):
            a, i = raw_plane(low, high, above, below, p)
            return a[i, m, :, edge]

        own[m] = own_strip(at[2], load)


def pack_z2(own, y_above, y_below, out):
    gx, gy, gz = pos()
    edge = edge_tiles(gz)
    for m in range(MODES):
        out[m, 0:CY, :] = own[m]
        out[m, CY:PY, :] = own_strip(gz, lambda p, m=m: raw_halo(y_above, y_below, m, p, edge), 8)


def strip_kernel2(
    mask, y_above, y_below, ends, bulk, out, side, edges, strips, table, sb, one, two, held, left
):
    gx, gy, gz = at = pos()
    sub, lane = sub_lane()
    fill_strips(table, gy, gz)

    def source(m, p):
        return raw_halo(y_above, y_below, m, p)

    strip_sweeps(MODES, at, table, source, ends, (sb, one, two), edges, strips)
    copies = []
    for m in range(MODES):
        for x in range(CX):
            for i in range(CY // 8):
                rows = slice(8 * i, 8 * i + 8)
                pair = []
                for j in range(2):
                    cols = slice(LANES * j, LANES * j + LANES)
                    value = pair_tile(m, x, i, j, bulk, strips, sub)
                    held[m, x, rows, cols] = value * mask[x, rows, cols].astype(F32)
                    pair.append(value)
                side[m, x, rows, :] = jnp.where(gz == 0, pair[1], pair[0])
            if x % 4 == 3:
                part = (m, slice(x - 3, x + 1))
                copy = pltpu.make_async_copy(held.at[part], out.at[part], left.at[len(copies)])
                copy.start()
                copies.append(copy)
    for copy in copies:
        copy.wait()


def final_kernel(mask, z_in, bulk_edges, strip_edges, side, given, out, held, left):
    gx, gy, gz = pos()
    sub, lane = sub_lane()
    at_end = beside_halo(gz, lane)
    beside = at_end[0] | at_end[1]
    edge = edge_tiles(gz)
    scale = strip_scale(gx, gy)
    copies = []
    for m in range(MODES):
        z_state = z_sweeps(m, scale, z_in[m], bulk_edges, strip_edges)
        for x in range(CX):
            for i in range(CY // 8):
                rows = slice(8 * i, 8 * i + 8)
                value = side[m, x, rows, :] + jnp.where(beside, z_tile(z_state, x, i), 0.0)
                held[m, x, rows, :] = value * mask[x, rows, edge].astype(F32)
            if x % 4 == 3:
                planes = slice(x - 3, x + 1)
                copy = pltpu.make_async_copy(
                    held.at[m, planes], out.at[m, planes, :, edge], left.at[len(copies)]
                )
                copy.start()
                copies.append(copy)
    for copy in copies:
        copy.wait()


def whole(x):
    return pl.BlockSpec(x.shape, lambda i: (0,) * x.ndim)


def call(kernel, name, outs, args, specs=None, out_specs=None, scratch=(), flops=0, aliases=None):
    specs = specs or {}
    shapes = tuple(jax.ShapeDtypeStruct(s, F32) for s in outs)
    out_specs = out_specs or {}
    out_specs = tuple(out_specs.get(i, whole(s)) for i, s in enumerate(shapes))
    return pl.pallas_call(
        kernel,
        grid=(1,),
        out_shape=shapes if len(shapes) > 1 else shapes[0],
        in_specs=[specs.get(i, whole(a)) for i, a in enumerate(args)],
        scratch_shapes=[pltpu.VMEM(s, F32) if isinstance(s, tuple) else s for s in scratch],
        compiler_params=pltpu.CompilerParams(vmem_limit_bytes=24 * 1024 * 1024),
        cost_estimate=pl.CostEstimate(flops=flops, bytes_accessed=2_000_000, transcendentals=0),
        name=name,
        out_specs=out_specs if len(shapes) > 1 else out_specs[0],
        input_output_aliases=aliases or {},
    )(*args)


HBM = pl.BlockSpec(memory_space=pltpu.HBM)


def ring(axis, step):
    size = lax.axis_size(axis)
    return [(i, (i + step) % size) for i in range(size)]


def shift(x, axis, step):
    return lax.ppermute(x, axis, ring(axis, step))


def sweep_outs(fields):
    return (
        [(fields, CX, CY, CZ), (fields, ITERS, PX, 2, 1, CZ), (fields, ITERS, CY, LANES)],
        [(3, CY, CZ)] + [(fields, PX, CY, CZ)] * 3,
        [(fields, CX, 16, CZ), (fields, ITERS, 16, LANES)],
        [(3, 16, CZ)] + [(fields, PX, 16, CZ)] * 3,
    )


def local(mode_fields, design, solid_mask, eigenvalues, mode_order):
    selector = (mode_order[:MODES, None] == jnp.arange(eigenvalues.shape[0], dtype=jnp.int32)).astype(F32)
    chosen = jnp.sum(selector * eigenvalues[None, :], axis=1) * (0.125 * 0.25)
    lams = jnp.broadcast_to(chosen[:, None, None], (MODES, 8, LANES))
    bulk_outs, bulk_scratch, strip_outs, strip_scratch = sweep_outs(1)

    src, down, up = call(
        pack_x1, "pack_x1", [(CX, CY, CZ), (W + 6, CY, CZ), (W, CY, CZ)],
        tuple(pltpu.with_memory_space_constraint(x, pltpu.HBM) for x in (design, solid_mask, mode_fields)),
        {0: HBM, 1: HBM, 2: HBM},
        scratch=[(CX, CY, CZ), pltpu.VMEM((CX, CY, CZ), jnp.int32), pltpu.SemaphoreType.DMA((2 * CX + 6,))],
    )
    above, below = shift(down, "gx", -1), shift(up, "gx", 1)
    field = (MODES, CX - 1, CY, CZ)
    stiff, mass, columns, first_rows = call(
        energy_kernel, "energy", [field, field, (2, CY, LANES), (8, 8, CZ)], (mode_fields,), flops=40_000_000
    )

    down, up = call(
        pack_y1, "pack_y1", [(16, 8, CZ), (8, 8, CZ)], (src, first_rows, columns, above, below)
    )
    y_above, y_below = shift(down, "gy", -1), shift(up, "gy", 1)
    plane = (MODES, CY, CZ)
    bulk, ends, bulk_edges, stiff7, mass7, own, rims = call(
        bulk_kernel1, "bulk1", bulk_outs + [plane, plane, (1, CY, LANES), (2, CY, LANES)],
        (src, mode_fields, columns, above, below), scratch=bulk_scratch, flops=30_000_000,
    )

    z_in = shift(call(pack_z1, "pack_z1", [(2, PY, LANES)], (own, rims, y_above, y_below)), "gz", 1)
    strips, strip_edges, rim, packed = call(
        strip_kernel1, "strips1", strip_outs + [(MODES, 2, 8, CZ), (PY, LANES)],
        (mode_fields, rims, above, y_above, y_below, ends),
        scratch=strip_scratch + [(3, 16, CZ)] * 2, flops=20_000_000,
    )
    half = (W, MODES, CY, CZ)
    energies = (stiff, mass, stiff7, mass7, rim)
    low, z_parts = call(
        raw_kernel1, "raw1", [half, (3, CY, LANES)],
        (lams, z_in, packed, bulk, bulk_edges, strips, strip_edges, *energies),
    )
    above = shift(low, "gx", -1)
    high = call(raw_kernel2, "raw2", [half], (lams, z_parts, bulk, strips, *energies), flops=60_000_000)
    below = shift(high, "gx", 1)

    bulk_outs, bulk_scratch, strip_outs, strip_scratch = sweep_outs(MODES)
    planes = (low, high, above, below)
    down, up = call(pack_y2, "pack_y2", [(CX + 3, 8, CZ)] * 2, planes)
    y_above, y_below = shift(down, "gy", -1), shift(up, "gy", 1)
    bulk, ends, bulk_edges, own = call(
        bulk_kernel2, "bulk2", bulk_outs + [(MODES, CY, LANES)], planes,
        scratch=bulk_scratch, flops=40_000_000,
    )
    z_in = shift(call(pack_z2, "pack_z2", [(MODES, PY, LANES)], (own, y_above, y_below)), "gz", 1)
    result = (MODES, CX, CY, CZ)
    out, side, strip_edges = call(
        strip_kernel2, "strips2", [result, (MODES, CX, CY, LANES), strip_outs[1]],
        (solid_mask, y_above, y_below, ends, bulk), out_specs={0: HBM},
        scratch=[strip_outs[0]] + strip_scratch + [result, pltpu.SemaphoreType.DMA((4,))],
        flops=20_000_000,
    )
    return call(
        final_kernel, "final", [result],
        (solid_mask, z_in, bulk_edges, strip_edges, side, out), {5: HBM}, {0: HBM},
        scratch=[(MODES, CX, CY, LANES), pltpu.SemaphoreType.DMA((4,))], aliases={5: 0},
    )


def solution(mesh):
    return jax.shard_map(
        local,
        mesh=mesh,
        in_specs=(
            P(None, None, "gx", "gy", "gz"),
            P("gx", "gy", "gz"),
            P("gx", "gy", "gz"),
            P(),
            P(),
        ),
        out_specs=P(None, "gx", "gy", "gz"),
        check_vma=False,
    )
```

```python
import jax
import jax.numpy as jnp
from jax import lax
from jax.experimental import pallas as pl
from jax.experimental.pallas import tpu as pltpu
from jax.sharding import PartitionSpec as P

ITERS = 4
MODES = 2
CX, CY, CZ = 8, 32, 256
W = ITERS
PX = CX + 2 * W
PY = CY + 8
NODES = CX + 1
LANES = 128

poisson = 0.3
radius_sq = 3.0
stiff_floor = 0.001
LAME = poisson / ((1.0 + poisson) * (1.0 - 2.0 * poisson))
SHEAR = 0.5 / (1.0 + poisson)

F32 = jnp.float32


def iota(shape, dim):
    return lax.broadcasted_iota(jnp.int32, shape, dim)


def pos():
    return tuple(lax.axis_index(a) for a in ("gx", "gy", "gz"))


def sub_lane():
    return iota((8, LANES), 0), iota((8, LANES), 1)


def total_of(terms):
    terms = [t for t in terms if t is not None]
    while len(terms) > 1:
        pairs = [terms[i] + terms[i + 1] for i in range(0, len(terms) - 1, 2)]
        terms = pairs + ([terms[-1]] if len(terms) % 2 else [])
    return terms[0]


def scales(count, inside):
    outside = jnp.zeros(count.shape, F32)
    end = jnp.where(inside, radius_sq / (1.0 + radius_sq * (count + 1.0)), 0.0)
    mid = jnp.where(inside, radius_sq / (1.0 + radius_sq * (count + 2.0)), 0.0)
    return outside, end, mid


def yz_scales(y, z, gy, gz):
    y, z = y + gy * CY, z + gz * CZ
    inside = (y >= 0) & (y < 8 * CY)
    count = 4.0
    for place, last in ((y, 8 * CY - 1), (z, 2 * CZ - 1)):
        count = count - (place == 0).astype(F32) - (place == last).astype(F32)
    return scales(count, inside)


def kind_of(gx, plane):
    x = gx * CX + plane - W
    out = (x < 0) | (x > 8 * CX - 1)
    end = (x == 0) | (x == 8 * CX - 1)
    return jnp.where(out, 0, jnp.where(end, 1, 2))


def fill_bulk(table, gy, gz):
    shape = (CY, CZ)
    for i, part in enumerate(yz_scales(iota(shape, 0), iota(shape, 1), gy, gz)):
        table[i] = part


def fill_strips(table, gy, gz):
    shape = (16, CZ)
    row = iota(shape, 0)
    top = jnp.where(row < 4, row + CY, row + CY - 8)
    bottom = jnp.where(row < 12, row - 8, row - 16)
    for i, part in enumerate(yz_scales(jnp.where(row < 8, top, bottom), iota(shape, 1), gy, gz)):
        table[i] = part


def strip_scale(gx, gy):
    shape = (PY, LANES)
    row = iota(shape, 0)
    y = jnp.where(row < CY + W, row, row - PY) + gy * CY
    x = gx * CX - W + lax.div(iota(shape, 1), 8)
    inside = (y >= 0) & (y < 8 * CY) & (x >= 0) & (x < 8 * CX)
    count = 6.0
    for place, last in ((y, 8 * CY - 1), (x, 8 * CX - 1)):
        count = count - (place == 0).astype(F32) - (place == last).astype(F32)
    return jnp.where(inside, radius_sq / (1.0 + radius_sq * count), 0.0)


def tiles_of(ref, index, rows, cols):
    return [
        [ref[index + (slice(8 * i, 8 * i + 8), slice(LANES * j, LANES * j + LANES))] for j in range(cols)]
        for i in range(rows)
    ]


def along_lanes(row, lane):
    right = [pltpu.roll(t, 1, 1) for t in row]
    left = [pltpu.roll(t, LANES - 1, 1) for t in row]
    out = []
    for j in range(len(row)):
        before = right[j - 1] if j else 0.0
        after = left[j + 1] if j + 1 < len(row) else 0.0
        out.append(
            jnp.where(lane == 0, before, right[j]) + jnp.where(lane == LANES - 1, after, left[j])
        )
    return out


def along_rows(tiles, sub):
    rows, cols = len(tiles), len(tiles[0])
    down = [[pltpu.roll(t, 1, 0) for t in row] for row in tiles]
    up = [[pltpu.roll(t, 7, 0) for t in row] for row in tiles]
    out = []
    for i in range(rows):
        line = []
        for j in range(cols):
            before = down[i - 1][j] if i else 0.0
            after = up[i + 1][j] if i + 1 < rows else 0.0
            line.append(jnp.where(sub == 0, before, down[i][j]) + jnp.where(sub == 7, after, up[i][j]))
        out.append(line)
    return out


def turn_edge(tile, p, gz):
    return pltpu.roll(tile, lax.rem(8 * p + 5 - 2 * gz, LANES), 1)


def kind_at(gx, p):
    return 2 if W < p < PX - W - 1 else kind_of(gx, p)


def bulk_sweeps(fields, where, table, source, states, ends, edges, out):
    gx, gy, gz = where
    sub, lane = sub_lane()
    sb = states[0]
    for p in range(PX):
        kind = kind_at(gx, p)
        for m in range(fields):
            for i in range(CY // 8):
                rows = slice(8 * i, 8 * i + 8)
                sb[m, p, rows, :] = source(m, p, i) * (table[kind, rows, :] * (1.0 / radius_sq))
    for k in range(ITERS):
        old = states[0] if k == 0 else states[1 + (k - 1) % 2]
        new = states[1 + k % 2]
        for m in range(fields):
            edge = [jnp.zeros((8, LANES), F32)] * (CY // 8)
            for p in range(k + 1, PX - 1 - k):
                kind = kind_at(gx, p)
                mid = tiles_of(old, (m, p), CY // 8, 2)
                yy = along_rows(mid, sub)
                for i in range(CY // 8):
                    zz = along_lanes(mid[i], lane)
                    rows = slice(8 * i, 8 * i + 8)
                    for j in range(2):
                        cols = slice(LANES * j, LANES * j + LANES)
                        total = old[m, p - 1, rows, cols] + old[m, p + 1, rows, cols]
                        total = total + (yy[i][j] + zz[j])
                        value = sb[m, p, rows, cols] + table[kind, rows, cols] * total
                        if k + 1 < ITERS:
                            new[m, p, rows, cols] = value
                        else:
                            out[m, p - W, rows, cols] = value
                    side = jnp.where(gz == 0, mid[i][1], mid[i][0])
                    edge[i] = jnp.where(lane == 8 * p + 4 - gz, turn_edge(side, p, gz), edge[i])
                for j in range(2):
                    cols = slice(LANES * j, LANES * j + LANES)
                    ends[m, k, p, 0, 0:1, cols] = mid[CY // 8 - 1][j][7:8]
                    ends[m, k, p, 1, 0:1, cols] = mid[0][j][0:1]
            for i in range(CY // 8):
                edges[m, k, 8 * i : 8 * i + 8, :] = edge[i]


def strip_sweeps(fields, where, table, source, ends, states, edges, out):
    gx, gy, gz = where
    sub, lane = sub_lane()
    sb = states[0]
    wide = iota((8, CZ), 0)
    for p in range(PX):
        kind = kind_at(gx, p)
        for m in range(fields):
            halo = source(m, p) * (1.0 / radius_sq)
            sb[m, p, 0:8, :] = jnp.where(wide < 4, halo * table[kind, 0:8, :], 0.0)
            sb[m, p, 8:16, :] = jnp.where(wide < 4, 0.0, halo * table[kind, 8:16, :])
    for k in range(ITERS):
        old = states[0] if k == 0 else states[1 + (k - 1) % 2]
        new = states[1 + k % 2]
        for m in range(fields):
            edge = [jnp.zeros((8, LANES), F32)] * 2
            for p in range(k + 1, PX - 1 - k):
                kind = kind_at(gx, p)
                mid = tiles_of(old, (m, p), 2, 2)
                for i in range(2):
                    rows = slice(8 * i, 8 * i + 8)
                    zz = along_lanes(mid[i], lane)
                    for j in range(2):
                        cols = slice(LANES * j, LANES * j + LANES)
                        end = jnp.broadcast_to(ends[m, k, p, i, 0:1, cols], (8, LANES))
                        down = pltpu.roll(mid[i][j], 1, 0)
                        up = pltpu.roll(mid[i][j], 7, 0)
                        if i == 0:
                            down = jnp.where(sub == 4, 0.0, down) + jnp.where(sub == 0, end, 0.0)
                        else:
                            up = jnp.where(sub == 3, 0.0, up) + jnp.where(sub == 7, end, 0.0)
                        total = old[m, p - 1, rows, cols] + old[m, p + 1, rows, cols]
                        total = total + (down + up) + zz[j]
                        value = sb[m, p, rows, cols] + table[kind, rows, cols] * total
                        if k + 1 < ITERS:
                            new[m, p, rows, cols] = value
                        else:
                            out[m, p - W, rows, cols] = value
                    side = jnp.where(gz == 0, mid[i][1], mid[i][0])
                    edge[i] = jnp.where(lane == 8 * p + 4 - gz, turn_edge(side, p, gz), edge[i])
            for i in range(2):
                edges[m, k, 8 * i : 8 * i + 8, :] = edge[i]


def z_sweeps(m, scale, halo, bulk_edges, strip_edges):
    sub = iota((8, LANES), 0)
    column = lax.rem(iota((PY, LANES), 1), 8)
    base = halo * (scale * (1.0 / radius_sq))
    state = base
    for k in range(ITERS):
        top, bottom = strip_edges[m, k, 0:8, :], strip_edges[m, k, 8:16, :]
        own = bulk_edges[m, k]
        fed = jnp.concatenate(
            [
                own[0:8] + jnp.where(sub < 4, bottom, 0.0),
                own[8 : CY - 8],
                own[CY - 8 : CY] + jnp.where(sub < 4, 0.0, top),
                jnp.where(sub < 4, top, bottom),
            ],
            axis=0,
        )
        total = pltpu.roll(state, 8, 1) + pltpu.roll(state, LANES - 8, 1)
        total = total + pltpu.roll(state, 1, 0) + pltpu.roll(state, PY - 1, 0)
        total = total + jnp.where(column == 0, 0.0, pltpu.roll(state, 1, 1))
        total = total + jnp.where(column == 7, 0.0, pltpu.roll(state, LANES - 1, 1))
        state = base + scale * (total + fed)
    return state


def pair_tile(m, x, i, j, bulk, strips, sub):
    rows, cols = slice(8 * i, 8 * i + 8), slice(LANES * j, LANES * j + LANES)
    value = bulk[m, x, rows, cols]
    if i == 0:
        value = value + jnp.where(sub < 4, strips[m, x, 8:16, cols], 0.0)
    if i == CY // 8 - 1:
        value = value + jnp.where(sub < 4, 0.0, strips[m, x, 0:8, cols])
    return value


def z_tile(z_state, x, i):
    return pltpu.roll(z_state[8 * i : 8 * i + 8], (LANES - 4 - 8 * (x + W)) % LANES, 1)


def beside_halo(gz, lane):
    return (lane < 4 * gz), (lane >= LANES - 4 * (1 - gz))


def pack_strip(gz, tile, p, acc, lane):
    first = 8 * p + 4 * gz
    turned = pltpu.roll(tile, (8 * p + 4) % LANES, 1)
    return jnp.where((lane >= first) & (lane < first + 4), turned, acc)


def own_strip(gz, load, rows=CY):
    lane = iota((rows, LANES), 1)
    acc = jnp.zeros((rows, LANES), F32)
    for p in range(PX):
        acc = pack_strip(gz, load(p), p, acc, lane)
    return acc


def edge_tiles(gz):
    return pl.ds(pl.multiple_of((1 - gz) * LANES, LANES), LANES)


def energy_terms(prev, cur):
    (paa, pad, pda, pdd), (caa, cad, cda, cdd) = prev, cur
    u, v, w = 0, 1, 2
    aad = [cad[i] + pad[i] for i in range(3)]
    ada = [cda[i] + pda[i] for i in range(3)]
    add = [cdd[i] + pdd[i] for i in range(3)]
    daa = [caa[i] - paa[i] for i in range(3)]
    dad = [cad[i] - pad[i] for i in range(3)]
    dda = [cda[i] - pda[i] for i in range(3)]
    ddd = [cdd[i] - pdd[i] for i in range(3)]

    def sq(x):
        return x * x

    trace = sq(daa[u] + ada[v] + aad[w])
    lines = sq(dda[v] + dad[w]) + sq(dda[u] + add[w]) + sq(dad[u] + add[v])
    diag = sq(daa[u]) + sq(ada[v]) + sq(aad[w])
    shear = sq(ada[u] + daa[v]) + sq(aad[u] + daa[w]) + sq(aad[v] + ada[w])
    mixed = sq(dda[u]) + sq(dda[v]) + sq(dad[u]) + sq(dad[w]) + sq(add[v]) + sq(add[w])
    cross = sq(add[u] + dad[v]) + sq(add[u] + dda[w]) + sq(dad[v] + dda[w])
    cubic = sq(ddd[u]) + sq(ddd[v]) + sq(ddd[w])
    return (
        LAME * (trace + lines * (1.0 / 3.0))
        + SHEAR * (2.0 * diag + shear + mixed + cross * (1.0 / 3.0))
        + ((LAME + 4.0 * SHEAR) / 9.0) * cubic
    )


def y_parts(pairs):
    aa = [a0 + a1 for a0, d0, a1, d1 in pairs]
    ad = [d0 + d1 for a0, d0, a1, d1 in pairs]
    da = [a1 - a0 for a0, d0, a1, d1 in pairs]
    dd = [d1 - d0 for a0, d0, a1, d1 in pairs]
    return aa, ad, da, dd


def mass_of(parts):
    return total_of([x * x for part in parts for x in part])


def z_pair(here):
    after = pltpu.roll(here, CZ - 1, 1)
    return here + after, after - here


def own_parts(load, chunk):
    sub = iota((8, CZ), 0)
    pairs = []
    for c in range(3):
        a0, d0 = z_pair(load(c, 8 * chunk))
        following = min(chunk + 1, CY // 8 - 1)
        a1, d1 = z_pair(load(c, 8 * following))

        def next_row(t, n):
            return jnp.where(sub == 7, pltpu.roll(n, 7, 0), pltpu.roll(t, 7, 0))

        pairs.append((a0, d0, next_row(a0, a1), next_row(d0, d1)))
    return y_parts(pairs)


def pack_columns(load, lane):
    first = jnp.zeros((CY, LANES), F32)
    last = first
    for m in range(MODES):
        for c in range(3):
            for x in range(CX):
                to = 32 * m + NODES * c + x
                here = lane == to
                first = jnp.where(here, pltpu.roll(load(m, c, x, 0), to, 1), first)
                last = jnp.where(here, pltpu.roll(load(m, c, x, 1), to + 1, 1), last)
    return first, last


def with_plane8(packed, above, keep_x, last):
    cols = slice(CZ - LANES, CZ) if last else slice(0, LANES)
    rows = packed.shape[0]
    lane = iota(packed.shape, 1)
    for m in range(MODES):
        for c in range(3):
            to = 32 * m + NODES * c + CX
            turned = pltpu.roll(above[W + 3 * m + c, 0:rows, cols], to + last, 1)
            packed = jnp.where(lane == to, turned * keep_x, packed)
    return packed


def row32_of(y_above, last):
    cols = slice(CZ - LANES, CZ) if last else slice(0, LANES)
    sub, lane = sub_lane()
    tile = jnp.zeros((8, LANES), F32)
    for m in range(MODES):
        for c in range(3):
            for x in range(CX):
                to = 32 * m + NODES * c + x
                row = jnp.broadcast_to(y_above[W + 3 * m + c, x : x + 1, cols], (8, LANES))
                tile = jnp.where(lane == to, pltpu.roll(row, to + last, 1), tile)
    return jnp.where(sub == 0, tile, 0.0)


def with_row32(packed, row, from_above, keep_x, keep_y, last):
    cols = slice(CZ - LANES, CZ) if last else slice(0, LANES)
    sub, lane = sub_lane()
    for m in range(MODES):
        for c in range(3):
            to = 32 * m + NODES * c + CX
            n = 3 * m + c
            corner = jnp.broadcast_to(from_above[W - 1, n : n + 1, cols] * keep_x, (8, LANES))
            row = jnp.where((lane == to) & (sub == 0), pltpu.roll(corner, to + last, 1), row)
    return jnp.concatenate([packed, row * keep_y], axis=0)


def pack_x1(design, mask, modes, src, down, up, field, solid, arrived):
    copies = []
    for x in range(CX):
        copies.append(pltpu.make_async_copy(design.at[x], field.at[x], arrived.at[2 * x]))
        copies.append(pltpu.make_async_copy(mask.at[x], solid.at[x], arrived.at[2 * x + 1]))
    for n in range(3 * MODES):
        to = down.at[W + n]
        copies.append(pltpu.make_async_copy(modes.at[n // 3, n % 3, 0], to, arrived.at[2 * CX + n]))
    for copy in copies:
        copy.start()
    for x in range(CX):
        copies[2 * x].wait()
        copies[2 * x + 1].wait()
        plane = field[x] * solid[x].astype(F32)
        src[x] = plane
        if x < W:
            down[x] = plane
        if x >= CX - W:
            up[x - (CX - W)] = plane
    for copy in copies[2 * CX :]:
        copy.wait()


def energy_kernel(modes, stiff, mass, columns):
    lane = iota((CY, LANES), 1)
    columns[0], columns[1] = pack_columns(
        lambda m, c, x, j: modes[m, c, x, :, LANES * j : LANES * j + LANES], lane
    )

    def mode_step(m, carry):
        for chunk in range(CY // 8):
            rows = slice(8 * chunk, 8 * chunk + 8)
            prev = prev_mass = None
            for x in range(CX):
                cur = own_parts(lambda c, r: modes[m, c, x, r : r + 8, :], chunk)
                cur_mass = mass_of(cur)
                if x:
                    stiff[m, x - 1, rows, :] = energy_terms(prev, cur)
                    mass[m, x - 1, rows, :] = cur_mass + prev_mass
                prev, prev_mass = cur, cur_mass
        return carry

    lax.fori_loop(0, MODES, mode_step, 0)


def pick_plane(own, above, below, p):
    if p < W:
        return below, p
    if p < W + CX:
        return own, p - W
    return above, p - W - CX


def pack_y1(src, modes, down, up):
    low = iota((8, CZ), 0) < 4
    for q in range(W):
        down[q] = jnp.where(low, src[q, 0:8, :], pltpu.roll(src[q + W, 0:8, :], 4, 0))
        up[q] = jnp.where(low, pltpu.roll(src[q + W, 24:32, :], 4, 0), src[q, 24:32, :])
    for m in range(MODES):
        for c in range(3):
            for x in range(CX):
                down[W + 3 * m + c, x : x + 1, :] = modes[m, c, x, 0:1, :]


def own_halo(y_above, y_below, x, lanes=slice(None)):
    a, b = y_above[x % W, :, lanes], y_below[x % W, :, lanes]
    if x >= W:
        a, b = pltpu.roll(a, 4, 0), pltpu.roll(b, 4, 0)
    return jnp.where(iota(a.shape, 0) < 4, a, b)


def pack_e1(y_above, y_below, ahead, down, up):
    for i in range(W - 1):
        down[i] = own_halo(y_above, y_below, i)
        up[i] = own_halo(y_above, y_below, CX - 1 - i)
    down[W - 1] = jnp.zeros((8, CZ), F32)
    for n in range(3 * MODES):
        down[W - 1, n : n + 1, :] = y_above[W + n, 0:1, :]


def halo_tile(y_above, y_below, from_above, from_below, p, lanes=slice(None)):
    if W <= p < W + CX:
        return own_halo(y_above, y_below, p - W, lanes)
    if 0 < p < W:
        return from_below[W - 1 - p, :, lanes]
    if W + CX <= p < PX - 1:
        return from_above[p - W - CX, :, lanes]
    return jnp.zeros(y_above[0, :, lanes].shape, F32)


def bulk_kernel1(
    src, modes, columns, above, below, y_above,
    bulk, ends, edges, stiff, mass, own, rims, row32, table, sb, one, two,
):
    at = pos()
    gx, gy, gz = at
    fill_bulk(table, gy, gz)

    def source(m, p, i):
        a, at_plane = pick_plane(src, above, below, p)
        return a[at_plane, 8 * i : 8 * i + 8, :]

    bulk_sweeps(1, at, table, source, (sb, one, two), ends, edges, bulk)
    edge = edge_tiles(gz)
    own[0] = own_strip(gz, lambda p: plane_edge(src, above, below, p, edge))
    keep = jnp.where(gx < 7, 1.0, 0.0)
    for last in range(2):
        rims[last] = with_plane8(columns[last], above, keep, last)
        row32[last] = row32_of(y_above, last)
    for m in range(MODES):
        for chunk in range(CY // 8):
            rows = slice(8 * chunk, 8 * chunk + 8)
            prev = own_parts(lambda c, r: modes[m, c, CX - 1, r : r + 8, :], chunk)
            cur = own_parts(lambda c, r: above[W + 3 * m + c, r : r + 8, :] * keep, chunk)
            stiff[m, rows, :] = energy_terms(prev, cur)
            mass[m, rows, :] = mass_of(cur) + mass_of(prev)


def plane_edge(own, above, below, p, edge):
    a, i = pick_plane(own, above, below, p)
    return a[i, :, edge]


def pack_z1(own, rims, row32, y_above, y_below, from_above, from_below, out):
    gx, gy, gz = pos()
    edge = edge_tiles(gz)
    halos = (y_above, y_below, from_above, from_below)
    out[0, 0:CY, :] = own[0]
    out[0, CY:PY, :] = own_strip(gz, lambda p: halo_tile(*halos, p, edge), 8)
    keep_x = jnp.where(gx < 7, 1.0, 0.0)
    keep_y = jnp.where(gy < 7, 1.0, 0.0)
    out[1] = with_row32(rims[0], row32[0], from_above, keep_x, keep_y, 0)


def strip_kernel1(
    modes, rims, row32, above, y_above, y_below, from_above, from_below, ends,
    strips, edges, rim, packed, table, sb, one, two, near, far,
):
    at = pos()
    gx, gy, gz = at
    fill_strips(table, gy, gz)
    halos = (y_above, y_below, from_above, from_below)
    strip_sweeps(
        1, at, table, lambda m, p: halo_tile(*halos, p), ends, (sb, one, two), edges, strips
    )
    keep_x = jnp.where(gx < 7, 1.0, 0.0)
    keep_y = jnp.where(gy < 7, 1.0, 0.0)
    packed[...] = with_row32(rims[1], row32[1], from_above, keep_x, keep_y, 1)
    for m in range(MODES):
        for c in range(3):
            n = 3 * m + c
            for x in range(CX):
                near[c, x : x + 1, :] = modes[m, c, x, CY - 1 : CY, :]
            near[c, CX : CX + 1, :] = above[W + n, CY - 1 : CY, :] * keep_x
            far[c, 0:CX, :] = y_above[W + n] * keep_y
            far[c, CX : CX + 1, :] = from_above[W - 1, n : n + 1, :] * (keep_x * keep_y)

        def parts(first):
            pairs = []
            for c in range(3):
                a0, d0 = z_pair(near[c, first : first + 8, :])
                a1, d1 = z_pair(far[c, first : first + 8, :])
                pairs.append((a0, d0, a1, d1))
            return y_parts(pairs)

        prev, cur = parts(0), parts(1)
        rim[m, 0] = energy_terms(prev, cur)
        rim[m, 1] = mass_of(cur) + mass_of(prev)


def raw_planes(
    planes, lams, gz, z_state, column_stiff, column_mass, bulk, strips,
    stiff, mass, stiff7, mass7, rim, out,
):
    sub, lane = sub_lane()
    beside = beside_halo(gz, lane)
    factor = 3.0 * (1.0 - stiff_floor) / 16.0
    for x in planes:
        for i in range(CY // 8):
            rows = slice(8 * i, 8 * i + 8)
            correction = z_tile(z_state, x, i)
            for j in range(2):
                cols = slice(LANES * j, LANES * j + LANES)
                phys = pair_tile(0, x, i, j, bulk, strips, sub) + jnp.where(beside[j], correction, 0.0)
                phys = (factor * phys) * phys
                for m in range(MODES):
                    if x < CX - 1:
                        k, e = stiff[m, x, rows, cols], mass[m, x, rows, cols]
                    else:
                        k, e = stiff7[m, rows, cols], mass7[m, rows, cols]
                    if i == CY // 8 - 1:
                        k = jnp.where(sub == 7, jnp.broadcast_to(rim[m, 0, x : x + 1, cols], (8, LANES)), k)
                        e = jnp.where(sub == 7, jnp.broadcast_to(rim[m, 1, x : x + 1, cols], (8, LANES)), e)
                    if j == 1:
                        by = LANES - 1 - (32 * m + x)
                        k = jnp.where(lane == LANES - 1, pltpu.roll(column_stiff[rows, :], by, 1), k)
                        e = jnp.where(lane == LANES - 1, pltpu.roll(column_mass[rows, :], by, 1), e)
                    out[x % W, m, rows, cols] = phys * k - lams[m] * e


def raw_kernel1(
    lams, z_in, packed, bulk, bulk_edges, strips, strip_edges,
    stiff, mass, stiff7, mass7, rim, low, z_parts,
):
    gx, gy, gz = pos()
    z_state = z_sweeps(0, strip_scale(gx, gy), z_in[0], bulk_edges, strip_edges)

    near, far = packed[...], z_in[1] * jnp.where(gz < 1, 1.0, 0.0)
    a0, d0 = near + far, far - near
    a1, d1 = pltpu.roll(a0, PY - 1, 0), pltpu.roll(d0, PY - 1, 0)
    parts = [(x[0][0:CY]) for x in y_parts([(a0, d0, a1, d1)])]

    def turned(t, by):
        return pltpu.roll(t, (LANES - by) % LANES, 1) if by else t

    prev = [[turned(t, NODES * c) for c in range(3)] for t in parts]
    cur = [[turned(t, NODES * c + 1) for c in range(3)] for t in parts]
    column_stiff = energy_terms(prev, cur)
    column_mass = mass_of(cur) + mass_of(prev)
    z_parts[0], z_parts[1], z_parts[2] = z_state[0:CY], column_stiff, column_mass
    raw_planes(
        range(W), lams, gz, z_state, column_stiff, column_mass, bulk, strips,
        stiff, mass, stiff7, mass7, rim, low,
    )


def raw_kernel2(
    lams, z_parts, bulk, strips, stiff, mass, stiff7, mass7, rim, high
):
    gx, gy, gz = pos()
    raw_planes(
        range(W, CX), lams, gz, z_parts[0], z_parts.at[1], z_parts.at[2], bulk, strips,
        stiff, mass, stiff7, mass7, rim, high,
    )


def raw_plane(low, high, above, below, p):
    if p < W:
        return below, p
    if p < 2 * W:
        return low, p - W
    if p < 3 * W:
        return high, p - 2 * W
    return above, p - 3 * W


def pack_y2(low, high, down, up):
    first = iota((8, CZ), 0) < 4
    for x in range(CX):
        a, i = (low, x) if x < W else (high, x - W)
        down[x] = jnp.where(first, a[i, 0, 0:8, :], pltpu.roll(a[i, 1, 0:8, :], 4, 0))
        up[x] = jnp.where(first, pltpu.roll(a[i, 0, 24:32, :], 4, 0), a[i, 1, 24:32, :])


def own_raw_halo(y_above, y_below, m, x, lanes=slice(None)):
    a, b = y_above[x, :, lanes], y_below[x, :, lanes]
    if m == 0:
        b = pltpu.roll(b, 4, 0)
    else:
        a = pltpu.roll(a, 4, 0)
    return jnp.where(iota(a.shape, 0) < 4, a, b)


def pack_e2(y_above, y_below, down, up):
    for i in range(W - 1):
        for m in range(MODES):
            down[MODES * i + m] = own_raw_halo(y_above, y_below, m, i)
            up[MODES * i + m] = own_raw_halo(y_above, y_below, m, CX - 1 - i)


def raw_halo(y_above, y_below, from_above, from_below, m, p, lanes=slice(None)):
    if W <= p < W + CX:
        return own_raw_halo(y_above, y_below, m, p - W, lanes)
    if 0 < p < W:
        return from_below[MODES * (W - 1 - p) + m, :, lanes]
    if W + CX <= p < PX - 1:
        return from_above[MODES * (p - W - CX) + m, :, lanes]
    return jnp.zeros(y_above[0, :, lanes].shape, F32)


def bulk_kernel2(low, high, above, below, bulk, ends, edges, own, table, sb, one, two):
    at = pos()
    fill_bulk(table, at[1], at[2])

    def source(m, p, i):
        a, at_plane = raw_plane(low, high, above, below, p)
        return a[at_plane, m, 8 * i : 8 * i + 8, :]

    bulk_sweeps(MODES, at, table, source, (sb, one, two), ends, edges, bulk)
    edge = edge_tiles(at[2])
    for m in range(MODES):

        def load(p, m=m):
            a, i = raw_plane(low, high, above, below, p)
            return a[i, m, :, edge]

        own[m] = own_strip(at[2], load)


def pack_z2(own, y_above, y_below, from_above, from_below, out):
    gx, gy, gz = pos()
    edge = edge_tiles(gz)
    halos = (y_above, y_below, from_above, from_below)
    for m in range(MODES):
        out[m, 0:CY, :] = own[m]
        out[m, CY:PY, :] = own_strip(gz, lambda p, m=m: raw_halo(*halos, m, p, edge), 8)


def strip_kernel2(
    mask, y_above, y_below, from_above, from_below, ends, bulk,
    out, side, edges, strips, table, sb, one, two, held, left,
):
    gx, gy, gz = at = pos()
    sub, lane = sub_lane()
    fill_strips(table, gy, gz)

    def source(m, p):
        return raw_halo(y_above, y_below, from_above, from_below, m, p)

    strip_sweeps(MODES, at, table, source, ends, (sb, one, two), edges, strips)
    copies = []
    for m in range(MODES):
        for x in range(CX):
            for i in range(CY // 8):
                rows = slice(8 * i, 8 * i + 8)
                pair = []
                for j in range(2):
                    cols = slice(LANES * j, LANES * j + LANES)
                    value = pair_tile(m, x, i, j, bulk, strips, sub)
                    held[m, x, rows, cols] = value * mask[x, rows, cols].astype(F32)
                    pair.append(value)
                side[m, x, rows, :] = jnp.where(gz == 0, pair[1], pair[0])
            if x % 4 == 3:
                part = (m, slice(x - 3, x + 1))
                copy = pltpu.make_async_copy(held.at[part], out.at[part], left.at[len(copies)])
                copy.start()
                copies.append(copy)
    for copy in copies:
        copy.wait()


def final_kernel(mask, z_in, bulk_edges, strip_edges, side, given, out, held, left):
    gx, gy, gz = pos()
    sub, lane = sub_lane()
    at_end = beside_halo(gz, lane)
    beside = at_end[0] | at_end[1]
    edge = edge_tiles(gz)
    scale = strip_scale(gx, gy)
    copies = []
    for m in range(MODES):
        z_state = z_sweeps(m, scale, z_in[m], bulk_edges, strip_edges)
        for x in range(CX):
            for i in range(CY // 8):
                rows = slice(8 * i, 8 * i + 8)
                value = side[m, x, rows, :] + jnp.where(beside, z_tile(z_state, x, i), 0.0)
                held[m, x, rows, :] = value * mask[x, rows, edge].astype(F32)
            if x % 4 == 3:
                planes = slice(x - 3, x + 1)
                copy = pltpu.make_async_copy(
                    held.at[m, planes], out.at[m, planes, :, edge], left.at[len(copies)]
                )
                copy.start()
                copies.append(copy)
    for copy in copies:
        copy.wait()


def whole(x):
    return pl.BlockSpec(x.shape, lambda i: (0,) * x.ndim)


def call(kernel, name, outs, args, specs=None, out_specs=None, scratch=(), flops=0, aliases=None):
    specs = specs or {}
    shapes = tuple(jax.ShapeDtypeStruct(s, F32) for s in outs)
    out_specs = out_specs or {}
    out_specs = tuple(out_specs.get(i, whole(s)) for i, s in enumerate(shapes))
    return pl.pallas_call(
        kernel,
        grid=(1,),
        out_shape=shapes if len(shapes) > 1 else shapes[0],
        in_specs=[specs.get(i, whole(a)) for i, a in enumerate(args)],
        scratch_shapes=[pltpu.VMEM(s, F32) if isinstance(s, tuple) else s for s in scratch],
        compiler_params=pltpu.CompilerParams(vmem_limit_bytes=24 * 1024 * 1024),
        cost_estimate=pl.CostEstimate(flops=flops, bytes_accessed=2_000_000, transcendentals=0),
        name=name,
        out_specs=out_specs if len(shapes) > 1 else out_specs[0],
        input_output_aliases=aliases or {},
    )(*args)


HBM = pl.BlockSpec(memory_space=pltpu.HBM)


def ring(axis, step):
    size = lax.axis_size(axis)
    return [(i, (i + step) % size) for i in range(size)]


def shift(x, axis, step):
    return lax.ppermute(x, axis, ring(axis, step))


def sweep_outs(fields):
    return (
        [(fields, CX, CY, CZ), (fields, ITERS, PX, 2, 1, CZ), (fields, ITERS, CY, LANES)],
        [(3, CY, CZ)] + [(fields, PX, CY, CZ)] * 3,
        [(fields, CX, 16, CZ), (fields, ITERS, 16, LANES)],
        [(3, 16, CZ)] + [(fields, PX, 16, CZ)] * 3,
    )


def local(mode_fields, design, solid_mask, eigenvalues, mode_order):
    selector = (mode_order[:MODES, None] == jnp.arange(eigenvalues.shape[0], dtype=jnp.int32)).astype(F32)
    chosen = jnp.sum(selector * eigenvalues[None, :], axis=1) * (0.125 * 0.25)
    lams = jnp.broadcast_to(chosen[:, None, None], (MODES, 8, LANES))
    bulk_outs, bulk_scratch, strip_outs, strip_scratch = sweep_outs(1)

    src, down, up = call(
        pack_x1, "pack_x1", [(CX, CY, CZ), (W + 6, CY, CZ), (W, CY, CZ)],
        tuple(pltpu.with_memory_space_constraint(x, pltpu.HBM) for x in (design, solid_mask, mode_fields)),
        {0: HBM, 1: HBM, 2: HBM},
        scratch=[(CX, CY, CZ), pltpu.VMEM((CX, CY, CZ), jnp.int32), pltpu.SemaphoreType.DMA((2 * CX + 6,))],
    )
    above, below = shift(down, "gx", -1), shift(up, "gx", 1)
    field = (MODES, CX - 1, CY, CZ)
    down, up = call(pack_y1, "pack_y1", [(W + 6, 8, CZ), (W, 8, CZ)], (src, mode_fields))
    y_above, y_below = shift(down, "gy", -1), shift(up, "gy", 1)
    stiff, mass, columns = call(
        energy_kernel, "energy", [field, field, (2, CY, LANES)], (mode_fields,), flops=40_000_000
    )

    down, up = call(pack_e1, "pack_e1", [(W, 8, CZ), (W - 1, 8, CZ)], (y_above, y_below, columns))
    halos = (y_above, y_below, shift(down, "gx", -1), shift(up, "gx", 1))
    plane = (MODES, CY, CZ)
    bulk, ends, bulk_edges, stiff7, mass7, own, rims, row32 = call(
        bulk_kernel1, "bulk1",
        bulk_outs + [plane, plane, (1, CY, LANES), (2, CY, LANES), (2, 8, LANES)],
        (src, mode_fields, columns, above, below, y_above), scratch=bulk_scratch, flops=30_000_000,
    )

    z_in = shift(call(pack_z1, "pack_z1", [(2, PY, LANES)], (own, rims, row32, *halos)), "gz", 1)
    strips, strip_edges, rim, packed = call(
        strip_kernel1, "strips1", strip_outs + [(MODES, 2, 8, CZ), (PY, LANES)],
        (mode_fields, rims, row32, above, *halos, ends),
        scratch=strip_scratch + [(3, 16, CZ)] * 2, flops=20_000_000,
    )
    half = (W, MODES, CY, CZ)
    energies = (stiff, mass, stiff7, mass7, rim)
    low, z_parts = call(
        raw_kernel1, "raw1", [half, (3, CY, LANES)],
        (lams, z_in, packed, bulk, bulk_edges, strips, strip_edges, *energies),
    )
    above = shift(low, "gx", -1)
    high = call(raw_kernel2, "raw2", [half], (lams, z_parts, bulk, strips, *energies), flops=60_000_000)
    below = shift(high, "gx", 1)

    bulk_outs, bulk_scratch, strip_outs, strip_scratch = sweep_outs(MODES)
    planes = (low, high, above, below)
    down, up = call(pack_y2, "pack_y2", [(CX, 8, CZ)] * 2, (low, high))
    y_above, y_below = shift(down, "gy", -1), shift(up, "gy", 1)
    edge = (MODES * (W - 1), 8, CZ)
    down, up = call(pack_e2, "pack_e2", [edge] * 2, (y_above, y_below))
    halos = (y_above, y_below, shift(down, "gx", -1), shift(up, "gx", 1))
    bulk, ends, bulk_edges, own = call(
        bulk_kernel2, "bulk2", bulk_outs + [(MODES, CY, LANES)], planes,
        scratch=bulk_scratch, flops=40_000_000,
    )
    z_in = shift(call(pack_z2, "pack_z2", [(MODES, PY, LANES)], (own, *halos)), "gz", 1)
    result = (MODES, CX, CY, CZ)
    out, side, strip_edges = call(
        strip_kernel2, "strips2", [result, (MODES, CX, CY, LANES), strip_outs[1]],
        (solid_mask, *halos, ends, bulk), out_specs={0: HBM},
        scratch=[strip_outs[0]] + strip_scratch + [result, pltpu.SemaphoreType.DMA((4,))],
        flops=20_000_000,
    )
    return call(
        final_kernel, "final", [result],
        (solid_mask, z_in, bulk_edges, strip_edges, side, out), {5: HBM}, {0: HBM},
        scratch=[(MODES, CX, CY, LANES), pltpu.SemaphoreType.DMA((4,))], aliases={5: 0},
    )


def solution(mesh):
    return jax.shard_map(
        local,
        mesh=mesh,
        in_specs=(
            P(None, None, "gx", "gy", "gz"),
            P("gx", "gy", "gz"),
            P("gx", "gy", "gz"),
            P(),
            P(),
        ),
        out_specs=P(None, "gx", "gy", "gz"),
        check_vma=False,
    )
```

```python
import functools

import jax
import jax.numpy as jnp
from jax import lax
from jax.experimental import pallas as pl
from jax.experimental.pallas import tpu as pltpu
from jax.sharding import PartitionSpec as P

ITERS = 4
MODES = 2
CX, CY, CZ = 8, 32, 256
W = ITERS
PX = CX + 2 * W
PY = CY + 8
NODES = CX + 1
LANES = 128

poisson = 0.3
radius_sq = 3.0
stiff_floor = 0.001
LAME = poisson / ((1.0 + poisson) * (1.0 - 2.0 * poisson))
SHEAR = 0.5 / (1.0 + poisson)

F32 = jnp.float32


def iota(shape, dim):
    return lax.broadcasted_iota(jnp.int32, shape, dim)


def pos():
    return tuple(lax.axis_index(a) for a in ("gx", "gy", "gz"))


def sub_lane():
    return iota((8, LANES), 0), iota((8, LANES), 1)


def total_of(terms):
    terms = [t for t in terms if t is not None]
    while len(terms) > 1:
        pairs = [terms[i] + terms[i + 1] for i in range(0, len(terms) - 1, 2)]
        terms = pairs + ([terms[-1]] if len(terms) % 2 else [])
    return terms[0]


def scales(count, inside):
    outside = jnp.zeros(count.shape, F32)
    end = jnp.where(inside, radius_sq / (1.0 + radius_sq * (count + 1.0)), 0.0)
    mid = jnp.where(inside, radius_sq / (1.0 + radius_sq * (count + 2.0)), 0.0)
    return outside, end, mid


def yz_scales(y, z, gy, gz):
    y, z = y + gy * CY, z + gz * CZ
    inside = (y >= 0) & (y < 8 * CY)
    count = 4.0
    for place, last in ((y, 8 * CY - 1), (z, 2 * CZ - 1)):
        count = count - (place == 0).astype(F32) - (place == last).astype(F32)
    return scales(count, inside)


def kind_of(gx, plane):
    x = gx * CX + plane - W
    out = (x < 0) | (x > 8 * CX - 1)
    end = (x == 0) | (x == 8 * CX - 1)
    return jnp.where(out, 0, jnp.where(end, 1, 2))


def fill_bulk(table, gy, gz):
    shape = (CY, CZ)
    for i, part in enumerate(yz_scales(iota(shape, 0), iota(shape, 1), gy, gz)):
        table[i] = part


def fill_strips(table, gy, gz):
    shape = (16, CZ)
    row = iota(shape, 0)
    top = jnp.where(row < 4, row + CY, row + CY - 8)
    bottom = jnp.where(row < 12, row - 8, row - 16)
    for i, part in enumerate(yz_scales(jnp.where(row < 8, top, bottom), iota(shape, 1), gy, gz)):
        table[i] = part


def strip_scale(gx, gy):
    shape = (PY, LANES)
    row = iota(shape, 0)
    y = jnp.where(row < CY + W, row, row - PY) + gy * CY
    x = gx * CX - W + lax.div(iota(shape, 1), 8)
    inside = (y >= 0) & (y < 8 * CY) & (x >= 0) & (x < 8 * CX)
    count = 6.0
    for place, last in ((y, 8 * CY - 1), (x, 8 * CX - 1)):
        count = count - (place == 0).astype(F32) - (place == last).astype(F32)
    return jnp.where(inside, radius_sq / (1.0 + radius_sq * count), 0.0)


def tiles_of(ref, index, rows, cols):
    return [
        [ref[index + (slice(8 * i, 8 * i + 8), slice(LANES * j, LANES * j + LANES))] for j in range(cols)]
        for i in range(rows)
    ]


def along_lanes(row, lane):
    right = [pltpu.roll(t, 1, 1) for t in row]
    left = [pltpu.roll(t, LANES - 1, 1) for t in row]
    out = []
    for j in range(len(row)):
        before = right[j - 1] if j else 0.0
        after = left[j + 1] if j + 1 < len(row) else 0.0
        out.append(
            jnp.where(lane == 0, before, right[j]) + jnp.where(lane == LANES - 1, after, left[j])
        )
    return out


def along_rows(tiles, sub):
    rows, cols = len(tiles), len(tiles[0])
    down = [[pltpu.roll(t, 1, 0) for t in row] for row in tiles]
    up = [[pltpu.roll(t, 7, 0) for t in row] for row in tiles]
    out = []
    for i in range(rows):
        line = []
        for j in range(cols):
            before = down[i - 1][j] if i else 0.0
            after = up[i + 1][j] if i + 1 < rows else 0.0
            line.append(jnp.where(sub == 0, before, down[i][j]) + jnp.where(sub == 7, after, up[i][j]))
        out.append(line)
    return out


def turn_edge(tile, p, gz):
    return pltpu.roll(tile, lax.rem(8 * p + 5 - 2 * gz, LANES), 1)


def kind_at(gx, p):
    return 2 if W < p < PX - W - 1 else kind_of(gx, p)


def bulk_sweeps(fields, where, table, source, states, ends, edges, out):
    gx, gy, gz = where
    sub, lane = sub_lane()
    sb = states[0]
    for p in range(PX):
        kind = kind_at(gx, p)
        for m in range(fields):
            for i in range(CY // 8):
                rows = slice(8 * i, 8 * i + 8)
                sb[m, p, rows, :] = source(m, p, i) * (table[kind, rows, :] * (1.0 / radius_sq))
    for k in range(ITERS):
        old = states[0] if k == 0 else states[1 + (k - 1) % 2]
        new = states[1 + k % 2]
        for m in range(fields):
            edge = [jnp.zeros((8, LANES), F32)] * (CY // 8)
            for p in range(k + 1, PX - 1 - k):
                kind = kind_at(gx, p)
                mid = tiles_of(old, (m, p), CY // 8, 2)
                yy = along_rows(mid, sub)
                for i in range(CY // 8):
                    zz = along_lanes(mid[i], lane)
                    rows = slice(8 * i, 8 * i + 8)
                    for j in range(2):
                        cols = slice(LANES * j, LANES * j + LANES)
                        total = old[m, p - 1, rows, cols] + old[m, p + 1, rows, cols]
                        total = total + (yy[i][j] + zz[j])
                        value = sb[m, p, rows, cols] + table[kind, rows, cols] * total
                        if k + 1 < ITERS:
                            new[m, p, rows, cols] = value
                        else:
                            out[m, p - W, rows, cols] = value
                    side = jnp.where(gz == 0, mid[i][1], mid[i][0])
                    edge[i] = jnp.where(lane == 8 * p + 4 - gz, turn_edge(side, p, gz), edge[i])
                for j in range(2):
                    cols = slice(LANES * j, LANES * j + LANES)
                    ends[m, k, p, 0, 0:1, cols] = mid[CY // 8 - 1][j][7:8]
                    ends[m, k, p, 1, 0:1, cols] = mid[0][j][0:1]
            for i in range(CY // 8):
                edges[m, k, 8 * i : 8 * i + 8, :] = edge[i]


def strip_sweeps(fields, where, table, source, ends, states, edges, out):
    gx, gy, gz = where
    sub, lane = sub_lane()
    sb = states[0]
    wide = iota((8, CZ), 0)
    for p in range(PX):
        kind = kind_at(gx, p)
        for m in range(fields):
            halo = source(m, p) * (1.0 / radius_sq)
            sb[m, p, 0:8, :] = jnp.where(wide < 4, halo * table[kind, 0:8, :], 0.0)
            sb[m, p, 8:16, :] = jnp.where(wide < 4, 0.0, halo * table[kind, 8:16, :])
    for k in range(ITERS):
        old = states[0] if k == 0 else states[1 + (k - 1) % 2]
        new = states[1 + k % 2]
        for m in range(fields):
            edge = [jnp.zeros((8, LANES), F32)] * 2
            for p in range(k + 1, PX - 1 - k):
                kind = kind_at(gx, p)
                mid = tiles_of(old, (m, p), 2, 2)
                for i in range(2):
                    rows = slice(8 * i, 8 * i + 8)
                    zz = along_lanes(mid[i], lane)
                    for j in range(2):
                        cols = slice(LANES * j, LANES * j + LANES)
                        end = jnp.broadcast_to(ends[m, k, p, i, 0:1, cols], (8, LANES))
                        down = pltpu.roll(mid[i][j], 1, 0)
                        up = pltpu.roll(mid[i][j], 7, 0)
                        if i == 0:
                            down = jnp.where(sub == 4, 0.0, down) + jnp.where(sub == 0, end, 0.0)
                        else:
                            up = jnp.where(sub == 3, 0.0, up) + jnp.where(sub == 7, end, 0.0)
                        total = old[m, p - 1, rows, cols] + old[m, p + 1, rows, cols]
                        total = total + (down + up) + zz[j]
                        value = sb[m, p, rows, cols] + table[kind, rows, cols] * total
                        if k + 1 < ITERS:
                            new[m, p, rows, cols] = value
                        else:
                            out[m, p - W, rows, cols] = value
                    side = jnp.where(gz == 0, mid[i][1], mid[i][0])
                    edge[i] = jnp.where(lane == 8 * p + 4 - gz, turn_edge(side, p, gz), edge[i])
            for i in range(2):
                edges[m, k, 8 * i : 8 * i + 8, :] = edge[i]


def z_sweeps(m, scale, halo, bulk_edges, strip_edges):
    sub = iota((8, LANES), 0)
    column = lax.rem(iota((PY, LANES), 1), 8)
    base = halo * (scale * (1.0 / radius_sq))
    state = base
    for k in range(ITERS):
        top, bottom = strip_edges[m, k, 0:8, :], strip_edges[m, k, 8:16, :]
        own = bulk_edges[m, k]
        fed = jnp.concatenate(
            [
                own[0:8] + jnp.where(sub < 4, bottom, 0.0),
                own[8 : CY - 8],
                own[CY - 8 : CY] + jnp.where(sub < 4, 0.0, top),
                jnp.where(sub < 4, top, bottom),
            ],
            axis=0,
        )
        total = pltpu.roll(state, 8, 1) + pltpu.roll(state, LANES - 8, 1)
        total = total + pltpu.roll(state, 1, 0) + pltpu.roll(state, PY - 1, 0)
        total = total + jnp.where(column == 0, 0.0, pltpu.roll(state, 1, 1))
        total = total + jnp.where(column == 7, 0.0, pltpu.roll(state, LANES - 1, 1))
        state = base + scale * (total + fed)
    return state


def pair_tile(m, x, i, j, bulk, strips, sub):
    rows, cols = slice(8 * i, 8 * i + 8), slice(LANES * j, LANES * j + LANES)
    value = bulk[m, x, rows, cols]
    if i == 0:
        value = value + jnp.where(sub < 4, strips[m, x, 8:16, cols], 0.0)
    if i == CY // 8 - 1:
        value = value + jnp.where(sub < 4, 0.0, strips[m, x, 0:8, cols])
    return value


def z_tile(z_state, x, i):
    return pltpu.roll(z_state[8 * i : 8 * i + 8], (LANES - 4 - 8 * (x + W)) % LANES, 1)


def beside_halo(gz, lane):
    return (lane < 4 * gz), (lane >= LANES - 4 * (1 - gz))


def pack_strip(gz, tile, p, acc, lane):
    first = 8 * p + 4 * gz
    turned = pltpu.roll(tile, (8 * p + 4) % LANES, 1)
    return jnp.where((lane >= first) & (lane < first + 4), turned, acc)


def own_strip(gz, load, rows=CY):
    lane = iota((rows, LANES), 1)
    acc = jnp.zeros((rows, LANES), F32)
    for p in range(PX):
        acc = pack_strip(gz, load(p), p, acc, lane)
    return acc


def edge_tiles(gz):
    return pl.ds(pl.multiple_of((1 - gz) * LANES, LANES), LANES)


def energy_terms(prev, cur):
    (paa, pad, pda, pdd), (caa, cad, cda, cdd) = prev, cur
    u, v, w = 0, 1, 2
    aad = [cad[i] + pad[i] for i in range(3)]
    ada = [cda[i] + pda[i] for i in range(3)]
    add = [cdd[i] + pdd[i] for i in range(3)]
    daa = [caa[i] - paa[i] for i in range(3)]
    dad = [cad[i] - pad[i] for i in range(3)]
    dda = [cda[i] - pda[i] for i in range(3)]
    ddd = [cdd[i] - pdd[i] for i in range(3)]

    def sq(x):
        return x * x

    trace = sq(daa[u] + ada[v] + aad[w])
    lines = sq(dda[v] + dad[w]) + sq(dda[u] + add[w]) + sq(dad[u] + add[v])
    diag = sq(daa[u]) + sq(ada[v]) + sq(aad[w])
    shear = sq(ada[u] + daa[v]) + sq(aad[u] + daa[w]) + sq(aad[v] + ada[w])
    mixed = sq(dda[u]) + sq(dda[v]) + sq(dad[u]) + sq(dad[w]) + sq(add[v]) + sq(add[w])
    cross = sq(add[u] + dad[v]) + sq(add[u] + dda[w]) + sq(dad[v] + dda[w])
    cubic = sq(ddd[u]) + sq(ddd[v]) + sq(ddd[w])
    return (
        LAME * (trace + lines * (1.0 / 3.0))
        + SHEAR * (2.0 * diag + shear + mixed + cross * (1.0 / 3.0))
        + ((LAME + 4.0 * SHEAR) / 9.0) * cubic
    )


def y_parts(pairs):
    aa = [a0 + a1 for a0, d0, a1, d1 in pairs]
    ad = [d0 + d1 for a0, d0, a1, d1 in pairs]
    da = [a1 - a0 for a0, d0, a1, d1 in pairs]
    dd = [d1 - d0 for a0, d0, a1, d1 in pairs]
    return aa, ad, da, dd


def mass_of(parts):
    return total_of([x * x for part in parts for x in part])


def z_pair(here):
    after = pltpu.roll(here, CZ - 1, 1)
    return here + after, after - here


def own_parts(load, chunk):
    sub = iota((8, CZ), 0)
    pairs = []
    for c in range(3):
        a0, d0 = z_pair(load(c, 8 * chunk))
        following = min(chunk + 1, CY // 8 - 1)
        a1, d1 = z_pair(load(c, 8 * following))

        def next_row(t, n):
            return jnp.where(sub == 7, pltpu.roll(n, 7, 0), pltpu.roll(t, 7, 0))

        pairs.append((a0, d0, next_row(a0, a1), next_row(d0, d1)))
    return y_parts(pairs)


def pack_columns(load, lane):
    first = jnp.zeros((CY, LANES), F32)
    last = first
    for m in range(MODES):
        for c in range(3):
            for x in range(CX):
                to = 32 * m + NODES * c + x
                here = lane == to
                first = jnp.where(here, pltpu.roll(load(m, c, x, 0), to, 1), first)
                last = jnp.where(here, pltpu.roll(load(m, c, x, 1), to + 1, 1), last)
    return first, last


def with_plane8(packed, above, keep_x, last):
    cols = slice(CZ - LANES, CZ) if last else slice(0, LANES)
    rows = packed.shape[0]
    lane = iota(packed.shape, 1)
    for m in range(MODES):
        for c in range(3):
            to = 32 * m + NODES * c + CX
            turned = pltpu.roll(above[W + 3 * m + c, 0:rows, cols], to + last, 1)
            packed = jnp.where(lane == to, turned * keep_x, packed)
    return packed


def row32_of(y_above, last):
    cols = slice(CZ - LANES, CZ) if last else slice(0, LANES)
    sub, lane = sub_lane()
    tile = jnp.zeros((8, LANES), F32)
    for m in range(MODES):
        for c in range(3):
            for x in range(CX):
                to = 32 * m + NODES * c + x
                row = jnp.broadcast_to(y_above[W + 3 * m + c, x : x + 1, cols], (8, LANES))
                tile = jnp.where(lane == to, pltpu.roll(row, to + last, 1), tile)
    return jnp.where(sub == 0, tile, 0.0)


def with_row32(packed, row, from_above, keep_x, keep_y, last):
    cols = slice(CZ - LANES, CZ) if last else slice(0, LANES)
    sub, lane = sub_lane()
    for m in range(MODES):
        for c in range(3):
            to = 32 * m + NODES * c + CX
            n = 3 * m + c
            corner = jnp.broadcast_to(from_above[W - 1, n : n + 1, cols] * keep_x, (8, LANES))
            row = jnp.where((lane == to) & (sub == 0), pltpu.roll(corner, to + last, 1), row)
    return jnp.concatenate([packed, row * keep_y], axis=0)


def pack_x1(
    design, mask, modes, eigenvalues, order, src, down, up, lams, field, solid, values, chosen, arrived
):
    copies = []
    for half in (slice(0, W), slice(W, CX)):
        copies.append((design.at[half], field.at[half]))
        copies.append((mask.at[half], solid.at[half]))
    for m in range(MODES):
        copies.append((modes.at[m, :, 0], down.at[W + 3 * m : W + 3 * m + 3]))
    copies += [(eigenvalues, values), (order, chosen)]
    copies = [pltpu.make_async_copy(a, b, arrived.at[n]) for n, (a, b) in enumerate(copies)]
    for copy in copies:
        copy.start()
    for x in range(CX):
        if x % W == 0:
            copies[2 * (x // W)].wait()
            copies[2 * (x // W) + 1].wait()
        plane = field[x] * solid[x].astype(F32)
        src[x] = plane
        if x < W:
            down[x] = plane
        else:
            up[x - W] = plane
    for copy in copies[4:]:
        copy.wait()
    for m in range(MODES):
        lams[m] = jnp.full((8, LANES), values[chosen[m]] * (0.125 * 0.25), F32)


def energy_kernel(modes, stiff, mass, columns):
    lane = iota((CY, LANES), 1)
    columns[0], columns[1] = pack_columns(
        lambda m, c, x, j: modes[m, c, x, :, LANES * j : LANES * j + LANES], lane
    )

    def mode_step(m, carry):
        for chunk in range(CY // 8):
            rows = slice(8 * chunk, 8 * chunk + 8)
            prev = prev_mass = None
            for x in range(CX):
                cur = own_parts(lambda c, r: modes[m, c, x, r : r + 8, :], chunk)
                cur_mass = mass_of(cur)
                if x:
                    stiff[m, x - 1, rows, :] = energy_terms(prev, cur)
                    mass[m, x - 1, rows, :] = cur_mass + prev_mass
                prev, prev_mass = cur, cur_mass
        return carry

    lax.fori_loop(0, MODES, mode_step, 0)


def pick_plane(own, above, below, p):
    if p < W:
        return below, p
    if p < W + CX:
        return own, p - W
    return above, p - W - CX


def pack_y1(src, modes, down, up):
    low = iota((8, CZ), 0) < 4
    for q in range(W):
        down[q] = jnp.where(low, src[q, 0:8, :], pltpu.roll(src[q + W, 0:8, :], 4, 0))
        up[q] = jnp.where(low, pltpu.roll(src[q + W, 24:32, :], 4, 0), src[q, 24:32, :])
    for m in range(MODES):
        for c in range(3):
            for x in range(CX):
                down[W + 3 * m + c, x : x + 1, :] = modes[m, c, x, 0:1, :]


def own_halo(y_above, y_below, x, lanes=slice(None)):
    a, b = y_above[x % W, :, lanes], y_below[x % W, :, lanes]
    if x >= W:
        a, b = pltpu.roll(a, 4, 0), pltpu.roll(b, 4, 0)
    return jnp.where(iota(a.shape, 0) < 4, a, b)


def pack_e1(y_above, y_below, ahead, down, up):
    for i in range(W - 1):
        down[i] = own_halo(y_above, y_below, i)
        up[i] = own_halo(y_above, y_below, CX - 1 - i)
    down[W - 1] = jnp.zeros((8, CZ), F32)
    for n in range(3 * MODES):
        down[W - 1, n : n + 1, :] = y_above[W + n, 0:1, :]


def halo_tile(y_above, y_below, from_above, from_below, p, lanes=slice(None)):
    if W <= p < W + CX:
        return own_halo(y_above, y_below, p - W, lanes)
    if 0 < p < W:
        return from_below[W - 1 - p, :, lanes]
    if W + CX <= p < PX - 1:
        return from_above[p - W - CX, :, lanes]
    return jnp.zeros(y_above[0, :, lanes].shape, F32)


def bulk_kernel1(
    src, modes, columns, above, below, y_above,
    bulk, ends, edges, stiff, mass, own, rims, row32, table, sb, one, two,
):
    at = pos()
    gx, gy, gz = at
    fill_bulk(table, gy, gz)

    def source(m, p, i):
        a, at_plane = pick_plane(src, above, below, p)
        return a[at_plane, 8 * i : 8 * i + 8, :]

    bulk_sweeps(1, at, table, source, (sb, one, two), ends, edges, bulk)
    edge = edge_tiles(gz)
    own[0] = own_strip(gz, lambda p: plane_edge(src, above, below, p, edge))
    keep = jnp.where(gx < 7, 1.0, 0.0)
    for last in range(2):
        rims[last] = with_plane8(columns[last], above, keep, last)
        row32[last] = row32_of(y_above, last)
    for m in range(MODES):
        for chunk in range(CY // 8):
            rows = slice(8 * chunk, 8 * chunk + 8)
            prev = own_parts(lambda c, r: modes[m, c, CX - 1, r : r + 8, :], chunk)
            cur = own_parts(lambda c, r: above[W + 3 * m + c, r : r + 8, :] * keep, chunk)
            stiff[m, rows, :] = energy_terms(prev, cur)
            mass[m, rows, :] = mass_of(cur) + mass_of(prev)


def plane_edge(own, above, below, p, edge):
    a, i = pick_plane(own, above, below, p)
    return a[i, :, edge]


def pack_z1(own, rims, row32, y_above, y_below, from_above, from_below, out):
    gx, gy, gz = pos()
    edge = edge_tiles(gz)
    halos = (y_above, y_below, from_above, from_below)
    out[0, 0:CY, :] = own[0]
    out[0, CY:PY, :] = own_strip(gz, lambda p: halo_tile(*halos, p, edge), 8)
    keep_x = jnp.where(gx < 7, 1.0, 0.0)
    keep_y = jnp.where(gy < 7, 1.0, 0.0)
    out[1] = with_row32(rims[0], row32[0], from_above, keep_x, keep_y, 0)


def strip_kernel1(
    modes, rims, row32, above, y_above, y_below, from_above, from_below, ends,
    strips, edges, rim, packed, table, sb, one, two, near, far,
):
    at = pos()
    gx, gy, gz = at
    fill_strips(table, gy, gz)
    halos = (y_above, y_below, from_above, from_below)
    strip_sweeps(
        1, at, table, lambda m, p: halo_tile(*halos, p), ends, (sb, one, two), edges, strips
    )
    keep_x = jnp.where(gx < 7, 1.0, 0.0)
    keep_y = jnp.where(gy < 7, 1.0, 0.0)
    packed[...] = with_row32(rims[1], row32[1], from_above, keep_x, keep_y, 1)
    for m in range(MODES):
        for c in range(3):
            n = 3 * m + c
            for x in range(CX):
                near[c, x : x + 1, :] = modes[m, c, x, CY - 1 : CY, :]
            near[c, CX : CX + 1, :] = above[W + n, CY - 1 : CY, :] * keep_x
            far[c, 0:CX, :] = y_above[W + n] * keep_y
            far[c, CX : CX + 1, :] = from_above[W - 1, n : n + 1, :] * (keep_x * keep_y)

        def parts(first):
            pairs = []
            for c in range(3):
                a0, d0 = z_pair(near[c, first : first + 8, :])
                a1, d1 = z_pair(far[c, first : first + 8, :])
                pairs.append((a0, d0, a1, d1))
            return y_parts(pairs)

        prev, cur = parts(0), parts(1)
        rim[m, 0] = energy_terms(prev, cur)
        rim[m, 1] = mass_of(cur) + mass_of(prev)


def raw_planes(
    planes, lams, gz, z_state, column_stiff, column_mass, bulk, strips,
    stiff, mass, stiff7, mass7, rim, out,
):
    sub, lane = sub_lane()
    beside = beside_halo(gz, lane)
    factor = 3.0 * (1.0 - stiff_floor) / 16.0
    for x in planes:
        for i in range(CY // 8):
            rows = slice(8 * i, 8 * i + 8)
            correction = z_tile(z_state, x, i)
            for j in range(2):
                cols = slice(LANES * j, LANES * j + LANES)
                phys = pair_tile(0, x, i, j, bulk, strips, sub) + jnp.where(beside[j], correction, 0.0)
                phys = (factor * phys) * phys
                for m in range(MODES):
                    if x < CX - 1:
                        k, e = stiff[m, x, rows, cols], mass[m, x, rows, cols]
                    else:
                        k, e = stiff7[m, rows, cols], mass7[m, rows, cols]
                    if i == CY // 8 - 1:
                        k = jnp.where(sub == 7, jnp.broadcast_to(rim[m, 0, x : x + 1, cols], (8, LANES)), k)
                        e = jnp.where(sub == 7, jnp.broadcast_to(rim[m, 1, x : x + 1, cols], (8, LANES)), e)
                    if j == 1:
                        by = LANES - 1 - (32 * m + x)
                        k = jnp.where(lane == LANES - 1, pltpu.roll(column_stiff[rows, :], by, 1), k)
                        e = jnp.where(lane == LANES - 1, pltpu.roll(column_mass[rows, :], by, 1), e)
                    out[x % W, m, rows, cols] = phys * k - lams[m] * e


def raw_kernel1(
    lams, z_in, packed, bulk, bulk_edges, strips, strip_edges,
    stiff, mass, stiff7, mass7, rim, low, z_parts,
):
    gx, gy, gz = pos()
    z_state = z_sweeps(0, strip_scale(gx, gy), z_in[0], bulk_edges, strip_edges)

    near, far = packed[...], z_in[1] * jnp.where(gz < 1, 1.0, 0.0)
    a0, d0 = near + far, far - near
    a1, d1 = pltpu.roll(a0, PY - 1, 0), pltpu.roll(d0, PY - 1, 0)
    parts = [(x[0][0:CY]) for x in y_parts([(a0, d0, a1, d1)])]

    def turned(t, by):
        return pltpu.roll(t, (LANES - by) % LANES, 1) if by else t

    prev = [[turned(t, NODES * c) for c in range(3)] for t in parts]
    cur = [[turned(t, NODES * c + 1) for c in range(3)] for t in parts]
    column_stiff = energy_terms(prev, cur)
    column_mass = mass_of(cur) + mass_of(prev)
    z_parts[0], z_parts[1], z_parts[2] = z_state[0:CY], column_stiff, column_mass
    raw_planes(
        range(W), lams, gz, z_state, column_stiff, column_mass, bulk, strips,
        stiff, mass, stiff7, mass7, rim, low,
    )


def raw_kernel2(
    lams, z_parts, bulk, strips, stiff, mass, stiff7, mass7, rim, high
):
    gx, gy, gz = pos()
    raw_planes(
        range(W, CX), lams, gz, z_parts[0], z_parts.at[1], z_parts.at[2], bulk, strips,
        stiff, mass, stiff7, mass7, rim, high,
    )


def raw_plane(low, high, above, below, p):
    if p < W:
        return below, p
    if p < 2 * W:
        return low, p - W
    if p < 3 * W:
        return high, p - 2 * W
    return above, p - 3 * W


def pack_y2(low, high, down, up):
    first = iota((8, CZ), 0) < 4
    for x in range(CX):
        a, i = (low, x) if x < W else (high, x - W)
        down[x] = jnp.where(first, a[i, 0, 0:8, :], pltpu.roll(a[i, 1, 0:8, :], 4, 0))
        up[x] = jnp.where(first, pltpu.roll(a[i, 0, 24:32, :], 4, 0), a[i, 1, 24:32, :])


def own_raw_halo(y_above, y_below, m, x, lanes=slice(None)):
    a, b = y_above[x, :, lanes], y_below[x, :, lanes]
    if m == 0:
        b = pltpu.roll(b, 4, 0)
    else:
        a = pltpu.roll(a, 4, 0)
    return jnp.where(iota(a.shape, 0) < 4, a, b)


def pack_e2(y_above, y_below, ahead, down, up):
    for i in range(W - 1):
        for m in range(MODES):
            down[MODES * i + m] = own_raw_halo(y_above, y_below, m, i)
            up[MODES * i + m] = own_raw_halo(y_above, y_below, m, CX - 1 - i)


def raw_halo(y_above, y_below, from_above, from_below, m, p, lanes=slice(None)):
    if W <= p < W + CX:
        return own_raw_halo(y_above, y_below, m, p - W, lanes)
    if 0 < p < W:
        return from_below[MODES * (W - 1 - p) + m, :, lanes]
    if W + CX <= p < PX - 1:
        return from_above[MODES * (p - W - CX) + m, :, lanes]
    return jnp.zeros(y_above[0, :, lanes].shape, F32)


def bulk_kernel2(m, low, high, above, below, bulk, ends, edges, own, table, sb, one, two):
    at = pos()
    fill_bulk(table, at[1], at[2])

    def source(_, p, i):
        a, at_plane = raw_plane(low, high, above, below, p)
        return a[at_plane, m, 8 * i : 8 * i + 8, :]

    bulk_sweeps(1, at, table, source, (sb, one, two), ends, edges, bulk)
    edge = edge_tiles(at[2])

    def load(p):
        a, i = raw_plane(low, high, above, below, p)
        return a[i, m, :, edge]

    own[0] = own_strip(at[2], load)


def pack_z2(own0, own1, y_above, y_below, from_above, from_below, out):
    gx, gy, gz = pos()
    edge = edge_tiles(gz)
    halos = (y_above, y_below, from_above, from_below)
    for m, own in enumerate((own0, own1)):
        out[m, 0:CY, :] = own[0]
        out[m, CY:PY, :] = own_strip(gz, lambda p, m=m: raw_halo(*halos, m, p, edge), 8)


def strip_kernel2(
    mask, y_above, y_below, from_above, from_below, ends0, ends1, bulk0, bulk1,
    out, side, edges0, edges1, table, strips0, strips1, a0, a1, b0, b1, c0, c1, held, left,
):
    gx, gy, gz = at = pos()
    sub, lane = sub_lane()
    fill_strips(table, gy, gz)
    states = ((a0, b0, c0), (a1, b1, c1))
    copies = []
    for m in range(MODES):
        ends, bulk, edges = (ends0, ends1)[m], (bulk0, bulk1)[m], (edges0, edges1)[m]
        strips = (strips0, strips1)[m]

        def source(_, p, m=m):
            return raw_halo(y_above, y_below, from_above, from_below, m, p)

        strip_sweeps(1, at, table, source, ends, states[m], edges, strips)
        for x in range(CX):
            for i in range(CY // 8):
                rows = slice(8 * i, 8 * i + 8)
                pair = []
                for j in range(2):
                    cols = slice(LANES * j, LANES * j + LANES)
                    value = pair_tile(0, x, i, j, bulk, strips, sub)
                    held[m, x, rows, cols] = value * mask[x, rows, cols].astype(F32)
                    pair.append(value)
                side[m, x, rows, :] = jnp.where(gz == 0, pair[1], pair[0])
            if x % 4 == 3:
                part = (m, slice(x - 3, x + 1))
                copy = pltpu.make_async_copy(held.at[part], out.at[part], left.at[len(copies)])
                copy.start()
                copies.append(copy)
    for copy in copies:
        copy.wait()


def final_kernel(mask, z_in, bulk_edges0, bulk_edges1, strip_edges0, strip_edges1, side, given, out, held, left):
    gx, gy, gz = pos()
    sub, lane = sub_lane()
    at_end = beside_halo(gz, lane)
    beside = at_end[0] | at_end[1]
    edge = edge_tiles(gz)
    scale = strip_scale(gx, gy)
    copies = []
    for m in range(MODES):
        edges = ((bulk_edges0, strip_edges0), (bulk_edges1, strip_edges1))[m]
        z_state = z_sweeps(0, scale, z_in[m], *edges)
        for x in range(CX):
            for i in range(CY // 8):
                rows = slice(8 * i, 8 * i + 8)
                value = side[m, x, rows, :] + jnp.where(beside, z_tile(z_state, x, i), 0.0)
                held[m, x, rows, :] = value * mask[x, rows, edge].astype(F32)
            if x % 4 == 3:
                planes = slice(x - 3, x + 1)
                copy = pltpu.make_async_copy(
                    held.at[m, planes], out.at[m, planes, :, edge], left.at[len(copies)]
                )
                copy.start()
                copies.append(copy)
    for copy in copies:
        copy.wait()


def whole(x):
    return pl.BlockSpec(x.shape, lambda i: (0,) * x.ndim)


def call(kernel, name, outs, args, specs=None, out_specs=None, scratch=(), flops=0, aliases=None):
    specs = specs or {}
    shapes = tuple(jax.ShapeDtypeStruct(s, F32) for s in outs)
    out_specs = out_specs or {}
    out_specs = tuple(out_specs.get(i, whole(s)) for i, s in enumerate(shapes))
    return pl.pallas_call(
        kernel,
        grid=(1,),
        out_shape=shapes if len(shapes) > 1 else shapes[0],
        in_specs=[specs.get(i, whole(a)) for i, a in enumerate(args)],
        scratch_shapes=[pltpu.VMEM(s, F32) if isinstance(s, tuple) else s for s in scratch],
        compiler_params=pltpu.CompilerParams(vmem_limit_bytes=24 * 1024 * 1024),
        cost_estimate=pl.CostEstimate(flops=flops, bytes_accessed=2_000_000, transcendentals=0),
        name=name,
        out_specs=out_specs if len(shapes) > 1 else out_specs[0],
        input_output_aliases=aliases or {},
    )(*args)


HBM = pl.BlockSpec(memory_space=pltpu.HBM)


def ring(axis, step):
    size = lax.axis_size(axis)
    return [(i, (i + step) % size) for i in range(size)]


def shift(x, axis, step):
    return lax.ppermute(x, axis, ring(axis, step))


def sweep_outs(fields):
    return (
        [(fields, CX, CY, CZ), (fields, ITERS, PX, 2, 1, CZ), (fields, ITERS, CY, LANES)],
        [(3, CY, CZ)] + [(fields, PX, CY, CZ)] * 3,
        [(fields, CX, 16, CZ), (fields, ITERS, 16, LANES)],
        [(3, 16, CZ)] + [(fields, PX, 16, CZ)] * 3,
    )


def local(mode_fields, design, solid_mask, eigenvalues, mode_order):
    bulk_outs, bulk_scratch, strip_outs, strip_scratch = sweep_outs(1)

    inputs = (design, solid_mask, mode_fields, eigenvalues, mode_order)
    src, down, up, lams = call(
        pack_x1, "pack_x1", [(CX, CY, CZ), (W + 6, CY, CZ), (W, CY, CZ), (MODES, 8, LANES)],
        tuple(pltpu.with_memory_space_constraint(x, pltpu.HBM) for x in inputs),
        {i: HBM for i in range(5)},
        scratch=[
            (CX, CY, CZ), pltpu.VMEM((CX, CY, CZ), jnp.int32), pltpu.SMEM((eigenvalues.size,), F32),
            pltpu.SMEM((mode_order.size,), jnp.int32), pltpu.SemaphoreType.DMA((8,)),
        ],
    )
    above, below = shift(down, "gx", -1), shift(up, "gx", 1)
    field = (MODES, CX - 1, CY, CZ)
    down, up = call(pack_y1, "pack_y1", [(W + 6, 8, CZ), (W, 8, CZ)], (src, mode_fields))
    y_above, y_below = shift(down, "gy", -1), shift(up, "gy", 1)
    stiff, mass, columns = call(
        energy_kernel, "energy", [field, field, (2, CY, LANES)], (mode_fields,), flops=40_000_000
    )

    down, up = call(pack_e1, "pack_e1", [(W, 8, CZ), (W - 1, 8, CZ)], (y_above, y_below, columns))
    halos = (y_above, y_below, shift(down, "gx", -1), shift(up, "gx", 1))
    plane = (MODES, CY, CZ)
    bulk, ends, bulk_edges, stiff7, mass7, own, rims, row32 = call(
        bulk_kernel1, "bulk1",
        bulk_outs + [plane, plane, (1, CY, LANES), (2, CY, LANES), (2, 8, LANES)],
        (src, mode_fields, columns, above, below, y_above), scratch=bulk_scratch, flops=30_000_000,
    )

    z_in = shift(call(pack_z1, "pack_z1", [(2, PY, LANES)], (own, rims, row32, *halos)), "gz", 1)
    strips, strip_edges, rim, packed = call(
        strip_kernel1, "strips1", strip_outs + [(MODES, 2, 8, CZ), (PY, LANES)],
        (mode_fields, rims, row32, above, *halos, ends),
        scratch=strip_scratch + [(3, 16, CZ)] * 2, flops=20_000_000,
    )
    half = (W, MODES, CY, CZ)
    energies = (stiff, mass, stiff7, mass7, rim)
    low, z_parts = call(
        raw_kernel1, "raw1", [half, (3, CY, LANES)],
        (lams, z_in, packed, bulk, bulk_edges, strips, strip_edges, *energies),
    )
    above = shift(low, "gx", -1)
    high = call(raw_kernel2, "raw2", [half], (lams, z_parts, bulk, strips, *energies), flops=60_000_000)
    below = shift(high, "gx", 1)

    planes = (low, high, above, below)
    down, up = call(pack_y2, "pack_y2", [(CX, 8, CZ)] * 2, (low, high))
    y_above, y_below = shift(down, "gy", -1), shift(up, "gy", 1)
    bulks = [
        call(
            functools.partial(bulk_kernel2, m), f"bulk2_{m}", bulk_outs + [(1, CY, LANES)], planes,
            scratch=bulk_scratch, flops=20_000_000,
        )
        for m in range(MODES)
    ]
    bulk, ends, bulk_edges, own = zip(*bulks)
    edge = (MODES * (W - 1), 8, CZ)
    down, up = call(pack_e2, "pack_e2", [edge] * 2, (y_above, y_below, own[0]))
    halos = (y_above, y_below, shift(down, "gx", -1), shift(up, "gx", 1))
    z_in = shift(call(pack_z2, "pack_z2", [(MODES, PY, LANES)], (*own, *halos)), "gz", 1)
    result = (MODES, CX, CY, CZ)
    strips, edges = strip_outs
    table, state = strip_scratch[0], strip_scratch[1]
    out, side, *strip_edges = call(
        strip_kernel2, "strips2", [result, (MODES, CX, CY, LANES), edges, edges],
        (solid_mask, *halos, *ends, *bulk), out_specs={0: HBM},
        scratch=[table, strips, strips] + [state] * 6 + [result, pltpu.SemaphoreType.DMA((4,))],
        flops=20_000_000,
    )
    return call(
        final_kernel, "final", [result],
        (solid_mask, z_in, *bulk_edges, *strip_edges, side, out), {7: HBM}, {0: HBM},
        scratch=[(MODES, CX, CY, LANES), pltpu.SemaphoreType.DMA((4,))], aliases={7: 0},
    )


def solution(mesh):
    return jax.shard_map(
        local,
        mesh=mesh,
        in_specs=(
            P(None, None, "gx", "gy", "gz"),
            P("gx", "gy", "gz"),
            P("gx", "gy", "gz"),
            P(),
            P(),
        ),
        out_specs=P(None, "gx", "gy", "gz"),
        check_vma=False,
    )
```

```python
import functools

import jax
import jax.numpy as jnp
from jax import lax
from jax.experimental import pallas as pl
from jax.experimental.pallas import tpu as pltpu
from jax.sharding import PartitionSpec as P

ITERS = 4
MODES = 2
CX, CY, CZ = 8, 32, 256
W = ITERS
PX = CX + 2 * W
PY = CY + 8
NODES = CX + 1
LANES = 128

poisson = 0.3
radius_sq = 3.0
stiff_floor = 0.001
LAME = poisson / ((1.0 + poisson) * (1.0 - 2.0 * poisson))
SHEAR = 0.5 / (1.0 + poisson)

F32 = jnp.float32


def iota(shape, dim):
    return lax.broadcasted_iota(jnp.int32, shape, dim)


def pos():
    return tuple(lax.axis_index(a) for a in ("gx", "gy", "gz"))


def sub_lane():
    return iota((8, LANES), 0), iota((8, LANES), 1)


def even(axis):
    return lax.rem(lax.axis_index(axis), 2) == 0


class Pick:
    def __init__(self, cond, yes, no):
        self.cond, self.yes, self.no = cond, yes, no

    def __getitem__(self, index):
        return jnp.where(self.cond, self.yes[index], self.no[index])


def neighbours(axis, first, second):
    cond = even(axis)
    return Pick(cond, first, second), Pick(cond, second, first)


def put(axis, first, second, index, down, up):
    cond = even(axis)
    first[index] = jnp.where(cond, up, down)
    second[index] = jnp.where(cond, down, up)


def total_of(terms):
    terms = [t for t in terms if t is not None]
    while len(terms) > 1:
        pairs = [terms[i] + terms[i + 1] for i in range(0, len(terms) - 1, 2)]
        terms = pairs + ([terms[-1]] if len(terms) % 2 else [])
    return terms[0]


def scales(count, inside):
    outside = jnp.zeros(count.shape, F32)
    end = jnp.where(inside, radius_sq / (1.0 + radius_sq * (count + 1.0)), 0.0)
    mid = jnp.where(inside, radius_sq / (1.0 + radius_sq * (count + 2.0)), 0.0)
    return outside, end, mid


def yz_scales(y, z, gy, gz):
    y, z = y + gy * CY, z + gz * CZ
    inside = (y >= 0) & (y < 8 * CY)
    count = 4.0
    for place, last in ((y, 8 * CY - 1), (z, 2 * CZ - 1)):
        count = count - (place == 0).astype(F32) - (place == last).astype(F32)
    return scales(count, inside)


def kind_of(gx, plane):
    x = gx * CX + plane - W
    out = (x < 0) | (x > 8 * CX - 1)
    end = (x == 0) | (x == 8 * CX - 1)
    return jnp.where(out, 0, jnp.where(end, 1, 2))


def fill_bulk(table, gy, gz):
    shape = (CY, CZ)
    for i, part in enumerate(yz_scales(iota(shape, 0), iota(shape, 1), gy, gz)):
        table[i] = part


def fill_strips(table, gy, gz):
    shape = (16, CZ)
    row = iota(shape, 0)
    top = jnp.where(row < 4, row + CY, row + CY - 8)
    bottom = jnp.where(row < 12, row - 8, row - 16)
    for i, part in enumerate(yz_scales(jnp.where(row < 8, top, bottom), iota(shape, 1), gy, gz)):
        table[i] = part


def strip_scale(gx, gy):
    shape = (PY, LANES)
    row = iota(shape, 0)
    y = jnp.where(row < CY + W, row, row - PY) + gy * CY
    x = gx * CX - W + lax.div(iota(shape, 1), 8)
    inside = (y >= 0) & (y < 8 * CY) & (x >= 0) & (x < 8 * CX)
    count = 6.0
    for place, last in ((y, 8 * CY - 1), (x, 8 * CX - 1)):
        count = count - (place == 0).astype(F32) - (place == last).astype(F32)
    return jnp.where(inside, radius_sq / (1.0 + radius_sq * count), 0.0)


def tiles_of(ref, index, rows, cols):
    return [
        [ref[index + (slice(8 * i, 8 * i + 8), slice(LANES * j, LANES * j + LANES))] for j in range(cols)]
        for i in range(rows)
    ]


def along_lanes(row, lane):
    right = [pltpu.roll(t, 1, 1) for t in row]
    left = [pltpu.roll(t, LANES - 1, 1) for t in row]
    out = []
    for j in range(len(row)):
        before = right[j - 1] if j else 0.0
        after = left[j + 1] if j + 1 < len(row) else 0.0
        out.append(
            jnp.where(lane == 0, before, right[j]) + jnp.where(lane == LANES - 1, after, left[j])
        )
    return out


def along_rows(tiles, sub):
    rows, cols = len(tiles), len(tiles[0])
    down = [[pltpu.roll(t, 1, 0) for t in row] for row in tiles]
    up = [[pltpu.roll(t, 7, 0) for t in row] for row in tiles]
    out = []
    for i in range(rows):
        line = []
        for j in range(cols):
            before = down[i - 1][j] if i else 0.0
            after = up[i + 1][j] if i + 1 < rows else 0.0
            line.append(jnp.where(sub == 0, before, down[i][j]) + jnp.where(sub == 7, after, up[i][j]))
        out.append(line)
    return out


def turn_edge(tile, p, gz):
    return pltpu.roll(tile, lax.rem(8 * p + 5 - 2 * gz, LANES), 1)


def kind_at(gx, p):
    return 2 if W < p < PX - W - 1 else kind_of(gx, p)


def bulk_sweeps(fields, where, table, source, states, ends, edges, out):
    gx, gy, gz = where
    sub, lane = sub_lane()
    sb = states[0]
    for p in range(PX):
        kind = kind_at(gx, p)
        for m in range(fields):
            for i in range(CY // 8):
                rows = slice(8 * i, 8 * i + 8)
                sb[m, p, rows, :] = source(m, p, i) * (table[kind, rows, :] * (1.0 / radius_sq))
    for k in range(ITERS):
        old = states[0] if k == 0 else states[1 + (k - 1) % 2]
        new = states[1 + k % 2]
        for m in range(fields):
            edge = [jnp.zeros((8, LANES), F32)] * (CY // 8)
            for p in range(k + 1, PX - 1 - k):
                kind = kind_at(gx, p)
                mid = tiles_of(old, (m, p), CY // 8, 2)
                yy = along_rows(mid, sub)
                for i in range(CY // 8):
                    zz = along_lanes(mid[i], lane)
                    rows = slice(8 * i, 8 * i + 8)
                    for j in range(2):
                        cols = slice(LANES * j, LANES * j + LANES)
                        total = old[m, p - 1, rows, cols] + old[m, p + 1, rows, cols]
                        total = total + (yy[i][j] + zz[j])
                        value = sb[m, p, rows, cols] + table[kind, rows, cols] * total
                        if k + 1 < ITERS:
                            new[m, p, rows, cols] = value
                        else:
                            out[m, p - W, rows, cols] = value
                    side = jnp.where(gz == 0, mid[i][1], mid[i][0])
                    edge[i] = jnp.where(lane == 8 * p + 4 - gz, turn_edge(side, p, gz), edge[i])
                for j in range(2):
                    cols = slice(LANES * j, LANES * j + LANES)
                    ends[m, k, p, 0, 0:1, cols] = mid[CY // 8 - 1][j][7:8]
                    ends[m, k, p, 1, 0:1, cols] = mid[0][j][0:1]
            for i in range(CY // 8):
                edges[m, k, 8 * i : 8 * i + 8, :] = edge[i]


def strip_sweeps(fields, where, table, source, ends, states, edges, out):
    gx, gy, gz = where
    sub, lane = sub_lane()
    sb = states[0]
    wide = iota((8, CZ), 0)
    for p in range(PX):
        kind = kind_at(gx, p)
        for m in range(fields):
            halo = source(m, p) * (1.0 / radius_sq)
            sb[m, p, 0:8, :] = jnp.where(wide < 4, halo * table[kind, 0:8, :], 0.0)
            sb[m, p, 8:16, :] = jnp.where(wide < 4, 0.0, halo * table[kind, 8:16, :])
    for k in range(ITERS):
        old = states[0] if k == 0 else states[1 + (k - 1) % 2]
        new = states[1 + k % 2]
        for m in range(fields):
            edge = [jnp.zeros((8, LANES), F32)] * 2
            for p in range(k + 1, PX - 1 - k):
                kind = kind_at(gx, p)
                mid = tiles_of(old, (m, p), 2, 2)
                for i in range(2):
                    rows = slice(8 * i, 8 * i + 8)
                    zz = along_lanes(mid[i], lane)
                    for j in range(2):
                        cols = slice(LANES * j, LANES * j + LANES)
                        end = jnp.broadcast_to(ends[m, k, p, i, 0:1, cols], (8, LANES))
                        down = pltpu.roll(mid[i][j], 1, 0)
                        up = pltpu.roll(mid[i][j], 7, 0)
                        if i == 0:
                            down = jnp.where(sub == 4, 0.0, down) + jnp.where(sub == 0, end, 0.0)
                        else:
                            up = jnp.where(sub == 3, 0.0, up) + jnp.where(sub == 7, end, 0.0)
                        total = old[m, p - 1, rows, cols] + old[m, p + 1, rows, cols]
                        total = total + (down + up) + zz[j]
                        value = sb[m, p, rows, cols] + table[kind, rows, cols] * total
                        if k + 1 < ITERS:
                            new[m, p, rows, cols] = value
                        else:
                            out[m, p - W, rows, cols] = value
                    side = jnp.where(gz == 0, mid[i][1], mid[i][0])
                    edge[i] = jnp.where(lane == 8 * p + 4 - gz, turn_edge(side, p, gz), edge[i])
            for i in range(2):
                edges[m, k, 8 * i : 8 * i + 8, :] = edge[i]


def z_sweeps(m, scale, halo, bulk_edges, strip_edges):
    sub = iota((8, LANES), 0)
    column = lax.rem(iota((PY, LANES), 1), 8)
    base = halo * (scale * (1.0 / radius_sq))
    state = base
    for k in range(ITERS):
        top, bottom = strip_edges[m, k, 0:8, :], strip_edges[m, k, 8:16, :]
        own = bulk_edges[m, k]
        fed = jnp.concatenate(
            [
                own[0:8] + jnp.where(sub < 4, bottom, 0.0),
                own[8 : CY - 8],
                own[CY - 8 : CY] + jnp.where(sub < 4, 0.0, top),
                jnp.where(sub < 4, top, bottom),
            ],
            axis=0,
        )
        total = pltpu.roll(state, 8, 1) + pltpu.roll(state, LANES - 8, 1)
        total = total + pltpu.roll(state, 1, 0) + pltpu.roll(state, PY - 1, 0)
        total = total + jnp.where(column == 0, 0.0, pltpu.roll(state, 1, 1))
        total = total + jnp.where(column == 7, 0.0, pltpu.roll(state, LANES - 1, 1))
        state = base + scale * (total + fed)
    return state


def pair_tile(m, x, i, j, bulk, strips, sub):
    rows, cols = slice(8 * i, 8 * i + 8), slice(LANES * j, LANES * j + LANES)
    value = bulk[m, x, rows, cols]
    if i == 0:
        value = value + jnp.where(sub < 4, strips[m, x, 8:16, cols], 0.0)
    if i == CY // 8 - 1:
        value = value + jnp.where(sub < 4, 0.0, strips[m, x, 0:8, cols])
    return value


def z_tile(z_state, x, i):
    return pltpu.roll(z_state[8 * i : 8 * i + 8], (LANES - 4 - 8 * (x + W)) % LANES, 1)


def beside_halo(gz, lane):
    return (lane < 4 * gz), (lane >= LANES - 4 * (1 - gz))


def pack_strip(gz, tile, p, acc, lane):
    first = 8 * p + 4 * gz
    turned = pltpu.roll(tile, (8 * p + 4) % LANES, 1)
    return jnp.where((lane >= first) & (lane < first + 4), turned, acc)


def own_strip(gz, load, rows=CY):
    lane = iota((rows, LANES), 1)
    acc = jnp.zeros((rows, LANES), F32)
    for p in range(PX):
        acc = pack_strip(gz, load(p), p, acc, lane)
    return acc


def edge_tiles(gz):
    return pl.ds(pl.multiple_of((1 - gz) * LANES, LANES), LANES)


def energy_terms(prev, cur):
    (paa, pad, pda, pdd), (caa, cad, cda, cdd) = prev, cur
    u, v, w = 0, 1, 2
    aad = [cad[i] + pad[i] for i in range(3)]
    ada = [cda[i] + pda[i] for i in range(3)]
    add = [cdd[i] + pdd[i] for i in range(3)]
    daa = [caa[i] - paa[i] for i in range(3)]
    dad = [cad[i] - pad[i] for i in range(3)]
    dda = [cda[i] - pda[i] for i in range(3)]
    ddd = [cdd[i] - pdd[i] for i in range(3)]

    def sq(x):
        return x * x

    trace = sq(daa[u] + ada[v] + aad[w])
    lines = sq(dda[v] + dad[w]) + sq(dda[u] + add[w]) + sq(dad[u] + add[v])
    diag = sq(daa[u]) + sq(ada[v]) + sq(aad[w])
    shear = sq(ada[u] + daa[v]) + sq(aad[u] + daa[w]) + sq(aad[v] + ada[w])
    mixed = sq(dda[u]) + sq(dda[v]) + sq(dad[u]) + sq(dad[w]) + sq(add[v]) + sq(add[w])
    cross = sq(add[u] + dad[v]) + sq(add[u] + dda[w]) + sq(dad[v] + dda[w])
    cubic = sq(ddd[u]) + sq(ddd[v]) + sq(ddd[w])
    return (
        LAME * (trace + lines * (1.0 / 3.0))
        + SHEAR * (2.0 * diag + shear + mixed + cross * (1.0 / 3.0))
        + ((LAME + 4.0 * SHEAR) / 9.0) * cubic
    )


def y_parts(pairs):
    aa = [a0 + a1 for a0, d0, a1, d1 in pairs]
    ad = [d0 + d1 for a0, d0, a1, d1 in pairs]
    da = [a1 - a0 for a0, d0, a1, d1 in pairs]
    dd = [d1 - d0 for a0, d0, a1, d1 in pairs]
    return aa, ad, da, dd


def mass_of(parts):
    return total_of([x * x for part in parts for x in part])


def z_pair(here):
    after = pltpu.roll(here, CZ - 1, 1)
    return here + after, after - here


def own_parts(load, chunk):
    sub = iota((8, CZ), 0)
    pairs = []
    for c in range(3):
        a0, d0 = z_pair(load(c, 8 * chunk))
        following = min(chunk + 1, CY // 8 - 1)
        a1, d1 = z_pair(load(c, 8 * following))

        def next_row(t, n):
            return jnp.where(sub == 7, pltpu.roll(n, 7, 0), pltpu.roll(t, 7, 0))

        pairs.append((a0, d0, next_row(a0, a1), next_row(d0, d1)))
    return y_parts(pairs)


def pack_columns(load, lane):
    first = jnp.zeros((CY, LANES), F32)
    last = first
    for m in range(MODES):
        for c in range(3):
            for x in range(CX):
                to = 32 * m + NODES * c + x
                here = lane == to
                first = jnp.where(here, pltpu.roll(load(m, c, x, 0), to, 1), first)
                last = jnp.where(here, pltpu.roll(load(m, c, x, 1), to + 1, 1), last)
    return first, last


def with_plane8(packed, above, keep_x, last):
    cols = slice(CZ - LANES, CZ) if last else slice(0, LANES)
    rows = packed.shape[0]
    lane = iota(packed.shape, 1)
    for m in range(MODES):
        for c in range(3):
            to = 32 * m + NODES * c + CX
            turned = pltpu.roll(above[W + 3 * m + c, 0:rows, cols], to + last, 1)
            packed = jnp.where(lane == to, turned * keep_x, packed)
    return packed


def row32_of(y_above, last):
    cols = slice(CZ - LANES, CZ) if last else slice(0, LANES)
    sub, lane = sub_lane()
    tile = jnp.zeros((8, LANES), F32)
    for m in range(MODES):
        for c in range(3):
            for x in range(CX):
                to = 32 * m + NODES * c + x
                row = jnp.broadcast_to(y_above[W + 3 * m + c, x : x + 1, cols], (8, LANES))
                tile = jnp.where(lane == to, pltpu.roll(row, to + last, 1), tile)
    return jnp.where(sub == 0, tile, 0.0)


def with_row32(packed, row, from_above, keep_x, keep_y, last):
    cols = slice(CZ - LANES, CZ) if last else slice(0, LANES)
    sub, lane = sub_lane()
    for m in range(MODES):
        for c in range(3):
            to = 32 * m + NODES * c + CX
            n = 3 * m + c
            corner = jnp.broadcast_to(from_above[W - 1, n : n + 1, cols] * keep_x, (8, LANES))
            row = jnp.where((lane == to) & (sub == 0), pltpu.roll(corner, to + last, 1), row)
    return jnp.concatenate([packed, row * keep_y], axis=0)


def pack_x1(
    design, mask, modes, eigenvalues, order, src, first, second, lams, field, solid, rim, values, chosen, arrived
):
    copies = []
    for half in (slice(0, W), slice(W, CX)):
        copies.append((design.at[half], field.at[half]))
        copies.append((mask.at[half], solid.at[half]))
    for m in range(MODES):
        copies.append((modes.at[m, :, 0], rim.at[3 * m : 3 * m + 3]))
    copies += [(eigenvalues, values), (order, chosen)]
    copies = [pltpu.make_async_copy(a, b, arrived.at[n]) for n, (a, b) in enumerate(copies)]
    for copy in copies:
        copy.start()
    for copy in copies[:4]:
        copy.wait()
    for x in range(W):
        low, high = (field[p] * solid[p].astype(F32) for p in (x, x + W))
        src[x], src[x + W] = low, high
        put("gx", first, second, x, low, high)
    for copy in copies[4:]:
        copy.wait()
    first[W : W + 6] = rim[...]
    second[W : W + 6] = rim[...]
    for m in range(MODES):
        lams[m] = jnp.full((8, LANES), values[chosen[m]] * (0.125 * 0.25), F32)


def energy_kernel(modes, stiff, mass, columns):
    lane = iota((CY, LANES), 1)
    columns[0], columns[1] = pack_columns(
        lambda m, c, x, j: modes[m, c, x, :, LANES * j : LANES * j + LANES], lane
    )

    def mode_step(m, carry):
        for chunk in range(CY // 8):
            rows = slice(8 * chunk, 8 * chunk + 8)
            prev = prev_mass = None
            for x in range(CX):
                cur = own_parts(lambda c, r: modes[m, c, x, r : r + 8, :], chunk)
                cur_mass = mass_of(cur)
                if x:
                    stiff[m, x - 1, rows, :] = energy_terms(prev, cur)
                    mass[m, x - 1, rows, :] = cur_mass + prev_mass
                prev, prev_mass = cur, cur_mass
        return carry

    lax.fori_loop(0, MODES, mode_step, 0)


def pick_plane(own, above, below, p):
    if p < W:
        return below, p
    if p < W + CX:
        return own, p - W
    return above, p - W - CX


def pack_y1(src, modes, first, second):
    low = iota((8, CZ), 0) < 4
    for q in range(W):
        down = jnp.where(low, src[q, 0:8, :], pltpu.roll(src[q + W, 0:8, :], 4, 0))
        up = jnp.where(low, pltpu.roll(src[q + W, 24:32, :], 4, 0), src[q, 24:32, :])
        put("gy", first, second, q, down, up)
    for m in range(MODES):
        for c in range(3):
            for x in range(CX):
                for out in (first, second):
                    out[W + 3 * m + c, x : x + 1, :] = modes[m, c, x, 0:1, :]


def own_halo(y_above, y_below, x, lanes=slice(None)):
    a, b = y_above[x % W, :, lanes], y_below[x % W, :, lanes]
    if x >= W:
        a, b = pltpu.roll(a, 4, 0), pltpu.roll(b, 4, 0)
    return jnp.where(iota(a.shape, 0) < 4, a, b)


def pack_e1(y_first, y_second, ahead, first, second):
    y_above, y_below = neighbours("gy", y_first, y_second)
    for i in range(W - 1):
        down, up = (own_halo(y_above, y_below, x) for x in (i, CX - 1 - i))
        put("gx", first, second, i, down, up)
    for out in (first, second):
        out[W - 1] = jnp.zeros((8, CZ), F32)
        for n in range(3 * MODES):
            out[W - 1, n : n + 1, :] = y_above[W + n, 0:1, :]


def halo_tile(y_above, y_below, from_above, from_below, p, lanes=slice(None)):
    if W <= p < W + CX:
        return own_halo(y_above, y_below, p - W, lanes)
    if 0 < p < W:
        return from_below[W - 1 - p, :, lanes]
    if W + CX <= p < PX - 1:
        return from_above[p - W - CX, :, lanes]
    return jnp.zeros(y_above[0, :, lanes].shape, F32)


def bulk_kernel1(
    src, modes, columns, x_first, x_second, y_first, y_second,
    bulk, ends, edges, stiff, mass, own, rims, row32, table, sb, one, two,
):
    above, below = neighbours("gx", x_first, x_second)
    y_above, y_below = neighbours("gy", y_first, y_second)
    at = pos()
    gx, gy, gz = at
    fill_bulk(table, gy, gz)

    def source(m, p, i):
        a, at_plane = pick_plane(src, above, below, p)
        return a[at_plane, 8 * i : 8 * i + 8, :]

    bulk_sweeps(1, at, table, source, (sb, one, two), ends, edges, bulk)
    edge = edge_tiles(gz)
    own[0] = own_strip(gz, lambda p: plane_edge(src, above, below, p, edge))
    keep = jnp.where(gx < 7, 1.0, 0.0)
    for last in range(2):
        rims[last] = with_plane8(columns[last], above, keep, last)
        row32[last] = row32_of(y_above, last)
    for m in range(MODES):
        for chunk in range(CY // 8):
            rows = slice(8 * chunk, 8 * chunk + 8)
            prev = own_parts(lambda c, r: modes[m, c, CX - 1, r : r + 8, :], chunk)
            cur = own_parts(lambda c, r: above[W + 3 * m + c, r : r + 8, :] * keep, chunk)
            stiff[m, rows, :] = energy_terms(prev, cur)
            mass[m, rows, :] = mass_of(cur) + mass_of(prev)


def plane_edge(own, above, below, p, edge):
    a, i = pick_plane(own, above, below, p)
    return a[i, :, edge]


def pack_z1(own, rims, row32, y_first, y_second, e_first, e_second, out):
    gx, gy, gz = pos()
    edge = edge_tiles(gz)
    halos = (*neighbours("gy", y_first, y_second), *neighbours("gx", e_first, e_second))
    from_above = halos[2]
    out[0, 0:CY, :] = own[0]
    out[0, CY:PY, :] = own_strip(gz, lambda p: halo_tile(*halos, p, edge), 8)
    keep_x = jnp.where(gx < 7, 1.0, 0.0)
    keep_y = jnp.where(gy < 7, 1.0, 0.0)
    out[1] = with_row32(rims[0], row32[0], from_above, keep_x, keep_y, 0)


def strip_kernel1(
    modes, rims, row32, x_first, x_second, y_first, y_second, e_first, e_second, ends,
    strips, edges, rim, packed, table, sb, one, two, near, far,
):
    at = pos()
    gx, gy, gz = at
    fill_strips(table, gy, gz)
    halos = (*neighbours("gy", y_first, y_second), *neighbours("gx", e_first, e_second))
    y_above, y_below, from_above, from_below = halos
    above, below = neighbours("gx", x_first, x_second)
    strip_sweeps(
        1, at, table, lambda m, p: halo_tile(*halos, p), ends, (sb, one, two), edges, strips
    )
    keep_x = jnp.where(gx < 7, 1.0, 0.0)
    keep_y = jnp.where(gy < 7, 1.0, 0.0)
    packed[...] = with_row32(rims[1], row32[1], from_above, keep_x, keep_y, 1)
    for m in range(MODES):
        for c in range(3):
            n = 3 * m + c
            for x in range(CX):
                near[c, x : x + 1, :] = modes[m, c, x, CY - 1 : CY, :]
            near[c, CX : CX + 1, :] = above[W + n, CY - 1 : CY, :] * keep_x
            far[c, 0:CX, :] = y_above[W + n] * keep_y
            far[c, CX : CX + 1, :] = from_above[W - 1, n : n + 1, :] * (keep_x * keep_y)

        def parts(first):
            pairs = []
            for c in range(3):
                a0, d0 = z_pair(near[c, first : first + 8, :])
                a1, d1 = z_pair(far[c, first : first + 8, :])
                pairs.append((a0, d0, a1, d1))
            return y_parts(pairs)

        prev, cur = parts(0), parts(1)
        rim[m, 0] = energy_terms(prev, cur)
        rim[m, 1] = mass_of(cur) + mass_of(prev)


def raw_planes(
    planes, lams, gz, z_state, column_stiff, column_mass, bulk, strips,
    stiff, mass, stiff7, mass7, rim, store,
):
    sub, lane = sub_lane()
    beside = beside_halo(gz, lane)
    factor = 3.0 * (1.0 - stiff_floor) / 16.0
    for x in planes:
        for i in range(CY // 8):
            rows = slice(8 * i, 8 * i + 8)
            correction = z_tile(z_state, x, i)
            for j in range(2):
                cols = slice(LANES * j, LANES * j + LANES)
                phys = pair_tile(0, x, i, j, bulk, strips, sub) + jnp.where(beside[j], correction, 0.0)
                phys = (factor * phys) * phys
                for m in range(MODES):
                    if x < CX - 1:
                        k, e = stiff[m, x, rows, cols], mass[m, x, rows, cols]
                    else:
                        k, e = stiff7[m, rows, cols], mass7[m, rows, cols]
                    if i == CY // 8 - 1:
                        k = jnp.where(sub == 7, jnp.broadcast_to(rim[m, 0, x : x + 1, cols], (8, LANES)), k)
                        e = jnp.where(sub == 7, jnp.broadcast_to(rim[m, 1, x : x + 1, cols], (8, LANES)), e)
                    if j == 1:
                        by = LANES - 1 - (32 * m + x)
                        k = jnp.where(lane == LANES - 1, pltpu.roll(column_stiff[rows, :], by, 1), k)
                        e = jnp.where(lane == LANES - 1, pltpu.roll(column_mass[rows, :], by, 1), e)
                    store((x % W, m, rows, cols), phys * k - lams[m] * e)


def raw_kernel1(
    lams, z_in, packed, bulk, bulk_edges, strips, strip_edges,
    stiff, mass, stiff7, mass7, rim, low, z_parts,
):
    gx, gy, gz = pos()
    z_state = z_sweeps(0, strip_scale(gx, gy), z_in[0], bulk_edges, strip_edges)

    near, far = packed[...], z_in[1] * jnp.where(gz < 1, 1.0, 0.0)
    a0, d0 = near + far, far - near
    a1, d1 = pltpu.roll(a0, PY - 1, 0), pltpu.roll(d0, PY - 1, 0)
    parts = [(x[0][0:CY]) for x in y_parts([(a0, d0, a1, d1)])]

    def turned(t, by):
        return pltpu.roll(t, (LANES - by) % LANES, 1) if by else t

    prev = [[turned(t, NODES * c) for c in range(3)] for t in parts]
    cur = [[turned(t, NODES * c + 1) for c in range(3)] for t in parts]
    column_stiff = energy_terms(prev, cur)
    column_mass = mass_of(cur) + mass_of(prev)
    z_parts[0], z_parts[1], z_parts[2] = z_state[0:CY], column_stiff, column_mass
    raw_planes(
        range(W), lams, gz, z_state, column_stiff, column_mass, bulk, strips,
        stiff, mass, stiff7, mass7, rim, low.__setitem__,
    )


def raw_kernel2(
    lams, z_parts, bulk, strips, stiff, mass, stiff7, mass7, rim, low, high, first, second
):
    gx, gy, gz = pos()

    def store(index, value):
        high[index] = value
        put("gx", first, second, index, low[index], value)

    raw_planes(
        range(W, CX), lams, gz, z_parts[0], z_parts.at[1], z_parts.at[2], bulk, strips,
        stiff, mass, stiff7, mass7, rim, store,
    )


def raw_plane(low, high, above, below, p):
    if p < W:
        return below, p
    if p < 2 * W:
        return low, p - W
    if p < 3 * W:
        return high, p - 2 * W
    return above, p - 3 * W


def pack_y2(low, high, first, second):
    top = iota((8, CZ), 0) < 4
    for x in range(CX):
        a, i = (low, x) if x < W else (high, x - W)
        down = jnp.where(top, a[i, 0, 0:8, :], pltpu.roll(a[i, 1, 0:8, :], 4, 0))
        up = jnp.where(top, pltpu.roll(a[i, 0, 24:32, :], 4, 0), a[i, 1, 24:32, :])
        put("gy", first, second, x, down, up)


def own_raw_halo(y_above, y_below, m, x, lanes=slice(None)):
    a, b = y_above[x, :, lanes], y_below[x, :, lanes]
    if m == 0:
        b = pltpu.roll(b, 4, 0)
    else:
        a = pltpu.roll(a, 4, 0)
    return jnp.where(iota(a.shape, 0) < 4, a, b)


def pack_e2(y_first, y_second, ahead, first, second):
    y_above, y_below = neighbours("gy", y_first, y_second)
    for i in range(W - 1):
        for m in range(MODES):
            down, up = (own_raw_halo(y_above, y_below, m, x) for x in (i, CX - 1 - i))
            put("gx", first, second, MODES * i + m, down, up)


def raw_halo(y_above, y_below, from_above, from_below, m, p, lanes=slice(None)):
    if W <= p < W + CX:
        return own_raw_halo(y_above, y_below, m, p - W, lanes)
    if 0 < p < W:
        return from_below[MODES * (W - 1 - p) + m, :, lanes]
    if W + CX <= p < PX - 1:
        return from_above[MODES * (p - W - CX) + m, :, lanes]
    return jnp.zeros(y_above[0, :, lanes].shape, F32)


def bulk_kernel2(m, low, high, x_first, x_second, bulk, ends, edges, own, table, sb, one, two):
    above, below = neighbours("gx", x_first, x_second)
    at = pos()
    fill_bulk(table, at[1], at[2])

    def source(_, p, i):
        a, at_plane = raw_plane(low, high, above, below, p)
        return a[at_plane, m, 8 * i : 8 * i + 8, :]

    bulk_sweeps(1, at, table, source, (sb, one, two), ends, edges, bulk)
    edge = edge_tiles(at[2])

    def load(p):
        a, i = raw_plane(low, high, above, below, p)
        return a[i, m, :, edge]

    own[0] = own_strip(at[2], load)


def pack_z2(own0, own1, y_first, y_second, e_first, e_second, out):
    gx, gy, gz = pos()
    edge = edge_tiles(gz)
    halos = (*neighbours("gy", y_first, y_second), *neighbours("gx", e_first, e_second))
    for m, own in enumerate((own0, own1)):
        out[m, 0:CY, :] = own[0]
        out[m, CY:PY, :] = own_strip(gz, lambda p, m=m: raw_halo(*halos, m, p, edge), 8)


def strip_kernel2(
    mask, y_first, y_second, e_first, e_second, ends0, ends1, bulk0, bulk1,
    out, side, edges0, edges1, table, strips0, strips1, a0, a1, b0, b1, c0, c1, held, left,
):
    gx, gy, gz = at = pos()
    halos = (*neighbours("gy", y_first, y_second), *neighbours("gx", e_first, e_second))
    sub, lane = sub_lane()
    fill_strips(table, gy, gz)
    states = ((a0, b0, c0), (a1, b1, c1))
    copies = []
    for m in range(MODES):
        ends, bulk, edges = (ends0, ends1)[m], (bulk0, bulk1)[m], (edges0, edges1)[m]
        strips = (strips0, strips1)[m]

        def source(_, p, m=m):
            return raw_halo(*halos, m, p)

        strip_sweeps(1, at, table, source, ends, states[m], edges, strips)
        for x in range(CX):
            for i in range(CY // 8):
                rows = slice(8 * i, 8 * i + 8)
                pair = []
                for j in range(2):
                    cols = slice(LANES * j, LANES * j + LANES)
                    value = pair_tile(0, x, i, j, bulk, strips, sub)
                    held[m, x, rows, cols] = value * mask[x, rows, cols].astype(F32)
                    pair.append(value)
                side[m, x, rows, :] = jnp.where(gz == 0, pair[1], pair[0])
            if x % 4 == 3:
                part = (m, slice(x - 3, x + 1))
                copy = pltpu.make_async_copy(held.at[part], out.at[part], left.at[len(copies)])
                copy.start()
                copies.append(copy)
    for copy in copies:
        copy.wait()


def final_kernel(mask, z_in, bulk_edges0, bulk_edges1, strip_edges0, strip_edges1, side, given, out, held, left):
    gx, gy, gz = pos()
    sub, lane = sub_lane()
    at_end = beside_halo(gz, lane)
    beside = at_end[0] | at_end[1]
    edge = edge_tiles(gz)
    scale = strip_scale(gx, gy)
    copies = []
    for m in range(MODES):
        edges = ((bulk_edges0, strip_edges0), (bulk_edges1, strip_edges1))[m]
        z_state = z_sweeps(0, scale, z_in[m], *edges)
        for x in range(CX):
            for i in range(CY // 8):
                rows = slice(8 * i, 8 * i + 8)
                value = side[m, x, rows, :] + jnp.where(beside, z_tile(z_state, x, i), 0.0)
                held[m, x, rows, :] = value * mask[x, rows, edge].astype(F32)
            if x % 4 == 3:
                planes = slice(x - 3, x + 1)
                copy = pltpu.make_async_copy(
                    held.at[m, planes], out.at[m, planes, :, edge], left.at[len(copies)]
                )
                copy.start()
                copies.append(copy)
    for copy in copies:
        copy.wait()


def whole(x):
    return pl.BlockSpec(x.shape, lambda i: (0,) * x.ndim)


def call(kernel, name, outs, args, specs=None, out_specs=None, scratch=(), flops=0, aliases=None):
    specs = specs or {}
    shapes = tuple(jax.ShapeDtypeStruct(s, F32) for s in outs)
    out_specs = out_specs or {}
    out_specs = tuple(out_specs.get(i, whole(s)) for i, s in enumerate(shapes))
    return pl.pallas_call(
        kernel,
        grid=(1,),
        out_shape=shapes if len(shapes) > 1 else shapes[0],
        in_specs=[specs.get(i, whole(a)) for i, a in enumerate(args)],
        scratch_shapes=[pltpu.VMEM(s, F32) if isinstance(s, tuple) else s for s in scratch],
        compiler_params=pltpu.CompilerParams(vmem_limit_bytes=24 * 1024 * 1024),
        cost_estimate=pl.CostEstimate(flops=flops, bytes_accessed=2_000_000, transcendentals=0),
        name=name,
        out_specs=out_specs if len(shapes) > 1 else out_specs[0],
        input_output_aliases=aliases or {},
    )(*args)


HBM = pl.BlockSpec(memory_space=pltpu.HBM)


def swap(x, axis, start):
    size = lax.axis_size(axis)
    other = {i: i + 1 if i % 2 == start else i - 1 for i in range(size)}
    return lax.ppermute(x, axis, [(i, j if 0 <= j < size else i) for i, j in other.items()])


def swaps(axis, pair):
    second = swap(pair[1], axis, 1)
    return swap(pair[0], axis, 0), second


def sweep_outs(fields):
    return (
        [(fields, CX, CY, CZ), (fields, ITERS, PX, 2, 1, CZ), (fields, ITERS, CY, LANES)],
        [(3, CY, CZ)] + [(fields, PX, CY, CZ)] * 3,
        [(fields, CX, 16, CZ), (fields, ITERS, 16, LANES)],
        [(3, 16, CZ)] + [(fields, PX, 16, CZ)] * 3,
    )


def local(mode_fields, design, solid_mask, eigenvalues, mode_order):
    bulk_outs, bulk_scratch, strip_outs, strip_scratch = sweep_outs(1)

    inputs = (design, solid_mask, mode_fields, eigenvalues, mode_order)
    src, first, second, lams = call(
        pack_x1, "pack_x1", [(CX, CY, CZ), (W + 6, CY, CZ), (W + 6, CY, CZ), (MODES, 8, LANES)],
        tuple(pltpu.with_memory_space_constraint(x, pltpu.HBM) for x in inputs),
        {i: HBM for i in range(5)},
        scratch=[
            (CX, CY, CZ), pltpu.VMEM((CX, CY, CZ), jnp.int32), (6, CY, CZ), pltpu.SMEM((eigenvalues.size,), F32),
            pltpu.SMEM((mode_order.size,), jnp.int32), pltpu.SemaphoreType.DMA((8,)),
        ],
    )
    x_pair = swaps("gx", (first, second))
    field = (MODES, CX - 1, CY, CZ)
    y_pair = swaps("gy", call(pack_y1, "pack_y1", [(W + 6, 8, CZ)] * 2, (src, mode_fields)))
    stiff, mass, columns = call(
        energy_kernel, "energy", [field, field, (2, CY, LANES)], (mode_fields,), flops=40_000_000
    )

    edge_pair = swaps("gx", call(pack_e1, "pack_e1", [(W, 8, CZ)] * 2, (*y_pair, columns)))
    halos = (*y_pair, *edge_pair)
    plane = (MODES, CY, CZ)
    bulk, ends, bulk_edges, stiff7, mass7, own, rims, row32 = call(
        bulk_kernel1, "bulk1",
        bulk_outs + [plane, plane, (1, CY, LANES), (2, CY, LANES), (2, 8, LANES)],
        (src, mode_fields, columns, *x_pair, *y_pair), scratch=bulk_scratch, flops=30_000_000,
    )

    z_in = swap(call(pack_z1, "pack_z1", [(2, PY, LANES)], (own, rims, row32, *halos)), "gz", 0)
    strips, strip_edges, rim, packed = call(
        strip_kernel1, "strips1", strip_outs + [(MODES, 2, 8, CZ), (PY, LANES)],
        (mode_fields, rims, row32, *x_pair, *halos, ends),
        scratch=strip_scratch + [(3, 16, CZ)] * 2, flops=20_000_000,
    )
    half = (W, MODES, CY, CZ)
    energies = (stiff, mass, stiff7, mass7, rim)
    low, z_parts = call(
        raw_kernel1, "raw1", [half, (3, CY, LANES)],
        (lams, z_in, packed, bulk, bulk_edges, strips, strip_edges, *energies),
    )
    high, first, second = call(
        raw_kernel2, "raw2", [half] * 3, (lams, z_parts, bulk, strips, *energies, low), flops=5_000_000
    )
    planes = (low, high, *swaps("gx", (first, second)))
    y_pair = swaps("gy", call(pack_y2, "pack_y2", [(CX, 8, CZ)] * 2, (low, high)))
    bulks = [
        call(
            functools.partial(bulk_kernel2, m), f"bulk2_{m}", bulk_outs + [(1, CY, LANES)], planes,
            scratch=bulk_scratch, flops=20_000_000,
        )
        for m in range(MODES)
    ]
    bulk, ends, bulk_edges, own = zip(*bulks)
    edge = (MODES * (W - 1), 8, CZ)
    halos = (*y_pair, *swaps("gx", call(pack_e2, "pack_e2", [edge] * 2, (*y_pair, own[0]))))
    z_in = swap(call(pack_z2, "pack_z2", [(MODES, PY, LANES)], (*own, *halos)), "gz", 0)
    result = (MODES, CX, CY, CZ)
    strips, edges = strip_outs
    table, state = strip_scratch[0], strip_scratch[1]
    out, side, *strip_edges = call(
        strip_kernel2, "strips2", [result, (MODES, CX, CY, LANES), edges, edges],
        (solid_mask, *halos, *ends, *bulk), out_specs={0: HBM},
        scratch=[table, strips, strips] + [state] * 6 + [result, pltpu.SemaphoreType.DMA((4,))],
        flops=20_000_000,
    )
    return call(
        final_kernel, "final", [result],
        (solid_mask, z_in, *bulk_edges, *strip_edges, side, out), {7: HBM}, {0: HBM},
        scratch=[(MODES, CX, CY, LANES), pltpu.SemaphoreType.DMA((4,))], aliases={7: 0},
    )


def solution(mesh):
    return jax.shard_map(
        local,
        mesh=mesh,
        in_specs=(
            P(None, None, "gx", "gy", "gz"),
            P("gx", "gy", "gz"),
            P("gx", "gy", "gz"),
            P(),
            P(),
        ),
        out_specs=P(None, "gx", "gy", "gz"),
        check_vma=False,
    )
```

```python
import functools

import jax
import jax.numpy as jnp
import numpy as np
from jax import lax
from jax.experimental import pallas as pl
from jax.experimental.pallas import tpu as pltpu
from jax.sharding import PartitionSpec as P

ITERS = 4
MODES = 2
CX, CY, CZ = 8, 32, 256
W = ITERS
PX = CX + 2 * W
PY = CY + 8
NODES = CX + 1
LANES = 128

poisson = 0.3
radius_sq = 3.0
stiff_floor = 0.001
LAME = poisson / ((1.0 + poisson) * (1.0 - 2.0 * poisson))
SHEAR = 0.5 / (1.0 + poisson)

F32 = jnp.float32


def iota(shape, dim):
    return lax.broadcasted_iota(jnp.int32, shape, dim)


def pos():
    return tuple(lax.axis_index(a) for a in ("gx", "gy", "gz"))


def sub_lane():
    return iota((8, LANES), 0), iota((8, LANES), 1)


def even(axis):
    return lax.rem(lax.axis_index(axis), 2) == 0


class Pick:
    def __init__(self, cond, yes, no):
        self.cond, self.yes, self.no = cond, yes, no

    def __getitem__(self, index):
        return jnp.where(self.cond, self.yes[index], self.no[index])


def neighbours(axis, first, second):
    cond = even(axis)
    return Pick(cond, first, second), Pick(cond, second, first)


def put(axis, first, second, index, down, up):
    cond = even(axis)
    first[index] = jnp.where(cond, up, down)
    second[index] = jnp.where(cond, down, up)


def total_of(terms):
    terms = [t for t in terms if t is not None]
    while len(terms) > 1:
        pairs = [terms[i] + terms[i + 1] for i in range(0, len(terms) - 1, 2)]
        terms = pairs + ([terms[-1]] if len(terms) % 2 else [])
    return terms[0]


def scales(count, inside):
    outside = jnp.zeros(count.shape, F32)
    end = jnp.where(inside, radius_sq / (1.0 + radius_sq * (count + 1.0)), 0.0)
    mid = jnp.where(inside, radius_sq / (1.0 + radius_sq * (count + 2.0)), 0.0)
    return outside, end, mid


def yz_scales(y, z, gy, gz):
    y, z = y + gy * CY, z + gz * CZ
    inside = (y >= 0) & (y < 8 * CY)
    count = 4.0
    for place, last in ((y, 8 * CY - 1), (z, 2 * CZ - 1)):
        count = count - (place == 0).astype(F32) - (place == last).astype(F32)
    return scales(count, inside)


def kind_of(gx, plane):
    x = gx * CX + plane - W
    out = (x < 0) | (x > 8 * CX - 1)
    end = (x == 0) | (x == 8 * CX - 1)
    return jnp.where(out, 0, jnp.where(end, 1, 2))


def fill_bulk(table, gy, gz):
    shape = (CY, CZ)
    for i, part in enumerate(yz_scales(iota(shape, 0), iota(shape, 1), gy, gz)):
        table[i] = part


def fill_strips(table, gy, gz):
    shape = (16, CZ)
    row = iota(shape, 0)
    top = jnp.where(row < 4, row + CY, row + CY - 8)
    bottom = jnp.where(row < 12, row - 8, row - 16)
    for i, part in enumerate(yz_scales(jnp.where(row < 8, top, bottom), iota(shape, 1), gy, gz)):
        table[i] = part


def strip_scale(gx, gy):
    shape = (PY, LANES)
    row = iota(shape, 0)
    y = jnp.where(row < CY + W, row, row - PY) + gy * CY
    x = gx * CX - W + lax.div(iota(shape, 1), 8)
    inside = (y >= 0) & (y < 8 * CY) & (x >= 0) & (x < 8 * CX)
    count = 6.0
    for place, last in ((y, 8 * CY - 1), (x, 8 * CX - 1)):
        count = count - (place == 0).astype(F32) - (place == last).astype(F32)
    return jnp.where(inside, radius_sq / (1.0 + radius_sq * count), 0.0)


def tiles_of(ref, index, rows, cols):
    return [
        [ref[index + (slice(8 * i, 8 * i + 8), slice(LANES * j, LANES * j + LANES))] for j in range(cols)]
        for i in range(rows)
    ]


def along_lanes(row, lane):
    right = [pltpu.roll(t, 1, 1) for t in row]
    left = [pltpu.roll(t, LANES - 1, 1) for t in row]
    out = []
    for j in range(len(row)):
        before = right[j - 1] if j else 0.0
        after = left[j + 1] if j + 1 < len(row) else 0.0
        out.append(
            jnp.where(lane == 0, before, right[j]) + jnp.where(lane == LANES - 1, after, left[j])
        )
    return out


def along_rows(tiles, sub):
    rows, cols = len(tiles), len(tiles[0])
    down = [[pltpu.roll(t, 1, 0) for t in row] for row in tiles]
    up = [[pltpu.roll(t, 7, 0) for t in row] for row in tiles]
    out = []
    for i in range(rows):
        line = []
        for j in range(cols):
            before = down[i - 1][j] if i else 0.0
            after = up[i + 1][j] if i + 1 < rows else 0.0
            line.append(jnp.where(sub == 0, before, down[i][j]) + jnp.where(sub == 7, after, up[i][j]))
        out.append(line)
    return out


def turn_edge(tile, p, gz):
    return pltpu.roll(tile, lax.rem(8 * p + 5 - 2 * gz, LANES), 1)


def kind_at(gx, p):
    return 2 if W < p < PX - W - 1 else kind_of(gx, p)


def bulk_sweeps(fields, where, table, source, states, ends, edges, out):
    gx, gy, gz = where
    sub, lane = sub_lane()
    sb = states[0]
    for p in range(PX):
        kind = kind_at(gx, p)
        for m in range(fields):
            for i in range(CY // 8):
                rows = slice(8 * i, 8 * i + 8)
                sb[m, p, rows, :] = source(m, p, i) * (table[kind, rows, :] * (1.0 / radius_sq))
    for k in range(ITERS):
        old = states[0] if k == 0 else states[1 + (k - 1) % 2]
        new = states[1 + k % 2]
        for m in range(fields):
            edge = [jnp.zeros((8, LANES), F32)] * (CY // 8)
            for p in range(k + 1, PX - 1 - k):
                kind = kind_at(gx, p)
                mid = tiles_of(old, (m, p), CY // 8, 2)
                yy = along_rows(mid, sub)
                for i in range(CY // 8):
                    zz = along_lanes(mid[i], lane)
                    rows = slice(8 * i, 8 * i + 8)
                    for j in range(2):
                        cols = slice(LANES * j, LANES * j + LANES)
                        total = old[m, p - 1, rows, cols] + old[m, p + 1, rows, cols]
                        total = total + (yy[i][j] + zz[j])
                        value = sb[m, p, rows, cols] + table[kind, rows, cols] * total
                        if k + 1 < ITERS:
                            new[m, p, rows, cols] = value
                        else:
                            out[m, p - W, rows, cols] = value
                    side = jnp.where(gz == 0, mid[i][1], mid[i][0])
                    edge[i] = jnp.where(lane == 8 * p + 4 - gz, turn_edge(side, p, gz), edge[i])
                for j in range(2):
                    cols = slice(LANES * j, LANES * j + LANES)
                    ends[m, k, p, 0, 0:1, cols] = mid[CY // 8 - 1][j][7:8]
                    ends[m, k, p, 1, 0:1, cols] = mid[0][j][0:1]
            for i in range(CY // 8):
                edges[m, k, 8 * i : 8 * i + 8, :] = edge[i]


def strip_sweeps(fields, where, table, source, ends, states, edges, out):
    gx, gy, gz = where
    sub, lane = sub_lane()
    sb = states[0]
    wide = iota((8, CZ), 0)
    for p in range(PX):
        kind = kind_at(gx, p)
        for m in range(fields):
            halo = source(m, p) * (1.0 / radius_sq)
            sb[m, p, 0:8, :] = jnp.where(wide < 4, halo * table[kind, 0:8, :], 0.0)
            sb[m, p, 8:16, :] = jnp.where(wide < 4, 0.0, halo * table[kind, 8:16, :])
    for k in range(ITERS):
        old = states[0] if k == 0 else states[1 + (k - 1) % 2]
        new = states[1 + k % 2]
        for m in range(fields):
            edge = [jnp.zeros((8, LANES), F32)] * 2
            for p in range(k + 1, PX - 1 - k):
                kind = kind_at(gx, p)
                mid = tiles_of(old, (m, p), 2, 2)
                for i in range(2):
                    rows = slice(8 * i, 8 * i + 8)
                    zz = along_lanes(mid[i], lane)
                    for j in range(2):
                        cols = slice(LANES * j, LANES * j + LANES)
                        end = jnp.broadcast_to(ends[m, k, p, i, 0:1, cols], (8, LANES))
                        down = pltpu.roll(mid[i][j], 1, 0)
                        up = pltpu.roll(mid[i][j], 7, 0)
                        if i == 0:
                            down = jnp.where(sub == 4, 0.0, down) + jnp.where(sub == 0, end, 0.0)
                        else:
                            up = jnp.where(sub == 3, 0.0, up) + jnp.where(sub == 7, end, 0.0)
                        total = old[m, p - 1, rows, cols] + old[m, p + 1, rows, cols]
                        total = total + (down + up) + zz[j]
                        value = sb[m, p, rows, cols] + table[kind, rows, cols] * total
                        if k + 1 < ITERS:
                            new[m, p, rows, cols] = value
                        else:
                            out[m, p - W, rows, cols] = value
                    side = jnp.where(gz == 0, mid[i][1], mid[i][0])
                    edge[i] = jnp.where(lane == 8 * p + 4 - gz, turn_edge(side, p, gz), edge[i])
            for i in range(2):
                edges[m, k, 8 * i : 8 * i + 8, :] = edge[i]


def z_sweeps(m, scale, halo, bulk_edges, strip_edges):
    sub = iota((8, LANES), 0)
    column = lax.rem(iota((PY, LANES), 1), 8)
    base = halo * (scale * (1.0 / radius_sq))
    state = base
    for k in range(ITERS):
        top, bottom = strip_edges[m, k, 0:8, :], strip_edges[m, k, 8:16, :]
        own = bulk_edges[m, k]
        fed = jnp.concatenate(
            [
                own[0:8] + jnp.where(sub < 4, bottom, 0.0),
                own[8 : CY - 8],
                own[CY - 8 : CY] + jnp.where(sub < 4, 0.0, top),
                jnp.where(sub < 4, top, bottom),
            ],
            axis=0,
        )
        total = pltpu.roll(state, 8, 1) + pltpu.roll(state, LANES - 8, 1)
        total = total + pltpu.roll(state, 1, 0) + pltpu.roll(state, PY - 1, 0)
        total = total + jnp.where(column == 0, 0.0, pltpu.roll(state, 1, 1))
        total = total + jnp.where(column == 7, 0.0, pltpu.roll(state, LANES - 1, 1))
        state = base + scale * (total + fed)
    return state


def pair_tile(m, x, i, j, bulk, strips, sub):
    rows, cols = slice(8 * i, 8 * i + 8), slice(LANES * j, LANES * j + LANES)
    value = bulk[m, x, rows, cols]
    if i == 0:
        value = value + jnp.where(sub < 4, strips[m, x, 8:16, cols], 0.0)
    if i == CY // 8 - 1:
        value = value + jnp.where(sub < 4, 0.0, strips[m, x, 0:8, cols])
    return value


def z_tile(z_state, x, i):
    return pltpu.roll(z_state[8 * i : 8 * i + 8], (LANES - 4 - 8 * (x + W)) % LANES, 1)


def beside_halo(gz, lane):
    return (lane < 4 * gz), (lane >= LANES - 4 * (1 - gz))


def pack_strip(gz, tile, p, acc, lane):
    first = 8 * p + 4 * gz
    turned = pltpu.roll(tile, (8 * p + 4) % LANES, 1)
    return jnp.where((lane >= first) & (lane < first + 4), turned, acc)


def own_strip(gz, load, rows=CY):
    lane = iota((rows, LANES), 1)
    acc = jnp.zeros((rows, LANES), F32)
    for p in range(PX):
        acc = pack_strip(gz, load(p), p, acc, lane)
    return acc


def edge_tiles(gz):
    return pl.ds(pl.multiple_of((1 - gz) * LANES, LANES), LANES)


def energy_terms(prev, cur):
    (paa, pad, pda, pdd), (caa, cad, cda, cdd) = prev, cur
    u, v, w = 0, 1, 2
    aad = [cad[i] + pad[i] for i in range(3)]
    ada = [cda[i] + pda[i] for i in range(3)]
    add = [cdd[i] + pdd[i] for i in range(3)]
    daa = [caa[i] - paa[i] for i in range(3)]
    dad = [cad[i] - pad[i] for i in range(3)]
    dda = [cda[i] - pda[i] for i in range(3)]
    ddd = [cdd[i] - pdd[i] for i in range(3)]

    def sq(x):
        return x * x

    trace = sq(daa[u] + ada[v] + aad[w])
    lines = sq(dda[v] + dad[w]) + sq(dda[u] + add[w]) + sq(dad[u] + add[v])
    diag = sq(daa[u]) + sq(ada[v]) + sq(aad[w])
    shear = sq(ada[u] + daa[v]) + sq(aad[u] + daa[w]) + sq(aad[v] + ada[w])
    mixed = sq(dda[u]) + sq(dda[v]) + sq(dad[u]) + sq(dad[w]) + sq(add[v]) + sq(add[w])
    cross = sq(add[u] + dad[v]) + sq(add[u] + dda[w]) + sq(dad[v] + dda[w])
    cubic = sq(ddd[u]) + sq(ddd[v]) + sq(ddd[w])
    return (
        LAME * (trace + lines * (1.0 / 3.0))
        + SHEAR * (2.0 * diag + shear + mixed + cross * (1.0 / 3.0))
        + ((LAME + 4.0 * SHEAR) / 9.0) * cubic
    )


def y_parts(pairs):
    aa = [a0 + a1 for a0, d0, a1, d1 in pairs]
    ad = [d0 + d1 for a0, d0, a1, d1 in pairs]
    da = [a1 - a0 for a0, d0, a1, d1 in pairs]
    dd = [d1 - d0 for a0, d0, a1, d1 in pairs]
    return aa, ad, da, dd


def mass_of(parts):
    return total_of([x * x for part in parts for x in part])


def z_pair(here):
    after = pltpu.roll(here, CZ - 1, 1)
    return here + after, after - here


def own_parts(load, chunk):
    sub = iota((8, CZ), 0)
    pairs = []
    for c in range(3):
        a0, d0 = z_pair(load(c, 8 * chunk))
        following = min(chunk + 1, CY // 8 - 1)
        a1, d1 = z_pair(load(c, 8 * following))

        def next_row(t, n):
            return jnp.where(sub == 7, pltpu.roll(n, 7, 0), pltpu.roll(t, 7, 0))

        pairs.append((a0, d0, next_row(a0, a1), next_row(d0, d1)))
    return y_parts(pairs)


def pack_columns(load, lane):
    first = jnp.zeros((CY, LANES), F32)
    last = first
    for m in range(MODES):
        for c in range(3):
            for x in range(CX):
                to = 32 * m + NODES * c + x
                here = lane == to
                first = jnp.where(here, pltpu.roll(load(m, c, x, 0), to, 1), first)
                last = jnp.where(here, pltpu.roll(load(m, c, x, 1), to + 1, 1), last)
    return first, last


def with_plane8(packed, above, keep_x, last):
    cols = slice(CZ - LANES, CZ) if last else slice(0, LANES)
    rows = packed.shape[0]
    lane = iota(packed.shape, 1)
    for m in range(MODES):
        for c in range(3):
            to = 32 * m + NODES * c + CX
            turned = pltpu.roll(above[W + 3 * m + c, 0:rows, cols], to + last, 1)
            packed = jnp.where(lane == to, turned * keep_x, packed)
    return packed


def row32_of(y_above, last):
    cols = slice(CZ - LANES, CZ) if last else slice(0, LANES)
    sub, lane = sub_lane()
    tile = jnp.zeros((8, LANES), F32)
    for m in range(MODES):
        for c in range(3):
            for x in range(CX):
                to = 32 * m + NODES * c + x
                row = jnp.broadcast_to(y_above[W + 3 * m + c, x : x + 1, cols], (8, LANES))
                tile = jnp.where(lane == to, pltpu.roll(row, to + last, 1), tile)
    return jnp.where(sub == 0, tile, 0.0)


def with_row32(packed, row, from_above, keep_x, keep_y, last):
    cols = slice(CZ - LANES, CZ) if last else slice(0, LANES)
    sub, lane = sub_lane()
    for m in range(MODES):
        for c in range(3):
            to = 32 * m + NODES * c + CX
            n = 3 * m + c
            corner = jnp.broadcast_to(from_above[W - 1, n : n + 1, cols] * keep_x, (8, LANES))
            row = jnp.where((lane == to) & (sub == 0), pltpu.roll(corner, to + last, 1), row)
    return jnp.concatenate([packed, row * keep_y], axis=0)


def pack_x1(
    design, mask, modes, eigenvalues, order, src, first, second, lams, field, solid, rim, values, chosen, arrived
):
    copies = []
    for half in (slice(0, W), slice(W, CX)):
        copies.append((design.at[half], field.at[half]))
        copies.append((mask.at[half], solid.at[half]))
    for m in range(MODES):
        copies.append((modes.at[m, :, 0], rim.at[3 * m : 3 * m + 3]))
    copies += [(eigenvalues, values), (order, chosen)]
    copies = [pltpu.make_async_copy(a, b, arrived.at[n]) for n, (a, b) in enumerate(copies)]
    for copy in copies:
        copy.start()
    for copy in copies[:4]:
        copy.wait()
    for x in range(W):
        low, high = (field[p] * solid[p].astype(F32) for p in (x, x + W))
        src[x], src[x + W] = low, high
        put("gx", first, second, x, low, high)
    for copy in copies[4:]:
        copy.wait()
    first[W : W + 6] = rim[...]
    second[W : W + 6] = rim[...]
    for m in range(MODES):
        lams[m] = jnp.full((8, LANES), values[chosen[m]] * (0.125 * 0.25), F32)


def energy_kernel(modes, stiff, mass, columns):
    lane = iota((CY, LANES), 1)
    columns[0], columns[1] = pack_columns(
        lambda m, c, x, j: modes[m, c, x, :, LANES * j : LANES * j + LANES], lane
    )

    def mode_step(m, carry):
        for chunk in range(CY // 8):
            rows = slice(8 * chunk, 8 * chunk + 8)
            prev = prev_mass = None
            for x in range(CX):
                cur = own_parts(lambda c, r: modes[m, c, x, r : r + 8, :], chunk)
                cur_mass = mass_of(cur)
                if x:
                    stiff[m, x - 1, rows, :] = energy_terms(prev, cur)
                    mass[m, x - 1, rows, :] = cur_mass + prev_mass
                prev, prev_mass = cur, cur_mass
        return carry

    lax.fori_loop(0, MODES, mode_step, 0)


def pick_plane(own, above, below, p):
    if p < W:
        return below, p
    if p < W + CX:
        return own, p - W
    return above, p - W - CX


def pack_y1(src, modes, first, second):
    low = iota((8, CZ), 0) < 4
    for q in range(W):
        down = jnp.where(low, src[q, 0:8, :], pltpu.roll(src[q + W, 0:8, :], 4, 0))
        up = jnp.where(low, pltpu.roll(src[q + W, 24:32, :], 4, 0), src[q, 24:32, :])
        put("gy", first, second, q, down, up)
    for m in range(MODES):
        for c in range(3):
            for x in range(CX):
                for out in (first, second):
                    out[W + 3 * m + c, x : x + 1, :] = modes[m, c, x, 0:1, :]


def own_halo(y_above, y_below, x, lanes=slice(None)):
    a, b = y_above[x % W, :, lanes], y_below[x % W, :, lanes]
    if x >= W:
        a, b = pltpu.roll(a, 4, 0), pltpu.roll(b, 4, 0)
    return jnp.where(iota(a.shape, 0) < 4, a, b)


def pack_e1(y_first, y_second, ahead, first, second):
    y_above, y_below = neighbours("gy", y_first, y_second)
    for i in range(W - 1):
        down, up = (own_halo(y_above, y_below, x) for x in (i, CX - 1 - i))
        put("gx", first, second, i, down, up)
    for out in (first, second):
        out[W - 1] = jnp.zeros((8, CZ), F32)
        for n in range(3 * MODES):
            out[W - 1, n : n + 1, :] = y_above[W + n, 0:1, :]


def halo_tile(y_above, y_below, from_above, from_below, p, lanes=slice(None)):
    if W <= p < W + CX:
        return own_halo(y_above, y_below, p - W, lanes)
    if 0 < p < W:
        return from_below[W - 1 - p, :, lanes]
    if W + CX <= p < PX - 1:
        return from_above[p - W - CX, :, lanes]
    return jnp.zeros(y_above[0, :, lanes].shape, F32)


def bulk_kernel1(
    src, modes, columns, x_first, x_second, y_first, y_second,
    bulk, ends, edges, stiff, mass, own, rims, row32, table, sb, one, two,
):
    above, below = neighbours("gx", x_first, x_second)
    y_above, y_below = neighbours("gy", y_first, y_second)
    at = pos()
    gx, gy, gz = at
    fill_bulk(table, gy, gz)

    def source(m, p, i):
        a, at_plane = pick_plane(src, above, below, p)
        return a[at_plane, 8 * i : 8 * i + 8, :]

    bulk_sweeps(1, at, table, source, (sb, one, two), ends, edges, bulk)
    edge = edge_tiles(gz)
    own[0] = own_strip(gz, lambda p: plane_edge(src, above, below, p, edge))
    keep = jnp.where(gx < 7, 1.0, 0.0)
    for last in range(2):
        rims[last] = with_plane8(columns[last], above, keep, last)
        row32[last] = row32_of(y_above, last)
    for m in range(MODES):
        for chunk in range(CY // 8):
            rows = slice(8 * chunk, 8 * chunk + 8)
            prev = own_parts(lambda c, r: modes[m, c, CX - 1, r : r + 8, :], chunk)
            cur = own_parts(lambda c, r: above[W + 3 * m + c, r : r + 8, :] * keep, chunk)
            stiff[m, rows, :] = energy_terms(prev, cur)
            mass[m, rows, :] = mass_of(cur) + mass_of(prev)


def plane_edge(own, above, below, p, edge):
    a, i = pick_plane(own, above, below, p)
    return a[i, :, edge]


def pack_z1(own, rims, row32, y_first, y_second, e_first, e_second, out):
    gx, gy, gz = pos()
    edge = edge_tiles(gz)
    halos = (*neighbours("gy", y_first, y_second), *neighbours("gx", e_first, e_second))
    from_above = halos[2]
    out[0, 0:CY, :] = own[0]
    out[0, CY:PY, :] = own_strip(gz, lambda p: halo_tile(*halos, p, edge), 8)
    keep_x = jnp.where(gx < 7, 1.0, 0.0)
    keep_y = jnp.where(gy < 7, 1.0, 0.0)
    out[1] = with_row32(rims[0], row32[0], from_above, keep_x, keep_y, 0)


def strip_kernel1(
    modes, rims, row32, x_first, x_second, y_first, y_second, e_first, e_second, ends,
    strips, edges, rim, packed, table, sb, one, two, near, far,
):
    at = pos()
    gx, gy, gz = at
    fill_strips(table, gy, gz)
    halos = (*neighbours("gy", y_first, y_second), *neighbours("gx", e_first, e_second))
    y_above, y_below, from_above, from_below = halos
    above, below = neighbours("gx", x_first, x_second)
    strip_sweeps(
        1, at, table, lambda m, p: halo_tile(*halos, p), ends, (sb, one, two), edges, strips
    )
    keep_x = jnp.where(gx < 7, 1.0, 0.0)
    keep_y = jnp.where(gy < 7, 1.0, 0.0)
    packed[...] = with_row32(rims[1], row32[1], from_above, keep_x, keep_y, 1)
    for m in range(MODES):
        for c in range(3):
            n = 3 * m + c
            for x in range(CX):
                near[c, x : x + 1, :] = modes[m, c, x, CY - 1 : CY, :]
            near[c, CX : CX + 1, :] = above[W + n, CY - 1 : CY, :] * keep_x
            far[c, 0:CX, :] = y_above[W + n] * keep_y
            far[c, CX : CX + 1, :] = from_above[W - 1, n : n + 1, :] * (keep_x * keep_y)

        def parts(first):
            pairs = []
            for c in range(3):
                a0, d0 = z_pair(near[c, first : first + 8, :])
                a1, d1 = z_pair(far[c, first : first + 8, :])
                pairs.append((a0, d0, a1, d1))
            return y_parts(pairs)

        prev, cur = parts(0), parts(1)
        rim[m, 0] = energy_terms(prev, cur)
        rim[m, 1] = mass_of(cur) + mass_of(prev)


def raw_planes(
    planes, lams, gz, z_state, column_stiff, column_mass, bulk, strips,
    stiff, mass, stiff7, mass7, rim, store,
):
    sub, lane = sub_lane()
    beside = beside_halo(gz, lane)
    factor = 3.0 * (1.0 - stiff_floor) / 16.0
    for x in planes:
        for i in range(CY // 8):
            rows = slice(8 * i, 8 * i + 8)
            correction = z_tile(z_state, x, i)
            for j in range(2):
                cols = slice(LANES * j, LANES * j + LANES)
                phys = pair_tile(0, x, i, j, bulk, strips, sub) + jnp.where(beside[j], correction, 0.0)
                phys = (factor * phys) * phys
                for m in range(MODES):
                    if x < CX - 1:
                        k, e = stiff[m, x, rows, cols], mass[m, x, rows, cols]
                    else:
                        k, e = stiff7[m, rows, cols], mass7[m, rows, cols]
                    if i == CY // 8 - 1:
                        k = jnp.where(sub == 7, jnp.broadcast_to(rim[m, 0, x : x + 1, cols], (8, LANES)), k)
                        e = jnp.where(sub == 7, jnp.broadcast_to(rim[m, 1, x : x + 1, cols], (8, LANES)), e)
                    if j == 1:
                        by = LANES - 1 - (32 * m + x)
                        k = jnp.where(lane == LANES - 1, pltpu.roll(column_stiff[rows, :], by, 1), k)
                        e = jnp.where(lane == LANES - 1, pltpu.roll(column_mass[rows, :], by, 1), e)
                    store((x % W, m, rows, cols), phys * k - lams[m] * e)


def raw_kernel1(
    lams, z_in, packed, bulk, bulk_edges, strips, strip_edges,
    stiff, mass, stiff7, mass7, rim, low, z_parts,
):
    gx, gy, gz = pos()
    z_state = z_sweeps(0, strip_scale(gx, gy), z_in[0], bulk_edges, strip_edges)

    near, far = packed[...], z_in[1] * jnp.where(gz < 1, 1.0, 0.0)
    a0, d0 = near + far, far - near
    a1, d1 = pltpu.roll(a0, PY - 1, 0), pltpu.roll(d0, PY - 1, 0)
    parts = [(x[0][0:CY]) for x in y_parts([(a0, d0, a1, d1)])]

    def turned(t, by):
        return pltpu.roll(t, (LANES - by) % LANES, 1) if by else t

    prev = [[turned(t, NODES * c) for c in range(3)] for t in parts]
    cur = [[turned(t, NODES * c + 1) for c in range(3)] for t in parts]
    column_stiff = energy_terms(prev, cur)
    column_mass = mass_of(cur) + mass_of(prev)
    z_parts[0], z_parts[1], z_parts[2] = z_state[0:CY], column_stiff, column_mass
    raw_planes(
        range(W), lams, gz, z_state, column_stiff, column_mass, bulk, strips,
        stiff, mass, stiff7, mass7, rim, low.__setitem__,
    )


def raw_kernel2(
    lams, z_parts, bulk, strips, stiff, mass, stiff7, mass7, rim, low, high, first, second
):
    gx, gy, gz = pos()

    def store(index, value):
        high[index] = value
        put("gx", first, second, index, low[index], value)

    raw_planes(
        range(W, CX), lams, gz, z_parts[0], z_parts.at[1], z_parts.at[2], bulk, strips,
        stiff, mass, stiff7, mass7, rim, store,
    )


def raw_plane(low, high, above, below, p):
    if p < W:
        return below, p
    if p < 2 * W:
        return low, p - W
    if p < 3 * W:
        return high, p - 2 * W
    return above, p - 3 * W


def pack_y2(low, high, first, second):
    top = iota((8, CZ), 0) < 4
    for x in range(CX):
        a, i = (low, x) if x < W else (high, x - W)
        down = jnp.where(top, a[i, 0, 0:8, :], pltpu.roll(a[i, 1, 0:8, :], 4, 0))
        up = jnp.where(top, pltpu.roll(a[i, 0, 24:32, :], 4, 0), a[i, 1, 24:32, :])
        put("gy", first, second, x, down, up)


def own_raw_halo(y_above, y_below, m, x, lanes=slice(None)):
    a, b = y_above[x, :, lanes], y_below[x, :, lanes]
    if m == 0:
        b = pltpu.roll(b, 4, 0)
    else:
        a = pltpu.roll(a, 4, 0)
    return jnp.where(iota(a.shape, 0) < 4, a, b)


def pack_e2(y_first, y_second, ahead, first, second):
    y_above, y_below = neighbours("gy", y_first, y_second)
    for i in range(W - 1):
        for m in range(MODES):
            down, up = (own_raw_halo(y_above, y_below, m, x) for x in (i, CX - 1 - i))
            put("gx", first, second, MODES * i + m, down, up)


def raw_halo(y_above, y_below, from_above, from_below, m, p, lanes=slice(None)):
    if W <= p < W + CX:
        return own_raw_halo(y_above, y_below, m, p - W, lanes)
    if 0 < p < W:
        return from_below[MODES * (W - 1 - p) + m, :, lanes]
    if W + CX <= p < PX - 1:
        return from_above[MODES * (p - W - CX) + m, :, lanes]
    return jnp.zeros(y_above[0, :, lanes].shape, F32)


def bulk_kernel2(m, low, high, x_first, x_second, bulk, ends, edges, own, table, sb, one, two):
    above, below = neighbours("gx", x_first, x_second)
    at = pos()
    fill_bulk(table, at[1], at[2])

    def source(_, p, i):
        a, at_plane = raw_plane(low, high, above, below, p)
        return a[at_plane, m, 8 * i : 8 * i + 8, :]

    bulk_sweeps(1, at, table, source, (sb, one, two), ends, edges, bulk)
    edge = edge_tiles(at[2])

    def load(p):
        a, i = raw_plane(low, high, above, below, p)
        return a[i, m, :, edge]

    own[0] = own_strip(at[2], load)


def pack_z2(own0, own1, y_first, y_second, e_first, e_second, out):
    gx, gy, gz = pos()
    edge = edge_tiles(gz)
    halos = (*neighbours("gy", y_first, y_second), *neighbours("gx", e_first, e_second))
    for m, own in enumerate((own0, own1)):
        out[m, 0:CY, :] = own[0]
        out[m, CY:PY, :] = own_strip(gz, lambda p, m=m: raw_halo(*halos, m, p, edge), 8)


def strip_kernel2(
    mask, y_first, y_second, e_first, e_second, ends0, ends1, bulk0, bulk1,
    out, side, edges0, edges1, table, strips0, strips1, a0, a1, b0, b1, c0, c1, held, left,
):
    gx, gy, gz = at = pos()
    halos = (*neighbours("gy", y_first, y_second), *neighbours("gx", e_first, e_second))
    sub, lane = sub_lane()
    fill_strips(table, gy, gz)
    states = ((a0, b0, c0), (a1, b1, c1))
    copies = []
    for m in range(MODES):
        ends, bulk, edges = (ends0, ends1)[m], (bulk0, bulk1)[m], (edges0, edges1)[m]
        strips = (strips0, strips1)[m]

        def source(_, p, m=m):
            return raw_halo(*halos, m, p)

        strip_sweeps(1, at, table, source, ends, states[m], edges, strips)
        for x in range(CX):
            for i in range(CY // 8):
                rows = slice(8 * i, 8 * i + 8)
                pair = []
                for j in range(2):
                    cols = slice(LANES * j, LANES * j + LANES)
                    value = pair_tile(0, x, i, j, bulk, strips, sub)
                    held[m, x, rows, cols] = value * mask[x, rows, cols].astype(F32)
                    pair.append(value)
                side[m, x, rows, :] = jnp.where(gz == 0, pair[1], pair[0])
            if x % 4 == 3:
                part = (m, slice(x - 3, x + 1))
                copy = pltpu.make_async_copy(held.at[part], out.at[part], left.at[len(copies)])
                copy.start()
                copies.append(copy)
    for copy in copies:
        copy.wait()


def final_kernel(mask, z_in, bulk_edges0, bulk_edges1, strip_edges0, strip_edges1, side, given, out, held, left):
    gx, gy, gz = pos()
    sub, lane = sub_lane()
    at_end = beside_halo(gz, lane)
    beside = at_end[0] | at_end[1]
    edge = edge_tiles(gz)
    scale = strip_scale(gx, gy)
    copies = []
    for m in range(MODES):
        edges = ((bulk_edges0, strip_edges0), (bulk_edges1, strip_edges1))[m]
        z_state = z_sweeps(0, scale, z_in[m], *edges)
        for x in range(CX):
            for i in range(CY // 8):
                rows = slice(8 * i, 8 * i + 8)
                value = side[m, x, rows, :] + jnp.where(beside, z_tile(z_state, x, i), 0.0)
                held[m, x, rows, :] = value * mask[x, rows, edge].astype(F32)
            if x % 4 == 3:
                planes = slice(x - 3, x + 1)
                copy = pltpu.make_async_copy(
                    held.at[m, planes], out.at[m, planes, :, edge], left.at[len(copies)]
                )
                copy.start()
                copies.append(copy)
    for copy in copies:
        copy.wait()


def whole(x):
    return pl.BlockSpec(x.shape, lambda i: (0,) * x.ndim)


def call(kernel, name, outs, args, specs=None, out_specs=None, scratch=(), flops=0, aliases=None):
    specs = specs or {}
    shapes = tuple(jax.ShapeDtypeStruct(s, F32) for s in outs)
    out_specs = out_specs or {}
    out_specs = tuple(out_specs.get(i, whole(s)) for i, s in enumerate(shapes))
    return pl.pallas_call(
        kernel,
        grid=(1,),
        out_shape=shapes if len(shapes) > 1 else shapes[0],
        in_specs=[specs.get(i, whole(a)) for i, a in enumerate(args)],
        scratch_shapes=[pltpu.VMEM(s, F32) if isinstance(s, tuple) else s for s in scratch],
        compiler_params=pltpu.CompilerParams(vmem_limit_bytes=24 * 1024 * 1024),
        cost_estimate=pl.CostEstimate(flops=flops, bytes_accessed=2_000_000, transcendentals=0),
        name=name,
        out_specs=out_specs if len(shapes) > 1 else out_specs[0],
        input_output_aliases=aliases or {},
    )(*args)


HBM = pl.BlockSpec(memory_space=pltpu.HBM)


AXES = ("gx", "gy", "gz")
BESIDE = {"gx": "gz", "gy": "gx"}


def swap(x, axis, start):
    sizes = [lax.axis_size(a) for a in AXES]
    pairs = []
    for place in np.ndindex(*sizes):
        other = list(place)
        at = AXES.index(axis)
        other[at] += 1 if place[at] % 2 == start else -1
        if not 0 <= other[at] < sizes[at]:
            other = list(place)
            other[AXES.index(BESIDE[axis])] ^= 1
        pairs.append(tuple(int(np.ravel_multi_index(p, sizes)) for p in (place, other)))
    return lax.ppermute(x, AXES, pairs)


def swaps(axis, pair):
    second = swap(pair[1], axis, 1)
    return swap(pair[0], axis, 0), second


def sweep_outs(fields):
    return (
        [(fields, CX, CY, CZ), (fields, ITERS, PX, 2, 1, CZ), (fields, ITERS, CY, LANES)],
        [(3, CY, CZ)] + [(fields, PX, CY, CZ)] * 3,
        [(fields, CX, 16, CZ), (fields, ITERS, 16, LANES)],
        [(3, 16, CZ)] + [(fields, PX, 16, CZ)] * 3,
    )


def local(mode_fields, design, solid_mask, eigenvalues, mode_order):
    bulk_outs, bulk_scratch, strip_outs, strip_scratch = sweep_outs(1)

    inputs = (design, solid_mask, mode_fields, eigenvalues, mode_order)
    src, first, second, lams = call(
        pack_x1, "pack_x1", [(CX, CY, CZ), (W + 6, CY, CZ), (W + 6, CY, CZ), (MODES, 8, LANES)],
        tuple(pltpu.with_memory_space_constraint(x, pltpu.HBM) for x in inputs),
        {i: HBM for i in range(5)},
        scratch=[
            (CX, CY, CZ), pltpu.VMEM((CX, CY, CZ), jnp.int32), (6, CY, CZ), pltpu.SMEM((eigenvalues.size,), F32),
            pltpu.SMEM((mode_order.size,), jnp.int32), pltpu.SemaphoreType.DMA((8,)),
        ],
    )
    x_pair = swaps("gx", (first, second))
    field = (MODES, CX - 1, CY, CZ)
    y_pair = swaps("gy", call(pack_y1, "pack_y1", [(W + 6, 8, CZ)] * 2, (src, mode_fields)))
    stiff, mass, columns = call(
        energy_kernel, "energy", [field, field, (2, CY, LANES)], (mode_fields,), flops=40_000_000
    )

    edge_pair = swaps("gx", call(pack_e1, "pack_e1", [(W, 8, CZ)] * 2, (*y_pair, columns)))
    halos = (*y_pair, *edge_pair)
    plane = (MODES, CY, CZ)
    bulk, ends, bulk_edges, stiff7, mass7, own, rims, row32 = call(
        bulk_kernel1, "bulk1",
        bulk_outs + [plane, plane, (1, CY, LANES), (2, CY, LANES), (2, 8, LANES)],
        (src, mode_fields, columns, *x_pair, *y_pair), scratch=bulk_scratch, flops=30_000_000,
    )

    z_in = swap(call(pack_z1, "pack_z1", [(2, PY, LANES)], (own, rims, row32, *halos)), "gz", 0)
    strips, strip_edges, rim, packed = call(
        strip_kernel1, "strips1", strip_outs + [(MODES, 2, 8, CZ), (PY, LANES)],
        (mode_fields, rims, row32, *x_pair, *halos, ends),
        scratch=strip_scratch + [(3, 16, CZ)] * 2, flops=20_000_000,
    )
    half = (W, MODES, CY, CZ)
    energies = (stiff, mass, stiff7, mass7, rim)
    low, z_parts = call(
        raw_kernel1, "raw1", [half, (3, CY, LANES)],
        (lams, z_in, packed, bulk, bulk_edges, strips, strip_edges, *energies),
    )
    high, first, second = call(
        raw_kernel2, "raw2", [half] * 3, (lams, z_parts, bulk, strips, *energies, low), flops=5_000_000
    )
    planes = (low, high, *swaps("gx", (first, second)))
    y_pair = swaps("gy", call(pack_y2, "pack_y2", [(CX, 8, CZ)] * 2, (low, high)))
    bulks = [
        call(
            functools.partial(bulk_kernel2, m), f"bulk2_{m}", bulk_outs + [(1, CY, LANES)], planes,
            scratch=bulk_scratch, flops=20_000_000,
        )
        for m in range(MODES)
    ]
    bulk, ends, bulk_edges, own = zip(*bulks)
    edge = (MODES * (W - 1), 8, CZ)
    halos = (*y_pair, *swaps("gx", call(pack_e2, "pack_e2", [edge] * 2, (*y_pair, own[0]))))
    z_in = swap(call(pack_z2, "pack_z2", [(MODES, PY, LANES)], (*own, *halos)), "gz", 0)
    result = (MODES, CX, CY, CZ)
    strips, edges = strip_outs
    table, state = strip_scratch[0], strip_scratch[1]
    out, side, *strip_edges = call(
        strip_kernel2, "strips2", [result, (MODES, CX, CY, LANES), edges, edges],
        (solid_mask, *halos, *ends, *bulk), out_specs={0: HBM},
        scratch=[table, strips, strips] + [state] * 6 + [result, pltpu.SemaphoreType.DMA((4,))],
        flops=20_000_000,
    )
    return call(
        final_kernel, "final", [result],
        (solid_mask, z_in, *bulk_edges, *strip_edges, side, out), {7: HBM}, {0: HBM},
        scratch=[(MODES, CX, CY, LANES), pltpu.SemaphoreType.DMA((4,))], aliases={7: 0},
    )


def solution(mesh):
    return jax.shard_map(
        local,
        mesh=mesh,
        in_specs=(
            P(None, None, "gx", "gy", "gz"),
            P("gx", "gy", "gz"),
            P("gx", "gy", "gz"),
            P(),
            P(),
        ),
        out_specs=P(None, "gx", "gy", "gz"),
        check_vma=False,
    )
```

```python
import functools

import jax
import jax.numpy as jnp
import numpy as np
from jax import lax
from jax.experimental import pallas as pl
from jax.experimental.pallas import tpu as pltpu
from jax.sharding import PartitionSpec as P

ITERS = 4
MODES = 2
CX, CY, CZ = 8, 32, 256
W = ITERS
PX = CX + 2 * W
PY = CY + 8
NODES = CX + 1
LANES = 128

poisson = 0.3
radius_sq = 3.0
stiff_floor = 0.001
LAME = poisson / ((1.0 + poisson) * (1.0 - 2.0 * poisson))
SHEAR = 0.5 / (1.0 + poisson)

F32 = jnp.float32


def iota(shape, dim):
    return lax.broadcasted_iota(jnp.int32, shape, dim)


def pos():
    return tuple(lax.axis_index(a) for a in ("gx", "gy", "gz"))


def sub_lane():
    return iota((8, LANES), 0), iota((8, LANES), 1)


def odd(axis):
    return lax.rem(lax.axis_index(axis), 2) == 1


class Pick:
    def __init__(self, cond, yes, no):
        self.cond, self.yes, self.no = cond, yes, no

    def __getitem__(self, index):
        return jnp.where(self.cond, self.yes[index], self.no[index])


def neighbours(axis, first, second):
    cond = odd(axis)
    return Pick(cond, first, second), Pick(cond, second, first)


def put(axis, first, second, index, down, up):
    cond = odd(axis)
    first[index] = jnp.where(cond, up, down)
    second[index] = jnp.where(cond, down, up)


def total_of(terms):
    terms = [t for t in terms if t is not None]
    while len(terms) > 1:
        pairs = [terms[i] + terms[i + 1] for i in range(0, len(terms) - 1, 2)]
        terms = pairs + ([terms[-1]] if len(terms) % 2 else [])
    return terms[0]


def scales(count, inside):
    outside = jnp.zeros(count.shape, F32)
    end = jnp.where(inside, radius_sq / (1.0 + radius_sq * (count + 1.0)), 0.0)
    mid = jnp.where(inside, radius_sq / (1.0 + radius_sq * (count + 2.0)), 0.0)
    return outside, end, mid


def yz_scales(y, z, gy, gz):
    y, z = y + gy * CY, z + gz * CZ
    inside = (y >= 0) & (y < 8 * CY)
    count = 4.0
    for place, last in ((y, 8 * CY - 1), (z, 2 * CZ - 1)):
        count = count - (place == 0).astype(F32) - (place == last).astype(F32)
    return scales(count, inside)


def kind_of(gx, plane):
    x = gx * CX + plane - W
    out = (x < 0) | (x > 8 * CX - 1)
    end = (x == 0) | (x == 8 * CX - 1)
    return jnp.where(out, 0, jnp.where(end, 1, 2))


def fill_bulk(table, gy, gz):
    shape = (CY, CZ)
    for i, part in enumerate(yz_scales(iota(shape, 0), iota(shape, 1), gy, gz)):
        table[i] = part


def fill_strips(table, gy, gz):
    shape = (16, CZ)
    row = iota(shape, 0)
    top = jnp.where(row < 4, row + CY, row + CY - 8)
    bottom = jnp.where(row < 12, row - 8, row - 16)
    for i, part in enumerate(yz_scales(jnp.where(row < 8, top, bottom), iota(shape, 1), gy, gz)):
        table[i] = part


def strip_scale(gx, gy):
    shape = (PY, LANES)
    row = iota(shape, 0)
    y = jnp.where(row < CY + W, row, row - PY) + gy * CY
    x = gx * CX - W + lax.div(iota(shape, 1), 8)
    inside = (y >= 0) & (y < 8 * CY) & (x >= 0) & (x < 8 * CX)
    count = 6.0
    for place, last in ((y, 8 * CY - 1), (x, 8 * CX - 1)):
        count = count - (place == 0).astype(F32) - (place == last).astype(F32)
    return jnp.where(inside, radius_sq / (1.0 + radius_sq * count), 0.0)


def tiles_of(ref, index, rows, cols):
    return [
        [ref[index + (slice(8 * i, 8 * i + 8), slice(LANES * j, LANES * j + LANES))] for j in range(cols)]
        for i in range(rows)
    ]


def along_lanes(row, lane):
    right = [pltpu.roll(t, 1, 1) for t in row]
    left = [pltpu.roll(t, LANES - 1, 1) for t in row]
    out = []
    for j in range(len(row)):
        before = right[j - 1] if j else 0.0
        after = left[j + 1] if j + 1 < len(row) else 0.0
        out.append(
            jnp.where(lane == 0, before, right[j]) + jnp.where(lane == LANES - 1, after, left[j])
        )
    return out


def along_rows(tiles, sub):
    rows, cols = len(tiles), len(tiles[0])
    down = [[pltpu.roll(t, 1, 0) for t in row] for row in tiles]
    up = [[pltpu.roll(t, 7, 0) for t in row] for row in tiles]
    out = []
    for i in range(rows):
        line = []
        for j in range(cols):
            before = down[i - 1][j] if i else 0.0
            after = up[i + 1][j] if i + 1 < rows else 0.0
            line.append(jnp.where(sub == 0, before, down[i][j]) + jnp.where(sub == 7, after, up[i][j]))
        out.append(line)
    return out


def turn_edge(tile, p, gz):
    return pltpu.roll(tile, lax.rem(8 * p + 5 - 2 * gz, LANES), 1)


def kind_at(gx, p):
    return 2 if W < p < PX - W - 1 else kind_of(gx, p)


def bulk_sweeps(fields, where, table, source, states, ends, edges, out):
    gx, gy, gz = where
    sub, lane = sub_lane()
    sb = states[0]
    for p in range(PX):
        kind = kind_at(gx, p)
        for m in range(fields):
            for i in range(CY // 8):
                rows = slice(8 * i, 8 * i + 8)
                sb[m, p, rows, :] = source(m, p, i) * (table[kind, rows, :] * (1.0 / radius_sq))
    for k in range(ITERS):
        old = states[0] if k == 0 else states[1 + (k - 1) % 2]
        new = states[1 + k % 2]
        for m in range(fields):
            edge = [jnp.zeros((8, LANES), F32)] * (CY // 8)
            for p in range(k + 1, PX - 1 - k):
                kind = kind_at(gx, p)
                mid = tiles_of(old, (m, p), CY // 8, 2)
                yy = along_rows(mid, sub)
                for i in range(CY // 8):
                    zz = along_lanes(mid[i], lane)
                    rows = slice(8 * i, 8 * i + 8)
                    for j in range(2):
                        cols = slice(LANES * j, LANES * j + LANES)
                        total = old[m, p - 1, rows, cols] + old[m, p + 1, rows, cols]
                        total = total + (yy[i][j] + zz[j])
                        value = sb[m, p, rows, cols] + table[kind, rows, cols] * total
                        if k + 1 < ITERS:
                            new[m, p, rows, cols] = value
                        else:
                            out[m, p - W, rows, cols] = value
                    side = jnp.where(gz == 0, mid[i][1], mid[i][0])
                    edge[i] = jnp.where(lane == 8 * p + 4 - gz, turn_edge(side, p, gz), edge[i])
                for j in range(2):
                    cols = slice(LANES * j, LANES * j + LANES)
                    ends[m, k, p, 0, 0:1, cols] = mid[CY // 8 - 1][j][7:8]
                    ends[m, k, p, 1, 0:1, cols] = mid[0][j][0:1]
            for i in range(CY // 8):
                edges[m, k, 8 * i : 8 * i + 8, :] = edge[i]


def strip_sweeps(fields, where, table, source, ends, states, edges, out):
    gx, gy, gz = where
    sub, lane = sub_lane()
    sb = states[0]
    wide = iota((8, CZ), 0)
    for p in range(PX):
        kind = kind_at(gx, p)
        for m in range(fields):
            halo = source(m, p) * (1.0 / radius_sq)
            sb[m, p, 0:8, :] = jnp.where(wide < 4, halo * table[kind, 0:8, :], 0.0)
            sb[m, p, 8:16, :] = jnp.where(wide < 4, 0.0, halo * table[kind, 8:16, :])
    for k in range(ITERS):
        old = states[0] if k == 0 else states[1 + (k - 1) % 2]
        new = states[1 + k % 2]
        for m in range(fields):
            edge = [jnp.zeros((8, LANES), F32)] * 2
            for p in range(k + 1, PX - 1 - k):
                kind = kind_at(gx, p)
                mid = tiles_of(old, (m, p), 2, 2)
                for i in range(2):
                    rows = slice(8 * i, 8 * i + 8)
                    zz = along_lanes(mid[i], lane)
                    for j in range(2):
                        cols = slice(LANES * j, LANES * j + LANES)
                        end = jnp.broadcast_to(ends[m, k, p, i, 0:1, cols], (8, LANES))
                        down = pltpu.roll(mid[i][j], 1, 0)
                        up = pltpu.roll(mid[i][j], 7, 0)
                        if i == 0:
                            down = jnp.where(sub == 4, 0.0, down) + jnp.where(sub == 0, end, 0.0)
                        else:
                            up = jnp.where(sub == 3, 0.0, up) + jnp.where(sub == 7, end, 0.0)
                        total = old[m, p - 1, rows, cols] + old[m, p + 1, rows, cols]
                        total = total + (down + up) + zz[j]
                        value = sb[m, p, rows, cols] + table[kind, rows, cols] * total
                        if k + 1 < ITERS:
                            new[m, p, rows, cols] = value
                        else:
                            out[m, p - W, rows, cols] = value
                    side = jnp.where(gz == 0, mid[i][1], mid[i][0])
                    edge[i] = jnp.where(lane == 8 * p + 4 - gz, turn_edge(side, p, gz), edge[i])
            for i in range(2):
                edges[m, k, 8 * i : 8 * i + 8, :] = edge[i]


def z_sweeps(m, scale, halo, bulk_edges, strip_edges):
    sub = iota((8, LANES), 0)
    column = lax.rem(iota((PY, LANES), 1), 8)
    base = halo * (scale * (1.0 / radius_sq))
    state = base
    for k in range(ITERS):
        top, bottom = strip_edges[m, k, 0:8, :], strip_edges[m, k, 8:16, :]
        own = bulk_edges[m, k]
        fed = jnp.concatenate(
            [
                own[0:8] + jnp.where(sub < 4, bottom, 0.0),
                own[8 : CY - 8],
                own[CY - 8 : CY] + jnp.where(sub < 4, 0.0, top),
                jnp.where(sub < 4, top, bottom),
            ],
            axis=0,
        )
        total = pltpu.roll(state, 8, 1) + pltpu.roll(state, LANES - 8, 1)
        total = total + pltpu.roll(state, 1, 0) + pltpu.roll(state, PY - 1, 0)
        total = total + jnp.where(column == 0, 0.0, pltpu.roll(state, 1, 1))
        total = total + jnp.where(column == 7, 0.0, pltpu.roll(state, LANES - 1, 1))
        state = base + scale * (total + fed)
    return state


def pair_tile(m, x, i, j, bulk, strips, sub):
    rows, cols = slice(8 * i, 8 * i + 8), slice(LANES * j, LANES * j + LANES)
    value = bulk[m, x, rows, cols]
    if i == 0:
        value = value + jnp.where(sub < 4, strips[m, x, 8:16, cols], 0.0)
    if i == CY // 8 - 1:
        value = value + jnp.where(sub < 4, 0.0, strips[m, x, 0:8, cols])
    return value


def z_tile(z_state, x, i):
    return pltpu.roll(z_state[8 * i : 8 * i + 8], (LANES - 4 - 8 * (x + W)) % LANES, 1)


def beside_halo(gz, lane):
    return (lane < 4 * gz), (lane >= LANES - 4 * (1 - gz))


def pack_strip(gz, tile, p, acc, lane):
    first = 8 * p + 4 * gz
    turned = pltpu.roll(tile, (8 * p + 4) % LANES, 1)
    return jnp.where((lane >= first) & (lane < first + 4), turned, acc)


def own_strip(gz, load, rows=CY):
    lane = iota((rows, LANES), 1)
    acc = jnp.zeros((rows, LANES), F32)
    for p in range(PX):
        acc = pack_strip(gz, load(p), p, acc, lane)
    return acc


def edge_tiles(gz):
    return pl.ds(pl.multiple_of((1 - gz) * LANES, LANES), LANES)


def energy_terms(prev, cur):
    (paa, pad, pda, pdd), (caa, cad, cda, cdd) = prev, cur
    u, v, w = 0, 1, 2
    aad = [cad[i] + pad[i] for i in range(3)]
    ada = [cda[i] + pda[i] for i in range(3)]
    add = [cdd[i] + pdd[i] for i in range(3)]
    daa = [caa[i] - paa[i] for i in range(3)]
    dad = [cad[i] - pad[i] for i in range(3)]
    dda = [cda[i] - pda[i] for i in range(3)]
    ddd = [cdd[i] - pdd[i] for i in range(3)]

    def sq(x):
        return x * x

    trace = sq(daa[u] + ada[v] + aad[w])
    lines = sq(dda[v] + dad[w]) + sq(dda[u] + add[w]) + sq(dad[u] + add[v])
    diag = sq(daa[u]) + sq(ada[v]) + sq(aad[w])
    shear = sq(ada[u] + daa[v]) + sq(aad[u] + daa[w]) + sq(aad[v] + ada[w])
    mixed = sq(dda[u]) + sq(dda[v]) + sq(dad[u]) + sq(dad[w]) + sq(add[v]) + sq(add[w])
    cross = sq(add[u] + dad[v]) + sq(add[u] + dda[w]) + sq(dad[v] + dda[w])
    cubic = sq(ddd[u]) + sq(ddd[v]) + sq(ddd[w])
    return (
        LAME * (trace + lines * (1.0 / 3.0))
        + SHEAR * (2.0 * diag + shear + mixed + cross * (1.0 / 3.0))
        + ((LAME + 4.0 * SHEAR) / 9.0) * cubic
    )


def y_parts(pairs):
    aa = [a0 + a1 for a0, d0, a1, d1 in pairs]
    ad = [d0 + d1 for a0, d0, a1, d1 in pairs]
    da = [a1 - a0 for a0, d0, a1, d1 in pairs]
    dd = [d1 - d0 for a0, d0, a1, d1 in pairs]
    return aa, ad, da, dd


def mass_of(parts):
    return total_of([x * x for part in parts for x in part])


def z_pair(here):
    after = pltpu.roll(here, CZ - 1, 1)
    return here + after, after - here


def own_parts(load, chunk):
    sub = iota((8, CZ), 0)
    pairs = []
    for c in range(3):
        a0, d0 = z_pair(load(c, 8 * chunk))
        following = min(chunk + 1, CY // 8 - 1)
        a1, d1 = z_pair(load(c, 8 * following))

        def next_row(t, n):
            return jnp.where(sub == 7, pltpu.roll(n, 7, 0), pltpu.roll(t, 7, 0))

        pairs.append((a0, d0, next_row(a0, a1), next_row(d0, d1)))
    return y_parts(pairs)


def pack_columns(load, lane):
    first = jnp.zeros((CY, LANES), F32)
    last = first
    for m in range(MODES):
        for c in range(3):
            for x in range(CX):
                to = 32 * m + NODES * c + x
                here = lane == to
                first = jnp.where(here, pltpu.roll(load(m, c, x, 0), to, 1), first)
                last = jnp.where(here, pltpu.roll(load(m, c, x, 1), to + 1, 1), last)
    return first, last


def with_plane8(packed, above, keep_x, last):
    cols = slice(CZ - LANES, CZ) if last else slice(0, LANES)
    rows = packed.shape[0]
    lane = iota(packed.shape, 1)
    for m in range(MODES):
        for c in range(3):
            to = 32 * m + NODES * c + CX
            turned = pltpu.roll(above[W + 3 * m + c, 0:rows, cols], to + last, 1)
            packed = jnp.where(lane == to, turned * keep_x, packed)
    return packed


def row32_of(y_above, last):
    cols = slice(CZ - LANES, CZ) if last else slice(0, LANES)
    sub, lane = sub_lane()
    tile = jnp.zeros((8, LANES), F32)
    for m in range(MODES):
        for c in range(3):
            for x in range(CX):
                to = 32 * m + NODES * c + x
                row = jnp.broadcast_to(y_above[W + 3 * m + c, x : x + 1, cols], (8, LANES))
                tile = jnp.where(lane == to, pltpu.roll(row, to + last, 1), tile)
    return jnp.where(sub == 0, tile, 0.0)


def with_row32(packed, row, from_above, keep_x, keep_y, last):
    cols = slice(CZ - LANES, CZ) if last else slice(0, LANES)
    sub, lane = sub_lane()
    for m in range(MODES):
        for c in range(3):
            to = 32 * m + NODES * c + CX
            n = 3 * m + c
            corner = jnp.broadcast_to(from_above[W - 1, n : n + 1, cols] * keep_x, (8, LANES))
            row = jnp.where((lane == to) & (sub == 0), pltpu.roll(corner, to + last, 1), row)
    return jnp.concatenate([packed, row * keep_y], axis=0)


def pack_x1(
    design, mask, modes, eigenvalues, order, src, first, second, lams, field, solid, rim, values, chosen, arrived
):
    copies = []
    for half in (slice(0, W), slice(W, CX)):
        copies.append((design.at[half], field.at[half]))
        copies.append((mask.at[half], solid.at[half]))
    for m in range(MODES):
        copies.append((modes.at[m, :, 0], rim.at[3 * m : 3 * m + 3]))
    copies += [(eigenvalues, values), (order, chosen)]
    copies = [pltpu.make_async_copy(a, b, arrived.at[n]) for n, (a, b) in enumerate(copies)]
    for copy in copies:
        copy.start()
    for copy in copies[:4]:
        copy.wait()
    for x in range(W):
        low, high = (field[p] * solid[p].astype(F32) for p in (x, x + W))
        src[x], src[x + W] = low, high
        put("gx", first, second, x, low, high)
    for copy in copies[4:]:
        copy.wait()
    first[W : W + 6] = rim[...]
    second[W : W + 6] = rim[...]
    for m in range(MODES):
        lams[m] = jnp.full((8, LANES), values[chosen[m]] * (0.125 * 0.25), F32)


def energy_kernel(modes, stiff, mass, columns):
    lane = iota((CY, LANES), 1)
    columns[0], columns[1] = pack_columns(
        lambda m, c, x, j: modes[m, c, x, :, LANES * j : LANES * j + LANES], lane
    )

    def mode_step(m, carry):
        for chunk in range(CY // 8):
            rows = slice(8 * chunk, 8 * chunk + 8)
            prev = prev_mass = None
            for x in range(CX):
                cur = own_parts(lambda c, r: modes[m, c, x, r : r + 8, :], chunk)
                cur_mass = mass_of(cur)
                if x:
                    stiff[m, x - 1, rows, :] = energy_terms(prev, cur)
                    mass[m, x - 1, rows, :] = cur_mass + prev_mass
                prev, prev_mass = cur, cur_mass
        return carry

    lax.fori_loop(0, MODES, mode_step, 0)


def pick_plane(own, above, below, p):
    if p < W:
        return below, p
    if p < W + CX:
        return own, p - W
    return above, p - W - CX


def pack_y1(src, modes, first, second):
    low = iota((8, CZ), 0) < 4
    for q in range(W):
        down = jnp.where(low, src[q, 0:8, :], pltpu.roll(src[q + W, 0:8, :], 4, 0))
        up = jnp.where(low, pltpu.roll(src[q + W, 24:32, :], 4, 0), src[q, 24:32, :])
        put("gy", first, second, q, down, up)
    for m in range(MODES):
        for c in range(3):
            for x in range(CX):
                for out in (first, second):
                    out[W + 3 * m + c, x : x + 1, :] = modes[m, c, x, 0:1, :]


def own_halo(y_above, y_below, x, lanes=slice(None)):
    a, b = y_above[x % W, :, lanes], y_below[x % W, :, lanes]
    if x >= W:
        a, b = pltpu.roll(a, 4, 0), pltpu.roll(b, 4, 0)
    return jnp.where(iota(a.shape, 0) < 4, a, b)


def pack_e1(y_first, y_second, ahead, first, second):
    y_above, y_below = neighbours("gy", y_first, y_second)
    for i in range(W - 1):
        down, up = (own_halo(y_above, y_below, x) for x in (i, CX - 1 - i))
        put("gx", first, second, i, down, up)
    for out in (first, second):
        out[W - 1] = jnp.zeros((8, CZ), F32)
        for n in range(3 * MODES):
            out[W - 1, n : n + 1, :] = y_above[W + n, 0:1, :]


def halo_tile(y_above, y_below, from_above, from_below, p, lanes=slice(None)):
    if W <= p < W + CX:
        return own_halo(y_above, y_below, p - W, lanes)
    if 0 < p < W:
        return from_below[W - 1 - p, :, lanes]
    if W + CX <= p < PX - 1:
        return from_above[p - W - CX, :, lanes]
    return jnp.zeros(y_above[0, :, lanes].shape, F32)


def bulk_kernel1(
    src, modes, columns, x_first, x_second, y_first, y_second,
    bulk, ends, edges, stiff, mass, own, rims, row32, table, sb, one, two,
):
    above, below = neighbours("gx", x_first, x_second)
    y_above, y_below = neighbours("gy", y_first, y_second)
    at = pos()
    gx, gy, gz = at
    fill_bulk(table, gy, gz)

    def source(m, p, i):
        a, at_plane = pick_plane(src, above, below, p)
        return a[at_plane, 8 * i : 8 * i + 8, :]

    bulk_sweeps(1, at, table, source, (sb, one, two), ends, edges, bulk)
    edge = edge_tiles(gz)
    own[0] = own_strip(gz, lambda p: plane_edge(src, above, below, p, edge))
    keep = jnp.where(gx < 7, 1.0, 0.0)
    for last in range(2):
        rims[last] = with_plane8(columns[last], above, keep, last)
        row32[last] = row32_of(y_above, last)
    for m in range(MODES):
        for chunk in range(CY // 8):
            rows = slice(8 * chunk, 8 * chunk + 8)
            prev = own_parts(lambda c, r: modes[m, c, CX - 1, r : r + 8, :], chunk)
            cur = own_parts(lambda c, r: above[W + 3 * m + c, r : r + 8, :] * keep, chunk)
            stiff[m, rows, :] = energy_terms(prev, cur)
            mass[m, rows, :] = mass_of(cur) + mass_of(prev)


def plane_edge(own, above, below, p, edge):
    a, i = pick_plane(own, above, below, p)
    return a[i, :, edge]


def pack_z1(own, rims, row32, y_first, y_second, e_first, e_second, out):
    gx, gy, gz = pos()
    edge = edge_tiles(gz)
    halos = (*neighbours("gy", y_first, y_second), *neighbours("gx", e_first, e_second))
    from_above = halos[2]
    out[0, 0:CY, :] = own[0]
    out[0, CY:PY, :] = own_strip(gz, lambda p: halo_tile(*halos, p, edge), 8)
    keep_x = jnp.where(gx < 7, 1.0, 0.0)
    keep_y = jnp.where(gy < 7, 1.0, 0.0)
    out[1] = with_row32(rims[0], row32[0], from_above, keep_x, keep_y, 0)


def strip_kernel1(
    modes, rims, row32, x_first, x_second, y_first, y_second, e_first, e_second, ends,
    strips, edges, rim, packed, table, sb, one, two, near, far,
):
    at = pos()
    gx, gy, gz = at
    fill_strips(table, gy, gz)
    halos = (*neighbours("gy", y_first, y_second), *neighbours("gx", e_first, e_second))
    y_above, y_below, from_above, from_below = halos
    above, below = neighbours("gx", x_first, x_second)
    strip_sweeps(
        1, at, table, lambda m, p: halo_tile(*halos, p), ends, (sb, one, two), edges, strips
    )
    keep_x = jnp.where(gx < 7, 1.0, 0.0)
    keep_y = jnp.where(gy < 7, 1.0, 0.0)
    packed[...] = with_row32(rims[1], row32[1], from_above, keep_x, keep_y, 1)
    for m in range(MODES):
        for c in range(3):
            n = 3 * m + c
            for x in range(CX):
                near[c, x : x + 1, :] = modes[m, c, x, CY - 1 : CY, :]
            near[c, CX : CX + 1, :] = above[W + n, CY - 1 : CY, :] * keep_x
            far[c, 0:CX, :] = y_above[W + n] * keep_y
            far[c, CX : CX + 1, :] = from_above[W - 1, n : n + 1, :] * (keep_x * keep_y)

        def parts(first):
            pairs = []
            for c in range(3):
                a0, d0 = z_pair(near[c, first : first + 8, :])
                a1, d1 = z_pair(far[c, first : first + 8, :])
                pairs.append((a0, d0, a1, d1))
            return y_parts(pairs)

        prev, cur = parts(0), parts(1)
        rim[m, 0] = energy_terms(prev, cur)
        rim[m, 1] = mass_of(cur) + mass_of(prev)


def raw_planes(
    planes, lams, gz, z_state, column_stiff, column_mass, bulk, strips,
    stiff, mass, stiff7, mass7, rim, store,
):
    sub, lane = sub_lane()
    beside = beside_halo(gz, lane)
    factor = 3.0 * (1.0 - stiff_floor) / 16.0
    for x in planes:
        for i in range(CY // 8):
            rows = slice(8 * i, 8 * i + 8)
            correction = z_tile(z_state, x, i)
            for j in range(2):
                cols = slice(LANES * j, LANES * j + LANES)
                phys = pair_tile(0, x, i, j, bulk, strips, sub) + jnp.where(beside[j], correction, 0.0)
                phys = (factor * phys) * phys
                for m in range(MODES):
                    if x < CX - 1:
                        k, e = stiff[m, x, rows, cols], mass[m, x, rows, cols]
                    else:
                        k, e = stiff7[m, rows, cols], mass7[m, rows, cols]
                    if i == CY // 8 - 1:
                        k = jnp.where(sub == 7, jnp.broadcast_to(rim[m, 0, x : x + 1, cols], (8, LANES)), k)
                        e = jnp.where(sub == 7, jnp.broadcast_to(rim[m, 1, x : x + 1, cols], (8, LANES)), e)
                    if j == 1:
                        by = LANES - 1 - (32 * m + x)
                        k = jnp.where(lane == LANES - 1, pltpu.roll(column_stiff[rows, :], by, 1), k)
                        e = jnp.where(lane == LANES - 1, pltpu.roll(column_mass[rows, :], by, 1), e)
                    store((x % W, m, rows, cols), phys * k - lams[m] * e)


def raw_kernel1(
    lams, z_in, packed, bulk, bulk_edges, strips, strip_edges,
    stiff, mass, stiff7, mass7, rim, low, z_parts,
):
    gx, gy, gz = pos()
    z_state = z_sweeps(0, strip_scale(gx, gy), z_in[0], bulk_edges, strip_edges)

    near, far = packed[...], z_in[1] * jnp.where(gz < 1, 1.0, 0.0)
    a0, d0 = near + far, far - near
    a1, d1 = pltpu.roll(a0, PY - 1, 0), pltpu.roll(d0, PY - 1, 0)
    parts = [(x[0][0:CY]) for x in y_parts([(a0, d0, a1, d1)])]

    def turned(t, by):
        return pltpu.roll(t, (LANES - by) % LANES, 1) if by else t

    prev = [[turned(t, NODES * c) for c in range(3)] for t in parts]
    cur = [[turned(t, NODES * c + 1) for c in range(3)] for t in parts]
    column_stiff = energy_terms(prev, cur)
    column_mass = mass_of(cur) + mass_of(prev)
    z_parts[0], z_parts[1], z_parts[2] = z_state[0:CY], column_stiff, column_mass
    raw_planes(
        range(W), lams, gz, z_state, column_stiff, column_mass, bulk, strips,
        stiff, mass, stiff7, mass7, rim, low.__setitem__,
    )


def raw_kernel2(
    lams, z_parts, bulk, strips, stiff, mass, stiff7, mass7, rim, low, high, first, second
):
    gx, gy, gz = pos()

    def store(index, value):
        high[index] = value
        put("gx", first, second, index, low[index], value)

    raw_planes(
        range(W, CX), lams, gz, z_parts[0], z_parts.at[1], z_parts.at[2], bulk, strips,
        stiff, mass, stiff7, mass7, rim, store,
    )


def raw_plane(low, high, above, below, p):
    if p < W:
        return below, p
    if p < 2 * W:
        return low, p - W
    if p < 3 * W:
        return high, p - 2 * W
    return above, p - 3 * W


def pack_y2(low, high, first, second):
    top = iota((8, CZ), 0) < 4
    for x in range(CX):
        a, i = (low, x) if x < W else (high, x - W)
        down = jnp.where(top, a[i, 0, 0:8, :], pltpu.roll(a[i, 1, 0:8, :], 4, 0))
        up = jnp.where(top, pltpu.roll(a[i, 0, 24:32, :], 4, 0), a[i, 1, 24:32, :])
        put("gy", first, second, x, down, up)


def own_raw_halo(y_above, y_below, m, x, lanes=slice(None)):
    a, b = y_above[x, :, lanes], y_below[x, :, lanes]
    if m == 0:
        b = pltpu.roll(b, 4, 0)
    else:
        a = pltpu.roll(a, 4, 0)
    return jnp.where(iota(a.shape, 0) < 4, a, b)


def pack_e2(y_first, y_second, ahead, first, second):
    y_above, y_below = neighbours("gy", y_first, y_second)
    sub = iota((8, CZ), 0)

    def merged(near, far, rows):
        moved = jnp.where(sub < 4, pltpu.roll(far, rows, 0), pltpu.roll(far, 8 - rows, 0))
        return jnp.where((sub < rows) | (sub >= 8 - rows), near, moved)

    tiles = []
    for order in (range(W - 1), range(CX - 1, CX - W, -1)):
        halo = [[own_raw_halo(y_above, y_below, m, x) for m in range(MODES)] for x in order]
        side = [merged(halo[0][m], halo[2][m], 3) for m in range(MODES)]
        tiles.append(side + [merged(halo[1][0], halo[1][1], 2)])
    for n in range(MODES + 1):
        put("gx", first, second, n, tiles[0][n], tiles[1][n])


def raw_halo(y_above, y_below, from_above, from_below, m, p, lanes=slice(None)):
    if W <= p < W + CX:
        return own_raw_halo(y_above, y_below, m, p - W, lanes)
    away, side = (W - p, from_below) if p < W else (p - W - CX + 1, from_above)
    if away == W:
        return jnp.zeros(y_above[0, :, lanes].shape, F32)
    tile = side[MODES if away == 2 else m, :, lanes]
    inwards = 3 if away == 3 else 2 * m if away == 2 else 0
    if inwards:
        sub = iota(tile.shape, 0)
        tile = jnp.where(sub < 4, pltpu.roll(tile, 8 - inwards, 0), pltpu.roll(tile, inwards, 0))
    return tile


def bulk_kernel2(m, low, high, x_first, x_second, bulk, ends, edges, own, table, sb, one, two):
    above, below = neighbours("gx", x_first, x_second)
    at = pos()
    fill_bulk(table, at[1], at[2])

    def source(_, p, i):
        a, at_plane = raw_plane(low, high, above, below, p)
        return a[at_plane, m, 8 * i : 8 * i + 8, :]

    bulk_sweeps(1, at, table, source, (sb, one, two), ends, edges, bulk)
    edge = edge_tiles(at[2])

    def load(p):
        a, i = raw_plane(low, high, above, below, p)
        return a[i, m, :, edge]

    own[0] = own_strip(at[2], load)


def pack_z2(own0, own1, y_first, y_second, e_first, e_second, out):
    gx, gy, gz = pos()
    edge = edge_tiles(gz)
    halos = (*neighbours("gy", y_first, y_second), *neighbours("gx", e_first, e_second))
    for m, own in enumerate((own0, own1)):
        out[m, 0:CY, :] = own[0]
        out[m, CY:PY, :] = own_strip(gz, lambda p, m=m: raw_halo(*halos, m, p, edge), 8)


def strip_kernel2(
    mask, y_first, y_second, e_first, e_second, ends0, ends1, bulk0, bulk1,
    out, side, edges0, edges1, table, strips0, strips1, a0, a1, b0, b1, c0, c1, held, left,
):
    gx, gy, gz = at = pos()
    halos = (*neighbours("gy", y_first, y_second), *neighbours("gx", e_first, e_second))
    sub, lane = sub_lane()
    fill_strips(table, gy, gz)
    states = ((a0, b0, c0), (a1, b1, c1))
    copies = []
    for m in range(MODES):
        ends, bulk, edges = (ends0, ends1)[m], (bulk0, bulk1)[m], (edges0, edges1)[m]
        strips = (strips0, strips1)[m]

        def source(_, p, m=m):
            return raw_halo(*halos, m, p)

        strip_sweeps(1, at, table, source, ends, states[m], edges, strips)
        for x in range(CX):
            for i in range(CY // 8):
                rows = slice(8 * i, 8 * i + 8)
                pair = []
                for j in range(2):
                    cols = slice(LANES * j, LANES * j + LANES)
                    value = pair_tile(0, x, i, j, bulk, strips, sub)
                    held[m, x, rows, cols] = value * mask[x, rows, cols].astype(F32)
                    pair.append(value)
                side[m, x, rows, :] = jnp.where(gz == 0, pair[1], pair[0])
            if x % 4 == 3:
                part = (m, slice(x - 3, x + 1))
                copy = pltpu.make_async_copy(held.at[part], out.at[part], left.at[len(copies)])
                copy.start()
                copies.append(copy)
    for copy in copies:
        copy.wait()


def final_kernel(mask, z_in, bulk_edges0, bulk_edges1, strip_edges0, strip_edges1, side, given, out, held, left):
    gx, gy, gz = pos()
    sub, lane = sub_lane()
    at_end = beside_halo(gz, lane)
    beside = at_end[0] | at_end[1]
    edge = edge_tiles(gz)
    scale = strip_scale(gx, gy)
    copies = []
    fed = ((bulk_edges0, strip_edges0), (bulk_edges1, strip_edges1))
    z_states = [z_sweeps(0, scale, z_in[m], *fed[m]) for m in range(MODES)]
    for m in range(MODES):
        z_state = z_states[m]
        for x in range(CX):
            for i in range(CY // 8):
                rows = slice(8 * i, 8 * i + 8)
                value = side[m, x, rows, :] + jnp.where(beside, z_tile(z_state, x, i), 0.0)
                held[m, x, rows, :] = value * mask[x, rows, edge].astype(F32)
            if x % 4 == 3:
                planes = slice(x - 3, x + 1)
                copy = pltpu.make_async_copy(
                    held.at[m, planes], out.at[m, planes, :, edge], left.at[len(copies)]
                )
                copy.start()
                copies.append(copy)
    for copy in copies:
        copy.wait()


def whole(x):
    return pl.BlockSpec(x.shape, lambda i: (0,) * x.ndim)


def call(kernel, name, outs, args, specs=None, out_specs=None, scratch=(), flops=0, aliases=None):
    specs = specs or {}
    shapes = tuple(jax.ShapeDtypeStruct(s, F32) for s in outs)
    out_specs = out_specs or {}
    out_specs = tuple(out_specs.get(i, whole(s)) for i, s in enumerate(shapes))
    return pl.pallas_call(
        kernel,
        grid=(1,),
        out_shape=shapes if len(shapes) > 1 else shapes[0],
        in_specs=[specs.get(i, whole(a)) for i, a in enumerate(args)],
        scratch_shapes=[pltpu.VMEM(s, F32) if isinstance(s, tuple) else s for s in scratch],
        compiler_params=pltpu.CompilerParams(vmem_limit_bytes=24 * 1024 * 1024),
        cost_estimate=pl.CostEstimate(flops=flops, bytes_accessed=2_000_000, transcendentals=0),
        name=name,
        out_specs=out_specs if len(shapes) > 1 else out_specs[0],
        input_output_aliases=aliases or {},
    )(*args)


HBM = pl.BlockSpec(memory_space=pltpu.HBM)


AXES = ("gx", "gy", "gz")
BESIDE = {"gx": "gz", "gy": "gx"}


def swap(x, axis, start):
    sizes = [lax.axis_size(a) for a in AXES]
    pairs = []
    for place in np.ndindex(*sizes):
        other = list(place)
        at = AXES.index(axis)
        other[at] += 1 if place[at] % 2 == start else -1
        if not 0 <= other[at] < sizes[at]:
            other = list(place)
            other[AXES.index(BESIDE[axis])] ^= 1
        pairs.append(tuple(int(np.ravel_multi_index(p, sizes)) for p in (place, other)))
    return lax.ppermute(x, AXES, pairs)


def swaps(axis, pair):
    first = swap(pair[0], axis, 1)
    return first, swap(pair[1], axis, 0)


def sweep_outs(fields):
    return (
        [(fields, CX, CY, CZ), (fields, ITERS, PX, 2, 1, CZ), (fields, ITERS, CY, LANES)],
        [(3, CY, CZ)] + [(fields, PX, CY, CZ)] * 3,
        [(fields, CX, 16, CZ), (fields, ITERS, 16, LANES)],
        [(3, 16, CZ)] + [(fields, PX, 16, CZ)] * 3,
    )


def local(mode_fields, design, solid_mask, eigenvalues, mode_order):
    bulk_outs, bulk_scratch, strip_outs, strip_scratch = sweep_outs(1)

    inputs = (design, solid_mask, mode_fields, eigenvalues, mode_order)
    src, first, second, lams = call(
        pack_x1, "pack_x1", [(CX, CY, CZ), (W + 6, CY, CZ), (W + 6, CY, CZ), (MODES, 8, LANES)],
        tuple(pltpu.with_memory_space_constraint(x, pltpu.HBM) for x in inputs),
        {i: HBM for i in range(5)},
        scratch=[
            (CX, CY, CZ), pltpu.VMEM((CX, CY, CZ), jnp.int32), (6, CY, CZ), pltpu.SMEM((eigenvalues.size,), F32),
            pltpu.SMEM((mode_order.size,), jnp.int32), pltpu.SemaphoreType.DMA((8,)),
        ],
    )
    x_pair = swaps("gx", (first, second))
    field = (MODES, CX - 1, CY, CZ)
    y_pair = swaps("gy", call(pack_y1, "pack_y1", [(W + 6, 8, CZ)] * 2, (src, mode_fields)))
    stiff, mass, columns = call(
        energy_kernel, "energy", [field, field, (2, CY, LANES)], (mode_fields,), flops=40_000_000
    )

    edge_pair = swaps("gx", call(pack_e1, "pack_e1", [(W, 8, CZ)] * 2, (*y_pair, columns)))
    halos = (*y_pair, *edge_pair)
    plane = (MODES, CY, CZ)
    bulk, ends, bulk_edges, stiff7, mass7, own, rims, row32 = call(
        bulk_kernel1, "bulk1",
        bulk_outs + [plane, plane, (1, CY, LANES), (2, CY, LANES), (2, 8, LANES)],
        (src, mode_fields, columns, *x_pair, *y_pair), scratch=bulk_scratch, flops=30_000_000,
    )

    z_in = swap(call(pack_z1, "pack_z1", [(2, PY, LANES)], (own, rims, row32, *halos)), "gz", 0)
    strips, strip_edges, rim, packed = call(
        strip_kernel1, "strips1", strip_outs + [(MODES, 2, 8, CZ), (PY, LANES)],
        (mode_fields, rims, row32, *x_pair, *halos, ends),
        scratch=strip_scratch + [(3, 16, CZ)] * 2, flops=20_000_000,
    )
    half = (W, MODES, CY, CZ)
    energies = (stiff, mass, stiff7, mass7, rim)
    low, z_parts = call(
        raw_kernel1, "raw1", [half, (3, CY, LANES)],
        (lams, z_in, packed, bulk, bulk_edges, strips, strip_edges, *energies),
    )
    high, first, second = call(
        raw_kernel2, "raw2", [half] * 3, (lams, z_parts, bulk, strips, *energies, low), flops=5_000_000
    )
    planes = (low, high, *swaps("gx", (first, second)))
    y_pair = swaps("gy", call(pack_y2, "pack_y2", [(CX, 8, CZ)] * 2, (low, high)))
    bulks = [
        call(
            functools.partial(bulk_kernel2, m), f"bulk2_{m}", bulk_outs + [(1, CY, LANES)], planes,
            scratch=bulk_scratch, flops=20_000_000,
        )
        for m in range(MODES)
    ]
    bulk, ends, bulk_edges, own = zip(*bulks)
    edge = (MODES + 1, 8, CZ)
    halos = (*y_pair, *swaps("gx", call(pack_e2, "pack_e2", [edge] * 2, (*y_pair, own[0]))))
    z_in = swap(call(pack_z2, "pack_z2", [(MODES, PY, LANES)], (*own, *halos)), "gz", 0)
    result = (MODES, CX, CY, CZ)
    strips, edges = strip_outs
    table, state = strip_scratch[0], strip_scratch[1]
    out, side, *strip_edges = call(
        strip_kernel2, "strips2", [result, (MODES, CX, CY, LANES), edges, edges],
        (solid_mask, *halos, *ends, *bulk), out_specs={0: HBM},
        scratch=[table, strips, strips] + [state] * 6 + [result, pltpu.SemaphoreType.DMA((4,))],
        flops=20_000_000,
    )
    return call(
        final_kernel, "final", [result],
        (solid_mask, z_in, *bulk_edges, *strip_edges, side, out), {7: HBM}, {0: HBM},
        scratch=[(MODES, CX, CY, LANES), pltpu.SemaphoreType.DMA((4,))], aliases={7: 0},
    )


def solution(mesh):
    return jax.shard_map(
        local,
        mesh=mesh,
        in_specs=(
            P(None, None, "gx", "gy", "gz"),
            P("gx", "gy", "gz"),
            P("gx", "gy", "gz"),
            P(),
            P(),
        ),
        out_specs=P(None, "gx", "gy", "gz"),
        check_vma=False,
    )
```

```python
import functools

import jax
import jax.numpy as jnp
import numpy as np
from jax import lax
from jax.experimental import pallas as pl
from jax.experimental.pallas import tpu as pltpu
from jax.sharding import PartitionSpec as P

ITERS = 4
MODES = 2
CX, CY, CZ = 8, 32, 256
W = ITERS
PX = CX + 2 * W
PY = CY + 8
NODES = CX + 1
LANES = 128

poisson = 0.3
radius_sq = 3.0
stiff_floor = 0.001
LAME = poisson / ((1.0 + poisson) * (1.0 - 2.0 * poisson))
SHEAR = 0.5 / (1.0 + poisson)

F32 = jnp.float32


def iota(shape, dim):
    return lax.broadcasted_iota(jnp.int32, shape, dim)


def pos():
    return tuple(lax.axis_index(a) for a in ("gx", "gy", "gz"))


def sub_lane():
    return iota((8, LANES), 0), iota((8, LANES), 1)


def odd(axis):
    return lax.rem(lax.axis_index(axis), 2) == 1


class Pick:
    def __init__(self, cond, yes, no):
        self.cond, self.yes, self.no = cond, yes, no

    def __getitem__(self, index):
        return jnp.where(self.cond, self.yes[index], self.no[index])


def neighbours(axis, first, second):
    cond = odd(axis)
    return Pick(cond, first, second), Pick(cond, second, first)


def put(axis, first, second, index, down, up):
    cond = odd(axis)
    first[index] = jnp.where(cond, up, down)
    second[index] = jnp.where(cond, down, up)


def total_of(terms):
    terms = [t for t in terms if t is not None]
    while len(terms) > 1:
        pairs = [terms[i] + terms[i + 1] for i in range(0, len(terms) - 1, 2)]
        terms = pairs + ([terms[-1]] if len(terms) % 2 else [])
    return terms[0]


def scales(count, inside):
    outside = jnp.zeros(count.shape, F32)
    end = jnp.where(inside, radius_sq / (1.0 + radius_sq * (count + 1.0)), 0.0)
    mid = jnp.where(inside, radius_sq / (1.0 + radius_sq * (count + 2.0)), 0.0)
    return outside, end, mid


def yz_scales(y, z, gy, gz):
    y, z = y + gy * CY, z + gz * CZ
    inside = (y >= 0) & (y < 8 * CY)
    count = 4.0
    for place, last in ((y, 8 * CY - 1), (z, 2 * CZ - 1)):
        count = count - (place == 0).astype(F32) - (place == last).astype(F32)
    return scales(count, inside)


def kind_of(gx, plane):
    x = gx * CX + plane - W
    out = (x < 0) | (x > 8 * CX - 1)
    end = (x == 0) | (x == 8 * CX - 1)
    return jnp.where(out, 0, jnp.where(end, 1, 2))


def fill_bulk(table, gy, gz):
    shape = (CY, CZ)
    for i, part in enumerate(yz_scales(iota(shape, 0), iota(shape, 1), gy, gz)):
        table[i] = part


def fill_strips(table, gy, gz):
    shape = (16, CZ)
    row = iota(shape, 0)
    top = jnp.where(row < 4, row + CY, row + CY - 8)
    bottom = jnp.where(row < 12, row - 8, row - 16)
    for i, part in enumerate(yz_scales(jnp.where(row < 8, top, bottom), iota(shape, 1), gy, gz)):
        table[i] = part


def strip_scale(gx, gy):
    shape = (PY, LANES)
    row = iota(shape, 0)
    y = jnp.where(row < CY + W, row, row - PY) + gy * CY
    x = gx * CX - W + lax.div(iota(shape, 1), 8)
    inside = (y >= 0) & (y < 8 * CY) & (x >= 0) & (x < 8 * CX)
    count = 6.0
    for place, last in ((y, 8 * CY - 1), (x, 8 * CX - 1)):
        count = count - (place == 0).astype(F32) - (place == last).astype(F32)
    return jnp.where(inside, radius_sq / (1.0 + radius_sq * count), 0.0)


def tiles_of(ref, index, rows, cols):
    return [
        [ref[index + (slice(8 * i, 8 * i + 8), slice(LANES * j, LANES * j + LANES))] for j in range(cols)]
        for i in range(rows)
    ]


def along_lanes(row, lane):
    right = [pltpu.roll(t, 1, 1) for t in row]
    left = [pltpu.roll(t, LANES - 1, 1) for t in row]
    out = []
    for j in range(len(row)):
        before = right[j - 1] if j else 0.0
        after = left[j + 1] if j + 1 < len(row) else 0.0
        out.append(
            jnp.where(lane == 0, before, right[j]) + jnp.where(lane == LANES - 1, after, left[j])
        )
    return out


def along_rows(tiles, sub):
    rows, cols = len(tiles), len(tiles[0])
    down = [[pltpu.roll(t, 1, 0) for t in row] for row in tiles]
    up = [[pltpu.roll(t, 7, 0) for t in row] for row in tiles]
    out = []
    for i in range(rows):
        line = []
        for j in range(cols):
            before = down[i - 1][j] if i else 0.0
            after = up[i + 1][j] if i + 1 < rows else 0.0
            line.append(jnp.where(sub == 0, before, down[i][j]) + jnp.where(sub == 7, after, up[i][j]))
        out.append(line)
    return out


def turn_edge(tile, p, gz):
    return pltpu.roll(tile, lax.rem(8 * p + 5 - 2 * gz, LANES), 1)


def kind_at(gx, p):
    return 2 if W < p < PX - W - 1 else kind_of(gx, p)


def bulk_sweeps(fields, where, table, source, states, ends, edges, out):
    gx, gy, gz = where
    sub, lane = sub_lane()
    sb = states[0]
    for p in range(PX):
        kind = kind_at(gx, p)
        for m in range(fields):
            for i in range(CY // 8):
                rows = slice(8 * i, 8 * i + 8)
                sb[m, p, rows, :] = source(m, p, i) * (table[kind, rows, :] * (1.0 / radius_sq))
    for k in range(ITERS):
        old = states[0] if k == 0 else states[1 + (k - 1) % 2]
        new = states[1 + k % 2]
        for m in range(fields):
            edge = [jnp.zeros((8, LANES), F32)] * (CY // 8)
            for p in range(k + 1, PX - 1 - k):
                kind = kind_at(gx, p)
                mid = tiles_of(old, (m, p), CY // 8, 2)
                yy = along_rows(mid, sub)
                for i in range(CY // 8):
                    zz = along_lanes(mid[i], lane)
                    rows = slice(8 * i, 8 * i + 8)
                    for j in range(2):
                        cols = slice(LANES * j, LANES * j + LANES)
                        total = old[m, p - 1, rows, cols] + old[m, p + 1, rows, cols]
                        total = total + (yy[i][j] + zz[j])
                        value = sb[m, p, rows, cols] + table[kind, rows, cols] * total
                        if k + 1 < ITERS:
                            new[m, p, rows, cols] = value
                        else:
                            out[m, p - W, rows, cols] = value
                    side = jnp.where(gz == 0, mid[i][1], mid[i][0])
                    edge[i] = jnp.where(lane == 8 * p + 4 - gz, turn_edge(side, p, gz), edge[i])
                for j in range(2):
                    cols = slice(LANES * j, LANES * j + LANES)
                    ends[m, k, p, 0, 0:1, cols] = mid[CY // 8 - 1][j][7:8]
                    ends[m, k, p, 1, 0:1, cols] = mid[0][j][0:1]
            for i in range(CY // 8):
                edges[m, k, 8 * i : 8 * i + 8, :] = edge[i]


def strip_sweeps(fields, where, table, source, ends, states, edges, out):
    gx, gy, gz = where
    sub, lane = sub_lane()
    sb = states[0]
    wide = iota((8, CZ), 0)
    for p in range(PX):
        kind = kind_at(gx, p)
        for m in range(fields):
            halo = source(m, p) * (1.0 / radius_sq)
            sb[m, p, 0:8, :] = jnp.where(wide < 4, halo * table[kind, 0:8, :], 0.0)
            sb[m, p, 8:16, :] = jnp.where(wide < 4, 0.0, halo * table[kind, 8:16, :])
    for k in range(ITERS):
        old = states[0] if k == 0 else states[1 + (k - 1) % 2]
        new = states[1 + k % 2]
        for m in range(fields):
            edge = [jnp.zeros((8, LANES), F32)] * 2
            for p in range(k + 1, PX - 1 - k):
                kind = kind_at(gx, p)
                mid = tiles_of(old, (m, p), 2, 2)
                for i in range(2):
                    rows = slice(8 * i, 8 * i + 8)
                    zz = along_lanes(mid[i], lane)
                    for j in range(2):
                        cols = slice(LANES * j, LANES * j + LANES)
                        end = jnp.broadcast_to(ends[m, k, p, i, 0:1, cols], (8, LANES))
                        down = pltpu.roll(mid[i][j], 1, 0)
                        up = pltpu.roll(mid[i][j], 7, 0)
                        if i == 0:
                            down = jnp.where(sub == 4, 0.0, down) + jnp.where(sub == 0, end, 0.0)
                        else:
                            up = jnp.where(sub == 3, 0.0, up) + jnp.where(sub == 7, end, 0.0)
                        total = old[m, p - 1, rows, cols] + old[m, p + 1, rows, cols]
                        total = total + (down + up) + zz[j]
                        value = sb[m, p, rows, cols] + table[kind, rows, cols] * total
                        if k + 1 < ITERS:
                            new[m, p, rows, cols] = value
                        else:
                            out[m, p - W, rows, cols] = value
                    side = jnp.where(gz == 0, mid[i][1], mid[i][0])
                    edge[i] = jnp.where(lane == 8 * p + 4 - gz, turn_edge(side, p, gz), edge[i])
            for i in range(2):
                edges[m, k, 8 * i : 8 * i + 8, :] = edge[i]


def z_sweeps(m, scale, halo, bulk_edges, strip_edges):
    sub = iota((8, LANES), 0)
    column = lax.rem(iota((PY, LANES), 1), 8)
    base = halo * (scale * (1.0 / radius_sq))
    state = base
    for k in range(ITERS):
        top, bottom = strip_edges[m, k, 0:8, :], strip_edges[m, k, 8:16, :]
        own = bulk_edges[m, k]
        fed = jnp.concatenate(
            [
                own[0:8] + jnp.where(sub < 4, bottom, 0.0),
                own[8 : CY - 8],
                own[CY - 8 : CY] + jnp.where(sub < 4, 0.0, top),
                jnp.where(sub < 4, top, bottom),
            ],
            axis=0,
        )
        total = pltpu.roll(state, 8, 1) + pltpu.roll(state, LANES - 8, 1)
        total = total + pltpu.roll(state, 1, 0) + pltpu.roll(state, PY - 1, 0)
        total = total + jnp.where(column == 0, 0.0, pltpu.roll(state, 1, 1))
        total = total + jnp.where(column == 7, 0.0, pltpu.roll(state, LANES - 1, 1))
        state = base + scale * (total + fed)
    return state


def pair_tile(m, x, i, j, bulk, strips, sub):
    rows, cols = slice(8 * i, 8 * i + 8), slice(LANES * j, LANES * j + LANES)
    value = bulk[m, x, rows, cols]
    if i == 0:
        value = value + jnp.where(sub < 4, strips[m, x, 8:16, cols], 0.0)
    if i == CY // 8 - 1:
        value = value + jnp.where(sub < 4, 0.0, strips[m, x, 0:8, cols])
    return value


def z_tile(z_state, x, i):
    return pltpu.roll(z_state[8 * i : 8 * i + 8], (LANES - 4 - 8 * (x + W)) % LANES, 1)


def beside_halo(gz, lane):
    return (lane < 4 * gz), (lane >= LANES - 4 * (1 - gz))


def pack_strip(gz, tile, p, acc, lane):
    first = 8 * p + 4 * gz
    turned = pltpu.roll(tile, (8 * p + 4) % LANES, 1)
    return jnp.where((lane >= first) & (lane < first + 4), turned, acc)


def own_strip(gz, load, rows=CY):
    lane = iota((rows, LANES), 1)
    acc = jnp.zeros((rows, LANES), F32)
    for p in range(PX):
        acc = pack_strip(gz, load(p), p, acc, lane)
    return acc


def edge_tiles(gz):
    return pl.ds(pl.multiple_of((1 - gz) * LANES, LANES), LANES)


def energy_terms(prev, cur):
    (paa, pad, pda, pdd), (caa, cad, cda, cdd) = prev, cur
    u, v, w = 0, 1, 2
    aad = [cad[i] + pad[i] for i in range(3)]
    ada = [cda[i] + pda[i] for i in range(3)]
    add = [cdd[i] + pdd[i] for i in range(3)]
    daa = [caa[i] - paa[i] for i in range(3)]
    dad = [cad[i] - pad[i] for i in range(3)]
    dda = [cda[i] - pda[i] for i in range(3)]
    ddd = [cdd[i] - pdd[i] for i in range(3)]

    def sq(x):
        return x * x

    trace = sq(daa[u] + ada[v] + aad[w])
    lines = sq(dda[v] + dad[w]) + sq(dda[u] + add[w]) + sq(dad[u] + add[v])
    diag = sq(daa[u]) + sq(ada[v]) + sq(aad[w])
    shear = sq(ada[u] + daa[v]) + sq(aad[u] + daa[w]) + sq(aad[v] + ada[w])
    mixed = sq(dda[u]) + sq(dda[v]) + sq(dad[u]) + sq(dad[w]) + sq(add[v]) + sq(add[w])
    cross = sq(add[u] + dad[v]) + sq(add[u] + dda[w]) + sq(dad[v] + dda[w])
    cubic = sq(ddd[u]) + sq(ddd[v]) + sq(ddd[w])
    return (
        LAME * (trace + lines * (1.0 / 3.0))
        + SHEAR * (2.0 * diag + shear + mixed + cross * (1.0 / 3.0))
        + ((LAME + 4.0 * SHEAR) / 9.0) * cubic
    )


def y_parts(pairs):
    aa = [a0 + a1 for a0, d0, a1, d1 in pairs]
    ad = [d0 + d1 for a0, d0, a1, d1 in pairs]
    da = [a1 - a0 for a0, d0, a1, d1 in pairs]
    dd = [d1 - d0 for a0, d0, a1, d1 in pairs]
    return aa, ad, da, dd


def mass_of(parts):
    return total_of([x * x for part in parts for x in part])


def z_pair(here):
    after = pltpu.roll(here, CZ - 1, 1)
    return here + after, after - here


def own_parts(load, chunk):
    sub = iota((8, CZ), 0)
    pairs = []
    for c in range(3):
        a0, d0 = z_pair(load(c, 8 * chunk))
        following = min(chunk + 1, CY // 8 - 1)
        a1, d1 = z_pair(load(c, 8 * following))

        def next_row(t, n):
            return jnp.where(sub == 7, pltpu.roll(n, 7, 0), pltpu.roll(t, 7, 0))

        pairs.append((a0, d0, next_row(a0, a1), next_row(d0, d1)))
    return y_parts(pairs)


def pack_columns(load, lane):
    first = jnp.zeros((CY, LANES), F32)
    last = first
    for m in range(MODES):
        for c in range(3):
            for x in range(CX):
                to = 32 * m + NODES * c + x
                here = lane == to
                first = jnp.where(here, pltpu.roll(load(m, c, x, 0), to, 1), first)
                last = jnp.where(here, pltpu.roll(load(m, c, x, 1), to + 1, 1), last)
    return first, last


def with_plane8(packed, above, keep_x, last):
    cols = slice(CZ - LANES, CZ) if last else slice(0, LANES)
    rows = packed.shape[0]
    lane = iota(packed.shape, 1)
    for m in range(MODES):
        for c in range(3):
            to = 32 * m + NODES * c + CX
            turned = pltpu.roll(above[W + 3 * m + c, 0:rows, cols], to + last, 1)
            packed = jnp.where(lane == to, turned * keep_x, packed)
    return packed


def row32_of(y_above, last):
    cols = slice(CZ - LANES, CZ) if last else slice(0, LANES)
    sub, lane = sub_lane()
    tile = jnp.zeros((8, LANES), F32)
    for m in range(MODES):
        for c in range(3):
            for x in range(CX):
                to = 32 * m + NODES * c + x
                row = jnp.broadcast_to(y_above[W + 3 * m + c, x : x + 1, cols], (8, LANES))
                tile = jnp.where(lane == to, pltpu.roll(row, to + last, 1), tile)
    return jnp.where(sub == 0, tile, 0.0)


def with_row32(packed, row, from_above, keep_x, keep_y, last):
    cols = slice(CZ - LANES, CZ) if last else slice(0, LANES)
    sub, lane = sub_lane()
    for m in range(MODES):
        for c in range(3):
            to = 32 * m + NODES * c + CX
            n = 3 * m + c
            corner = jnp.broadcast_to(from_above[W - 1, n : n + 1, cols] * keep_x, (8, LANES))
            row = jnp.where((lane == to) & (sub == 0), pltpu.roll(corner, to + last, 1), row)
    return jnp.concatenate([packed, row * keep_y], axis=0)


def pack_x1(
    design, mask, modes, eigenvalues, order, src, first, second, lams, field, solid, rim, values, chosen, arrived
):
    copies = []
    for half in (slice(0, W), slice(W, CX)):
        copies.append((design.at[half], field.at[half]))
        copies.append((mask.at[half], solid.at[half]))
    for m in range(MODES):
        copies.append((modes.at[m, :, 0], rim.at[3 * m : 3 * m + 3]))
    copies += [(eigenvalues, values), (order, chosen)]
    copies = [pltpu.make_async_copy(a, b, arrived.at[n]) for n, (a, b) in enumerate(copies)]
    for copy in copies:
        copy.start()
    for copy in copies[:4]:
        copy.wait()
    for x in range(W):
        low, high = (field[p] * solid[p].astype(F32) for p in (x, x + W))
        src[x], src[x + W] = low, high
        put("gx", first, second, x, low, high)
    for copy in copies[4:]:
        copy.wait()
    first[W : W + 6] = rim[...]
    second[W : W + 6] = rim[...]
    for m in range(MODES):
        lams[m] = jnp.full((8, LANES), values[chosen[m]] * (0.125 * 0.25), F32)


def energy_kernel(modes, stiff, mass, columns):
    lane = iota((CY, LANES), 1)
    columns[0], columns[1] = pack_columns(
        lambda m, c, x, j: modes[m, c, x, :, LANES * j : LANES * j + LANES], lane
    )

    def mode_step(m, carry):
        for chunk in range(CY // 8):
            rows = slice(8 * chunk, 8 * chunk + 8)
            prev = prev_mass = None
            for x in range(CX):
                cur = own_parts(lambda c, r: modes[m, c, x, r : r + 8, :], chunk)
                cur_mass = mass_of(cur)
                if x:
                    stiff[m, x - 1, rows, :] = energy_terms(prev, cur)
                    mass[m, x - 1, rows, :] = cur_mass + prev_mass
                prev, prev_mass = cur, cur_mass
        return carry

    lax.fori_loop(0, MODES, mode_step, 0)


def pick_plane(own, above, below, p):
    if p < W:
        return below, p
    if p < W + CX:
        return own, p - W
    return above, p - W - CX


def pack_y1(src, modes, first, second):
    low = iota((8, CZ), 0) < 4
    for q in range(W):
        down = jnp.where(low, src[q, 0:8, :], pltpu.roll(src[q + W, 0:8, :], 4, 0))
        up = jnp.where(low, pltpu.roll(src[q + W, 24:32, :], 4, 0), src[q, 24:32, :])
        put("gy", first, second, q, down, up)
    for m in range(MODES):
        for c in range(3):
            for x in range(CX):
                for out in (first, second):
                    out[W + 3 * m + c, x : x + 1, :] = modes[m, c, x, 0:1, :]


def own_halo(y_above, y_below, x, lanes=slice(None)):
    a, b = y_above[x % W, :, lanes], y_below[x % W, :, lanes]
    if x >= W:
        a, b = pltpu.roll(a, 4, 0), pltpu.roll(b, 4, 0)
    return jnp.where(iota(a.shape, 0) < 4, a, b)


def pack_e1(y_first, y_second, ahead, first, second):
    y_above, y_below = neighbours("gy", y_first, y_second)
    for i in range(W - 1):
        down, up = (own_halo(y_above, y_below, x) for x in (i, CX - 1 - i))
        put("gx", first, second, i, down, up)
    for out in (first, second):
        out[W - 1] = jnp.zeros((8, CZ), F32)
        for n in range(3 * MODES):
            out[W - 1, n : n + 1, :] = y_above[W + n, 0:1, :]


def halo_tile(y_above, y_below, from_above, from_below, p, lanes=slice(None)):
    if W <= p < W + CX:
        return own_halo(y_above, y_below, p - W, lanes)
    if 0 < p < W:
        return from_below[W - 1 - p, :, lanes]
    if W + CX <= p < PX - 1:
        return from_above[p - W - CX, :, lanes]
    return jnp.zeros(y_above[0, :, lanes].shape, F32)


def bulk_kernel1(
    src, modes, columns, x_first, x_second, y_first, y_second,
    bulk, ends, edges, stiff, mass, own, rims, row32, table, sb, one, two,
):
    above, below = neighbours("gx", x_first, x_second)
    y_above, y_below = neighbours("gy", y_first, y_second)
    at = pos()
    gx, gy, gz = at
    fill_bulk(table, gy, gz)

    def source(m, p, i):
        a, at_plane = pick_plane(src, above, below, p)
        return a[at_plane, 8 * i : 8 * i + 8, :]

    bulk_sweeps(1, at, table, source, (sb, one, two), ends, edges, bulk)
    edge = edge_tiles(gz)
    own[0] = own_strip(gz, lambda p: plane_edge(src, above, below, p, edge))
    keep = jnp.where(gx < 7, 1.0, 0.0)
    for last in range(2):
        rims[last] = with_plane8(columns[last], above, keep, last)
        row32[last] = row32_of(y_above, last)
    for m in range(MODES):
        for chunk in range(CY // 8):
            rows = slice(8 * chunk, 8 * chunk + 8)
            prev = own_parts(lambda c, r: modes[m, c, CX - 1, r : r + 8, :], chunk)
            cur = own_parts(lambda c, r: above[W + 3 * m + c, r : r + 8, :] * keep, chunk)
            stiff[m, rows, :] = energy_terms(prev, cur)
            mass[m, rows, :] = mass_of(cur) + mass_of(prev)


def plane_edge(own, above, below, p, edge):
    a, i = pick_plane(own, above, below, p)
    return a[i, :, edge]


def pack_z1(own, rims, row32, y_first, y_second, e_first, e_second, out):
    gx, gy, gz = pos()
    edge = edge_tiles(gz)
    halos = (*neighbours("gy", y_first, y_second), *neighbours("gx", e_first, e_second))
    from_above = halos[2]
    out[0, 0:CY, :] = own[0]
    out[0, CY:PY, :] = own_strip(gz, lambda p: halo_tile(*halos, p, edge), 8)
    keep_x = jnp.where(gx < 7, 1.0, 0.0)
    keep_y = jnp.where(gy < 7, 1.0, 0.0)
    out[1] = with_row32(rims[0], row32[0], from_above, keep_x, keep_y, 0)


def strip_kernel1(
    modes, rims, row32, x_first, x_second, y_first, y_second, e_first, e_second, ends,
    strips, edges, rim, packed, table, sb, one, two, near, far,
):
    at = pos()
    gx, gy, gz = at
    fill_strips(table, gy, gz)
    halos = (*neighbours("gy", y_first, y_second), *neighbours("gx", e_first, e_second))
    y_above, y_below, from_above, from_below = halos
    above, below = neighbours("gx", x_first, x_second)
    strip_sweeps(
        1, at, table, lambda m, p: halo_tile(*halos, p), ends, (sb, one, two), edges, strips
    )
    keep_x = jnp.where(gx < 7, 1.0, 0.0)
    keep_y = jnp.where(gy < 7, 1.0, 0.0)
    packed[...] = with_row32(rims[1], row32[1], from_above, keep_x, keep_y, 1)
    for m in range(MODES):
        for c in range(3):
            n = 3 * m + c
            for x in range(CX):
                near[c, x : x + 1, :] = modes[m, c, x, CY - 1 : CY, :]
            near[c, CX : CX + 1, :] = above[W + n, CY - 1 : CY, :] * keep_x
            far[c, 0:CX, :] = y_above[W + n] * keep_y
            far[c, CX : CX + 1, :] = from_above[W - 1, n : n + 1, :] * (keep_x * keep_y)

        def parts(first):
            pairs = []
            for c in range(3):
                a0, d0 = z_pair(near[c, first : first + 8, :])
                a1, d1 = z_pair(far[c, first : first + 8, :])
                pairs.append((a0, d0, a1, d1))
            return y_parts(pairs)

        prev, cur = parts(0), parts(1)
        rim[m, 0] = energy_terms(prev, cur)
        rim[m, 1] = mass_of(cur) + mass_of(prev)


def raw_planes(
    planes, lams, gz, z_state, column_stiff, column_mass, bulk, strips,
    stiff, mass, stiff7, mass7, rim, store,
):
    sub, lane = sub_lane()
    beside = beside_halo(gz, lane)
    factor = 3.0 * (1.0 - stiff_floor) / 16.0
    for x in planes:
        for i in range(CY // 8):
            rows = slice(8 * i, 8 * i + 8)
            correction = z_tile(z_state, x, i)
            for j in range(2):
                cols = slice(LANES * j, LANES * j + LANES)
                phys = pair_tile(0, x, i, j, bulk, strips, sub) + jnp.where(beside[j], correction, 0.0)
                phys = (factor * phys) * phys
                for m in range(MODES):
                    if x < CX - 1:
                        k, e = stiff[m, x, rows, cols], mass[m, x, rows, cols]
                    else:
                        k, e = stiff7[m, rows, cols], mass7[m, rows, cols]
                    if i == CY // 8 - 1:
                        k = jnp.where(sub == 7, jnp.broadcast_to(rim[m, 0, x : x + 1, cols], (8, LANES)), k)
                        e = jnp.where(sub == 7, jnp.broadcast_to(rim[m, 1, x : x + 1, cols], (8, LANES)), e)
                    if j == 1:
                        by = LANES - 1 - (32 * m + x)
                        k = jnp.where(lane == LANES - 1, pltpu.roll(column_stiff[rows, :], by, 1), k)
                        e = jnp.where(lane == LANES - 1, pltpu.roll(column_mass[rows, :], by, 1), e)
                    store((x % W, m, rows, cols), phys * k - lams[m] * e)


def raw_kernel1(
    lams, z_in, packed, bulk, bulk_edges, strips, strip_edges,
    stiff, mass, stiff7, mass7, rim, low, z_parts,
):
    gx, gy, gz = pos()
    z_state = z_sweeps(0, strip_scale(gx, gy), z_in[0], bulk_edges, strip_edges)

    near, far = packed[...], z_in[1] * jnp.where(gz < 1, 1.0, 0.0)
    a0, d0 = near + far, far - near
    a1, d1 = pltpu.roll(a0, PY - 1, 0), pltpu.roll(d0, PY - 1, 0)
    parts = [(x[0][0:CY]) for x in y_parts([(a0, d0, a1, d1)])]

    def turned(t, by):
        return pltpu.roll(t, (LANES - by) % LANES, 1) if by else t

    prev = [[turned(t, NODES * c) for c in range(3)] for t in parts]
    cur = [[turned(t, NODES * c + 1) for c in range(3)] for t in parts]
    column_stiff = energy_terms(prev, cur)
    column_mass = mass_of(cur) + mass_of(prev)
    z_parts[0], z_parts[1], z_parts[2] = z_state[0:CY], column_stiff, column_mass
    raw_planes(
        range(W), lams, gz, z_state, column_stiff, column_mass, bulk, strips,
        stiff, mass, stiff7, mass7, rim, low.__setitem__,
    )


def raw_kernel2(
    lams, z_parts, bulk, strips, stiff, mass, stiff7, mass7, rim, low, high, first, second
):
    gx, gy, gz = pos()

    def store(index, value):
        high[index] = value
        put("gx", first, second, index, low[index], value)

    raw_planes(
        range(W, CX), lams, gz, z_parts[0], z_parts.at[1], z_parts.at[2], bulk, strips,
        stiff, mass, stiff7, mass7, rim, store,
    )


def raw_plane(low, high, above, below, p):
    if p < W:
        return below, p
    if p < 2 * W:
        return low, p - W
    if p < 3 * W:
        return high, p - 2 * W
    return above, p - 3 * W


def pack_y2(low, high, first, second):
    top = iota((8, CZ), 0) < 4
    for x in range(CX):
        a, i = (low, x) if x < W else (high, x - W)
        down = jnp.where(top, a[i, 0, 0:8, :], pltpu.roll(a[i, 1, 0:8, :], 4, 0))
        up = jnp.where(top, pltpu.roll(a[i, 0, 24:32, :], 4, 0), a[i, 1, 24:32, :])
        put("gy", first, second, x, down, up)


def own_raw_halo(y_above, y_below, m, x, lanes=slice(None)):
    a, b = y_above[x, :, lanes], y_below[x, :, lanes]
    if m == 0:
        b = pltpu.roll(b, 4, 0)
    else:
        a = pltpu.roll(a, 4, 0)
    return jnp.where(iota(a.shape, 0) < 4, a, b)


def pack_e2(y_first, y_second, ahead, first, second):
    y_above, y_below = neighbours("gy", y_first, y_second)
    sub = iota((8, CZ), 0)

    def merged(near, far, rows):
        moved = jnp.where(sub < 4, pltpu.roll(far, rows, 0), pltpu.roll(far, 8 - rows, 0))
        return jnp.where((sub < rows) | (sub >= 8 - rows), near, moved)

    tiles = []
    for order in (range(W - 1), range(CX - 1, CX - W, -1)):
        halo = [[own_raw_halo(y_above, y_below, m, x) for m in range(MODES)] for x in order]
        side = [merged(halo[0][m], halo[2][m], 3) for m in range(MODES)]
        tiles.append(side + [merged(halo[1][0], halo[1][1], 2)])
    for n in range(MODES + 1):
        put("gx", first, second, n, tiles[0][n], tiles[1][n])


def raw_halo(y_above, y_below, from_above, from_below, m, p, lanes=slice(None)):
    if W <= p < W + CX:
        return own_raw_halo(y_above, y_below, m, p - W, lanes)
    away, side = (W - p, from_below) if p < W else (p - W - CX + 1, from_above)
    if away == W:
        return jnp.zeros(y_above[0, :, lanes].shape, F32)
    tile = side[MODES if away == 2 else m, :, lanes]
    inwards = 3 if away == 3 else 2 * m if away == 2 else 0
    if inwards:
        sub = iota(tile.shape, 0)
        tile = jnp.where(sub < 4, pltpu.roll(tile, 8 - inwards, 0), pltpu.roll(tile, inwards, 0))
    return tile


def bulk_kernel2(m, low, high, x_first, x_second, bulk, ends, edges, own, table, sb, one, two):
    above, below = neighbours("gx", x_first, x_second)
    at = pos()
    fill_bulk(table, at[1], at[2])

    def source(_, p, i):
        a, at_plane = raw_plane(low, high, above, below, p)
        return a[at_plane, m, 8 * i : 8 * i + 8, :]

    bulk_sweeps(1, at, table, source, (sb, one, two), ends, edges, bulk)
    edge = edge_tiles(at[2])

    def load(p):
        a, i = raw_plane(low, high, above, below, p)
        return a[i, m, :, edge]

    own[0] = own_strip(at[2], load)


def pack_z2(own0, own1, y_first, y_second, e_first, e_second, out):
    gx, gy, gz = pos()
    edge = edge_tiles(gz)
    halos = (*neighbours("gy", y_first, y_second), *neighbours("gx", e_first, e_second))
    for m, own in enumerate((own0, own1)):
        out[m, 0:CY, :] = own[0]
        out[m, CY:PY, :] = own_strip(gz, lambda p, m=m: raw_halo(*halos, m, p, edge), 8)


def strip_kernel2(
    mask, y_first, y_second, e_first, e_second, ends0, ends1, bulk0, bulk1,
    out, side, edges0, edges1, table, strips0, strips1, a0, a1, b0, b1, c0, c1, held, left,
):
    gx, gy, gz = at = pos()
    halos = (*neighbours("gy", y_first, y_second), *neighbours("gx", e_first, e_second))
    sub, lane = sub_lane()
    fill_strips(table, gy, gz)
    states = ((a0, b0, c0), (a1, b1, c1))
    copies = []
    for m in range(MODES):
        ends, bulk, edges = (ends0, ends1)[m], (bulk0, bulk1)[m], (edges0, edges1)[m]
        strips = (strips0, strips1)[m]

        def source(_, p, m=m):
            return raw_halo(*halos, m, p)

        strip_sweeps(1, at, table, source, ends, states[m], edges, strips)
        for x in range(CX):
            for i in range(CY // 8):
                rows = slice(8 * i, 8 * i + 8)
                pair = []
                for j in range(2):
                    cols = slice(LANES * j, LANES * j + LANES)
                    value = pair_tile(0, x, i, j, bulk, strips, sub)
                    held[m, x, rows, cols] = value * mask[x, rows, cols].astype(F32)
                    pair.append(value)
                side[m, x, rows, :] = jnp.where(gz == 0, pair[1], pair[0])
            if x % 4 == 3:
                part = (m, slice(x - 3, x + 1))
                copy = pltpu.make_async_copy(held.at[part], out.at[part], left.at[len(copies)])
                copy.start()
                copies.append(copy)
    for copy in copies:
        copy.wait()


def final_kernel(mask, z_in, bulk_edges0, bulk_edges1, strip_edges0, strip_edges1, side, given, out, held, left):
    gx, gy, gz = pos()
    sub, lane = sub_lane()
    at_end = beside_halo(gz, lane)
    beside = at_end[0] | at_end[1]
    edge = edge_tiles(gz)
    scale = strip_scale(gx, gy)
    copies = []
    fed = ((bulk_edges0, strip_edges0), (bulk_edges1, strip_edges1))
    z_states = [z_sweeps(0, scale, z_in[m], *fed[m]) for m in range(MODES)]
    for m in range(MODES):
        z_state = z_states[m]
        for x in range(CX):
            for i in range(CY // 8):
                rows = slice(8 * i, 8 * i + 8)
                value = side[m, x, rows, :] + jnp.where(beside, z_tile(z_state, x, i), 0.0)
                held[m, x, rows, :] = value * mask[x, rows, edge].astype(F32)
            if x % 2:
                planes = slice(x - 1, x + 1)
                copy = pltpu.make_async_copy(
                    held.at[m, planes], out.at[m, planes, :, edge], left.at[len(copies)]
                )
                copy.start()
                copies.append(copy)
    for copy in copies:
        copy.wait()


def whole(x):
    return pl.BlockSpec(x.shape, lambda i: (0,) * x.ndim)


def call(kernel, name, outs, args, specs=None, out_specs=None, scratch=(), flops=0, aliases=None):
    specs = specs or {}
    shapes = tuple(jax.ShapeDtypeStruct(s, F32) for s in outs)
    out_specs = out_specs or {}
    out_specs = tuple(out_specs.get(i, whole(s)) for i, s in enumerate(shapes))
    return pl.pallas_call(
        kernel,
        grid=(1,),
        out_shape=shapes if len(shapes) > 1 else shapes[0],
        in_specs=[specs.get(i, whole(a)) for i, a in enumerate(args)],
        scratch_shapes=[pltpu.VMEM(s, F32) if isinstance(s, tuple) else s for s in scratch],
        compiler_params=pltpu.CompilerParams(vmem_limit_bytes=24 * 1024 * 1024),
        cost_estimate=pl.CostEstimate(flops=flops, bytes_accessed=2_000_000, transcendentals=0),
        name=name,
        out_specs=out_specs if len(shapes) > 1 else out_specs[0],
        input_output_aliases=aliases or {},
    )(*args)


HBM = pl.BlockSpec(memory_space=pltpu.HBM)


AXES = ("gx", "gy", "gz")
BESIDE = {"gx": "gz", "gy": "gx"}


def swap(x, axis, start):
    sizes = [lax.axis_size(a) for a in AXES]
    pairs = []
    for place in np.ndindex(*sizes):
        other = list(place)
        at = AXES.index(axis)
        other[at] += 1 if place[at] % 2 == start else -1
        if not 0 <= other[at] < sizes[at]:
            other = list(place)
            other[AXES.index(BESIDE[axis])] ^= 1
        pairs.append(tuple(int(np.ravel_multi_index(p, sizes)) for p in (place, other)))
    return lax.ppermute(x, AXES, pairs)


def swaps(axis, pair):
    first = swap(pair[0], axis, 1)
    return first, swap(pair[1], axis, 0)


def sweep_outs(fields):
    return (
        [(fields, CX, CY, CZ), (fields, ITERS, PX, 2, 1, CZ), (fields, ITERS, CY, LANES)],
        [(3, CY, CZ)] + [(fields, PX, CY, CZ)] * 3,
        [(fields, CX, 16, CZ), (fields, ITERS, 16, LANES)],
        [(3, 16, CZ)] + [(fields, PX, 16, CZ)] * 3,
    )


def local(mode_fields, design, solid_mask, eigenvalues, mode_order):
    bulk_outs, bulk_scratch, strip_outs, strip_scratch = sweep_outs(1)

    inputs = (design, solid_mask, mode_fields, eigenvalues, mode_order)
    src, first, second, lams = call(
        pack_x1, "pack_x1", [(CX, CY, CZ), (W + 6, CY, CZ), (W + 6, CY, CZ), (MODES, 8, LANES)],
        tuple(pltpu.with_memory_space_constraint(x, pltpu.HBM) for x in inputs),
        {i: HBM for i in range(5)},
        scratch=[
            (CX, CY, CZ), pltpu.VMEM((CX, CY, CZ), jnp.int32), (6, CY, CZ), pltpu.SMEM((eigenvalues.size,), F32),
            pltpu.SMEM((mode_order.size,), jnp.int32), pltpu.SemaphoreType.DMA((8,)),
        ],
    )
    x_pair = swaps("gx", (first, second))
    field = (MODES, CX - 1, CY, CZ)
    y_pair = swaps("gy", call(pack_y1, "pack_y1", [(W + 6, 8, CZ)] * 2, (src, mode_fields)))
    stiff, mass, columns = call(
        energy_kernel, "energy", [field, field, (2, CY, LANES)], (mode_fields,), flops=40_000_000
    )

    edge_pair = swaps("gx", call(pack_e1, "pack_e1", [(W, 8, CZ)] * 2, (*y_pair, columns)))
    halos = (*y_pair, *edge_pair)
    plane = (MODES, CY, CZ)
    bulk, ends, bulk_edges, stiff7, mass7, own, rims, row32 = call(
        bulk_kernel1, "bulk1",
        bulk_outs + [plane, plane, (1, CY, LANES), (2, CY, LANES), (2, 8, LANES)],
        (src, mode_fields, columns, *x_pair, *y_pair), scratch=bulk_scratch, flops=30_000_000,
    )

    z_in = swap(call(pack_z1, "pack_z1", [(2, PY, LANES)], (own, rims, row32, *halos)), "gz", 0)
    strips, strip_edges, rim, packed = call(
        strip_kernel1, "strips1", strip_outs + [(MODES, 2, 8, CZ), (PY, LANES)],
        (mode_fields, rims, row32, *x_pair, *halos, ends),
        scratch=strip_scratch + [(3, 16, CZ)] * 2, flops=20_000_000,
    )
    half = (W, MODES, CY, CZ)
    energies = (stiff, mass, stiff7, mass7, rim)
    low, z_parts = call(
        raw_kernel1, "raw1", [half, (3, CY, LANES)],
        (lams, z_in, packed, bulk, bulk_edges, strips, strip_edges, *energies),
    )
    high, first, second = call(
        raw_kernel2, "raw2", [half] * 3, (lams, z_parts, bulk, strips, *energies, low), flops=5_000_000
    )
    planes = (low, high, *swaps("gx", (first, second)))
    y_pair = swaps("gy", call(pack_y2, "pack_y2", [(CX, 8, CZ)] * 2, (low, high)))
    bulks = [
        call(
            functools.partial(bulk_kernel2, m), f"bulk2_{m}", bulk_outs + [(1, CY, LANES)], planes,
            scratch=bulk_scratch, flops=20_000_000,
        )
        for m in range(MODES)
    ]
    bulk, ends, bulk_edges, own = zip(*bulks)
    edge = (MODES + 1, 8, CZ)
    halos = (*y_pair, *swaps("gx", call(pack_e2, "pack_e2", [edge] * 2, (*y_pair, own[0]))))
    z_in = swap(call(pack_z2, "pack_z2", [(MODES, PY, LANES)], (*own, *halos)), "gz", 0)
    result = (MODES, CX, CY, CZ)
    strips, edges = strip_outs
    table, state = strip_scratch[0], strip_scratch[1]
    out, side, *strip_edges = call(
        strip_kernel2, "strips2", [result, (MODES, CX, CY, LANES), edges, edges],
        (solid_mask, *halos, *ends, *bulk), out_specs={0: HBM},
        scratch=[table, strips, strips] + [state] * 6 + [result, pltpu.SemaphoreType.DMA((4,))],
        flops=20_000_000,
    )
    return call(
        final_kernel, "final", [result],
        (solid_mask, z_in, *bulk_edges, *strip_edges, side, out), {7: HBM}, {0: HBM},
        scratch=[(MODES, CX, CY, LANES), pltpu.SemaphoreType.DMA((8,))], aliases={7: 0},
    )


def solution(mesh):
    return jax.shard_map(
        local,
        mesh=mesh,
        in_specs=(
            P(None, None, "gx", "gy", "gz"),
            P("gx", "gy", "gz"),
            P("gx", "gy", "gz"),
            P(),
            P(),
        ),
        out_specs=P(None, "gx", "gy", "gz"),
        check_vma=False,
    )
```
